32 devices in a mesh: seq: 4 (over z), fsdp: 8 (over y, x, core).
Axes of the slice: x: 2, y: 2, z: 4, core: 2. Of those that a mesh axis runs over, the one named last changes fastest.
Arguments:
- tokens: bfloat16 [8, 1280, 2048], P('fsdp', 'seq'), may hold values from -6 to 6
- cotangent: bfloat16 [8, 1280, 2048], P('fsdp', 'seq'), may hold values from -6 to 6
- lengths: int32 [8, 3], P('fsdp'), may hold values from 1 to 1200, 1280 in all within a row
- sets: int32 [8, 3], P('fsdp'), may hold values from 0 to 7
- routes: int32 [8, 1280, 8], P('fsdp', 'seq'), may hold values from 0 to 15, all different within a row; in each aligned block of 320 rows (0 to 319, 320 to 639, ..., all dimensions but the last counted through in order) at most 200 rows name the same one
- gain_attn: float32 [2048], replicated, may hold values from 0.25 to 1.75
- gain_query: float32 [2048], replicated, may hold values from 0.25 to 1.75
- gain_key: float32 [2048], replicated, may hold values from 0.25 to 1.75
- gain_mlp: float32 [2048], replicated, may hold values from 0.25 to 1.75
- query_key_value_weight: bfloat16 [2048, 6144], P('fsdp'), may hold values from -0.125 to 0.125
- out_weight: bfloat16 [2048, 2048], P('fsdp'), may hold values from -1 to 1
- router_weight: bfloat16 [2048, 16], P('fsdp'), may hold values from -0.0625 to 0.0625
- gate_up_weight: bfloat16 [16, 2048, 2048], P('fsdp'), may hold values from -0.125 to 0.125
- down_weight: bfloat16 [16, 1024, 2048], P('fsdp'), may hold values from -0.75 to 0.75
- attention_down_factors: bfloat16 [2048, 512], P('fsdp'), may hold values from -0.125 to 0.125
- attention_up_factors: bfloat16 [512, 2048], P('fsdp'), may hold values from -1.5 to 1.5
- router_down_factors: bfloat16 [2048, 128], P('fsdp'), may hold values from -0.125 to 0.125
- router_up_factors: bfloat16 [128, 16], P('fsdp'), may hold values from -0.375 to 0.375
- expert_input_down: bfloat16 [16, 2048, 256], P('fsdp'), may hold values from -0.125 to 0.125
- expert_input_up: bfloat16 [16, 2, 128, 1024], P('fsdp'), may hold values from -1.5 to 1.5
- expert_output_down: bfloat16 [16, 1024, 128], P('fsdp'), may hold values from -0.1875 to 0.1875
- expert_output_up: bfloat16 [16, 128, 2048], P('fsdp'), may hold values from -0.75 to 0.75
Outputs:
- output: bfloat16 [8, 1280, 2048], P('fsdp', 'seq')
- grad_tokens: float32 [8, 1280, 2048], P('fsdp', 'seq')
- grad_attn_down: float32 [2048, 512], P(('seq', 'fsdp'))
- grad_attn_up: float32 [512, 2048], P(('seq', 'fsdp'))
- grad_router_down: float32 [2048, 128], P(('seq', 'fsdp'))
- grad_router_up: float32 [128, 16], P(('seq', 'fsdp'))
- grad_in_down: float32 [16, 2048, 256], P('fsdp', 'seq')
- grad_in_up: float32 [16, 2, 128, 1024], P('fsdp', None, None, 'seq')
- grad_out_down: float32 [16, 1024, 128], P('fsdp', 'seq')
- grad_out_up: float32 [16, 128, 2048], P('fsdp', None, 'seq')
The draws below stay inside these ranges and needn't reach their ends.
Inputs may be any that keep to these rules, and one draw needn't show every extreme that they name: `routes`: each row names 8 different experts; among the 320 rows of one device (aligned blocks of 320 rows) no expert is named more than 200 times, a bound that some block reaches. `lengths`: each row sums to 1280; its largest entry is exactly 1200.
All inputs are finite; a program needn't handle non-finite values.
Results may differ from the reference program's by a relative error of at most 0.019.
Values may be sent and summed in bfloat16 or wider, within the bound.
A program may use at most 384 MiB of HBM per device.

```python
import math
import jax
import jax.numpy as jnp
import numpy as np
from jax import lax

MODEL_WIDTH = 2048
H = 16
HD = 128
EXPERT_HIDDEN = 1024
TOP = 8
EXPERT_TOTAL = 16
SETS = 8
ADAPTER_RANK = 16
ADAPTER_COLUMNS = 128
TOK_DEV = 320
PACKED = 3
BLOCK = 1280
LONGEST = 1200
GROUPS = 8
CAP = 200
GROUP_CAP = 800
SCORE_ROWS = 640


def with_ends(drawn, stream_key, least, high):
    dims = drawn.shape
    index_at = [jax.random.randint(jax.random.fold_in(stream_key, axis), (), 0, dims[axis]) for axis in range(len(dims))]
    drawn = drawn.at[tuple(index_at)].set(least)
    longest = dims.index(max(dims))
    index_at[longest] = (index_at[longest] + 1) % dims[longest]
    return drawn.at[tuple(index_at)].set(high)


def steps_of(stream_key, shape, shards, smallest, largest):
    def one(dim, blocks):
        heights = jax.random.uniform(jax.random.fold_in(jax.random.fold_in(stream_key, 6), dim), (blocks,), jnp.float32, smallest / len(shards), largest / len(shards))
        return jnp.repeat(jnp.exp(heights), shape[dim] // blocks).reshape((-1,) + (1,) * (len(shape) - dim - 1))

    factor_of = one(*shards[0])
    for cut in shards[1:]:
        factor_of = factor_of * one(*cut)
    return factor_of


def split_up(count, total, most, slope):
    loads = [(1 << 20) // math.isqrt(rank ** slope) + 1 for rank in range(2, count + 1)]
    rest, given = total - most - (count - 1), [1] * (count - 1)
    while rest > 0:
        free = [i for i in range(count - 1) if given[i] < most]
        whole, budget = sum([loads[i] for i in free]), rest
        for i in free:
            more = min(most - given[i], max(1, budget * loads[i] // whole), rest)
            given[i] = given[i] + more
            rest = rest - more
    return np.array([most] + given)


def ragged(own_key, number_of, total, most, slope):
    if number_of == 2:
        one = jax.random.randint(own_key, (), max(1, total - most), min(most, total - 1) + 1)
        return jnp.stack([one, total - one])
    tallies = jnp.asarray(split_up(number_of, total, most, slope), jnp.int32)
    twos = (number_of - 1) // 2
    donor, sink = tallies[1:1 + 2 * twos:2], tallies[2:2 + 2 * twos:2]
    slack = jnp.minimum(donor - 1, most - sink)
    passed = jax.random.randint(jax.random.fold_in(own_key, 1), (twos,), 0, 1 << 20) % (slack + 1)
    tallies = tallies.at[1:1 + 2 * twos:2].set(donor - passed).at[2:2 + 2 * twos:2].set(sink + passed)
    return tallies[jax.random.permutation(jax.random.fold_in(own_key, 2), number_of)]


def deal_out(rng, own, number, rows, amount, top, reach, skew):
    order = jax.random.permutation(rng, amount)
    crowded, common = load_shares(amount, rows * top, reach, skew, True), load_shares(amount, rows * top, reach, skew, False)
    places = jnp.arange(amount)

    def named(sizes, offset_by):
        used = int((sizes > 0).sum())
        fixed = max(1, used // 4)
        moved = fixed + (places - fixed + offset_by * (used - fixed)) % max(1, amount - fixed)
        return jnp.zeros((amount,), jnp.int32).at[order[jnp.where(places < fixed, places, moved)]].set(jnp.asarray(sizes, jnp.int32))

    sizes = jnp.where(number % 4 == 0, named(crowded, number // 4), named(common, number - number // 4 - 1))
    mixed = jax.random.permutation(jax.random.fold_in(own, 3), amount)
    giver, taker = mixed[0:amount // 2 * 2:2], mixed[1:amount // 2 * 2:2]
    slack = jnp.minimum(sizes[giver] - 1, reach - sizes[taker]) // 2
    slack = jnp.where((giver == order[0]) | (taker == order[0]) | (sizes[taker] == 0), 0, jnp.maximum(slack, 0))
    moved = jax.random.randint(jax.random.fold_in(own, 4), (amount // 2,), 0, 1 << 20) % (slack + 1)
    sizes = sizes.at[giver].add(-moved).at[taker].add(moved)
    items = jnp.searchsorted(jnp.cumsum(sizes), jnp.arange(rows * top), side="right").astype(jnp.int32)
    listing = items.reshape(top, rows).T
    listing = listing[jax.random.permutation(jax.random.fold_in(own, 1), rows)]
    offset_by = jax.random.randint(jax.random.fold_in(own, 2), (rows, 1), 0, top)
    return jnp.take_along_axis(listing, (jnp.arange(top)[None, :] + offset_by) % top, axis=1)


def load_shares(count, total, limit, slope, full):
    loads = [(1 << 20) // math.isqrt(standing ** slope) + 1 for standing in range(1, count + 1)]
    largest = limit if full else min(limit, max(-(-total // count), total * loads[0] // sum(loads)))
    least = 1 if total - largest >= count - 1 else 0
    given, spare = [largest] + [least] * (count - 1), total - largest - least * (count - 1)
    while spare > 0:
        free = [i for i in range(1, count) if given[i] < largest] or [i for i in range(1, count) if given[i] < limit]
        pool, remaining = sum([loads[i] for i in free]), spare
        for i in free:
            addition = min(limit - given[i], max(1, remaining * loads[i] // pool), spare)
            given[i] = given[i] + addition
            spare = spare - addition
    return np.array(given)


def scatter_about(own_key, dims, spread, most, pieces=(), kind=jnp.bfloat16):
    values = jax.random.normal(own_key, dims, jnp.float32) * spread
    if len(pieces) > 0:
        values = steps_of(own_key, dims, pieces, -0.22, 0.18) * values
    return jnp.clip(values, min=-most, max=most).astype(kind)


def setup_inputs(seed: int = 0) -> dict:
    key_list = jax.random.split(jax.random.key(seed), 23)
    tokens = scatter_about(key_list[0], (GROUPS, BLOCK, MODEL_WIDTH), 1.0, 6.0, ((0, 8), (1, 4)))
    cotangent = scatter_about(key_list[1], (GROUPS, BLOCK, MODEL_WIDTH), 1.0, 6.0, ((0, 8), (1, 4)))
    lengths = jax.vmap(lambda own: ragged(own, PACKED, BLOCK, LONGEST, 0))(jax.random.split(key_list[2], GROUPS)).reshape((GROUPS, PACKED)).astype(jnp.int32)
    sets = with_ends(jax.random.randint(key_list[3], (GROUPS, PACKED), 0, SETS), jax.random.fold_in(key_list[3], 1), 0, SETS - 1).astype(jnp.int32)
    routes_keys = jax.random.split(jax.random.fold_in(key_list[4], 1), GROUPS * BLOCK // TOK_DEV)
    routes_turns = jax.random.permutation(jax.random.fold_in(key_list[4], 3), GROUPS * BLOCK // TOK_DEV)
    routes = jax.vmap(lambda own, number: deal_out(jax.random.fold_in(key_list[4], 2), own, number, TOK_DEV, EXPERT_TOTAL, TOP, CAP, 1))(routes_keys, routes_turns).reshape((GROUPS, BLOCK, TOP))
    gain_attn = jnp.clip(1.0 + 0.15 * jax.random.normal(key_list[5], (MODEL_WIDTH,), jnp.float32), 0.25, 1.75)
    gain_query = jnp.clip(1.0 + 0.15 * jax.random.normal(key_list[6], (MODEL_WIDTH,), jnp.float32), 0.25, 1.75)
    gain_key = jnp.clip(1.0 + 0.15 * jax.random.normal(key_list[7], (MODEL_WIDTH,), jnp.float32), 0.25, 1.75)
    gain_mlp = jnp.clip(1.0 + 0.15 * jax.random.normal(key_list[8], (MODEL_WIDTH,), jnp.float32), 0.25, 1.75)
    query_key_value_weight = scatter_about(key_list[9], (MODEL_WIDTH, 3 * MODEL_WIDTH), MODEL_WIDTH ** -0.5, 0.125, ((0, 8),))
    out_weight = scatter_about(key_list[10], (MODEL_WIDTH, MODEL_WIDTH), (MODEL_WIDTH // 64) ** -0.5, 1.0, ((0, 8),))
    router_weight = scatter_about(key_list[11], (MODEL_WIDTH, EXPERT_TOTAL), (4 * MODEL_WIDTH) ** -0.5, 0.0625, ((0, 8),))
    gate_up_weight = scatter_about(key_list[12], (EXPERT_TOTAL, MODEL_WIDTH, 2 * EXPERT_HIDDEN), MODEL_WIDTH ** -0.5, 0.125, ((0, 8),))
    down_weight = scatter_about(key_list[13], (EXPERT_TOTAL, EXPERT_HIDDEN, MODEL_WIDTH), (max(1, 16384 // (EXPERT_TOTAL * EXPERT_TOTAL))) ** -0.5, 0.75, ((0, 8),))
    attention_down_factors = scatter_about(key_list[14], (MODEL_WIDTH, 4 * ADAPTER_COLUMNS), MODEL_WIDTH ** -0.5, 0.125, ((0, 8),))
    attention_up_factors = scatter_about(key_list[15], (4 * ADAPTER_COLUMNS, MODEL_WIDTH), ADAPTER_RANK ** -0.5, 1.5, ((0, 8),))
    router_down_factors = scatter_about(key_list[16], (MODEL_WIDTH, ADAPTER_COLUMNS), MODEL_WIDTH ** -0.5, 0.125, ((0, 8),))
    router_up_factors = scatter_about(key_list[17], (ADAPTER_COLUMNS, EXPERT_TOTAL), (16 * ADAPTER_RANK) ** -0.5, 0.375, ((0, 8),))
    expert_input_down = scatter_about(key_list[18], (EXPERT_TOTAL, MODEL_WIDTH, 2 * ADAPTER_COLUMNS), MODEL_WIDTH ** -0.5, 0.125, ((0, 8),))
    expert_input_up = scatter_about(key_list[19], (EXPERT_TOTAL, 2, ADAPTER_COLUMNS, EXPERT_HIDDEN), ADAPTER_RANK ** -0.5, 1.5, ((0, 8),))
    expert_output_down = scatter_about(key_list[20], (EXPERT_TOTAL, EXPERT_HIDDEN, ADAPTER_COLUMNS), EXPERT_HIDDEN ** -0.5, 0.1875, ((0, 8),))
    expert_output_up = scatter_about(key_list[21], (EXPERT_TOTAL, ADAPTER_COLUMNS, MODEL_WIDTH), (max(1, 16384 // (EXPERT_TOTAL * EXPERT_TOTAL))) ** -0.5, 0.75, ((0, 8),))
    return dict(tokens=tokens, cotangent=cotangent, lengths=lengths, sets=sets, routes=routes, gain_attn=gain_attn, gain_query=gain_query, gain_key=gain_key, gain_mlp=gain_mlp, query_key_value_weight=query_key_value_weight, out_weight=out_weight, router_weight=router_weight, gate_up_weight=gate_up_weight, down_weight=down_weight, attention_down_factors=attention_down_factors, attention_up_factors=attention_up_factors, router_down_factors=router_down_factors, router_up_factors=router_up_factors, expert_input_down=expert_input_down, expert_input_up=expert_input_up, expert_output_down=expert_output_down, expert_output_up=expert_output_up)


EPSILON = 1e-05
THETA = 10000.0

@jax.custom_vjp
def low(v):
    return lax.optimization_barrier(v.astype(jnp.bfloat16)).astype(jnp.float32)

@jax.custom_vjp
def reduced_backward(v):
    return v

def low_keep(v):
    return (low(v), None)

def low_pass(kept, grad):
    return (grad,)

def back_keep(v):
    return (v, None)

def back_low(kept, grad):
    return (low(grad),)
low.defvjp(low_keep, low_pass)
reduced_backward.defvjp(back_keep, back_low)

def multiplier(left, right):
    return jnp.dot(left, right, precision=lax.Precision.HIGHEST)

def einsum_high(form, left, right):
    return jnp.einsum(form, left, right, precision=lax.Precision.HIGHEST)

def rms_scale(values, gain):
    return values * lax.rsqrt(lax.optimization_barrier(jnp.mean(values * values, axis=-1, keepdims=True)) + EPSILON) * gain

def rotary(values, positions):
    half = values.shape[-1] // 2
    freqs = THETA ** (-(jnp.arange(half, dtype=jnp.float32) * 2.0 / values.shape[-1]))
    angles = positions.astype(jnp.float32)[:, None] * freqs[None, :]
    cosine = jnp.cos(angles)[:, None, :]
    sine = jnp.sin(angles)[:, None, :]
    first = values[..., :half]
    second = values[..., half:]
    return jnp.concatenate([first * cosine - second * sine, second * cosine + first * sine], axis=-1)

def token_meta(lengths_row, sets_row, places):
    ends = jnp.cumsum(lengths_row, dtype=jnp.int32)
    starts = ends - lengths_row
    member = ((places[:, None] >= starts[None, :]) & (places[:, None] < ends[None, :])).astype(jnp.int32)
    seq_ids = lax.optimization_barrier(jnp.sum(member * jnp.arange(lengths_row.shape[0], dtype=jnp.int32)[None, :], axis=1, dtype=jnp.int32))
    offsets = places - lax.optimization_barrier(jnp.sum(member * starts[None, :], axis=1, dtype=jnp.int32))
    chosen = lax.optimization_barrier(jnp.sum(member * sets_row[None, :], axis=1, dtype=jnp.int32))
    return (seq_ids, offsets, chosen)

def set_mask(chosen):
    column_range = jnp.arange(ADAPTER_COLUMNS, dtype=jnp.int32) // ADAPTER_RANK
    return (chosen[..., None] == column_range).astype(jnp.float32)

def attend(queries, keys, values, seq_ids):
    scale = HD ** (-0.5)
    places = jnp.arange(BLOCK, dtype=jnp.int32)

    def one_block(start):
        rows = lax.dynamic_slice_in_dim(queries, start, SCORE_ROWS, 0)
        row_ids = lax.dynamic_slice_in_dim(seq_ids, start, SCORE_ROWS, 0)
        row_places = start + jnp.arange(SCORE_ROWS, dtype=jnp.int32)
        scores = reduced_backward(einsum_high('qhd,khd->hqk', rows, keys) * scale)
        allowed = (places[None, :] <= row_places[:, None]) & (seq_ids[None, :] == row_ids[:, None])
        scores = jnp.where(allowed[None], scores, -1e+30)
        top = lax.optimization_barrier(jnp.max(scores, axis=-1, keepdims=True))
        weights = jnp.exp(scores - top)
        probs = weights / lax.optimization_barrier(jnp.sum(weights, axis=-1, keepdims=True))
        return einsum_high('hqk,khd->qhd', low(probs), values)
    starts = jnp.arange(BLOCK // SCORE_ROWS, dtype=jnp.int32) * SCORE_ROWS
    blocks = lax.map(jax.checkpoint(one_block), starts)
    return blocks.reshape(BLOCK, H, HD)

def layer(tokens, adapters, frozen, meta):
    attention_down_factors, attention_up_factors, router_down_factors, router_up_factors, expert_input_down, expert_input_up, expert_output_down, expert_output_up = adapters
    gain_attn, gain_query, gain_key, gain_mlp, query_key_value_weight, out_weight, router_weight, gate_up_weight, down_weight = frozen
    seq_ids, offsets, chosen, routes = meta
    column_span = ADAPTER_COLUMNS
    mask = set_mask(chosen)
    normalized_input = low(rms_scale(tokens, gain_attn))
    reduced_rows = low(multiplier(normalized_input, attention_down_factors[:, :3 * column_span]) * jnp.tile(mask, (1, 3)))
    adapter_term = jnp.concatenate([multiplier(reduced_rows[:, projection_index * column_span:(projection_index + 1) * column_span], attention_up_factors[projection_index * column_span:(projection_index + 1) * column_span]) for projection_index in range(3)], axis=1)
    projection_rows = reduced_backward(multiplier(normalized_input, query_key_value_weight) + adapter_term)
    queries = rotary(rms_scale(projection_rows[:, :MODEL_WIDTH], gain_query).reshape(BLOCK, H, HD), offsets)
    keys = rotary(rms_scale(projection_rows[:, MODEL_WIDTH:2 * MODEL_WIDTH], gain_key).reshape(BLOCK, H, HD), offsets)
    values = projection_rows[:, 2 * MODEL_WIDTH:].reshape(BLOCK, H, HD)
    queries = reduced_backward(low(queries))
    keys = reduced_backward(low(keys))
    values = reduced_backward(low(values))
    attended = reduced_backward(low(attend(queries, keys, values, seq_ids).reshape(BLOCK, MODEL_WIDTH)))
    out_lower = low(multiplier(attended, attention_down_factors[:, 3 * column_span:]) * mask)
    branch = reduced_backward(multiplier(attended, out_weight) + multiplier(out_lower, attention_up_factors[3 * column_span:]))
    middle = tokens + branch
    normed2 = low(rms_scale(middle, gain_mlp))
    router_lower = low(multiplier(normed2, router_down_factors) * mask)
    logits = multiplier(normed2, router_weight) + multiplier(router_lower, router_up_factors)
    probs = jax.nn.softmax(logits, axis=-1)
    gates = jnp.take_along_axis(probs, routes, axis=1)
    rows_total = BLOCK * TOP
    flat = routes.reshape(-1)
    hits = (flat[:, None] == jnp.arange(EXPERT_TOTAL, dtype=jnp.int32)[None, :]).astype(jnp.int32)
    ranks = lax.optimization_barrier(jnp.sum((jnp.cumsum(hits, axis=0, dtype=jnp.int32) - hits) * hits, axis=1, dtype=jnp.int32))
    table = jnp.full((EXPERT_TOTAL, GROUP_CAP), rows_total, jnp.int32).at[flat, ranks].set(jnp.arange(rows_total, dtype=jnp.int32))
    copies = reduced_backward(jnp.broadcast_to(normed2[:, None, :], (BLOCK, TOP, MODEL_WIDTH))).reshape(rows_total, MODEL_WIDTH)
    padded = jnp.concatenate([copies, jnp.zeros((1, MODEL_WIDTH), jnp.float32)], axis=0)
    taken = padded[table]
    row_sets = jnp.concatenate([jnp.repeat(chosen, TOP), jnp.full((1,), SETS, jnp.int32)])[table]
    row_mask = set_mask(row_sets)
    gate_up = einsum_high('ecd,edf->ecf', taken, gate_up_weight)
    lower_in = reduced_backward(low(einsum_high('ecd,edr->ecr', taken, expert_input_down) * jnp.concatenate([row_mask, row_mask], axis=-1)))
    gate_part = reduced_backward(gate_up[..., :EXPERT_HIDDEN] + einsum_high('ecr,erf->ecf', lower_in[..., :column_span], expert_input_up[:, 0]))
    up_part = reduced_backward(gate_up[..., EXPERT_HIDDEN:] + einsum_high('ecr,erf->ecf', lower_in[..., column_span:], expert_input_up[:, 1]))
    hidden = low(jax.nn.silu(gate_part) * up_part)
    lower_out = reduced_backward(low(einsum_high('ecf,efr->ecr', hidden, expert_output_down) * row_mask))
    result = reduced_backward(low(einsum_high('ecf,efd->ecd', hidden, down_weight) + einsum_high('ecr,erd->ecd', lower_out, expert_output_up)))
    returned = jnp.zeros((rows_total + 1, MODEL_WIDTH), jnp.float32).at[table].add(result)[:rows_total].reshape(BLOCK, TOP, MODEL_WIDTH)
    mixed = lax.optimization_barrier(jnp.sum(gates[:, :, None] * returned, axis=1))
    return middle + mixed

def reference(tokens, cotangent, lengths, sets, routes, gain_attn, gain_query, gain_key, gain_mlp, query_key_value_weight, out_weight, router_weight, gate_up_weight, down_weight, attention_down_factors, attention_up_factors, router_down_factors, router_up_factors, expert_input_down, expert_input_up, expert_output_down, expert_output_up):
    frozen = tuple((item.astype(jnp.float32) for item in (gain_attn, gain_query, gain_key, gain_mlp, query_key_value_weight, out_weight, router_weight, gate_up_weight, down_weight)))
    adapters = tuple((item.astype(jnp.float32) for item in (attention_down_factors, attention_up_factors, router_down_factors, router_up_factors, expert_input_down, expert_input_up, expert_output_down, expert_output_up)))
    places = jnp.arange(BLOCK, dtype=jnp.int32)

    def group_step(totals, inputs):
        block_tokens, block_cot, block_lengths, block_sets, block_routes = inputs
        seq_ids, offsets, chosen = token_meta(block_lengths, block_sets, places)
        meta = (seq_ids, offsets, chosen, block_routes)

        def forward(tok_in, adapt_in):
            return layer(tok_in, adapt_in, frozen, meta)
        outputs, pullback = jax.vjp(forward, block_tokens.astype(jnp.float32), adapters)
        grad_in, grad_adapt = pullback(block_cot.astype(jnp.float32))
        totals = jax.tree.map(lambda first, second: first + second, totals, grad_adapt)
        return (totals, (outputs.astype(jnp.bfloat16), grad_in))
    zeros = jax.tree.map(jnp.zeros_like, adapters)
    totals, stacked = lax.scan(group_step, zeros, (tokens, cotangent, lengths, sets, routes))
    return (stacked[0], stacked[1], totals[0], totals[1], totals[2], totals[3], totals[4], totals[5], totals[6], totals[7])
```

```python
import functools

import jax
import jax.numpy as jnp
from jax import lax
from jax.experimental import pallas as pl
from jax.experimental.pallas import tpu as pltpu
from jax.sharding import Mesh
from jax.sharding import PartitionSpec as P

MODEL_WIDTH = 2048
H = 16
HD = 128
EXPERT_HIDDEN = 1024
TOP = 8
EXP_DEV = 2
ADAPTER_RANK = 16
SPAN = 128
GROUPS = 4
GROUP_WIDTH = MODEL_WIDTH // GROUPS
HEADS = H // GROUPS

EPSILON = 1e-05
THETA = 10000.0
NEGATIVE = -1e30
BF = jnp.bfloat16
F32 = jnp.float32
ANY = pl.ANY
VMEM = pltpu.VMEM
SEQ = ("zh", "zl")
FSDP = ("c", "core")


def mm(left, right):
    return lax.dot_general(left, right, (((1,), (0,)), ((), ())), preferred_element_type=F32)


def mm_t(left, right):
    return lax.dot_general(left, right, (((1,), (1,)), ((), ())), preferred_element_type=F32)


def t_mm(left, right):
    return lax.dot_general(left, right, (((0,), (0,)), ((), ())), preferred_element_type=F32)


def exact(form, left, right):
    return jnp.einsum(form, left, right, precision=lax.Precision.HIGHEST, preferred_element_type=F32)


def rms_scale(values, gain):
    return values * lax.rsqrt(jnp.mean(values * values, axis=-1, keepdims=True) + EPSILON) * gain


def rms_back(values, gain, grad):
    inverse = lax.rsqrt(jnp.mean(values * values, axis=-1, keepdims=True) + EPSILON)
    scaled = grad * gain
    return inverse * scaled - values * inverse * inverse * inverse * jnp.mean(
        values * scaled, axis=-1, keepdims=True
    )


def token_meta(lengths_row, sets_row, places):
    count = lengths_row.shape[0]
    running = [lengths_row[0]]
    for n in range(1, count):
        running.append(running[-1] + lengths_row[n])
    ends = jnp.stack(running)
    starts = ends - lengths_row
    member = ((places[:, None] >= starts[None, :]) & (places[:, None] < ends[None, :])).astype(
        jnp.int32
    )
    seq_ids = jnp.sum(member * jnp.arange(count, dtype=jnp.int32)[None, :], axis=1)
    offsets = places - jnp.sum(member * starts[None, :], axis=1)
    chosen = jnp.sum(member * sets_row[None, :], axis=1)
    return (seq_ids, offsets, chosen)


def set_mask(chosen):
    column_range = jnp.arange(SPAN, dtype=jnp.int32) // ADAPTER_RANK
    return (chosen[..., None] == column_range).astype(F32)


def here():
    return tuple(lax.axis_index(n) for n in ("zh", "zl", "c", "core"))


def signal_all(peers):
    barrier = pltpu.get_barrier_semaphore()
    for peer in peers:
        pl.semaphore_signal(barrier, inc=1, device_id=peer, device_id_type=pl.DeviceIdType.MESH)
    pl.semaphore_wait(barrier, len(peers))


def remote(src, dst, send, recv, device):
    return pltpu.make_async_remote_copy(
        src_ref=src,
        dst_ref=dst,
        send_sem=send,
        recv_sem=recv,
        device_id=device,
        device_id_type=pl.DeviceIdType.MESH,
    )


def column_peers(zh, zl, c, core):
    return [
        (zh ^ a, zl ^ b, c, core ^ k)
        for a in range(2)
        for b in range(2)
        for k in range(2)
        if (a, b, k) != (0, 0, 0)
    ]


def gather_kernel(n_c, x_ref, w_ref, xg_ref, wg_ref, xs, xr, fs, fr, ws, wr, own):
    zh, zl, c, core = here()
    tok = x_ref.shape[0]
    half = tok // 2
    rows = w_ref.shape[0]
    plane = [(zh, zl, lax.rem(c + i, n_c), core ^ k) for i in range(n_c) for k in range(2)][2:]
    signal_all(column_peers(zh, zl, c, core) + plane)
    me = zh * 2 + zl
    for a in range(2):
        for k in range(2):
            piece = pl.ds(k * half, half)
            src, dst = x_ref.at[piece], xg_ref.at[me, piece]
            is_self = (core == zh) & (zl == a) & (core == k)

            @pl.when(is_self)
            def _():
                pltpu.make_async_copy(src, dst, xr.at[me]).start()

            @pl.when(jnp.logical_not(is_self))
            def _():
                remote(src, dst, xs.at[a, k], xr.at[me], (core, a, c, k)).start()

    f = c * 2 + core
    row_block = pl.ds(pl.multiple_of(f * rows, rows), rows)

    def pieces(group):
        for j in range(3):
            start = pl.multiple_of(j * MODEL_WIDTH + group * GROUP_WIDTH, GROUP_WIDTH)
            yield (
                w_ref.at[:, pl.ds(start, GROUP_WIDTH)],
                wg_ref.at[row_block, pl.ds(j * GROUP_WIDTH, GROUP_WIDTH)],
            )

    for src, dst in pieces(zl * 2 + core):
        pltpu.make_async_copy(src, dst, own).start()
    slots = [(i, k) for i in range(n_c) for k in range(2)][1:]
    for i, k in slots:
        target_c, target_core = lax.rem(c + i, n_c), core ^ k
        for src, dst in pieces(zl * 2 + target_core):
            remote(
                src, dst, ws.at[i * 2 + k], wr.at[i * 2 + k], (zh, zl, target_c, target_core)
            ).start()
    mine = pl.ds(pl.multiple_of(core * half, half), half)
    theirs = pl.ds(pl.multiple_of((1 - core) * half, half), half)
    sibling = (zh, zl, c, 1 - core)
    order = [zl ^ 0, zl ^ 1]
    for s in range(4):
        pltpu.make_async_copy(xg_ref.at[s, mine], xg_ref.at[s, mine], xr.at[s]).wait()
        remote(xg_ref.at[s, mine], xg_ref.at[s, mine], fs.at[s], fr.at[s], sibling).start()
    for s in range(4):
        got = xg_ref.at[s, theirs]
        pltpu.make_async_copy(got, got, fr.at[s]).wait()
    for s in range(4):
        got = xg_ref.at[s, mine]
        pltpu.make_async_copy(got, got, fs.at[s]).wait()
    for a in range(2):
        for k in range(2):
            is_self = (core == zh) & (zl == a) & (core == k)
            src = x_ref.at[pl.ds(k * half, half)]

            @pl.when(jnp.logical_not(is_self))
            def _():
                pltpu.make_async_copy(src, src, xs.at[a, k]).wait()

    block = wg_ref.at[row_block]
    pltpu.make_async_copy(block, block, own).wait()
    for i, k in slots:
        pltpu.make_async_copy(block, block, ws.at[i * 2 + k]).wait()
        source = lax.rem(c + n_c - i, n_c) * 2 + (core ^ k)
        got = wg_ref.at[pl.ds(pl.multiple_of(source * rows, rows), rows)]
        pltpu.make_async_copy(got, got, wr.at[i * 2 + k]).wait()


def gather_to_heads(x, w, n_c):
    tok, rows = x.shape[0], w.shape[0]
    n_f = 2 * n_c
    dma = pltpu.SemaphoreType.DMA
    return pl.pallas_call(
        functools.partial(gather_kernel, n_c),
        out_shape=(
            jax.ShapeDtypeStruct((4, tok, MODEL_WIDTH), BF),
            jax.ShapeDtypeStruct((n_f * rows, 3 * GROUP_WIDTH), BF),
        ),
        in_specs=[pl.BlockSpec(memory_space=ANY)] * 2,
        out_specs=[pl.BlockSpec(memory_space=ANY)] * 2,
        scratch_shapes=[
            dma((2, 2)),
            dma((4,)),
            dma((4,)),
            dma((4,)),
            dma((n_f,)),
            dma((n_f,)),
            dma,
        ],
        compiler_params=pltpu.CompilerParams(collective_id=0, has_side_effects=True),
        name="gather_to_heads",
    )(x, w)


def to_tokens_kernel(a_ref, o_ref, send, recv):
    zh, zl, c, core = here()
    signal_all(column_peers(zh, zl, c, core))
    group = zl * 2 + core
    columns = pl.ds(pl.multiple_of(group * GROUP_WIDTH, GROUP_WIDTH), GROUP_WIDTH)
    for s in range(4):
        a, b = s // 2, s % 2
        is_self = (a == zh) & (b == zl) & (core == zh)
        src, dst = a_ref.at[s], o_ref.at[:, columns]

        @pl.when(is_self)
        def _():
            pltpu.make_async_copy(src, dst, recv.at[group]).start()

        @pl.when(jnp.logical_not(is_self))
        def _():
            remote(src, dst, send.at[s], recv.at[group], (a, b, c, zh)).start()

    for s in range(4):
        a, b = s // 2, s % 2
        is_self = (a == zh) & (b == zl) & (core == zh)
        got = o_ref.at[:, pl.ds(s * GROUP_WIDTH, GROUP_WIDTH)]
        pltpu.make_async_copy(got, got, recv.at[s]).wait()

        @pl.when(jnp.logical_not(is_self))
        def _():
            pltpu.make_async_copy(a_ref.at[s], a_ref.at[s], send.at[s]).wait()


def to_tokens(rows):
    tok = rows.shape[1]
    dma = pltpu.SemaphoreType.DMA
    return pl.pallas_call(
        to_tokens_kernel,
        out_shape=jax.ShapeDtypeStruct((tok, MODEL_WIDTH), BF),
        in_specs=[pl.BlockSpec(memory_space=ANY)],
        out_specs=pl.BlockSpec(memory_space=ANY),
        scratch_shapes=[dma((4,)), dma((4,))],
        compiler_params=pltpu.CompilerParams(collective_id=1, has_side_effects=True),
        name="to_tokens",
    )(rows)


def to_heads_kernel(a_ref, o_ref, send, recv):
    zh, zl, c, core = here()
    signal_all(column_peers(zh, zl, c, core))
    me = zh * 2 + zl
    for g in range(4):
        b, k = g // 2, g % 2
        is_self = (core == zh) & (b == zl) & (core == k)
        src, dst = a_ref.at[:, pl.ds(g * GROUP_WIDTH, GROUP_WIDTH)], o_ref.at[me]

        @pl.when(is_self)
        def _():
            pltpu.make_async_copy(src, dst, recv.at[me]).start()

        @pl.when(jnp.logical_not(is_self))
        def _():
            remote(src, dst, send.at[g], recv.at[me], (core, b, c, k)).start()

    for g in range(4):
        b, k = g // 2, g % 2
        is_self = (core == zh) & (b == zl) & (core == k)
        pltpu.make_async_copy(o_ref.at[g], o_ref.at[g], recv.at[g]).wait()

        @pl.when(jnp.logical_not(is_self))
        def _():
            pltpu.make_async_copy(o_ref.at[g], o_ref.at[g], send.at[g]).wait()


def to_heads(rows):
    tok = rows.shape[0]
    dma = pltpu.SemaphoreType.DMA
    return pl.pallas_call(
        to_heads_kernel,
        out_shape=jax.ShapeDtypeStruct((4, tok, GROUP_WIDTH), BF),
        in_specs=[pl.BlockSpec(memory_space=ANY)],
        out_specs=pl.BlockSpec(memory_space=ANY),
        scratch_shapes=[dma((4,)), dma((4,))],
        compiler_params=pltpu.CompilerParams(collective_id=2, has_side_effects=True),
        name="to_heads",
    )(rows)


def sum_to_tokens_kernel(p_ref, o_ref, sib, chip, rx, ss, sr, send, recv):
    zh, zl, c, core = here()
    signal_all(column_peers(zh, zl, c, core))
    width = o_ref.shape[1]
    half = width // 2
    sibling = (zh, zl, c, 1 - core)
    mine = pl.ds(pl.multiple_of(core * half, half), half)
    theirs = pl.ds(pl.multiple_of((1 - core) * half, half), half)
    for s in range(4):
        remote(p_ref.at[s, :, theirs], sib.at[s], ss.at[s], sr.at[s], sibling).start()

    def is_self(s):
        return (s // 2 == zh) & (s % 2 == zl) & (core == zh)

    for s in range(4):
        pltpu.make_async_copy(sib.at[s], sib.at[s], sr.at[s]).wait()
        chip[s] = (p_ref[s, :, mine].astype(F32) + sib[s].astype(F32)).astype(BF)
        src, dst = chip.at[s], rx.at[zl, core]

        @pl.when(is_self(s))
        def _():
            pltpu.make_async_copy(src, dst, recv.at[zl, core]).start()

        @pl.when(jnp.logical_not(is_self(s)))
        def _():
            remote(src, dst, send.at[s], recv.at[zl, core], (s // 2, s % 2, c, zh)).start()

    for s in range(4):
        pltpu.make_async_copy(sib.at[s], sib.at[s], ss.at[s]).wait()

        @pl.when(jnp.logical_not(is_self(s)))
        def _():
            pltpu.make_async_copy(chip.at[s], chip.at[s], send.at[s]).wait()

    for k in range(2):
        for b in range(2):
            pltpu.make_async_copy(rx.at[b, k], rx.at[b, k], recv.at[b, k]).wait()
        o_ref[:, k * half : (k + 1) * half] = rx[0, k].astype(F32) + rx[1, k].astype(F32)


def sum_to_tokens(parts):
    _, tok, width = parts.shape
    half = width // 2
    dma = pltpu.SemaphoreType.DMA
    return pl.pallas_call(
        sum_to_tokens_kernel,
        out_shape=jax.ShapeDtypeStruct((tok, width), F32),
        in_specs=[pl.BlockSpec(memory_space=VMEM)],
        out_specs=pl.BlockSpec(memory_space=VMEM),
        scratch_shapes=[
            VMEM((4, tok, half), BF),
            VMEM((4, tok, half), BF),
            VMEM((2, 2, tok, half), BF),
            dma((4,)),
            dma((4,)),
            dma((4,)),
            dma((2, 2)),
        ],
        compiler_params=pltpu.CompilerParams(
            collective_id=3, has_side_effects=True, vmem_limit_bytes=40 * 2**20
        ),
        name="sum_to_tokens",
    )(parts)


def group_sum_kernel(x_ref, o_ref, rx, send, recv):
    zh, zl, c, core = here()
    peers = [(zh, zl, c, 1 - core), (zh, 1 - zl, c, core), (zh, 1 - zl, c, 1 - core)]
    signal_all(peers)
    copies = [remote(x_ref, rx.at[i], send.at[i], recv.at[i], p) for i, p in enumerate(peers)]
    for copy in copies:
        copy.start()
    for copy in copies:
        copy.wait()
    o_ref[...] = (x_ref[...] + rx[0]) + (rx[1] + rx[2])


def group_sum(values, identity):
    dma = pltpu.SemaphoreType.DMA
    return pl.pallas_call(
        group_sum_kernel,
        out_shape=jax.ShapeDtypeStruct(values.shape, F32),
        in_specs=[pl.BlockSpec(memory_space=VMEM)],
        out_specs=pl.BlockSpec(memory_space=VMEM),
        scratch_shapes=[VMEM((3, *values.shape), F32), dma((3,)), dma((3,))],
        compiler_params=pltpu.CompilerParams(collective_id=identity, has_side_effects=True),
        name="group_sum",
    )(values)


def turn(values, cosine, sine):
    return values * cosine + pltpu.roll(values, HD // 2, 1) * sine


def attention_rows(block):
    return 256 if block % 256 == 0 else block


def attend_kernel(
    pq, pk, pv, rq, rk, gq, gk, cosine, sine, seg_c, seg_r, q_ref, k_ref, v_ref, o_ref, lse_ref
):
    block = pq.shape[0]
    rows = attention_rows(block)
    scale = HD**-0.5
    q_ref[...] = turn(pq[...] * rq[...] * gq[...], cosine[...], sine[...]).astype(BF)
    k_ref[...] = turn(pk[...] * rk[...] * gk[...], cosine[...], sine[...]).astype(BF)
    v_ref[...] = pv[...].astype(BF)
    for i in range(block // rows):
        length = (i + 1) * rows
        own = slice(i * rows, length)
        scores = mm_t(q_ref[own], k_ref[:length]) * scale
        row = lax.broadcasted_iota(jnp.int32, (rows, length), 0) + i * rows
        column = lax.broadcasted_iota(jnp.int32, (rows, length), 1)
        allowed = (seg_c[own] == seg_r[:, :length]) & (column <= row)
        scores = jnp.where(allowed, scores, NEGATIVE)
        top = jnp.max(scores, axis=1, keepdims=True)
        weights = jnp.exp(scores - top)
        total = jnp.sum(weights, axis=1, keepdims=True)
        out = mm(weights.astype(BF), v_ref[:length]) / total
        o_ref[own] = out.astype(BF)
        lse_ref[0, own] = top + jnp.log(total)


def attend(projected, rq, rk, gq, gk, cosine, sine, seg_c, seg_r):
    block = projected.shape[0]
    head = lambda off: pl.BlockSpec((block, HD), lambda h: (0, off + h))
    gain = pl.BlockSpec((1, HD), lambda h: (0, h))
    fixed = lambda shape: pl.BlockSpec(shape, lambda h: (0, 0))
    wide = jax.ShapeDtypeStruct((block, GROUP_WIDTH), BF)
    return pl.pallas_call(
        attend_kernel,
        grid=(HEADS,),
        out_shape=(wide, wide, wide, wide, jax.ShapeDtypeStruct((HEADS, block, 1), F32)),
        in_specs=[
            head(0),
            head(HEADS),
            head(2 * HEADS),
            fixed((block, 1)),
            fixed((block, 1)),
            gain,
            gain,
            fixed((block, HD)),
            fixed((block, HD)),
            fixed((block, 1)),
            fixed((1, block)),
        ],
        out_specs=[head(0)] * 4 + [pl.BlockSpec((1, block, 1), lambda h: (h, 0, 0))],
        compiler_params=pltpu.CompilerParams(vmem_limit_bytes=60 * 2**20),
        name="attend",
    )(projected, projected, projected, rq, rk, gq, gk, cosine, sine, seg_c, seg_r)


def attend_back_kernel(
    q_ref,
    k_ref,
    v_ref,
    g_ref,
    lse_ref,
    pq,
    pk,
    gq,
    gk,
    cosine,
    sine,
    seg_c,
    seg_r,
    uq_ref,
    uk_ref,
    dv_ref,
    mq_ref,
    mk_ref,
    dk_acc,
    dv_acc,
):
    block = q_ref.shape[0]
    rows = attention_rows(block)
    scale = HD**-0.5
    dk_acc[...] = jnp.zeros_like(dk_acc)
    dv_acc[...] = jnp.zeros_like(dv_acc)

    def back(grad, raw, gain):
        turned = turn(grad.astype(BF).astype(F32), cosine_of, -sine_of)
        return turned, jnp.sum(raw * gain[...] * turned, axis=1, keepdims=True)

    for i in range(block // rows):
        length = (i + 1) * rows
        own = slice(i * rows, length)
        scores = mm_t(q_ref[own], k_ref[:length]) * scale
        row = lax.broadcasted_iota(jnp.int32, (rows, length), 0) + i * rows
        column = lax.broadcasted_iota(jnp.int32, (rows, length), 1)
        allowed = (seg_c[own] == seg_r[:, :length]) & (column <= row)
        probs = jnp.where(allowed, jnp.exp(scores - lse_ref[0, own]), 0.0)
        grad_probs = mm_t(g_ref[own], v_ref[:length])
        delta = jnp.sum(probs * grad_probs, axis=1, keepdims=True)
        grad_scores = (probs * (grad_probs - delta)).astype(BF)
        grad_q = mm(grad_scores, k_ref[:length]) * scale
        cosine_of, sine_of = cosine[own], sine[own]
        turned, moment = back(grad_q, pq[own], gq)
        uq_ref[own] = turned
        mq_ref[0, own] = moment
        dk_acc[:length] += t_mm(grad_scores, q_ref[own])
        dv_acc[:length] += t_mm(probs.astype(BF), g_ref[own])
    cosine_of, sine_of = cosine[...], sine[...]
    turned, moment = back(dk_acc[...] * scale, pk[...], gk)
    uk_ref[...] = turned
    mk_ref[0] = moment
    dv_ref[...] = dv_acc[...].astype(BF)


def attend_back(q, k, v, grad, lse, projected, gq, gk, cosine, sine, seg_c, seg_r):
    block = q.shape[0]
    head = lambda off: pl.BlockSpec((block, HD), lambda h: (0, off + h))
    gain = pl.BlockSpec((1, HD), lambda h: (0, h))
    fixed = lambda shape: pl.BlockSpec(shape, lambda h: (0, 0))
    column = pl.BlockSpec((1, block, 1), lambda h: (h, 0, 0))
    wide = lambda t: jax.ShapeDtypeStruct((block, GROUP_WIDTH), t)
    moment = jax.ShapeDtypeStruct((HEADS, block, 1), F32)
    return pl.pallas_call(
        attend_back_kernel,
        grid=(HEADS,),
        out_shape=(wide(F32), wide(F32), wide(BF), moment, moment),
        in_specs=[
            head(0),
            head(0),
            head(0),
            head(0),
            column,
            head(0),
            head(HEADS),
            gain,
            gain,
            fixed((block, HD)),
            fixed((block, HD)),
            fixed((block, 1)),
            fixed((1, block)),
        ],
        out_specs=[head(0)] * 3 + [column] * 2,
        scratch_shapes=[VMEM((block, HD), F32), VMEM((block, HD), F32)],
        compiler_params=pltpu.CompilerParams(vmem_limit_bytes=60 * 2**20),
        name="attend_back",
    )(q, k, v, grad, lse, projected, projected, gq, gk, cosine, sine, seg_c, seg_r)


WEIGHTS = 6


def experts_kernel(
    experts,
    slots,
    x_ref,
    g_ref,
    *refs,
):
    hbm = refs[:WEIGHTS]
    out_ref, row_ref = refs[WEIGHTS : WEIGHTS + 2]
    gid, giu, god, gou = refs[WEIGHTS + 2 : WEIGHTS + 6]
    w_gu, w_d, w_id, w_iu, w_od, w_ou, sems = refs[WEIGHTS + 6 :]
    held = (w_gu, w_d, w_id, w_iu, w_od, w_ou)
    tile, e = pl.program_id(0), pl.program_id(1)
    last_tile = pl.num_programs(0) - 1
    sources, tok = x_ref.shape[0], x_ref.shape[1]
    extra = x_ref.shape[2] - MODEL_WIDTH

    def load(n, expert):
        return pltpu.make_async_copy(hbm[n].at[expert], held[n], sems.at[n])

    first = (tile == 0) & (e == 0)
    more = jnp.logical_not((tile == last_tile) & (e == EXP_DEV - 1))
    following = lax.rem(e + 1, EXP_DEV)

    @pl.when(first)
    def _():
        for n in range(WEIGHTS):
            load(n, 0).start()
        for ref in (gid, giu, god, gou):
            ref[...] = jnp.zeros_like(ref)

    def refill(*names):
        @pl.when(more)
        def _():
            for n in names:
                load(n, following).start()

    number = lax.axis_index("c") * (2 * EXP_DEV) + lax.axis_index("core") * EXP_DEV + e
    lane = lax.broadcasted_iota(jnp.int32, (tok, extra), 1)
    slot = lax.broadcasted_iota(jnp.int32, (tok, slots), 1).astype(F32)
    pick, gate = [], []
    rows, grads, masks = [], [], []
    for d in range(sources):
        side = x_ref[d, :, MODEL_WIDTH:].astype(F32)
        read = lambda which: jnp.sum(jnp.where(which, side, 0.0), axis=1, keepdims=True)
        place = read(lane == number)
        gate_d = read((lane == experts + number) | (lane == 2 * experts + number))
        chosen = read(lane == 3 * experts)
        columns = (lax.broadcasted_iota(jnp.int32, (tok, SPAN), 1) // ADAPTER_RANK).astype(F32)
        mask_d = jnp.where(columns == chosen, 1.0, 0.0).astype(BF)
        pick_d = jnp.where(slot == place, 1.0, 0.0).astype(BF)
        pick.append(pick_d)
        gate.append(gate_d)
        rows.append(t_mm(pick_d, x_ref[d, :, :MODEL_WIDTH]))
        grads.append(t_mm(pick_d, (gate_d * g_ref[d].astype(F32)).astype(BF)))
        masks.append(t_mm(pick_d, mask_d))
    x = jnp.concatenate(rows, axis=0).astype(BF)
    grad = jnp.concatenate(grads, axis=0).astype(BF)
    mask = jnp.concatenate(masks, axis=0)
    mask2 = jnp.concatenate([mask, mask], axis=1)
    for n in range(WEIGHTS):
        load(n, e).wait()
    lower_in = (mm(x, w_id[...]) * mask2).astype(BF)
    lower_g, lower_u = lower_in[:, :SPAN], lower_in[:, SPAN:]
    gate_part = mm(x, w_gu[:, :EXPERT_HIDDEN]) + mm(lower_g, w_iu[0])
    up_part = mm(x, w_gu[:, EXPERT_HIDDEN:]) + mm(lower_u, w_iu[1])
    sigmoid = 1.0 / (1.0 + jnp.exp(-gate_part))
    activated = gate_part * sigmoid
    hidden = (activated * up_part).astype(BF)
    lower_out = (mm(hidden, w_od[...]) * mask).astype(BF)
    result = (mm(hidden, w_d[...]) + mm(lower_out, w_ou[...])).astype(BF).astype(F32)
    moments = []
    for d in range(sources):
        back = mm(pick[d], result[d * slots : (d + 1) * slots].astype(BF))
        moments.append(jnp.sum(back * g_ref[d].astype(F32), axis=1, keepdims=True))
        back = back * gate[d]

        @pl.when(e == 0)
        def _():
            out_ref[d] = back.astype(BF)

        @pl.when(e > 0)
        def _():
            out_ref[d] = (out_ref[d].astype(F32) + back).astype(BF)

    grad_lower_out = (mm_t(grad, w_ou[...]) * mask).astype(BF)
    grad_hidden = mm_t(grad, w_d[...]) + mm_t(grad_lower_out, w_od[...])
    refill(1, 4, 5)
    grad_up = (grad_hidden * activated).astype(BF)
    grad_gate = (
        grad_hidden * up_part * sigmoid * (1.0 + gate_part * (1.0 - sigmoid))
    ).astype(BF)
    grad_lower_in = (
        jnp.concatenate([mm_t(grad_gate, w_iu[0]), mm_t(grad_up, w_iu[1])], axis=1) * mask2
    ).astype(BF)
    grad_rows = (
        mm_t(grad_gate, w_gu[:, :EXPERT_HIDDEN])
        + mm_t(grad_up, w_gu[:, EXPERT_HIDDEN:])
        + mm_t(grad_lower_in, w_id[...])
    ).astype(BF).astype(F32)
    refill(0, 2, 3)
    for d in range(sources):
        back = mm(pick[d], grad_rows[d * slots : (d + 1) * slots].astype(BF))
        high = moments[d].astype(BF).astype(F32)
        low = moments[d] - high
        side = jnp.where(lane == number, high, 0.0) + jnp.where(lane == experts + number, low, 0.0)

        @pl.when(e == 0)
        def _():
            row_ref[d, :, :MODEL_WIDTH] = back.astype(BF)
            row_ref[d, :, MODEL_WIDTH:] = side.astype(BF)

        @pl.when(e > 0)
        def _():
            row_ref[d, :, :MODEL_WIDTH] = (row_ref[d, :, :MODEL_WIDTH].astype(F32) + back).astype(BF)
            row_ref[d, :, MODEL_WIDTH:] = (row_ref[d, :, MODEL_WIDTH:].astype(F32) + side).astype(BF)

    gid[e] += t_mm(x, grad_lower_in)
    giu[e, 0] += t_mm(lower_g, grad_gate)
    giu[e, 1] += t_mm(lower_u, grad_up)
    god[e] += t_mm(hidden, grad_lower_out)
    gou[e] += t_mm(lower_out, grad)


def run_experts(x, g, weights, experts, slots):
    sources, tok, wide = x.shape
    pair = 2
    grid = (sources // pair, EXP_DEV)
    by_tile = lambda w: pl.BlockSpec((pair, tok, w), lambda t, e: (t, 0, 0))
    shapes = (
        (EXP_DEV, MODEL_WIDTH, 2 * SPAN),
        (EXP_DEV, 2, SPAN, EXPERT_HIDDEN),
        (EXP_DEV, EXPERT_HIDDEN, SPAN),
        (EXP_DEV, SPAN, MODEL_WIDTH),
    )
    whole = [
        pl.BlockSpec(s, lambda t, e, n=len(s): (0,) * n, pipeline_mode=pl.Buffered(1))
        for s in shapes
    ]
    flops = 2 * sources * EXP_DEV * slots * MODEL_WIDTH * EXPERT_HIDDEN * 8
    return pl.pallas_call(
        functools.partial(experts_kernel, experts, slots),
        grid=grid,
        out_shape=(
            jax.ShapeDtypeStruct((sources, tok, MODEL_WIDTH), BF),
            jax.ShapeDtypeStruct((sources, tok, wide), BF),
            *(jax.ShapeDtypeStruct(s, F32) for s in shapes),
        ),
        in_specs=[by_tile(wide), by_tile(MODEL_WIDTH)]
        + [pl.BlockSpec(memory_space=ANY)] * WEIGHTS,
        out_specs=[by_tile(MODEL_WIDTH), by_tile(wide), *whole],
        scratch_shapes=[VMEM(w.shape[1:], BF) for w in weights]
        + [pltpu.SemaphoreType.DMA((WEIGHTS,))],
        compiler_params=pltpu.CompilerParams(vmem_limit_bytes=63 * 2**20),
        cost_estimate=pl.CostEstimate(flops=flops, bytes_accessed=10**8, transcendentals=10**7),
        name="experts",
    )(x, g, *weights)


def on_device(
    tokens,
    cotangent,
    lengths,
    sets,
    routes,
    gain_attn,
    gain_query,
    gain_key,
    gain_mlp,
    query_key_value_weight,
    out_weight,
    router_weight,
    gate_up_weight,
    down_weight,
    attention_down_factors,
    attention_up_factors,
    router_down_factors,
    router_up_factors,
    expert_input_down,
    expert_input_up,
    expert_output_down,
    expert_output_up,
):
    zh, zl, c, core = here()
    n_c = lax.axis_size("c")
    n_fsdp = 2 * n_c
    n_seq = lax.axis_size("zh") * lax.axis_size("zl")
    tok = tokens.shape[1]
    block = tok * n_seq
    experts = EXP_DEV * n_fsdp
    capacity = 5 * tok * TOP // (4 * experts)
    slots = -(-capacity // 8) * 8
    extra = -(-(3 * experts + 1) // 128) * 128
    span3 = 3 * SPAN
    group = zl * 2 + core
    shard = zh * 2 + zl

    both_lengths = lax.all_gather(
        jnp.concatenate([lengths[0], sets[0]]), "core", axis=0, tiled=False
    )
    held_lengths = lax.dynamic_index_in_dim(both_lengths, zh, 0, keepdims=False)
    count = lengths.shape[1]

    inputs = tokens[0].astype(F32)
    normalized = rms_scale(inputs, gain_attn).astype(BF)
    x_shards, qkv_rows = gather_to_heads(normalized, query_key_value_weight, n_c)

    rows_local = query_key_value_weight.shape[0]
    factors = jnp.concatenate(
        [
            attention_down_factors,
            attention_up_factors.reshape(rows_local, -1),
            router_down_factors,
            router_weight,
            router_up_factors.reshape(rows_local, -1),
        ],
        axis=1,
    )
    factor_width = factors.shape[1]
    factors = jnp.pad(factors, ((0, 0), (0, -factor_width % 128)))
    factors = lax.all_gather(factors, FSDP, axis=0, tiled=True)
    up_columns = attention_up_factors.size // rows_local
    down_full = factors[:, : 4 * SPAN]
    at = 4 * SPAN
    up_full = factors[:, at : at + up_columns].reshape(4 * SPAN, MODEL_WIDTH)
    at += up_columns
    rdown_full = factors[:, at : at + SPAN]
    at += SPAN
    router_full = factors[:, at : at + experts]
    at += experts
    rup_full = factors[:, at:factor_width].reshape(SPAN, experts)
    out_full = lax.all_gather(out_weight, FSDP, axis=0, tiled=True)
    grad_rows_all = lax.all_gather(cotangent[0], FSDP, axis=0, tiled=True)

    seq_local, _, chosen = token_meta(
        lengths[0], sets[0], shard * tok + jnp.arange(tok, dtype=jnp.int32)
    )
    mask = set_mask(chosen)
    seq_block, block_offsets, block_sets = token_meta(
        held_lengths[:count], held_lengths[count:], jnp.arange(block, dtype=jnp.int32)
    )
    mask3 = jnp.tile(set_mask(block_sets), (1, 3))
    half = HD // 2
    freqs = THETA ** (-(jnp.arange(half, dtype=F32) * 2.0 / HD))
    angles = block_offsets.astype(F32)[:, None] * freqs[None, :]
    cosine, sine = jnp.cos(angles), jnp.sin(angles)
    cosine = jnp.concatenate([cosine, cosine], axis=1)
    sine = jnp.concatenate([-sine, sine], axis=1)
    seg_c, seg_r = seq_block[:, None], seq_block[None, :]

    x_all = x_shards.reshape(block, MODEL_WIDTH)
    down3 = down_full[:, :span3]
    lowered = (mm(x_all, down3) * mask3).astype(BF)
    up_own = lax.dynamic_slice_in_dim(up_full[:span3], group * GROUP_WIDTH, GROUP_WIDTH, 1)
    none = jnp.zeros((SPAN, GROUP_WIDTH), BF)
    up_diagonal = jnp.concatenate(
        [
            jnp.concatenate(
                [up_own[j * SPAN : (j + 1) * SPAN] if i == j else none for i in range(3)], axis=1
            )
            for j in range(3)
        ],
        axis=0,
    )
    projected = mm(x_all, qkv_rows) + mm(lowered, up_diagonal)
    part_q, part_k = projected[:, :GROUP_WIDTH], projected[:, GROUP_WIDTH : 2 * GROUP_WIDTH]

    def over_group(first, second, identity):
        both = jnp.stack([first, second]).reshape(-1, 128)
        return group_sum(both, identity).reshape(2, block)

    squares = over_group(jnp.sum(part_q * part_q, axis=1), jnp.sum(part_k * part_k, axis=1), 4)
    inverse = lax.rsqrt(squares / MODEL_WIDTH + EPSILON)
    rq, rk = inverse[0][:, None], inverse[1][:, None]
    gains = [
        lax.dynamic_slice_in_dim(g, group * GROUP_WIDTH, GROUP_WIDTH)[None, :]
        for g in (gain_query, gain_key)
    ]
    q, k, v, attended_heads, lse = attend(
        projected, rq, rk, *gains, cosine, sine, seg_c, seg_r
    )
    attended = to_tokens(attended_heads.reshape(4, tok, GROUP_WIDTH))

    down_o, up_o = down_full[:, span3:], up_full[span3:]
    out_lower = (mm(attended, down_o) * mask).astype(BF)
    branch = mm(attended, out_full) + mm(out_lower, up_o)
    middle = inputs + branch
    normed2 = rms_scale(middle, gain_mlp).astype(BF)
    router_lower = (mm(normed2, rdown_full) * mask).astype(BF)
    logits = mm(normed2, router_full) + mm(router_lower, rup_full)
    probs = jax.nn.softmax(logits, axis=-1)
    hits = jnp.sum(
        (routes[0][:, :, None] == jnp.arange(experts, dtype=jnp.int32)[None, None, :]).astype(F32),
        axis=1,
    )
    place = jnp.arange(tok, dtype=jnp.int32)
    before = (place[None, :] < place[:, None]).astype(BF)
    ranks = jnp.where(hits > 0, mm(before, hits.astype(BF)), -1.0).astype(BF)
    gates = hits * probs
    gates_high = gates.astype(BF)
    gates_low = (gates - gates_high.astype(F32)).astype(BF)
    side = jnp.concatenate(
        [ranks, gates_high, gates_low, chosen.astype(BF)[:, None]], axis=1
    )
    payload = jnp.concatenate(
        [normed2, jnp.pad(side, ((0, 0), (0, extra - side.shape[1])))], axis=1
    )
    rows_all = lax.all_gather(payload, FSDP, axis=0, tiled=True)
    weights = (
        gate_up_weight,
        down_weight,
        expert_input_down,
        expert_input_up,
        expert_output_down,
        expert_output_up,
    )
    out_parts, row_parts, *expert_terms = run_experts(
        rows_all.reshape(n_fsdp, tok, MODEL_WIDTH + extra),
        grad_rows_all.reshape(n_fsdp, tok, MODEL_WIDTH),
        weights,
        experts,
        slots,
    )
    returned = lax.psum_scatter(
        row_parts.reshape(n_fsdp * tok, -1), FSDP, scatter_dimension=0, tiled=True
    )
    mixed = lax.psum_scatter(
        out_parts.reshape(n_fsdp * tok, -1), FSDP, scatter_dimension=0, tiled=True
    )
    output = (middle + mixed.astype(F32)).astype(BF)

    grad_out = cotangent[0].astype(F32)
    returned = returned.astype(F32)
    back = returned[:, MODEL_WIDTH:]
    grad_probs = back[:, :experts] + back[:, experts : 2 * experts]
    grad_logits = probs * (grad_probs - jnp.sum(probs * grad_probs, axis=-1, keepdims=True))
    grad_router_lower = exact("te,re->tr", grad_logits, rup_full.astype(F32)) * mask
    grad_normed2 = (
        returned[:, :MODEL_WIDTH]
        + mm_t(grad_logits.astype(BF), router_full)
        + mm_t(grad_router_lower.astype(BF), rdown_full)
    )
    grad_rup = t_mm(router_lower, grad_logits.astype(BF))
    grad_rdown = t_mm(normed2, grad_router_lower.astype(BF))
    grad_middle = grad_out + rms_back(middle, gain_mlp, grad_normed2)
    grad_branch = grad_middle.astype(BF)
    grad_out_lower = (mm_t(grad_branch, up_o) * mask).astype(BF)
    grad_attended = (mm_t(grad_branch, out_full) + mm_t(grad_out_lower, down_o)).astype(BF)
    head_grad = to_heads(grad_attended).reshape(block, GROUP_WIDTH)
    grad_up_o = t_mm(out_lower, grad_branch)
    grad_down_o = t_mm(attended, grad_out_lower)

    uq, uk, grad_v, mq, mk = attend_back(
        q, k, v, head_grad, lse, projected, *gains, cosine, sine, seg_c, seg_r
    )
    moments = over_group(jnp.sum(mq[..., 0], axis=0), jnp.sum(mk[..., 0], axis=0), 5) / MODEL_WIDTH

    def rms_inner(values, scale, gain, turned, moment):
        return (scale * gain * turned - values * (scale * scale * scale) * moment).astype(BF)

    grad_projected = jnp.concatenate(
        [
            rms_inner(part_q, rq, gains[0], uq, moments[0][:, None]),
            rms_inner(part_k, rk, gains[1], uk, moments[1][:, None]),
            grad_v,
        ],
        axis=1,
    )
    grad_lowered = (mm_t(grad_projected, up_diagonal) * mask3).astype(BF)
    grad_up_own = [
        t_mm(
            lowered[:, j * SPAN : (j + 1) * SPAN],
            grad_projected[:, j * GROUP_WIDTH : (j + 1) * GROUP_WIDTH],
        )
        for j in range(3)
    ]
    grad_down_qkv = t_mm(x_all, grad_lowered)
    grad_normed_part = (mm_t(grad_projected, qkv_rows) + mm_t(grad_lowered, down3)).astype(BF)
    grad_normed = sum_to_tokens(grad_normed_part.reshape(4, tok, MODEL_WIDTH))
    grad_inputs = grad_middle + rms_back(inputs, gain_attn, grad_normed)

    grad_down_all = jnp.concatenate([grad_down_qkv, grad_down_o], axis=1).astype(BF)
    wide_up = lax.dynamic_update_slice_in_dim(
        jnp.zeros((span3, MODEL_WIDTH), F32),
        jnp.concatenate(grad_up_own, axis=0),
        group * GROUP_WIDTH,
        1,
    )
    grad_up_all = jnp.concatenate([wide_up, grad_up_o], axis=0).astype(BF)
    terms = (grad_down_all, grad_up_all, grad_rdown.astype(BF), grad_rup.astype(BF))
    own_shapes = [(t.shape[0] // (n_seq * n_fsdp), t.shape[1]) for t in terms]
    flat = jnp.concatenate(
        [t.reshape(n_seq, n_fsdp, -1).transpose(1, 0, 2) for t in terms], axis=2
    )
    used = flat.shape[2]
    flat = jnp.pad(flat, ((0, 0), (0, 0), (0, -used % 1024))).reshape(n_fsdp * n_seq, -1, 128)
    flat = lax.psum_scatter(flat, FSDP, scatter_dimension=0, tiled=True)
    flat = lax.psum_scatter(flat, SEQ, scatter_dimension=0, tiled=True).astype(F32).reshape(-1)
    summed, at = [], 0
    for shape in own_shapes:
        size = shape[0] * shape[1]
        summed.append(flat[at : at + size].reshape(shape))
        at += size
    expert_sums = [
        lax.psum_scatter(t.astype(BF), SEQ, scatter_dimension=d, tiled=True).astype(F32)
        for t, d in zip(expert_terms, (1, 3, 1, 2), strict=True)
    ]
    return (output[None], grad_inputs[None], *summed, *expert_sums)


def solution(mesh):
    n_seq, n_fsdp = mesh.shape["seq"], mesh.shape["fsdp"]
    fine = Mesh(
        mesh.devices.reshape(2, n_seq // 2, n_fsdp // 2, 2), ("zh", "zl", "c", "core")
    )
    split = P(FSDP, SEQ, None)
    rows = P(FSDP, None)
    three = P(FSDP, None, None)
    in_specs = (
        split,
        split,
        rows,
        rows,
        split,
        P(),
        P(),
        P(),
        P(),
        rows,
        rows,
        rows,
        three,
        three,
        rows,
        rows,
        rows,
        rows,
        three,
        P(FSDP, None, None, None),
        three,
        three,
    )
    owners = P((*SEQ, *FSDP), None)
    out_specs = (
        split,
        split,
        owners,
        owners,
        owners,
        owners,
        split,
        P(FSDP, None, None, SEQ),
        split,
        P(FSDP, None, SEQ),
    )
    return jax.shard_map(
        on_device, mesh=fine, in_specs=in_specs, out_specs=out_specs, check_vma=False
    )
```

```python
import functools

import jax
import jax.numpy as jnp
from jax import lax
from jax.experimental import pallas as pl
from jax.experimental.pallas import tpu as pltpu
from jax.sharding import Mesh
from jax.sharding import PartitionSpec as P

MODEL_WIDTH = 2048
H = 16
HD = 128
EXPERT_HIDDEN = 1024
TOP = 8
EXP_DEV = 2
ADAPTER_RANK = 16
SPAN = 128
GROUPS = 4
GROUP_WIDTH = MODEL_WIDTH // GROUPS
HEADS = H // GROUPS

EPSILON = 1e-05
THETA = 10000.0
NEGATIVE = -1e30
BF = jnp.bfloat16
F32 = jnp.float32
ANY = pl.ANY
VMEM = pltpu.VMEM
SEQ = ("zh", "zl")
FSDP = ("c", "core")


def mm(left, right):
    return lax.dot_general(left, right, (((1,), (0,)), ((), ())), preferred_element_type=F32)


def mm_t(left, right):
    return lax.dot_general(left, right, (((1,), (1,)), ((), ())), preferred_element_type=F32)


def t_mm(left, right):
    return lax.dot_general(left, right, (((0,), (0,)), ((), ())), preferred_element_type=F32)


def exact(form, left, right):
    return jnp.einsum(form, left, right, precision=lax.Precision.HIGHEST, preferred_element_type=F32)


def rms_scale(values, gain):
    return values * lax.rsqrt(jnp.mean(values * values, axis=-1, keepdims=True) + EPSILON) * gain


def rms_back(values, gain, grad):
    inverse = lax.rsqrt(jnp.mean(values * values, axis=-1, keepdims=True) + EPSILON)
    scaled = grad * gain
    return inverse * scaled - values * inverse * inverse * inverse * jnp.mean(
        values * scaled, axis=-1, keepdims=True
    )


def token_meta(lengths_row, sets_row, places):
    count = lengths_row.shape[0]
    running = [lengths_row[0]]
    for n in range(1, count):
        running.append(running[-1] + lengths_row[n])
    ends = jnp.stack(running)
    starts = ends - lengths_row
    member = ((places[:, None] >= starts[None, :]) & (places[:, None] < ends[None, :])).astype(
        jnp.int32
    )
    seq_ids = jnp.sum(member * jnp.arange(count, dtype=jnp.int32)[None, :], axis=1)
    offsets = places - jnp.sum(member * starts[None, :], axis=1)
    chosen = jnp.sum(member * sets_row[None, :], axis=1)
    return (seq_ids, offsets, chosen)


def set_mask(chosen):
    column_range = jnp.arange(SPAN, dtype=jnp.int32) // ADAPTER_RANK
    return (chosen[..., None] == column_range).astype(F32)


def here():
    return tuple(lax.axis_index(n) for n in ("zh", "zl", "c", "core"))


def signal_all(peers):
    barrier = pltpu.get_barrier_semaphore()
    for peer in peers:
        pl.semaphore_signal(barrier, inc=1, device_id=peer, device_id_type=pl.DeviceIdType.MESH)
    pl.semaphore_wait(barrier, len(peers))


def remote(src, dst, send, recv, device):
    return pltpu.make_async_remote_copy(
        src_ref=src,
        dst_ref=dst,
        send_sem=send,
        recv_sem=recv,
        device_id=device,
        device_id_type=pl.DeviceIdType.MESH,
    )


def column_peers(zh, zl, c, core):
    return [
        (zh ^ a, zl ^ b, c, core ^ k)
        for a in range(2)
        for b in range(2)
        for k in range(2)
        if (a, b, k) != (0, 0, 0)
    ]


def gather_kernel(n_c, x_ref, w_ref, xg_ref, wg_ref, xs, xr, fs, fr, ws, wr, own):
    zh, zl, c, core = here()
    tok = x_ref.shape[0]
    half = tok // 2
    rows = w_ref.shape[0]
    plane = [(zh, zl, lax.rem(c + i, n_c), core ^ k) for i in range(n_c) for k in range(2)][2:]
    signal_all(column_peers(zh, zl, c, core) + plane)
    me = zh * 2 + zl
    for a in range(2):
        for k in range(2):
            piece = pl.ds(k * half, half)
            src, dst = x_ref.at[piece], xg_ref.at[me, piece]
            is_self = (core == zh) & (zl == a) & (core == k)

            @pl.when(is_self)
            def _():
                pltpu.make_async_copy(src, dst, xr.at[me]).start()

            @pl.when(jnp.logical_not(is_self))
            def _():
                remote(src, dst, xs.at[a, k], xr.at[me], (core, a, c, k)).start()

    f = c * 2 + core
    row_block = pl.ds(pl.multiple_of(f * rows, rows), rows)

    def pieces(group):
        for j in range(3):
            start = pl.multiple_of(j * MODEL_WIDTH + group * GROUP_WIDTH, GROUP_WIDTH)
            yield (
                w_ref.at[:, pl.ds(start, GROUP_WIDTH)],
                wg_ref.at[row_block, pl.ds(j * GROUP_WIDTH, GROUP_WIDTH)],
            )

    for src, dst in pieces(zl * 2 + core):
        pltpu.make_async_copy(src, dst, own).start()
    slots = [(i, k) for i in range(n_c) for k in range(2)][1:]
    for i, k in slots:
        target_c, target_core = lax.rem(c + i, n_c), core ^ k
        for src, dst in pieces(zl * 2 + target_core):
            remote(
                src, dst, ws.at[i * 2 + k], wr.at[i * 2 + k], (zh, zl, target_c, target_core)
            ).start()
    mine = pl.ds(pl.multiple_of(core * half, half), half)
    theirs = pl.ds(pl.multiple_of((1 - core) * half, half), half)
    sibling = (zh, zl, c, 1 - core)
    for s in range(4):
        pltpu.make_async_copy(xg_ref.at[s, mine], xg_ref.at[s, mine], xr.at[s]).wait()
        remote(xg_ref.at[s, mine], xg_ref.at[s, mine], fs.at[s], fr.at[s], sibling).start()
    for s in range(4):
        got = xg_ref.at[s, theirs]
        pltpu.make_async_copy(got, got, fr.at[s]).wait()
    for s in range(4):
        got = xg_ref.at[s, mine]
        pltpu.make_async_copy(got, got, fs.at[s]).wait()
    for a in range(2):
        for k in range(2):
            is_self = (core == zh) & (zl == a) & (core == k)
            src = x_ref.at[pl.ds(k * half, half)]

            @pl.when(jnp.logical_not(is_self))
            def _():
                pltpu.make_async_copy(src, src, xs.at[a, k]).wait()

    block = wg_ref.at[row_block]
    pltpu.make_async_copy(block, block, own).wait()
    for i, k in slots:
        pltpu.make_async_copy(block, block, ws.at[i * 2 + k]).wait()
        source = lax.rem(c + n_c - i, n_c) * 2 + (core ^ k)
        got = wg_ref.at[pl.ds(pl.multiple_of(source * rows, rows), rows)]
        pltpu.make_async_copy(got, got, wr.at[i * 2 + k]).wait()


def gather_to_heads(x, w, n_c):
    tok, rows = x.shape[0], w.shape[0]
    n_f = 2 * n_c
    dma = pltpu.SemaphoreType.DMA
    return pl.pallas_call(
        functools.partial(gather_kernel, n_c),
        out_shape=(
            jax.ShapeDtypeStruct((4, tok, MODEL_WIDTH), BF),
            jax.ShapeDtypeStruct((n_f * rows, 3 * GROUP_WIDTH), BF),
        ),
        in_specs=[pl.BlockSpec(memory_space=VMEM)] * 2,
        out_specs=[pl.BlockSpec(memory_space=ANY)] * 2,
        scratch_shapes=[
            dma((2, 2)),
            dma((4,)),
            dma((4,)),
            dma((4,)),
            dma((n_f,)),
            dma((n_f,)),
            dma,
        ],
        compiler_params=pltpu.CompilerParams(collective_id=0, has_side_effects=True),
        name="gather_to_heads",
    )(x, w)


def to_tokens_kernel(a_ref, o_ref, send, recv):
    zh, zl, c, core = here()
    signal_all(column_peers(zh, zl, c, core))
    group = zl * 2 + core
    columns = pl.ds(pl.multiple_of(group * GROUP_WIDTH, GROUP_WIDTH), GROUP_WIDTH)
    for s in range(4):
        a, b = s // 2, s % 2
        is_self = (a == zh) & (b == zl) & (core == zh)
        src, dst = a_ref.at[s], o_ref.at[:, columns]

        @pl.when(is_self)
        def _():
            pltpu.make_async_copy(src, dst, recv.at[group]).start()

        @pl.when(jnp.logical_not(is_self))
        def _():
            remote(src, dst, send.at[s], recv.at[group], (a, b, c, zh)).start()

    for s in range(4):
        a, b = s // 2, s % 2
        is_self = (a == zh) & (b == zl) & (core == zh)
        got = o_ref.at[:, pl.ds(s * GROUP_WIDTH, GROUP_WIDTH)]
        pltpu.make_async_copy(got, got, recv.at[s]).wait()

        @pl.when(jnp.logical_not(is_self))
        def _():
            pltpu.make_async_copy(a_ref.at[s], a_ref.at[s], send.at[s]).wait()


def to_tokens(rows):
    tok = rows.shape[1]
    dma = pltpu.SemaphoreType.DMA
    return pl.pallas_call(
        to_tokens_kernel,
        out_shape=jax.ShapeDtypeStruct((tok, MODEL_WIDTH), BF),
        in_specs=[pl.BlockSpec(memory_space=VMEM)],
        out_specs=pl.BlockSpec(memory_space=ANY),
        scratch_shapes=[dma((4,)), dma((4,))],
        compiler_params=pltpu.CompilerParams(collective_id=1, has_side_effects=True),
        name="to_tokens",
    )(rows)


def to_heads_kernel(a_ref, o_ref, send, recv):
    zh, zl, c, core = here()
    signal_all(column_peers(zh, zl, c, core))
    me = zh * 2 + zl
    for g in range(4):
        b, k = g // 2, g % 2
        is_self = (core == zh) & (b == zl) & (core == k)
        src, dst = a_ref.at[:, pl.ds(g * GROUP_WIDTH, GROUP_WIDTH)], o_ref.at[me]

        @pl.when(is_self)
        def _():
            pltpu.make_async_copy(src, dst, recv.at[me]).start()

        @pl.when(jnp.logical_not(is_self))
        def _():
            remote(src, dst, send.at[g], recv.at[me], (core, b, c, k)).start()

    for g in range(4):
        b, k = g // 2, g % 2
        is_self = (core == zh) & (b == zl) & (core == k)
        pltpu.make_async_copy(o_ref.at[g], o_ref.at[g], recv.at[g]).wait()

        @pl.when(jnp.logical_not(is_self))
        def _():
            pltpu.make_async_copy(o_ref.at[g], o_ref.at[g], send.at[g]).wait()


def to_heads(rows):
    tok = rows.shape[0]
    dma = pltpu.SemaphoreType.DMA
    return pl.pallas_call(
        to_heads_kernel,
        out_shape=jax.ShapeDtypeStruct((4, tok, GROUP_WIDTH), BF),
        in_specs=[pl.BlockSpec(memory_space=VMEM)],
        out_specs=pl.BlockSpec(memory_space=ANY),
        scratch_shapes=[dma((4,)), dma((4,))],
        compiler_params=pltpu.CompilerParams(collective_id=2, has_side_effects=True),
        name="to_heads",
    )(rows)


def sum_to_tokens_kernel(p_ref, o_ref, sib, chip, rx, ss, sr, send, recv):
    zh, zl, c, core = here()
    signal_all(column_peers(zh, zl, c, core))
    width = o_ref.shape[1]
    half = width // 2
    sibling = (zh, zl, c, 1 - core)
    mine = pl.ds(pl.multiple_of(core * half, half), half)
    theirs = pl.ds(pl.multiple_of((1 - core) * half, half), half)
    for s in range(4):
        remote(p_ref.at[s, :, theirs], sib.at[s], ss.at[s], sr.at[s], sibling).start()

    def is_self(s):
        return (s // 2 == zh) & (s % 2 == zl) & (core == zh)

    for s in range(4):
        pltpu.make_async_copy(sib.at[s], sib.at[s], sr.at[s]).wait()
        chip[s] = (p_ref[s, :, mine].astype(F32) + sib[s].astype(F32)).astype(BF)
        src, dst = chip.at[s], rx.at[zl, core]

        @pl.when(is_self(s))
        def _():
            pltpu.make_async_copy(src, dst, recv.at[zl, core]).start()

        @pl.when(jnp.logical_not(is_self(s)))
        def _():
            remote(src, dst, send.at[s], recv.at[zl, core], (s // 2, s % 2, c, zh)).start()

    for s in range(4):
        pltpu.make_async_copy(sib.at[s], sib.at[s], ss.at[s]).wait()

        @pl.when(jnp.logical_not(is_self(s)))
        def _():
            pltpu.make_async_copy(chip.at[s], chip.at[s], send.at[s]).wait()

    for k in range(2):
        for b in range(2):
            pltpu.make_async_copy(rx.at[b, k], rx.at[b, k], recv.at[b, k]).wait()
        o_ref[:, k * half : (k + 1) * half] = rx[0, k].astype(F32) + rx[1, k].astype(F32)


def sum_to_tokens(parts):
    _, tok, width = parts.shape
    half = width // 2
    dma = pltpu.SemaphoreType.DMA
    return pl.pallas_call(
        sum_to_tokens_kernel,
        out_shape=jax.ShapeDtypeStruct((tok, width), F32),
        in_specs=[pl.BlockSpec(memory_space=VMEM)],
        out_specs=pl.BlockSpec(memory_space=VMEM),
        scratch_shapes=[
            VMEM((4, tok, half), BF),
            VMEM((4, tok, half), BF),
            VMEM((2, 2, tok, half), BF),
            dma((4,)),
            dma((4,)),
            dma((4,)),
            dma((2, 2)),
        ],
        compiler_params=pltpu.CompilerParams(
            collective_id=3, has_side_effects=True, vmem_limit_bytes=40 * 2**20
        ),
        name="sum_to_tokens",
    )(parts)


def group_sum_kernel(x_ref, o_ref, rx, send, recv):
    zh, zl, c, core = here()
    peers = [(zh, zl, c, 1 - core), (zh, 1 - zl, c, core), (zh, 1 - zl, c, 1 - core)]
    signal_all(peers)
    copies = [remote(x_ref, rx.at[i], send.at[i], recv.at[i], p) for i, p in enumerate(peers)]
    for copy in copies:
        copy.start()
    for copy in copies:
        copy.wait()
    o_ref[...] = (x_ref[...] + rx[0]) + (rx[1] + rx[2])


def group_sum(values, identity):
    dma = pltpu.SemaphoreType.DMA
    return pl.pallas_call(
        group_sum_kernel,
        out_shape=jax.ShapeDtypeStruct(values.shape, F32),
        in_specs=[pl.BlockSpec(memory_space=VMEM)],
        out_specs=pl.BlockSpec(memory_space=VMEM),
        scratch_shapes=[VMEM((3, *values.shape), F32), dma((3,)), dma((3,))],
        compiler_params=pltpu.CompilerParams(collective_id=identity, has_side_effects=True),
        name="group_sum",
    )(values)


def turn(values, cosine, sine):
    return values * cosine + pltpu.roll(values, HD // 2, 1) * sine


def attention_rows(block):
    return 256 if block % 256 == 0 else block


def attend_kernel(
    pq, pk, pv, rq, rk, gq, gk, cosine, sine, seg_c, seg_r, q_ref, k_ref, v_ref, o_ref, lse_ref
):
    block = pq.shape[0]
    rows = attention_rows(block)
    scale = HD**-0.5
    q_ref[...] = turn(pq[...] * rq[...] * gq[...], cosine[...], sine[...]).astype(BF)
    k_ref[...] = turn(pk[...] * rk[...] * gk[...], cosine[...], sine[...]).astype(BF)
    v_ref[...] = pv[...].astype(BF)
    for i in range(block // rows):
        length = (i + 1) * rows
        own = slice(i * rows, length)
        scores = mm_t(q_ref[own], k_ref[:length]) * scale
        row = lax.broadcasted_iota(jnp.int32, (rows, length), 0) + i * rows
        column = lax.broadcasted_iota(jnp.int32, (rows, length), 1)
        allowed = (seg_c[own] == seg_r[:, :length]) & (column <= row)
        scores = jnp.where(allowed, scores, NEGATIVE)
        top = jnp.max(scores, axis=1, keepdims=True)
        weights = jnp.exp(scores - top)
        total = jnp.sum(weights, axis=1, keepdims=True)
        out = mm(weights.astype(BF), v_ref[:length]) / total
        o_ref[own] = out.astype(BF)
        lse_ref[0, own] = top + jnp.log(total)


def attend(projected, rq, rk, gq, gk, cosine, sine, seg_c, seg_r):
    block = projected.shape[0]
    head = lambda off: pl.BlockSpec((block, HD), lambda h: (0, off + h))
    gain = pl.BlockSpec((1, HD), lambda h: (0, h))
    fixed = lambda shape: pl.BlockSpec(shape, lambda h: (0, 0))
    wide = jax.ShapeDtypeStruct((block, GROUP_WIDTH), BF)
    return pl.pallas_call(
        attend_kernel,
        grid=(HEADS,),
        out_shape=(wide, wide, wide, wide, jax.ShapeDtypeStruct((HEADS, block, 1), F32)),
        in_specs=[
            head(0),
            head(HEADS),
            head(2 * HEADS),
            fixed((block, 1)),
            fixed((block, 1)),
            gain,
            gain,
            fixed((block, HD)),
            fixed((block, HD)),
            fixed((block, 1)),
            fixed((1, block)),
        ],
        out_specs=[head(0)] * 4 + [pl.BlockSpec((1, block, 1), lambda h: (h, 0, 0))],
        compiler_params=pltpu.CompilerParams(vmem_limit_bytes=60 * 2**20),
        name="attend",
    )(projected, projected, projected, rq, rk, gq, gk, cosine, sine, seg_c, seg_r)


def attend_back_kernel(
    q_ref,
    k_ref,
    v_ref,
    g_ref,
    lse_ref,
    pq,
    pk,
    gq,
    gk,
    cosine,
    sine,
    seg_c,
    seg_r,
    uq_ref,
    uk_ref,
    dv_ref,
    mq_ref,
    mk_ref,
    dk_acc,
    dv_acc,
):
    block = q_ref.shape[0]
    rows = attention_rows(block)
    scale = HD**-0.5
    dk_acc[...] = jnp.zeros_like(dk_acc)
    dv_acc[...] = jnp.zeros_like(dv_acc)

    def back(grad, raw, gain):
        turned = turn(grad.astype(BF).astype(F32), cosine_of, -sine_of)
        return turned, jnp.sum(raw * gain[...] * turned, axis=1, keepdims=True)

    for i in range(block // rows):
        length = (i + 1) * rows
        own = slice(i * rows, length)
        scores = mm_t(q_ref[own], k_ref[:length]) * scale
        row = lax.broadcasted_iota(jnp.int32, (rows, length), 0) + i * rows
        column = lax.broadcasted_iota(jnp.int32, (rows, length), 1)
        allowed = (seg_c[own] == seg_r[:, :length]) & (column <= row)
        probs = jnp.where(allowed, jnp.exp(scores - lse_ref[0, own]), 0.0)
        grad_probs = mm_t(g_ref[own], v_ref[:length])
        delta = jnp.sum(probs * grad_probs, axis=1, keepdims=True)
        grad_scores = (probs * (grad_probs - delta)).astype(BF)
        grad_q = mm(grad_scores, k_ref[:length]) * scale
        cosine_of, sine_of = cosine[own], sine[own]
        turned, moment = back(grad_q, pq[own], gq)
        uq_ref[own] = turned
        mq_ref[0, own] = moment
        dk_acc[:length] += t_mm(grad_scores, q_ref[own])
        dv_acc[:length] += t_mm(probs.astype(BF), g_ref[own])
    cosine_of, sine_of = cosine[...], sine[...]
    turned, moment = back(dk_acc[...] * scale, pk[...], gk)
    uk_ref[...] = turned
    mk_ref[0] = moment
    dv_ref[...] = dv_acc[...].astype(BF)


def attend_back(q, k, v, grad, lse, projected, gq, gk, cosine, sine, seg_c, seg_r):
    block = q.shape[0]
    head = lambda off: pl.BlockSpec((block, HD), lambda h: (0, off + h))
    gain = pl.BlockSpec((1, HD), lambda h: (0, h))
    fixed = lambda shape: pl.BlockSpec(shape, lambda h: (0, 0))
    column = pl.BlockSpec((1, block, 1), lambda h: (h, 0, 0))
    wide = lambda t: jax.ShapeDtypeStruct((block, GROUP_WIDTH), t)
    moment = jax.ShapeDtypeStruct((HEADS, block, 1), F32)
    return pl.pallas_call(
        attend_back_kernel,
        grid=(HEADS,),
        out_shape=(wide(F32), wide(F32), wide(BF), moment, moment),
        in_specs=[
            head(0),
            head(0),
            head(0),
            head(0),
            column,
            head(0),
            head(HEADS),
            gain,
            gain,
            fixed((block, HD)),
            fixed((block, HD)),
            fixed((block, 1)),
            fixed((1, block)),
        ],
        out_specs=[head(0)] * 3 + [column] * 2,
        scratch_shapes=[VMEM((block, HD), F32), VMEM((block, HD), F32)],
        compiler_params=pltpu.CompilerParams(vmem_limit_bytes=60 * 2**20),
        name="attend_back",
    )(q, k, v, grad, lse, projected, projected, gq, gk, cosine, sine, seg_c, seg_r)


WIDE_IN = MODEL_WIDTH + 2 * SPAN
WIDE_OUT = MODEL_WIDTH + SPAN
CHUNK = 16


def over_rows(count, body):
    def step(n, carry):
        body(pl.ds(pl.multiple_of(n * CHUNK, CHUNK), CHUNK))
        return carry

    lax.fori_loop(0, count // CHUNK, step, 0)


def wait_for(ref, sem):
    pltpu.make_async_copy(ref, ref, sem).wait()


def experts_kernel(n_c, experts, slots, comm, *refs):
    x_ref, g_ref, h_gu, h_d, h_id, h_iu, h_od, h_ou = refs[:8]
    refs = refs[8:]
    out_ref, row_ref, gid_o, giu_o, god_o, gou_o = refs[:6]
    refs = refs[6:]
    if comm:
        xg_ref, final = refs[:2]
        refs = refs[2:]
    else:
        xg_ref = x_ref
    (wb, db, xw, gw, xl, dr, gu, hl, dh, dgl, res, pick, gate, mom, mask) = refs[:15]
    (to, tr, gid, giu, god, gou, wsem, csem, osem) = refs[15:24]
    refs = refs[24:]
    zh, zl, c, core = here()
    tok = xw.shape[1]
    extra = xw.shape[2] - MODEL_WIDTH
    tiles = n_c
    f = c * 2 + core
    near = lambda i: (
        lax.rem(c // 2 + i // 2, 2) * 2 + lax.rem(lax.rem(c, 2) + lax.rem(i, 2), 2)
    )

    def pair(ref, p):
        return ref.at[pl.ds(p * 2, 2)]

    def load_in(expert):
        yield pltpu.make_async_copy(h_id.at[expert], wb.at[:MODEL_WIDTH, MODEL_WIDTH:], wsem.at[0])
        yield pltpu.make_async_copy(h_gu.at[expert], wb.at[:MODEL_WIDTH, :MODEL_WIDTH], wsem.at[1])
        for j in range(2):
            rows = slice(MODEL_WIDTH + j * SPAN, MODEL_WIDTH + (j + 1) * SPAN)
            columns = slice(j * EXPERT_HIDDEN, (j + 1) * EXPERT_HIDDEN)
            yield pltpu.make_async_copy(h_iu.at[expert, j], wb.at[rows, columns], wsem.at[2 + j])

    def load_out(expert):
        yield pltpu.make_async_copy(h_d.at[expert], db.at[:EXPERT_HIDDEN, :MODEL_WIDTH], wsem.at[4])
        yield pltpu.make_async_copy(h_od.at[expert], db.at[:EXPERT_HIDDEN, MODEL_WIDTH:], wsem.at[5])
        yield pltpu.make_async_copy(h_ou.at[expert], db.at[EXPERT_HIDDEN:, :MODEL_WIDTH], wsem.at[6])

    terms = ((gid, gid_o), (giu, giu_o), (god, god_o), (gou, gou_o))

    def term_copies(e):
        return [pltpu.make_async_copy(a, b.at[e], osem.at[n]) for n, (a, b) in enumerate(terms)]

    if comm:
        sib, la, lb, fx, fy, sums, sendx, recvx, sends, recvs = refs
        same = lambda i: (zh, zl, near(i), core)
        sibling = (zh, zl, c, 1 - core)
        low_half, high_half = pl.ds(0, tok // 2), pl.ds(tok // 2, tok // 2)
        signal_all([sibling, same(1), same(2)])
        first = [
            remote(x_ref, xg_ref.at[f], sendx.at[n], recvx.at[n], to_)
            for n, to_ in enumerate((sibling, same(1), same(2)))
        ]
        for copy in first:
            copy.start()
        fx1, fy1, fd1 = near(1) * 2 + core, near(2) * 2 + core, near(3) * 2 + core
        forward = [
            remote(xg_ref.at[fx1, low_half], xg_ref.at[fx1, low_half], sendx.at[3], recvx.at[3], same(2)),
            remote(xg_ref.at[fy1, high_half], xg_ref.at[fy1, high_half], sendx.at[4], recvx.at[4], same(1)),
            remote(xg_ref.at[fx1], xg_ref.at[fx1], sendx.at[5], recvx.at[5], sibling),
            remote(xg_ref.at[fy1], xg_ref.at[fy1], sendx.at[6], recvx.at[6], sibling),
        ]
        across = remote(xg_ref.at[fd1], xg_ref.at[fd1], sendx.at[7], recvx.at[7], sibling)

    for copy in (*load_in(0), *load_out(0)):
        copy.start()
    spare = EXPERT_HIDDEN
    wb[MODEL_WIDTH : MODEL_WIDTH + SPAN, spare:] = jnp.zeros((SPAN, WIDE_IN - spare), BF)
    wb[MODEL_WIDTH + SPAN :, :spare] = jnp.zeros((SPAN, spare), BF)
    for ref, _ in terms:
        ref[...] = jnp.zeros_like(ref)

    def order(s):
        e = s // tiles
        i = s + e * (2 * tiles - 1 - 2 * s)
        return e, i, (near(i) if comm else i)

    def fetch_x(p):
        return pltpu.make_async_copy(pair(xg_ref, p), xw, csem.at[0])

    def fetch_own():
        other = xg_ref.at[c * 2 + 1 - core]
        pltpu.make_async_copy(x_ref, xw.at[core], csem.at[0]).start()
        pltpu.make_async_copy(other, xw.at[1 - core], csem.at[0]).start()

    def fetch_g(p):
        return pltpu.make_async_copy(pair(g_ref, p), gw, csem.at[1])

    if comm:
        fetch_g(c).start()
        wait_for(xg_ref.at[c * 2 + 1 - core], recvx.at[0])
        fetch_own()
    else:
        fetch_g(0).start()
        fetch_x(0).start()

    def write_out(p):
        return pltpu.make_async_copy(to, pair(out_ref, p), csem.at[2])

    def write_row(p):
        return pltpu.make_async_copy(tr, pair(row_ref, p), csem.at[3])

    def read_out(p):
        return pltpu.make_async_copy(pair(out_ref, p), to, csem.at[4])

    def read_row(p):
        return pltpu.make_async_copy(pair(row_ref, p), tr, csem.at[5])

    both = 2 * slots
    steps = 2 * tiles
    part = lambda d: slice(d * slots, (d + 1) * slots)
    pieces = [
        (
            slice(r, r + CHUNK),
            slice(h * 512, (h + 1) * 512),
            slice(EXPERT_HIDDEN + h * 512, EXPERT_HIDDEN + (h + 1) * 512),
        )
        for r in range(0, both, CHUNK)
        for h in range(2)
    ]

    def step(s, carry):
        e, i, p = order(s)
        _, _, after = order(jnp.minimum(s + 1, steps - 1))
        number = c * (2 * EXP_DEV) + core * EXP_DEV + e
        fetch_x(p).wait()
        fetch_g(p).wait()
        lane = lax.broadcasted_iota(jnp.int32, (tok, extra), 1)
        lane_s = lax.broadcasted_iota(jnp.int32, (slots, extra), 1)
        for d in range(2):
            side = xw[d, :, MODEL_WIDTH:].astype(F32)
            place = jnp.sum(jnp.where(lane == number, side, 0.0), axis=1, keepdims=True)
            slot = lax.broadcasted_iota(jnp.int32, (tok, slots), 1).astype(F32)
            pick[d] = jnp.where(slot == place, 1.0, 0.0).astype(BF)
            sub = lax.broadcasted_iota(jnp.int32, (extra, tok), 0)
            place_t = jnp.sum(jnp.where(sub == number, side.T, 0.0), axis=0, keepdims=True)
            slot_t = lax.broadcasted_iota(jnp.int32, (slots, tok), 0).astype(F32)
            pickt = jnp.where(slot_t == place_t, 1.0, 0.0).astype(BF)
            xl[part(d), :MODEL_WIDTH] = mm(pickt, xw[d, :, :MODEL_WIDTH]).astype(BF)
            dr[part(d), :MODEL_WIDTH] = mm(pickt, gw[d]).astype(BF)
            side = mm(pickt, xw[d, :, MODEL_WIDTH:])
            read = lambda which: jnp.sum(jnp.where(which, side, 0.0), axis=1, keepdims=True)
            gate[part(d)] = read((lane_s == experts + number) | (lane_s == 2 * experts + number))
            columns = lax.broadcasted_iota(jnp.int32, (slots, SPAN), 1) // ADAPTER_RANK
            mask[part(d)] = jnp.where(columns.astype(F32) == read(lane_s == 3 * experts), 1.0, 0.0)

        @pl.when((s > 0) & (s <= tiles) if comm else s > 0)
        def _():
            write_row(p).wait()

        @pl.when(s > 0)
        def _():
            write_out(p).wait()

        @pl.when(e > 0)
        def _():
            read_out(p).start()
            read_row(p).start()

        @pl.when(s == 0)
        def _():
            for copy in (*load_in(0), *load_out(0)):
                copy.wait()

        @pl.when(s == tiles)
        def _():
            for copy in (*load_in(1), *load_out(1), *term_copies(0)):
                copy.wait()
            for ref, _ in terms:
                ref[...] = jnp.zeros_like(ref)

        mask2 = lambda: jnp.concatenate([mask[...], mask[...]], axis=1)
        xl[:, MODEL_WIDTH:] = (mm(xl[:, :MODEL_WIDTH], wb[:MODEL_WIDTH, MODEL_WIDTH:]) * mask2()).astype(BF)
        gu[...] = mm(xl[...], wb[:, :MODEL_WIDTH])

        for rows, a, b in pieces:
            gate_part = gu[rows, a]
            hl[rows, a] = (gate_part / (1.0 + jnp.exp(-gate_part)) * gu[rows, b]).astype(BF)
        hl[:, EXPERT_HIDDEN:] = (
            mm(hl[:, :EXPERT_HIDDEN], db[:EXPERT_HIDDEN, MODEL_WIDTH:]) * mask[...]
        ).astype(BF)
        for n in range(4):
            a = slice(n * 512, (n + 1) * 512)
            res[:, a] = (mm(hl[...], db[:, a]) * gate[...]).astype(BF)

        @pl.when(e > 0)
        def _():
            read_out(p).wait()

        def add_picked(target, d):
            for n in range(4):
                a = slice(n * 512, (n + 1) * 512)
                before = jnp.where(e > 0, target[d, :, a].astype(F32), 0.0)
                target[d, :, a] = (before + mm(pick[d], res[part(d), a])).astype(BF)

        for d in range(2):
            add_picked(to, d)
        write_out(p).start()

        @pl.when(s < steps - 1)
        def _():
            fetch_g(after).start()

        dr[:, MODEL_WIDTH:] = (
            mm_t(dr[:, :MODEL_WIDTH], db[EXPERT_HIDDEN:, :MODEL_WIDTH]) * mask[...]
        ).astype(BF)
        dh[...] = mm_t(dr[...], db[:EXPERT_HIDDEN, :])

        @pl.when(s == tiles - 1)
        def _():
            for copy in load_out(1):
                copy.start()

        mom[...] = jnp.zeros_like(mom)
        for rows, a, b in pieces:
            gate_part, up_part, grad = gu[rows, a], gu[rows, b], dh[rows, a]
            sigmoid = 1.0 / (1.0 + jnp.exp(-gate_part))
            activated = gate_part * sigmoid
            plain = grad * activated
            mom[rows] += jnp.sum(plain * up_part, axis=1, keepdims=True)
            dgl[rows, b] = (plain * gate[rows]).astype(BF)
            slope = sigmoid + activated - activated * sigmoid
            dgl[rows, a] = (grad * gate[rows] * up_part * slope).astype(BF)
        dgl[:, MODEL_WIDTH:] = (
            mm_t(dgl[:, :MODEL_WIDTH], wb[MODEL_WIDTH:, :MODEL_WIDTH]) * mask2()
        ).astype(BF)
        for n in range(4):
            a = slice(n * 512, (n + 1) * 512)
            res[:, a] = mm_t(dgl[...], wb[a, :]).astype(BF)

        @pl.when(s == tiles - 1)
        def _():
            for copy in load_in(1):
                copy.start()

        if comm:
            @pl.when(s == 0)
            def _():
                wait_for(xg_ref.at[fx1], recvx.at[1])
                forward[0].start()
                forward[2].start()
                wait_for(xg_ref.at[fy1], recvx.at[2])
                forward[1].start()
                forward[3].start()
                wait_for(xg_ref.at[fx1], recvx.at[5])

            @pl.when(s == 1)
            def _():
                wait_for(xg_ref.at[fd1, low_half], recvx.at[3])
                wait_for(xg_ref.at[fd1, high_half], recvx.at[4])
                across.start()
                wait_for(xg_ref.at[fy1], recvx.at[6])

            @pl.when(s == 2)
            def _():
                wait_for(xg_ref.at[fd1], recvx.at[7])

        @pl.when(s < steps - (2 if comm else 1))
        def _():
            fetch_x(after).start()

        if comm:

            @pl.when(s == steps - 2)
            def _():
                fetch_own()

        @pl.when(e > 0)
        def _():
            read_row(p).wait()

        for d in range(2):
            add_picked(tr, d)
            moment = mom[part(d)]
            high = moment.astype(BF).astype(F32)
            side = jnp.where(lane_s == number, high, 0.0) + jnp.where(
                lane_s == experts + number, moment - high, 0.0
            )
            before = jnp.where(e > 0, tr[d, :, MODEL_WIDTH:].astype(F32), 0.0)
            tr[d, :, MODEL_WIDTH:] = (before + mm(pick[d], side.astype(BF))).astype(BF)

        if comm:
            to_sibling = remote(
                tr.at[1 - core], sib.at[lax.rem(i, 2)], sends.at[lax.rem(i, 2)],
                recvs.at[lax.rem(i, 2)], sibling,
            )

            @pl.when(e == 0)
            def _():
                write_row(p).start()

            @pl.when(e > 0)
            def _():
                to_sibling.start()
        else:
            write_row(p).start()

        gid[...] += t_mm(xl[:, :MODEL_WIDTH], dgl[:, MODEL_WIDTH:])
        for j in range(2):
            giu[j] += t_mm(
                xl[:, MODEL_WIDTH + j * SPAN : MODEL_WIDTH + (j + 1) * SPAN],
                dgl[:, j * EXPERT_HIDDEN : (j + 1) * EXPERT_HIDDEN],
            )
        god[...] += t_mm(hl[:, :EXPERT_HIDDEN], (dr[:, MODEL_WIDTH:].astype(F32) * gate[...]).astype(BF))
        gou[...] += t_mm((hl[:, EXPERT_HIDDEN:].astype(F32) * gate[...]).astype(BF), dr[:, :MODEL_WIDTH])

        @pl.when(s == tiles - 1)
        def _():
            for copy in term_copies(0):
                copy.start()

        if comm:
            half = tok // 2

            def chip_sum(at, rows):
                return tr[core, rows].astype(F32) + sib[at, rows].astype(F32)

            @pl.when(e > 0)
            def _():
                to_sibling.wait()

            @pl.when(s == steps - 4)
            def _():
                def body(rows):
                    sums[0, rows] = chip_sum(1, rows).astype(BF)

                over_rows(tok, body)
                remote(sums.at[0, low_half], la, sends.at[2], recvs.at[2], same(1)).start()
                remote(sums.at[0, high_half], lb, sends.at[3], recvs.at[3], same(2)).start()

            @pl.when(s == steps - 3)
            def _():
                wait_for(la, recvs.at[2])

                def body(rows):
                    sums[1, rows] = (chip_sum(0, rows) + la[rows].astype(F32)).astype(BF)

                def rest(rows):
                    rows = pl.ds(pl.multiple_of(rows.start + half, CHUNK), CHUNK)
                    sums[1, rows] = chip_sum(0, rows).astype(BF)

                over_rows(half, body)
                over_rows(half, rest)
                remote(sums.at[1], fy, sends.at[4], recvs.at[4], same(2)).start()

            @pl.when(s == steps - 2)
            def _():
                wait_for(lb, recvs.at[3])

                def body(rows):
                    sums[2, rows] = chip_sum(1, rows).astype(BF)

                def rest(rows):
                    upper = pl.ds(pl.multiple_of(rows.start + half, CHUNK), CHUNK)
                    sums[2, upper] = (chip_sum(1, upper) + lb[rows].astype(F32)).astype(BF)

                over_rows(half, body)
                over_rows(half, rest)
                remote(sums.at[2], fx, sends.at[5], recvs.at[5], same(1)).start()

        return carry

    lax.fori_loop(0, steps, step, 0)
    for copy in term_copies(1):
        copy.start()
    _, _, last = order(steps - 1)
    write_out(last).wait()
    if comm:
        wait_for(fx, recvs.at[5])
        wait_for(fy, recvs.at[4])

        def body(rows):
            total = tr[core, rows].astype(F32) + sib[0, rows].astype(F32)
            final[rows] = (total + (fx[rows].astype(F32) + fy[rows].astype(F32))).astype(BF)

        over_rows(tok, body)
        wait_for(la, sends.at[2])
        wait_for(lb, sends.at[3])
        wait_for(fy, sends.at[4])
        wait_for(fx, sends.at[5])
        for copy in first:
            copy.wait_send()
        for copy in forward:
            copy.wait_send()
        across.wait_send()
    else:
        write_row(last).wait()
    for copy in term_copies(1):
        copy.wait()


def run_experts(x, g, weights, experts, slots, n_c, comm):
    tok, wide = x.shape[-2:]
    sources = 2 * n_c
    both = 2 * slots
    dma = pltpu.SemaphoreType.DMA
    term_shapes = (
        (MODEL_WIDTH, 2 * SPAN),
        (2, SPAN, EXPERT_HIDDEN),
        (EXPERT_HIDDEN, SPAN),
        (SPAN, MODEL_WIDTH),
    )
    any_spec = pl.BlockSpec(memory_space=ANY)
    out_shape = [
        jax.ShapeDtypeStruct((sources, tok, MODEL_WIDTH), BF),
        jax.ShapeDtypeStruct((sources, tok, wide), BF),
        *(jax.ShapeDtypeStruct((EXP_DEV, *s), F32) for s in term_shapes),
    ]
    out_specs = [any_spec] * 6
    scratch = [
        VMEM((WIDE_IN, WIDE_IN), BF),
        VMEM((EXPERT_HIDDEN + SPAN, WIDE_OUT), BF),
        VMEM((2, tok, wide), BF),
        VMEM((2, tok, MODEL_WIDTH), BF),
        VMEM((both, WIDE_IN), BF),
        VMEM((both, WIDE_OUT), BF),
        VMEM((both, MODEL_WIDTH), F32),
        VMEM((both, EXPERT_HIDDEN + SPAN), BF),
        VMEM((both, EXPERT_HIDDEN), F32),
        VMEM((both, WIDE_IN), BF),
        VMEM((both, MODEL_WIDTH), BF),
        VMEM((2, tok, slots), BF),
        VMEM((both, 1), F32),
        VMEM((both, 1), F32),
        VMEM((both, SPAN), F32),
        VMEM((2, tok, MODEL_WIDTH), BF),
        VMEM((2, tok, wide), BF),
        *(VMEM(s, F32) for s in term_shapes),
        dma((7,)),
        dma((6,)),
        dma((4,)),
    ]
    params = {}
    if comm:
        out_shape += [
            jax.ShapeDtypeStruct((sources, tok, wide), BF),
            jax.ShapeDtypeStruct((tok, wide), BF),
        ]
        out_specs += [any_spec, pl.BlockSpec(memory_space=VMEM)]
        scratch += [
            VMEM((2, tok, wide), BF),
            VMEM((tok // 2, wide), BF),
            VMEM((tok // 2, wide), BF),
            VMEM((tok, wide), BF),
            VMEM((tok, wide), BF),
            VMEM((3, tok, wide), BF),
            dma((8,)),
            dma((8,)),
            dma((6,)),
            dma((6,)),
        ]
        params = dict(collective_id=6, has_side_effects=True)
    flops = 2 * sources * EXP_DEV * slots * MODEL_WIDTH * EXPERT_HIDDEN * 8
    results = pl.pallas_call(
        functools.partial(experts_kernel, n_c, experts, slots, comm),
        out_shape=out_shape,
        in_specs=[any_spec] * 8,
        out_specs=out_specs,
        scratch_shapes=scratch,
        compiler_params=pltpu.CompilerParams(vmem_limit_bytes=63 * 2**20, **params),
        cost_estimate=pl.CostEstimate(flops=flops, bytes_accessed=10**8, transcendentals=10**7),
        name="experts",
    )(x, g, *weights)
    return results[0], (results[7] if comm else results[1]), results[2:6]


def on_device(
    tokens,
    cotangent,
    lengths,
    sets,
    routes,
    gain_attn,
    gain_query,
    gain_key,
    gain_mlp,
    query_key_value_weight,
    out_weight,
    router_weight,
    gate_up_weight,
    down_weight,
    attention_down_factors,
    attention_up_factors,
    router_down_factors,
    router_up_factors,
    expert_input_down,
    expert_input_up,
    expert_output_down,
    expert_output_up,
):
    zh, zl, c, core = here()
    n_c = lax.axis_size("c")
    n_fsdp = 2 * n_c
    n_seq = lax.axis_size("zh") * lax.axis_size("zl")
    tok = tokens.shape[1]
    block = tok * n_seq
    experts = EXP_DEV * n_fsdp
    capacity = 5 * tok * TOP // (4 * experts)
    slots = -(-capacity // 16) * 16
    extra = -(-(3 * experts + 1) // 128) * 128
    span3 = 3 * SPAN
    group = zl * 2 + core
    shard = zh * 2 + zl

    both_lengths = lax.all_gather(
        jnp.concatenate([lengths[0], sets[0]]), "core", axis=0, tiled=False
    )
    held_lengths = lax.dynamic_index_in_dim(both_lengths, zh, 0, keepdims=False)
    count = lengths.shape[1]

    inputs = tokens[0].astype(F32)
    normalized = rms_scale(inputs, gain_attn).astype(BF)
    x_shards, qkv_rows = gather_to_heads(normalized, query_key_value_weight, n_c)

    rows_local = query_key_value_weight.shape[0]
    factors = jnp.concatenate(
        [
            attention_down_factors,
            attention_up_factors.reshape(rows_local, -1),
            router_down_factors,
            router_weight,
            router_up_factors.reshape(rows_local, -1),
        ],
        axis=1,
    )
    factor_width = factors.shape[1]
    factors = jnp.pad(factors, ((0, 0), (0, -factor_width % 128)))
    factors = lax.all_gather(factors, FSDP, axis=0, tiled=True)
    up_columns = attention_up_factors.size // rows_local
    down_full = factors[:, : 4 * SPAN]
    at = 4 * SPAN
    up_full = factors[:, at : at + up_columns].reshape(4 * SPAN, MODEL_WIDTH)
    at += up_columns
    rdown_full = factors[:, at : at + SPAN]
    at += SPAN
    router_full = factors[:, at : at + experts]
    at += experts
    rup_full = factors[:, at:factor_width].reshape(SPAN, experts)
    out_full = lax.all_gather(out_weight, FSDP, axis=0, tiled=True)
    grad_rows_all = lax.all_gather(cotangent[0], FSDP, axis=0, tiled=True)

    seq_local, _, chosen = token_meta(
        lengths[0], sets[0], shard * tok + jnp.arange(tok, dtype=jnp.int32)
    )
    mask = set_mask(chosen)
    seq_block, block_offsets, block_sets = token_meta(
        held_lengths[:count], held_lengths[count:], jnp.arange(block, dtype=jnp.int32)
    )
    mask3 = jnp.tile(set_mask(block_sets), (1, 3))
    half = HD // 2
    freqs = THETA ** (-(jnp.arange(half, dtype=F32) * 2.0 / HD))
    angles = block_offsets.astype(F32)[:, None] * freqs[None, :]
    cosine, sine = jnp.cos(angles), jnp.sin(angles)
    cosine = jnp.concatenate([cosine, cosine], axis=1)
    sine = jnp.concatenate([-sine, sine], axis=1)
    seg_c, seg_r = seq_block[:, None], seq_block[None, :]

    x_all = x_shards.reshape(block, MODEL_WIDTH)
    down3 = down_full[:, :span3]
    lowered = (mm(x_all, down3) * mask3).astype(BF)
    up_own = lax.dynamic_slice_in_dim(up_full[:span3], group * GROUP_WIDTH, GROUP_WIDTH, 1)
    none = jnp.zeros((SPAN, GROUP_WIDTH), BF)
    up_diagonal = jnp.concatenate(
        [
            jnp.concatenate(
                [up_own[j * SPAN : (j + 1) * SPAN] if i == j else none for i in range(3)], axis=1
            )
            for j in range(3)
        ],
        axis=0,
    )
    projected = mm(x_all, qkv_rows) + mm(lowered, up_diagonal)
    part_q, part_k = projected[:, :GROUP_WIDTH], projected[:, GROUP_WIDTH : 2 * GROUP_WIDTH]

    def over_group(first, second, identity):
        both = jnp.stack([first, second]).reshape(-1, 128)
        return group_sum(both, identity).reshape(2, block)

    squares = over_group(jnp.sum(part_q * part_q, axis=1), jnp.sum(part_k * part_k, axis=1), 4)
    inverse = lax.rsqrt(squares / MODEL_WIDTH + EPSILON)
    rq, rk = inverse[0][:, None], inverse[1][:, None]
    gains = [
        lax.dynamic_slice_in_dim(g, group * GROUP_WIDTH, GROUP_WIDTH)[None, :]
        for g in (gain_query, gain_key)
    ]
    q, k, v, attended_heads, lse = attend(
        projected, rq, rk, *gains, cosine, sine, seg_c, seg_r
    )
    attended = to_tokens(attended_heads.reshape(4, tok, GROUP_WIDTH))

    down_o, up_o = down_full[:, span3:], up_full[span3:]
    out_lower = (mm(attended, down_o) * mask).astype(BF)
    branch = mm(attended, out_full) + mm(out_lower, up_o)
    middle = inputs + branch
    normed2 = rms_scale(middle, gain_mlp).astype(BF)
    router_lower = (mm(normed2, rdown_full) * mask).astype(BF)
    logits = mm(normed2, router_full) + mm(router_lower, rup_full)
    probs = jax.nn.softmax(logits, axis=-1)
    hits = jnp.sum(
        (routes[0][:, :, None] == jnp.arange(experts, dtype=jnp.int32)[None, None, :]).astype(F32),
        axis=1,
    )
    place = jnp.arange(tok, dtype=jnp.int32)
    before = (place[None, :] < place[:, None]).astype(BF)
    ranks = jnp.where(hits > 0, mm(before, hits.astype(BF)), -1.0).astype(BF)
    gates = hits * probs
    gates_high = gates.astype(BF)
    gates_low = (gates - gates_high.astype(F32)).astype(BF)
    side = jnp.concatenate(
        [ranks, gates_high, gates_low, chosen.astype(BF)[:, None]], axis=1
    )
    payload = jnp.concatenate(
        [normed2, jnp.pad(side, ((0, 0), (0, extra - side.shape[1])))], axis=1
    )
    weights = (
        gate_up_weight,
        down_weight,
        expert_input_down,
        expert_input_up,
        expert_output_down,
        expert_output_up,
    )
    grads_all = grad_rows_all.reshape(n_fsdp, tok, MODEL_WIDTH)
    if n_c == 4:
        out_parts, returned, expert_terms = run_experts(
            payload, grads_all, weights, experts, slots, n_c, True
        )
    else:
        rows_all = lax.all_gather(payload, FSDP, axis=0, tiled=True)
        out_parts, row_parts, expert_terms = run_experts(
            rows_all.reshape(n_fsdp, tok, -1), grads_all, weights, experts, slots, n_c, False
        )
        returned = lax.psum_scatter(
            row_parts.reshape(n_fsdp * tok, -1), FSDP, scatter_dimension=0, tiled=True
        )
    mixed = lax.psum_scatter(
        out_parts.reshape(n_fsdp * tok, -1), FSDP, scatter_dimension=0, tiled=True
    )
    output = (middle + mixed.astype(F32)).astype(BF)

    grad_out = cotangent[0].astype(F32)
    returned = returned.astype(F32)
    back = returned[:, MODEL_WIDTH:]
    grad_probs = back[:, :experts] + back[:, experts : 2 * experts]
    grad_logits = probs * (grad_probs - jnp.sum(probs * grad_probs, axis=-1, keepdims=True))
    grad_router_lower = exact("te,re->tr", grad_logits, rup_full.astype(F32)) * mask
    grad_normed2 = (
        returned[:, :MODEL_WIDTH]
        + mm_t(grad_logits.astype(BF), router_full)
        + mm_t(grad_router_lower.astype(BF), rdown_full)
    )
    grad_rup = t_mm(router_lower, grad_logits.astype(BF))
    grad_rdown = t_mm(normed2, grad_router_lower.astype(BF))
    grad_middle = grad_out + rms_back(middle, gain_mlp, grad_normed2)
    grad_branch = grad_middle.astype(BF)
    grad_out_lower = (mm_t(grad_branch, up_o) * mask).astype(BF)
    grad_attended = (mm_t(grad_branch, out_full) + mm_t(grad_out_lower, down_o)).astype(BF)
    head_grad = to_heads(grad_attended).reshape(block, GROUP_WIDTH)
    grad_up_o = t_mm(out_lower, grad_branch)
    grad_down_o = t_mm(attended, grad_out_lower)

    uq, uk, grad_v, mq, mk = attend_back(
        q, k, v, head_grad, lse, projected, *gains, cosine, sine, seg_c, seg_r
    )
    moments = over_group(jnp.sum(mq[..., 0], axis=0), jnp.sum(mk[..., 0], axis=0), 5) / MODEL_WIDTH

    def rms_inner(values, scale, gain, turned, moment):
        return (scale * gain * turned - values * (scale * scale * scale) * moment).astype(BF)

    grad_projected = jnp.concatenate(
        [
            rms_inner(part_q, rq, gains[0], uq, moments[0][:, None]),
            rms_inner(part_k, rk, gains[1], uk, moments[1][:, None]),
            grad_v,
        ],
        axis=1,
    )
    grad_lowered = (mm_t(grad_projected, up_diagonal) * mask3).astype(BF)
    grad_up_own = [
        t_mm(
            lowered[:, j * SPAN : (j + 1) * SPAN],
            grad_projected[:, j * GROUP_WIDTH : (j + 1) * GROUP_WIDTH],
        )
        for j in range(3)
    ]
    grad_down_qkv = t_mm(x_all, grad_lowered)
    grad_normed_part = (mm_t(grad_projected, qkv_rows) + mm_t(grad_lowered, down3)).astype(BF)
    grad_normed = sum_to_tokens(grad_normed_part.reshape(4, tok, MODEL_WIDTH))
    grad_inputs = grad_middle + rms_back(inputs, gain_attn, grad_normed)

    grad_down_all = jnp.concatenate([grad_down_qkv, grad_down_o], axis=1).astype(BF)
    wide_up = lax.dynamic_update_slice_in_dim(
        jnp.zeros((span3, MODEL_WIDTH), F32),
        jnp.concatenate(grad_up_own, axis=0),
        group * GROUP_WIDTH,
        1,
    )
    grad_up_all = jnp.concatenate([wide_up, grad_up_o], axis=0).astype(BF)
    terms = (grad_down_all, grad_up_all, grad_rdown.astype(BF), grad_rup.astype(BF))
    own_shapes = [(t.shape[0] // (n_seq * n_fsdp), t.shape[1]) for t in terms]
    flat = jnp.concatenate(
        [t.reshape(n_seq, n_fsdp, -1).transpose(1, 0, 2) for t in terms], axis=2
    )
    used = flat.shape[2]
    flat = jnp.pad(flat, ((0, 0), (0, 0), (0, -used % 1024))).reshape(n_fsdp * n_seq, -1, 128)
    flat = lax.psum_scatter(flat, FSDP, scatter_dimension=0, tiled=True)
    flat = lax.psum_scatter(flat, SEQ, scatter_dimension=0, tiled=True).astype(F32).reshape(-1)
    summed, at = [], 0
    for shape in own_shapes:
        size = shape[0] * shape[1]
        summed.append(flat[at : at + size].reshape(shape))
        at += size
    expert_sums = [
        lax.psum_scatter(t.astype(BF), SEQ, scatter_dimension=d, tiled=True).astype(F32)
        for t, d in zip(expert_terms, (1, 3, 1, 2), strict=True)
    ]
    return (output[None], grad_inputs[None], *summed, *expert_sums)


def solution(mesh):
    n_seq, n_fsdp = mesh.shape["seq"], mesh.shape["fsdp"]
    fine = Mesh(
        mesh.devices.reshape(2, n_seq // 2, n_fsdp // 2, 2), ("zh", "zl", "c", "core")
    )
    split = P(FSDP, SEQ, None)
    rows = P(FSDP, None)
    three = P(FSDP, None, None)
    in_specs = (
        split,
        split,
        rows,
        rows,
        split,
        P(),
        P(),
        P(),
        P(),
        rows,
        rows,
        rows,
        three,
        three,
        rows,
        rows,
        rows,
        rows,
        three,
        P(FSDP, None, None, None),
        three,
        three,
    )
    owners = P((*SEQ, *FSDP), None)
    out_specs = (
        split,
        split,
        owners,
        owners,
        owners,
        owners,
        split,
        P(FSDP, None, None, SEQ),
        split,
        P(FSDP, None, SEQ),
    )
    return jax.shard_map(
        on_device, mesh=fine, in_specs=in_specs, out_specs=out_specs, check_vma=False
    )
```

```python
import functools

import jax
import jax.numpy as jnp
from jax import lax
from jax.experimental import pallas as pl
from jax.experimental.pallas import tpu as pltpu
from jax.sharding import Mesh
from jax.sharding import PartitionSpec as P

MODEL_WIDTH = 2048
H = 16
HD = 128
EXPERT_HIDDEN = 1024
TOP = 8
EXP_DEV = 2
ADAPTER_RANK = 16
SPAN = 128
GROUPS = 4
GROUP_WIDTH = MODEL_WIDTH // GROUPS
HEADS = H // GROUPS

EPSILON = 1e-05
THETA = 10000.0
NEGATIVE = -1e30
BF = jnp.bfloat16
F32 = jnp.float32
ANY = pl.ANY
VMEM = pltpu.VMEM
SEQ = ("zh", "zl")
FSDP = ("c", "core")


def mm(left, right):
    return lax.dot_general(left, right, (((1,), (0,)), ((), ())), preferred_element_type=F32)


def mm_t(left, right):
    return lax.dot_general(left, right, (((1,), (1,)), ((), ())), preferred_element_type=F32)


def t_mm(left, right):
    return lax.dot_general(left, right, (((0,), (0,)), ((), ())), preferred_element_type=F32)


def exact(form, left, right):
    return jnp.einsum(form, left, right, precision=lax.Precision.HIGHEST, preferred_element_type=F32)


def rms_scale(values, gain):
    return values * lax.rsqrt(jnp.mean(values * values, axis=-1, keepdims=True) + EPSILON) * gain


def rms_back(values, gain, grad):
    inverse = lax.rsqrt(jnp.mean(values * values, axis=-1, keepdims=True) + EPSILON)
    scaled = grad * gain
    return inverse * scaled - values * inverse * inverse * inverse * jnp.mean(
        values * scaled, axis=-1, keepdims=True
    )


def token_meta(lengths_row, sets_row, places):
    count = lengths_row.shape[0]
    running = [lengths_row[0]]
    for n in range(1, count):
        running.append(running[-1] + lengths_row[n])
    ends = jnp.stack(running)
    starts = ends - lengths_row
    member = ((places[:, None] >= starts[None, :]) & (places[:, None] < ends[None, :])).astype(
        jnp.int32
    )
    seq_ids = jnp.sum(member * jnp.arange(count, dtype=jnp.int32)[None, :], axis=1)
    offsets = places - jnp.sum(member * starts[None, :], axis=1)
    chosen = jnp.sum(member * sets_row[None, :], axis=1)
    return (seq_ids, offsets, chosen)


def set_mask(chosen):
    column_range = jnp.arange(SPAN, dtype=jnp.int32) // ADAPTER_RANK
    return (chosen[..., None] == column_range).astype(F32)


def here():
    return tuple(lax.axis_index(n) for n in ("zh", "zl", "c", "core"))


def signal_all(peers):
    barrier = pltpu.get_barrier_semaphore()
    for peer in peers:
        pl.semaphore_signal(barrier, inc=1, device_id=peer, device_id_type=pl.DeviceIdType.MESH)
    pl.semaphore_wait(barrier, len(peers))


def remote(src, dst, send, recv, device):
    return pltpu.make_async_remote_copy(
        src_ref=src,
        dst_ref=dst,
        send_sem=send,
        recv_sem=recv,
        device_id=device,
        device_id_type=pl.DeviceIdType.MESH,
    )


def column_peers(zh, zl, c, core):
    return [
        (zh ^ a, zl ^ b, c, core ^ k)
        for a in range(2)
        for b in range(2)
        for k in range(2)
        if (a, b, k) != (0, 0, 0)
    ]


def gather_kernel(n_c, x_ref, w_ref, xg_ref, wg_ref, xs, xr, fs, fr, ws, wr, own):
    zh, zl, c, core = here()
    tok = x_ref.shape[0]
    half = tok // 2
    rows = w_ref.shape[0]
    plane = [(zh, zl, lax.rem(c + i, n_c), core ^ k) for i in range(n_c) for k in range(2)][2:]
    signal_all(column_peers(zh, zl, c, core) + plane)
    me = zh * 2 + zl
    for a in range(2):
        for k in range(2):
            piece = pl.ds(k * half, half)
            src, dst = x_ref.at[piece], xg_ref.at[me, piece]
            is_self = (core == zh) & (zl == a) & (core == k)

            @pl.when(is_self)
            def _():
                pltpu.make_async_copy(src, dst, xr.at[me]).start()

            @pl.when(jnp.logical_not(is_self))
            def _():
                remote(src, dst, xs.at[a, k], xr.at[me], (core, a, c, k)).start()

    f = c * 2 + core
    row_block = pl.ds(pl.multiple_of(f * rows, rows), rows)

    def pieces(group):
        for j in range(3):
            start = pl.multiple_of(j * MODEL_WIDTH + group * GROUP_WIDTH, GROUP_WIDTH)
            yield (
                w_ref.at[:, pl.ds(start, GROUP_WIDTH)],
                wg_ref.at[row_block, pl.ds(j * GROUP_WIDTH, GROUP_WIDTH)],
            )

    for src, dst in pieces(zl * 2 + core):
        pltpu.make_async_copy(src, dst, own).start()
    slots = [(i, k) for i in range(n_c) for k in range(2)][1:]
    for i, k in slots:
        target_c, target_core = lax.rem(c + i, n_c), core ^ k
        for src, dst in pieces(zl * 2 + target_core):
            remote(
                src, dst, ws.at[i * 2 + k], wr.at[i * 2 + k], (zh, zl, target_c, target_core)
            ).start()
    mine = pl.ds(pl.multiple_of(core * half, half), half)
    theirs = pl.ds(pl.multiple_of((1 - core) * half, half), half)
    sibling = (zh, zl, c, 1 - core)
    for s in range(4):
        pltpu.make_async_copy(xg_ref.at[s, mine], xg_ref.at[s, mine], xr.at[s]).wait()
        remote(xg_ref.at[s, mine], xg_ref.at[s, mine], fs.at[s], fr.at[s], sibling).start()
    for s in range(4):
        got = xg_ref.at[s, theirs]
        pltpu.make_async_copy(got, got, fr.at[s]).wait()
    for s in range(4):
        got = xg_ref.at[s, mine]
        pltpu.make_async_copy(got, got, fs.at[s]).wait()
    for a in range(2):
        for k in range(2):
            is_self = (core == zh) & (zl == a) & (core == k)
            src = x_ref.at[pl.ds(k * half, half)]

            @pl.when(jnp.logical_not(is_self))
            def _():
                pltpu.make_async_copy(src, src, xs.at[a, k]).wait()

    block = wg_ref.at[row_block]
    pltpu.make_async_copy(block, block, own).wait()
    for i, k in slots:
        pltpu.make_async_copy(block, block, ws.at[i * 2 + k]).wait()
        source = lax.rem(c + n_c - i, n_c) * 2 + (core ^ k)
        got = wg_ref.at[pl.ds(pl.multiple_of(source * rows, rows), rows)]
        pltpu.make_async_copy(got, got, wr.at[i * 2 + k]).wait()


def gather_to_heads(x, w, n_c):
    tok, rows = x.shape[0], w.shape[0]
    n_f = 2 * n_c
    dma = pltpu.SemaphoreType.DMA
    return pl.pallas_call(
        functools.partial(gather_kernel, n_c),
        out_shape=(
            jax.ShapeDtypeStruct((4, tok, MODEL_WIDTH), BF),
            jax.ShapeDtypeStruct((n_f * rows, 3 * GROUP_WIDTH), BF),
        ),
        in_specs=[pl.BlockSpec(memory_space=VMEM)] * 2,
        out_specs=[pl.BlockSpec(memory_space=ANY)] * 2,
        scratch_shapes=[
            dma((2, 2)),
            dma((4,)),
            dma((4,)),
            dma((4,)),
            dma((n_f,)),
            dma((n_f,)),
            dma,
        ],
        compiler_params=pltpu.CompilerParams(collective_id=0, has_side_effects=True),
        name="gather_to_heads",
    )(x, w)


def to_tokens_kernel(a_ref, o_ref, send, recv):
    zh, zl, c, core = here()
    signal_all(column_peers(zh, zl, c, core))
    group = zl * 2 + core
    columns = pl.ds(pl.multiple_of(group * GROUP_WIDTH, GROUP_WIDTH), GROUP_WIDTH)
    for s in range(4):
        a, b = s // 2, s % 2
        is_self = (a == zh) & (b == zl) & (core == zh)
        src, dst = a_ref.at[s], o_ref.at[:, columns]

        @pl.when(is_self)
        def _():
            pltpu.make_async_copy(src, dst, recv.at[group]).start()

        @pl.when(jnp.logical_not(is_self))
        def _():
            remote(src, dst, send.at[s], recv.at[group], (a, b, c, zh)).start()

    for s in range(4):
        a, b = s // 2, s % 2
        is_self = (a == zh) & (b == zl) & (core == zh)
        got = o_ref.at[:, pl.ds(s * GROUP_WIDTH, GROUP_WIDTH)]
        pltpu.make_async_copy(got, got, recv.at[s]).wait()

        @pl.when(jnp.logical_not(is_self))
        def _():
            pltpu.make_async_copy(a_ref.at[s], a_ref.at[s], send.at[s]).wait()


def to_tokens(rows):
    tok = rows.shape[1]
    dma = pltpu.SemaphoreType.DMA
    return pl.pallas_call(
        to_tokens_kernel,
        out_shape=jax.ShapeDtypeStruct((tok, MODEL_WIDTH), BF),
        in_specs=[pl.BlockSpec(memory_space=VMEM)],
        out_specs=pl.BlockSpec(memory_space=ANY),
        scratch_shapes=[dma((4,)), dma((4,))],
        compiler_params=pltpu.CompilerParams(collective_id=1, has_side_effects=True),
        name="to_tokens",
    )(rows)


def to_heads_kernel(a_ref, o_ref, send, recv):
    zh, zl, c, core = here()
    signal_all(column_peers(zh, zl, c, core))
    me = zh * 2 + zl
    for g in range(4):
        b, k = g // 2, g % 2
        is_self = (core == zh) & (b == zl) & (core == k)
        src, dst = a_ref.at[:, pl.ds(g * GROUP_WIDTH, GROUP_WIDTH)], o_ref.at[me]

        @pl.when(is_self)
        def _():
            pltpu.make_async_copy(src, dst, recv.at[me]).start()

        @pl.when(jnp.logical_not(is_self))
        def _():
            remote(src, dst, send.at[g], recv.at[me], (core, b, c, k)).start()

    for g in range(4):
        b, k = g // 2, g % 2
        is_self = (core == zh) & (b == zl) & (core == k)
        pltpu.make_async_copy(o_ref.at[g], o_ref.at[g], recv.at[g]).wait()

        @pl.when(jnp.logical_not(is_self))
        def _():
            pltpu.make_async_copy(o_ref.at[g], o_ref.at[g], send.at[g]).wait()


def to_heads(rows):
    tok = rows.shape[0]
    dma = pltpu.SemaphoreType.DMA
    return pl.pallas_call(
        to_heads_kernel,
        out_shape=jax.ShapeDtypeStruct((4, tok, GROUP_WIDTH), BF),
        in_specs=[pl.BlockSpec(memory_space=VMEM)],
        out_specs=pl.BlockSpec(memory_space=ANY),
        scratch_shapes=[dma((4,)), dma((4,))],
        compiler_params=pltpu.CompilerParams(collective_id=2, has_side_effects=True),
        name="to_heads",
    )(rows)


def sum_to_tokens_kernel(p_ref, o_ref, sib, chip, rx, ss, sr, send, recv):
    zh, zl, c, core = here()
    signal_all(column_peers(zh, zl, c, core))
    width = o_ref.shape[1]
    half = width // 2
    sibling = (zh, zl, c, 1 - core)
    mine = pl.ds(pl.multiple_of(core * half, half), half)
    theirs = pl.ds(pl.multiple_of((1 - core) * half, half), half)
    for s in range(4):
        remote(p_ref.at[s, :, theirs], sib.at[s], ss.at[s], sr.at[s], sibling).start()

    def is_self(s):
        return (s // 2 == zh) & (s % 2 == zl) & (core == zh)

    for s in range(4):
        pltpu.make_async_copy(sib.at[s], sib.at[s], sr.at[s]).wait()
        chip[s] = (p_ref[s, :, mine].astype(F32) + sib[s].astype(F32)).astype(BF)
        src, dst = chip.at[s], rx.at[zl, core]

        @pl.when(is_self(s))
        def _():
            pltpu.make_async_copy(src, dst, recv.at[zl, core]).start()

        @pl.when(jnp.logical_not(is_self(s)))
        def _():
            remote(src, dst, send.at[s], recv.at[zl, core], (s // 2, s % 2, c, zh)).start()

    for s in range(4):
        pltpu.make_async_copy(sib.at[s], sib.at[s], ss.at[s]).wait()

        @pl.when(jnp.logical_not(is_self(s)))
        def _():
            pltpu.make_async_copy(chip.at[s], chip.at[s], send.at[s]).wait()

    for k in range(2):
        for b in range(2):
            pltpu.make_async_copy(rx.at[b, k], rx.at[b, k], recv.at[b, k]).wait()
        o_ref[:, k * half : (k + 1) * half] = rx[0, k].astype(F32) + rx[1, k].astype(F32)


def sum_to_tokens(parts):
    _, tok, width = parts.shape
    half = width // 2
    dma = pltpu.SemaphoreType.DMA
    return pl.pallas_call(
        sum_to_tokens_kernel,
        out_shape=jax.ShapeDtypeStruct((tok, width), F32),
        in_specs=[pl.BlockSpec(memory_space=VMEM)],
        out_specs=pl.BlockSpec(memory_space=VMEM),
        scratch_shapes=[
            VMEM((4, tok, half), BF),
            VMEM((4, tok, half), BF),
            VMEM((2, 2, tok, half), BF),
            dma((4,)),
            dma((4,)),
            dma((4,)),
            dma((2, 2)),
        ],
        compiler_params=pltpu.CompilerParams(
            collective_id=3, has_side_effects=True, vmem_limit_bytes=40 * 2**20
        ),
        name="sum_to_tokens",
    )(parts)


def finish_kernel(n_c, p_ref, late, early, o_ref, flat, sib, chip, rx, got_l, stage, got_z, ss, sr, send, recv, ls, lr, zs, zr):
    zh, zl, c, core = here()
    plane = [(zh, zl, lax.rem(c + i, n_c), core ^ k) for i in range(n_c) for k in range(2)]
    signal_all(column_peers(zh, zl, c, core) + plane[2:])
    width = o_ref.shape[1]
    half = width // 2
    sibling = (zh, zl, c, 1 - core)
    mine = pl.ds(pl.multiple_of(core * half, half), half)
    theirs = pl.ds(pl.multiple_of((1 - core) * half, half), half)
    for s in range(4):
        remote(p_ref.at[s, :, theirs], sib.at[s], ss.at[s], sr.at[s], sibling).start()
    me = c * 2 + core
    def is_self(s):
        return (s // 2 == zh) & (s % 2 == zl) & (core == zh)

    for s in range(4):
        pltpu.make_async_copy(sib.at[s], sib.at[s], sr.at[s]).wait()
        chip[s] = (p_ref[s, :, mine].astype(F32) + sib[s].astype(F32)).astype(BF)
        src, dst = chip.at[s], rx.at[zl, core]

        @pl.when(is_self(s))
        def _():
            pltpu.make_async_copy(src, dst, recv.at[zl, core]).start()

        @pl.when(jnp.logical_not(is_self(s)))
        def _():
            remote(src, dst, send.at[s], recv.at[zl, core], (s // 2, s % 2, c, zh)).start()

    count = len(plane)
    for n in range(1, count):
        peer = plane[n]
        remote(late.at[peer[2] * 2 + peer[3]], got_l.at[n], ls.at[n], lr.at[n], peer).start()
    late_sum = late[me].astype(F32)
    for n in range(1, count):
        wait_for(got_l.at[n], lr.at[n])
        late_sum = late_sum + got_l[n].astype(F32)
    late_sum = late_sum.astype(BF)
    down, up, wide, rest = finish_rows(n_c)
    for q in range(4):
        stage[q, :down] = late_sum[q * down : (q + 1) * down]
        if q < 3:
            at = 4 * down + q * up
            stage[q, down : down + up] = late_sum[at : at + up]
            stage[q, down + up : down + wide] = jnp.zeros((wide - up, SPAN), BF)
        else:
            stage[q, down : down + wide] = early[:wide]
        at = wide + q * rest
        stage[q, down + wide :] = early[at : at + rest]
    seq = zh * 2 + zl
    for q in range(4):

        @pl.when(seq == q)
        def _():
            got_z[q] = stage[q]

        @pl.when(seq != q)
        def _():
            remote(stage.at[q], got_z.at[seq], zs.at[q], zr.at[seq], (q // 2, q % 2, c, core)).start()

    for k in range(2):
        for b in range(2):
            pltpu.make_async_copy(rx.at[b, k], rx.at[b, k], recv.at[b, k]).wait()
        o_ref[:, k * half : (k + 1) * half] = rx[0, k].astype(F32) + rx[1, k].astype(F32)

    for q in range(4):

        @pl.when(seq != q)
        def _():
            wait_for(got_z.at[q], zr.at[q])

    terms = [got_z[q].astype(F32) for q in range(4)]
    flat[...] = (terms[0] + terms[1]) + (terms[2] + terms[3])

    @pl.when(seq < 3)
    def _():
        for b in range(2):
            pair = got_z[b, down : down + up].astype(F32) + got_z[2 + b, down : down + up].astype(F32)
            flat[down + b * up : down + (b + 1) * up] = pair

    for s in range(4):
        pltpu.make_async_copy(sib.at[s], sib.at[s], ss.at[s]).wait()

        @pl.when(jnp.logical_not(is_self(s)))
        def _():
            pltpu.make_async_copy(chip.at[s], chip.at[s], send.at[s]).wait()

        @pl.when(seq != s)
        def _():
            wait_for(stage.at[s], zs.at[s])

    for n in range(1, count):
        wait_for(got_l.at[n], ls.at[n])


def finish_rows(n_c):
    n_f = 2 * n_c
    down, up = MODEL_WIDTH // (4 * n_f), SPAN // n_f
    return 3 * down, 8 * up, 16 * up, 2 * down + 16


def finish(parts, late, early, n_c):
    _, tok, width = parts.shape
    half = width // 2
    down, up, wide, rest = finish_rows(n_c)
    n_f = 2 * n_c
    dma = pltpu.SemaphoreType.DMA
    vmem = pl.BlockSpec(memory_space=VMEM)
    return pl.pallas_call(
        functools.partial(finish_kernel, n_c),
        out_shape=(
            jax.ShapeDtypeStruct((tok, width), F32),
            jax.ShapeDtypeStruct((down + wide + rest, SPAN), F32),
        ),
        in_specs=[vmem] * 3,
        out_specs=[vmem] * 2,
        scratch_shapes=[
            VMEM((4, tok, half), BF),
            VMEM((4, tok, half), BF),
            VMEM((2, 2, tok, half), BF),
            VMEM(late.shape, BF),
            VMEM((4, down + wide + rest, SPAN), BF),
            VMEM((4, down + wide + rest, SPAN), BF),
            dma((4,)),
            dma((4,)),
            dma((4,)),
            dma((2, 2)),
            dma((n_f,)),
            dma((n_f,)),
            dma((4,)),
            dma((4,)),
        ],
        compiler_params=pltpu.CompilerParams(
            collective_id=7, has_side_effects=True, vmem_limit_bytes=50 * 2**20
        ),
        name="finish",
    )(parts, late, early)


def group_sum_kernel(x_ref, o_ref, rx, send, recv):
    zh, zl, c, core = here()
    peers = [(zh, zl, c, 1 - core), (zh, 1 - zl, c, core), (zh, 1 - zl, c, 1 - core)]
    signal_all(peers)
    copies = [remote(x_ref, rx.at[i], send.at[i], recv.at[i], p) for i, p in enumerate(peers)]
    for copy in copies:
        copy.start()
    for copy in copies:
        copy.wait()
    o_ref[...] = (x_ref[...] + rx[0]) + (rx[1] + rx[2])


def group_sum(values, identity):
    dma = pltpu.SemaphoreType.DMA
    return pl.pallas_call(
        group_sum_kernel,
        out_shape=jax.ShapeDtypeStruct(values.shape, F32),
        in_specs=[pl.BlockSpec(memory_space=VMEM)],
        out_specs=pl.BlockSpec(memory_space=VMEM),
        scratch_shapes=[VMEM((3, *values.shape), F32), dma((3,)), dma((3,))],
        compiler_params=pltpu.CompilerParams(collective_id=identity, has_side_effects=True),
        name="group_sum",
    )(values)


def turn(values, cosine, sine):
    return values * cosine + pltpu.roll(values, HD // 2, 1) * sine


def attention_rows(block):
    return 256 if block % 256 == 0 else block


def attend_kernel(
    pq, pk, pv, rq, rk, gq, gk, cosine, sine, seg_c, seg_r, q_ref, k_ref, v_ref, o_ref, lse_ref
):
    block = pq.shape[0]
    rows = attention_rows(block)
    scale = HD**-0.5
    q_ref[...] = turn(pq[...] * rq[...] * gq[...], cosine[...], sine[...]).astype(BF)
    k_ref[...] = turn(pk[...] * rk[...] * gk[...], cosine[...], sine[...]).astype(BF)
    v_ref[...] = pv[...].astype(BF)
    for i in range(block // rows):
        length = (i + 1) * rows
        own = slice(i * rows, length)
        scores = mm_t(q_ref[own], k_ref[:length]) * scale
        row = lax.broadcasted_iota(jnp.int32, (rows, length), 0) + i * rows
        column = lax.broadcasted_iota(jnp.int32, (rows, length), 1)
        allowed = (seg_c[own] == seg_r[:, :length]) & (column <= row)
        scores = jnp.where(allowed, scores, NEGATIVE)
        top = jnp.max(scores, axis=1, keepdims=True)
        weights = jnp.exp(scores - top)
        total = jnp.sum(weights, axis=1, keepdims=True)
        out = mm(weights.astype(BF), v_ref[:length]) / total
        o_ref[own] = out.astype(BF)
        lse_ref[0, own] = top + jnp.log(total)


def attend(projected, rq, rk, gq, gk, cosine, sine, seg_c, seg_r):
    block = projected.shape[0]
    head = lambda off: pl.BlockSpec((block, HD), lambda h: (0, off + h))
    gain = pl.BlockSpec((1, HD), lambda h: (0, h))
    fixed = lambda shape: pl.BlockSpec(shape, lambda h: (0, 0))
    wide = jax.ShapeDtypeStruct((block, GROUP_WIDTH), BF)
    return pl.pallas_call(
        attend_kernel,
        grid=(HEADS,),
        out_shape=(wide, wide, wide, wide, jax.ShapeDtypeStruct((HEADS, block, 1), F32)),
        in_specs=[
            head(0),
            head(HEADS),
            head(2 * HEADS),
            fixed((block, 1)),
            fixed((block, 1)),
            gain,
            gain,
            fixed((block, HD)),
            fixed((block, HD)),
            fixed((block, 1)),
            fixed((1, block)),
        ],
        out_specs=[head(0)] * 4 + [pl.BlockSpec((1, block, 1), lambda h: (h, 0, 0))],
        compiler_params=pltpu.CompilerParams(vmem_limit_bytes=60 * 2**20),
        name="attend",
    )(projected, projected, projected, rq, rk, gq, gk, cosine, sine, seg_c, seg_r)


def attend_back_kernel(
    q_ref,
    k_ref,
    v_ref,
    g_ref,
    lse_ref,
    pq,
    pk,
    gq,
    gk,
    cosine,
    sine,
    seg_c,
    seg_r,
    uq_ref,
    uk_ref,
    dv_ref,
    mq_ref,
    mk_ref,
    dk_acc,
    dv_acc,
):
    block = q_ref.shape[0]
    rows = attention_rows(block)
    scale = HD**-0.5
    dk_acc[...] = jnp.zeros_like(dk_acc)
    dv_acc[...] = jnp.zeros_like(dv_acc)

    def back(grad, raw, gain):
        turned = turn(grad.astype(BF).astype(F32), cosine_of, -sine_of)
        return turned, jnp.sum(raw * gain[...] * turned, axis=1, keepdims=True)

    for i in range(block // rows):
        length = (i + 1) * rows
        own = slice(i * rows, length)
        scores = mm_t(q_ref[own], k_ref[:length]) * scale
        row = lax.broadcasted_iota(jnp.int32, (rows, length), 0) + i * rows
        column = lax.broadcasted_iota(jnp.int32, (rows, length), 1)
        allowed = (seg_c[own] == seg_r[:, :length]) & (column <= row)
        probs = jnp.where(allowed, jnp.exp(scores - lse_ref[0, own]), 0.0)
        grad_probs = mm_t(g_ref[own], v_ref[:length])
        delta = jnp.sum(probs * grad_probs, axis=1, keepdims=True)
        grad_scores = (probs * (grad_probs - delta)).astype(BF)
        grad_q = mm(grad_scores, k_ref[:length]) * scale
        cosine_of, sine_of = cosine[own], sine[own]
        turned, moment = back(grad_q, pq[own], gq)
        uq_ref[own] = turned
        mq_ref[0, own] = moment
        dk_acc[:length] += t_mm(grad_scores, q_ref[own])
        dv_acc[:length] += t_mm(probs.astype(BF), g_ref[own])
    cosine_of, sine_of = cosine[...], sine[...]
    turned, moment = back(dk_acc[...] * scale, pk[...], gk)
    uk_ref[...] = turned
    mk_ref[0] = moment
    dv_ref[...] = dv_acc[...].astype(BF)


def attend_back(q, k, v, grad, lse, projected, gq, gk, cosine, sine, seg_c, seg_r):
    block = q.shape[0]
    head = lambda off: pl.BlockSpec((block, HD), lambda h: (0, off + h))
    gain = pl.BlockSpec((1, HD), lambda h: (0, h))
    fixed = lambda shape: pl.BlockSpec(shape, lambda h: (0, 0))
    column = pl.BlockSpec((1, block, 1), lambda h: (h, 0, 0))
    wide = lambda t: jax.ShapeDtypeStruct((block, GROUP_WIDTH), t)
    moment = jax.ShapeDtypeStruct((HEADS, block, 1), F32)
    return pl.pallas_call(
        attend_back_kernel,
        grid=(HEADS,),
        out_shape=(wide(F32), wide(F32), wide(BF), moment, moment),
        in_specs=[
            head(0),
            head(0),
            head(0),
            head(0),
            column,
            head(0),
            head(HEADS),
            gain,
            gain,
            fixed((block, HD)),
            fixed((block, HD)),
            fixed((block, 1)),
            fixed((1, block)),
        ],
        out_specs=[head(0)] * 3 + [column] * 2,
        scratch_shapes=[VMEM((block, HD), F32), VMEM((block, HD), F32)],
        compiler_params=pltpu.CompilerParams(vmem_limit_bytes=60 * 2**20),
        name="attend_back",
    )(q, k, v, grad, lse, projected, projected, gq, gk, cosine, sine, seg_c, seg_r)


WIDE_IN = MODEL_WIDTH + 2 * SPAN
WIDE_OUT = MODEL_WIDTH + SPAN
CHUNK = 16
TERM_PARTS = 4
TERM_ROWS = MODEL_WIDTH // 4 + 2 * SPAN + SPAN + 2 * SPAN


def over_rows(count, body):
    def step(n, carry):
        body(pl.ds(pl.multiple_of(n * CHUNK, CHUNK), CHUNK))
        return carry

    lax.fori_loop(0, count // CHUNK, step, 0)


def wait_for(ref, sem):
    pltpu.make_async_copy(ref, ref, sem).wait()


def experts_kernel(n_c, experts, slots, comm, *refs):
    x_ref, g_ref, h_gu, h_d, h_id, h_iu, h_od, h_ou = refs[:8]
    refs = refs[8:]
    out_ref, row_ref, terms_o = refs[:3]
    refs = refs[3:]
    if comm:
        xg_ref, final, first_o = refs[:3]
        refs = refs[3:]
    else:
        xg_ref = x_ref
    (wb, db, xw, gw, xl, dr, gu, hl, dh, dgl, res, pick, gate, mom, mask) = refs[:15]
    (to, tr, gid, giu, god, gou, packed, wsem, csem, osem) = refs[15:25]
    refs = refs[25:]
    zh, zl, c, core = here()
    tok = xw.shape[1]
    extra = xw.shape[2] - MODEL_WIDTH
    tiles = n_c
    f = c * 2 + core
    near = lambda i: (
        lax.rem(c // 2 + i // 2, 2) * 2 + lax.rem(lax.rem(c, 2) + lax.rem(i, 2), 2)
    )

    def pair(ref, p):
        return ref.at[pl.ds(p * 2, 2)]

    def load_in(expert):
        yield pltpu.make_async_copy(h_id.at[expert], wb.at[:MODEL_WIDTH, MODEL_WIDTH:], wsem.at[0])
        yield pltpu.make_async_copy(h_gu.at[expert], wb.at[:MODEL_WIDTH, :MODEL_WIDTH], wsem.at[1])
        for j in range(2):
            rows = slice(MODEL_WIDTH + j * SPAN, MODEL_WIDTH + (j + 1) * SPAN)
            columns = slice(j * EXPERT_HIDDEN, (j + 1) * EXPERT_HIDDEN)
            yield pltpu.make_async_copy(h_iu.at[expert, j], wb.at[rows, columns], wsem.at[2 + j])

    def load_out(expert):
        yield pltpu.make_async_copy(h_d.at[expert], db.at[:EXPERT_HIDDEN, :MODEL_WIDTH], wsem.at[4])
        yield pltpu.make_async_copy(h_od.at[expert], db.at[:EXPERT_HIDDEN, MODEL_WIDTH:], wsem.at[5])
        yield pltpu.make_async_copy(h_ou.at[expert], db.at[EXPERT_HIDDEN:, :MODEL_WIDTH], wsem.at[6])

    terms = (gid, giu, god, gou)

    def term_copy(e):
        return pltpu.make_async_copy(packed, terms_o if comm else terms_o.at[:, e], osem.at[0])

    def send_first_terms():
        pltpu.make_async_copy(packed.at[seq], first_o.at[seq], osem.at[0]).start()
        for q in range(TERM_PARTS):

            @pl.when(seq != q)
            def _():
                remote(packed.at[q], first_o.at[seq], tsend.at[q], trecv.at[seq], (q // 2, q % 2, c, core)).start()

    def wait_first_terms(sent):
        for q in range(TERM_PARTS):

            @pl.when(seq != q)
            def _():
                if sent:
                    wait_for(packed.at[q], tsend.at[q])
                else:
                    wait_for(first_o.at[q], trecv.at[q])

        if sent:
            wait_for(packed.at[0], osem.at[0])

    def pack_terms():
        for q in range(TERM_PARTS):
            rows, columns = MODEL_WIDTH // 4, EXPERT_HIDDEN // 4
            packed[q, :rows] = gid[q * rows : (q + 1) * rows].astype(BF)
            for j in range(2):
                at = rows + j * SPAN
                packed[q, at : at + SPAN] = giu[j, :, q * columns : (q + 1) * columns].astype(BF)
            at = rows + 2 * SPAN
            for j in range(2):
                half = slice(j * SPAN, (j + 1) * SPAN)
                row = q * columns + j * SPAN
                packed[q, at : at + SPAN, half] = god[row : row + SPAN].astype(BF)
                column = q * rows + j * 256
                low = at + (j + 1) * SPAN
                packed[q, low : low + SPAN] = gou[:, column : column + 256].astype(BF)

    if comm:
        sib, la, lb, fx, fy, sums, sendx, recvx, sends, recvs, tsend, trecv = refs
        seq = zh * 2 + zl
        same = lambda i: (zh, zl, near(i), core)
        sibling = (zh, zl, c, 1 - core)
        low_half, high_half = pl.ds(0, tok // 2), pl.ds(tok // 2, tok // 2)
        column = [(zh ^ 1, zl, c, core), (zh, zl ^ 1, c, core), (zh ^ 1, zl ^ 1, c, core)]
        signal_all([sibling, same(1), same(2), *column])
        first = [
            remote(x_ref, xg_ref.at[f], sendx.at[n], recvx.at[n], to_)
            for n, to_ in enumerate((sibling, same(1), same(2)))
        ]
        for copy in first:
            copy.start()
        fx1, fy1, fd1 = near(1) * 2 + core, near(2) * 2 + core, near(3) * 2 + core
        forward = [
            remote(xg_ref.at[fx1, low_half], xg_ref.at[fx1, low_half], sendx.at[3], recvx.at[3], same(2)),
            remote(xg_ref.at[fy1, high_half], xg_ref.at[fy1, high_half], sendx.at[4], recvx.at[4], same(1)),
            remote(xg_ref.at[fx1], xg_ref.at[fx1], sendx.at[5], recvx.at[5], sibling),
            remote(xg_ref.at[fy1], xg_ref.at[fy1], sendx.at[6], recvx.at[6], sibling),
        ]
        across = remote(xg_ref.at[fd1], xg_ref.at[fd1], sendx.at[7], recvx.at[7], sibling)

    for copy in (*load_in(0), *load_out(0)):
        copy.start()
    spare = EXPERT_HIDDEN
    wb[MODEL_WIDTH : MODEL_WIDTH + SPAN, spare:] = jnp.zeros((SPAN, WIDE_IN - spare), BF)
    wb[MODEL_WIDTH + SPAN :, :spare] = jnp.zeros((SPAN, spare), BF)
    for ref in terms:
        ref[...] = jnp.zeros_like(ref)

    def order(s):
        e = s // tiles
        i = s + e * (2 * tiles - 1 - 2 * s)
        return e, i, (near(i) if comm else i)

    def fetch_x(p):
        return pltpu.make_async_copy(pair(xg_ref, p), xw, csem.at[0])

    def fetch_own():
        other = xg_ref.at[c * 2 + 1 - core]
        pltpu.make_async_copy(x_ref, xw.at[core], csem.at[0]).start()
        pltpu.make_async_copy(other, xw.at[1 - core], csem.at[0]).start()

    def fetch_g(p):
        return pltpu.make_async_copy(pair(g_ref, p), gw, csem.at[1])

    if comm:
        fetch_g(c).start()
        wait_for(xg_ref.at[c * 2 + 1 - core], recvx.at[0])
        fetch_own()
    else:
        fetch_g(0).start()
        fetch_x(0).start()

    def write_out(p):
        return pltpu.make_async_copy(to, pair(out_ref, p), csem.at[2])

    def write_row(p):
        return pltpu.make_async_copy(tr, pair(row_ref, p), csem.at[3])

    def read_out(p):
        return pltpu.make_async_copy(pair(out_ref, p), to, csem.at[4])

    def read_row(p):
        return pltpu.make_async_copy(pair(row_ref, p), tr, csem.at[5])

    both = 2 * slots
    steps = 2 * tiles
    part = lambda d: slice(d * slots, (d + 1) * slots)
    pieces = [
        (
            slice(r, r + CHUNK),
            slice(h * 512, (h + 1) * 512),
            slice(EXPERT_HIDDEN + h * 512, EXPERT_HIDDEN + (h + 1) * 512),
        )
        for r in range(0, both, CHUNK)
        for h in range(2)
    ]

    def step(s, carry):
        e, i, p = order(s)
        _, _, after = order(jnp.minimum(s + 1, steps - 1))
        number = c * (2 * EXP_DEV) + core * EXP_DEV + e
        fetch_x(p).wait()
        fetch_g(p).wait()
        lane = lax.broadcasted_iota(jnp.int32, (tok, extra), 1)
        lane_s = lax.broadcasted_iota(jnp.int32, (slots, extra), 1)
        for d in range(2):
            side = xw[d, :, MODEL_WIDTH:].astype(F32)
            place = jnp.sum(jnp.where(lane == number, side, 0.0), axis=1, keepdims=True)
            slot = lax.broadcasted_iota(jnp.int32, (tok, slots), 1).astype(F32)
            pick[d] = jnp.where(slot == place, 1.0, 0.0).astype(BF)
            sub = lax.broadcasted_iota(jnp.int32, (extra, tok), 0)
            place_t = jnp.sum(jnp.where(sub == number, side.T, 0.0), axis=0, keepdims=True)
            slot_t = lax.broadcasted_iota(jnp.int32, (slots, tok), 0).astype(F32)
            pickt = jnp.where(slot_t == place_t, 1.0, 0.0).astype(BF)
            xl[part(d), :MODEL_WIDTH] = mm(pickt, xw[d, :, :MODEL_WIDTH]).astype(BF)
            dr[part(d), :MODEL_WIDTH] = mm(pickt, gw[d]).astype(BF)
            side = mm(pickt, xw[d, :, MODEL_WIDTH:])
            read = lambda which: jnp.sum(jnp.where(which, side, 0.0), axis=1, keepdims=True)
            gate[part(d)] = read((lane_s == experts + number) | (lane_s == 2 * experts + number))
            columns = lax.broadcasted_iota(jnp.int32, (slots, SPAN), 1) // ADAPTER_RANK
            mask[part(d)] = jnp.where(columns.astype(F32) == read(lane_s == 3 * experts), 1.0, 0.0)

        @pl.when((s > 0) & (s <= tiles) if comm else s > 0)
        def _():
            write_row(p).wait()

        @pl.when(s > 0)
        def _():
            write_out(p).wait()

        @pl.when(e > 0)
        def _():
            read_out(p).start()
            read_row(p).start()

        @pl.when(s == 0)
        def _():
            for copy in (*load_in(0), *load_out(0)):
                copy.wait()

        @pl.when(s == tiles)
        def _():
            for copy in (*load_in(1), *load_out(1), *(() if comm else (term_copy(0),))):
                copy.wait()
            for ref in terms:
                ref[...] = jnp.zeros_like(ref)

        mask2 = lambda: jnp.concatenate([mask[...], mask[...]], axis=1)
        xl[:, MODEL_WIDTH:] = (mm(xl[:, :MODEL_WIDTH], wb[:MODEL_WIDTH, MODEL_WIDTH:]) * mask2()).astype(BF)
        gu[...] = mm(xl[...], wb[:, :MODEL_WIDTH])

        for rows, a, b in pieces:
            gate_part = gu[rows, a]
            hl[rows, a] = (gate_part / (1.0 + jnp.exp(-gate_part)) * gu[rows, b]).astype(BF)
        hl[:, EXPERT_HIDDEN:] = (
            mm(hl[:, :EXPERT_HIDDEN], db[:EXPERT_HIDDEN, MODEL_WIDTH:]) * mask[...]
        ).astype(BF)
        for n in range(4):
            a = slice(n * 512, (n + 1) * 512)
            res[:, a] = (mm(hl[...], db[:, a]) * gate[...]).astype(BF)

        @pl.when(e > 0)
        def _():
            read_out(p).wait()

        def add_picked(target, d):
            for n in range(4):
                a = slice(n * 512, (n + 1) * 512)
                before = jnp.where(e > 0, target[d, :, a].astype(F32), 0.0)
                target[d, :, a] = (before + mm(pick[d], res[part(d), a])).astype(BF)

        for d in range(2):
            add_picked(to, d)
        write_out(p).start()

        @pl.when(s < steps - 1)
        def _():
            fetch_g(after).start()

        dr[:, MODEL_WIDTH:] = (
            mm_t(dr[:, :MODEL_WIDTH], db[EXPERT_HIDDEN:, :MODEL_WIDTH]) * mask[...]
        ).astype(BF)
        dh[...] = mm_t(dr[...], db[:EXPERT_HIDDEN, :])

        @pl.when(s == tiles - 1)
        def _():
            for copy in load_out(1):
                copy.start()

        mom[...] = jnp.zeros_like(mom)
        for rows, a, b in pieces:
            gate_part, up_part, grad = gu[rows, a], gu[rows, b], dh[rows, a]
            sigmoid = 1.0 / (1.0 + jnp.exp(-gate_part))
            activated = gate_part * sigmoid
            plain = grad * activated
            mom[rows] += jnp.sum(plain * up_part, axis=1, keepdims=True)
            dgl[rows, b] = (plain * gate[rows]).astype(BF)
            slope = sigmoid + activated - activated * sigmoid
            dgl[rows, a] = (grad * gate[rows] * up_part * slope).astype(BF)
        dgl[:, MODEL_WIDTH:] = (
            mm_t(dgl[:, :MODEL_WIDTH], wb[MODEL_WIDTH:, :MODEL_WIDTH]) * mask2()
        ).astype(BF)
        for n in range(4):
            a = slice(n * 512, (n + 1) * 512)
            res[:, a] = mm_t(dgl[...], wb[a, :]).astype(BF)

        @pl.when(s == tiles - 1)
        def _():
            for copy in load_in(1):
                copy.start()

        if comm:
            @pl.when(s == 0)
            def _():
                wait_for(xg_ref.at[fx1], recvx.at[1])
                forward[0].start()
                forward[2].start()
                wait_for(xg_ref.at[fy1], recvx.at[2])
                forward[1].start()
                forward[3].start()
                wait_for(xg_ref.at[fx1], recvx.at[5])

            @pl.when(s == 1)
            def _():
                wait_for(xg_ref.at[fd1, low_half], recvx.at[3])
                wait_for(xg_ref.at[fd1, high_half], recvx.at[4])
                across.start()
                wait_for(xg_ref.at[fy1], recvx.at[6])

            @pl.when(s == 2)
            def _():
                wait_for(xg_ref.at[fd1], recvx.at[7])

        @pl.when(s < steps - (2 if comm else 1))
        def _():
            fetch_x(after).start()

        if comm:

            @pl.when(s == steps - 2)
            def _():
                fetch_own()

        @pl.when(e > 0)
        def _():
            read_row(p).wait()

        for d in range(2):
            add_picked(tr, d)
            moment = mom[part(d)]
            high = moment.astype(BF).astype(F32)
            side = jnp.where(lane_s == number, high, 0.0) + jnp.where(
                lane_s == experts + number, moment - high, 0.0
            )
            before = jnp.where(e > 0, tr[d, :, MODEL_WIDTH:].astype(F32), 0.0)
            tr[d, :, MODEL_WIDTH:] = (before + mm(pick[d], side.astype(BF))).astype(BF)

        if comm:
            to_sibling = remote(
                tr.at[1 - core], sib.at[lax.rem(i, 2)], sends.at[lax.rem(i, 2)],
                recvs.at[lax.rem(i, 2)], sibling,
            )

            @pl.when(e == 0)
            def _():
                write_row(p).start()

            @pl.when(e > 0)
            def _():
                to_sibling.start()
        else:
            write_row(p).start()

        gid[...] += t_mm(xl[:, :MODEL_WIDTH], dgl[:, MODEL_WIDTH:])
        for j in range(2):
            giu[j] += t_mm(
                xl[:, MODEL_WIDTH + j * SPAN : MODEL_WIDTH + (j + 1) * SPAN],
                dgl[:, j * EXPERT_HIDDEN : (j + 1) * EXPERT_HIDDEN],
            )
        god[...] += t_mm(hl[:, :EXPERT_HIDDEN], (dr[:, MODEL_WIDTH:].astype(F32) * gate[...]).astype(BF))
        gou[...] += t_mm((hl[:, EXPERT_HIDDEN:].astype(F32) * gate[...]).astype(BF), dr[:, :MODEL_WIDTH])

        @pl.when(s == tiles - 1)
        def _():
            pack_terms()
            if comm:
                send_first_terms()
            else:
                term_copy(0).start()

        if comm:
            half = tok // 2

            def chip_sum(at, rows):
                return tr[core, rows].astype(F32) + sib[at, rows].astype(F32)

            @pl.when(e > 0)
            def _():
                to_sibling.wait()

            @pl.when(s == steps - 4)
            def _():
                def body(rows):
                    sums[0, rows] = chip_sum(1, rows).astype(BF)

                over_rows(tok, body)
                remote(sums.at[0, low_half], la, sends.at[2], recvs.at[2], same(1)).start()
                remote(sums.at[0, high_half], lb, sends.at[3], recvs.at[3], same(2)).start()

            @pl.when(s == steps - 3)
            def _():
                wait_for(la, recvs.at[2])

                def body(rows):
                    sums[1, rows] = (chip_sum(0, rows) + la[rows].astype(F32)).astype(BF)

                def rest(rows):
                    rows = pl.ds(pl.multiple_of(rows.start + half, CHUNK), CHUNK)
                    sums[1, rows] = chip_sum(0, rows).astype(BF)

                over_rows(half, body)
                over_rows(half, rest)
                remote(sums.at[1], fy, sends.at[4], recvs.at[4], same(2)).start()

            @pl.when(s == steps - 2)
            def _():
                wait_for(lb, recvs.at[3])

                def body(rows):
                    sums[2, rows] = chip_sum(1, rows).astype(BF)

                def rest(rows):
                    upper = pl.ds(pl.multiple_of(rows.start + half, CHUNK), CHUNK)
                    sums[2, upper] = (chip_sum(1, upper) + lb[rows].astype(F32)).astype(BF)

                over_rows(half, body)
                over_rows(half, rest)
                remote(sums.at[2], fx, sends.at[5], recvs.at[5], same(1)).start()

        return carry

    lax.fori_loop(0, steps, step, 0)
    if comm:
        wait_first_terms(True)
    pack_terms()
    term_copy(1).start()
    _, _, last = order(steps - 1)
    write_out(last).wait()
    if comm:
        wait_for(fx, recvs.at[5])
        wait_for(fy, recvs.at[4])

        def body(rows):
            total = tr[core, rows].astype(F32) + sib[0, rows].astype(F32)
            final[rows] = (total + (fx[rows].astype(F32) + fy[rows].astype(F32))).astype(BF)

        over_rows(tok, body)
        wait_for(la, sends.at[2])
        wait_for(lb, sends.at[3])
        wait_for(fy, sends.at[4])
        wait_for(fx, sends.at[5])
        for copy in first:
            copy.wait_send()
        for copy in forward:
            copy.wait_send()
        across.wait_send()
        wait_first_terms(False)
    else:
        write_row(last).wait()
    term_copy(1).wait()


def run_experts(x, g, weights, experts, slots, n_c, comm):
    tok, wide = x.shape[-2:]
    sources = 2 * n_c
    both = 2 * slots
    dma = pltpu.SemaphoreType.DMA
    term_shapes = (
        (MODEL_WIDTH, 2 * SPAN),
        (2, SPAN, EXPERT_HIDDEN),
        (EXPERT_HIDDEN, SPAN),
        (SPAN, MODEL_WIDTH),
    )
    any_spec = pl.BlockSpec(memory_space=ANY)
    out_shape = [
        jax.ShapeDtypeStruct((sources, tok, MODEL_WIDTH), BF),
        jax.ShapeDtypeStruct((sources, tok, wide), BF),
        jax.ShapeDtypeStruct(
            (TERM_PARTS, TERM_ROWS, 256) if comm else (TERM_PARTS, EXP_DEV, TERM_ROWS, 256), BF
        ),
    ]
    out_specs = [any_spec] * 3
    scratch = [
        VMEM((WIDE_IN, WIDE_IN), BF),
        VMEM((EXPERT_HIDDEN + SPAN, WIDE_OUT), BF),
        VMEM((2, tok, wide), BF),
        VMEM((2, tok, MODEL_WIDTH), BF),
        VMEM((both, WIDE_IN), BF),
        VMEM((both, WIDE_OUT), BF),
        VMEM((both, MODEL_WIDTH), F32),
        VMEM((both, EXPERT_HIDDEN + SPAN), BF),
        VMEM((both, EXPERT_HIDDEN), F32),
        VMEM((both, WIDE_IN), BF),
        VMEM((both, MODEL_WIDTH), BF),
        VMEM((2, tok, slots), BF),
        VMEM((both, 1), F32),
        VMEM((both, 1), F32),
        VMEM((both, SPAN), F32),
        VMEM((2, tok, MODEL_WIDTH), BF),
        VMEM((2, tok, wide), BF),
        *(VMEM(s, F32) for s in term_shapes),
        VMEM((TERM_PARTS, TERM_ROWS, 256), BF),
        dma((7,)),
        dma((6,)),
        dma((1,)),
    ]
    params = {}
    if comm:
        out_shape += [
            jax.ShapeDtypeStruct((sources, tok, wide), BF),
            jax.ShapeDtypeStruct((tok, wide), BF),
            jax.ShapeDtypeStruct((TERM_PARTS, TERM_ROWS, 256), BF),
        ]
        out_specs += [any_spec, pl.BlockSpec(memory_space=VMEM), any_spec]
        scratch += [
            VMEM((2, tok, wide), BF),
            VMEM((tok // 2, wide), BF),
            VMEM((tok // 2, wide), BF),
            VMEM((tok, wide), BF),
            VMEM((tok, wide), BF),
            VMEM((3, tok, wide), BF),
            dma((8,)),
            dma((8,)),
            dma((6,)),
            dma((6,)),
            dma((TERM_PARTS,)),
            dma((TERM_PARTS,)),
        ]
        params = dict(collective_id=6, has_side_effects=True)
    flops = 2 * sources * EXP_DEV * slots * MODEL_WIDTH * EXPERT_HIDDEN * 8
    results = pl.pallas_call(
        functools.partial(experts_kernel, n_c, experts, slots, comm),
        out_shape=out_shape,
        in_specs=[any_spec] * 8,
        out_specs=out_specs,
        scratch_shapes=scratch,
        compiler_params=pltpu.CompilerParams(vmem_limit_bytes=63 * 2**20, **params),
        cost_estimate=pl.CostEstimate(flops=flops, bytes_accessed=10**8, transcendentals=10**7),
        name="experts",
    )(x, g, *weights)
    if comm:
        return results[0], results[4], (results[5], results[2])
    return results[0], results[1], results[2]


def late_kernel(n_f, dp, up, mask, low, x, dlow, packed):
    core = lax.axis_index("core")
    down_rows = MODEL_WIDTH // (4 * n_f)
    up_rows = SPAN // n_f
    base = 12 * down_rows
    packed[:, base:] = jnp.zeros((n_f, 24 * up_rows, SPAN), BF)
    for j in range(3):
        own = slice(j * SPAN, (j + 1) * SPAN)
        wide = slice(j * GROUP_WIDTH, (j + 1) * GROUP_WIDTH)
        lowered = (mm_t(dp[:, wide], up[own]) * mask[...]).astype(BF)
        dlow[:, own] = lowered
        grad_up = t_mm(low[:, own], dp[:, wide]).astype(BF)
        grad_down = t_mm(x[...], lowered).astype(BF)
        for f in range(n_f):
            for b in range(4):
                at = base + (j * 8 + core * 4 + b) * up_rows
                packed[f, pl.ds(pl.multiple_of(at, up_rows), up_rows)] = grad_up[
                    f * up_rows : (f + 1) * up_rows, b * SPAN : (b + 1) * SPAN
                ]
            for q in range(4):
                row = (q * n_f + f) * down_rows
                at = (q * 3 + j) * down_rows
                packed[f, at : at + down_rows] = grad_down[row : row + down_rows]


def late_gradients(grad_projected, up_own, mask, lowered, x, n_f):
    block = x.shape[0]
    rows = 12 * MODEL_WIDTH // (4 * n_f) + 24 * SPAN // n_f
    return pl.pallas_call(
        functools.partial(late_kernel, n_f),
        out_shape=(
            jax.ShapeDtypeStruct((block, 3 * SPAN), BF),
            jax.ShapeDtypeStruct((n_f, rows, SPAN), BF),
        ),
        in_specs=[pl.BlockSpec(memory_space=VMEM)] * 5,
        out_specs=[pl.BlockSpec(memory_space=VMEM)] * 2,
        compiler_params=pltpu.CompilerParams(vmem_limit_bytes=50 * 2**20),
        cost_estimate=pl.CostEstimate(flops=4 * 10**9, bytes_accessed=2 * 10**7, transcendentals=0),
        name="late_gradients",
    )(grad_projected, up_own, mask, lowered, x)


def on_device(
    tokens,
    cotangent,
    lengths,
    sets,
    routes,
    gain_attn,
    gain_query,
    gain_key,
    gain_mlp,
    query_key_value_weight,
    out_weight,
    router_weight,
    gate_up_weight,
    down_weight,
    attention_down_factors,
    attention_up_factors,
    router_down_factors,
    router_up_factors,
    expert_input_down,
    expert_input_up,
    expert_output_down,
    expert_output_up,
):
    zh, zl, c, core = here()
    n_c = lax.axis_size("c")
    n_fsdp = 2 * n_c
    n_seq = lax.axis_size("zh") * lax.axis_size("zl")
    tok = tokens.shape[1]
    block = tok * n_seq
    experts = EXP_DEV * n_fsdp
    capacity = 5 * tok * TOP // (4 * experts)
    slots = -(-capacity // 16) * 16
    extra = -(-(3 * experts + 1) // 128) * 128
    span3 = 3 * SPAN
    group = zl * 2 + core
    shard = zh * 2 + zl

    both_lengths = lax.all_gather(
        jnp.concatenate([lengths[0], sets[0]]), "core", axis=0, tiled=False
    )
    held_lengths = lax.dynamic_index_in_dim(both_lengths, zh, 0, keepdims=False)
    count = lengths.shape[1]

    inputs = tokens[0].astype(F32)
    normalized = rms_scale(inputs, gain_attn).astype(BF)
    x_shards, qkv_rows = gather_to_heads(normalized, query_key_value_weight, n_c)

    rows_local = query_key_value_weight.shape[0]
    factors = jnp.concatenate(
        [
            attention_down_factors,
            attention_up_factors.reshape(rows_local, -1),
            router_down_factors,
            router_weight,
            router_up_factors.reshape(rows_local, -1),
        ],
        axis=1,
    )
    factor_width = factors.shape[1]
    factors = jnp.pad(factors, ((0, 0), (0, -factor_width % 128)))
    factors = lax.all_gather(factors, FSDP, axis=0, tiled=True)
    up_columns = attention_up_factors.size // rows_local
    down_full = factors[:, : 4 * SPAN]
    at = 4 * SPAN
    up_full = factors[:, at : at + up_columns].reshape(4 * SPAN, MODEL_WIDTH)
    at += up_columns
    rdown_full = factors[:, at : at + SPAN]
    at += SPAN
    router_full = factors[:, at : at + experts]
    at += experts
    rup_full = factors[:, at:factor_width].reshape(SPAN, experts)
    out_full = lax.all_gather(out_weight, FSDP, axis=0, tiled=True)
    grad_rows_all = lax.all_gather(cotangent[0], FSDP, axis=0, tiled=True)

    seq_local, _, chosen = token_meta(
        lengths[0], sets[0], shard * tok + jnp.arange(tok, dtype=jnp.int32)
    )
    mask = set_mask(chosen)
    seq_block, block_offsets, block_sets = token_meta(
        held_lengths[:count], held_lengths[count:], jnp.arange(block, dtype=jnp.int32)
    )
    mask1 = set_mask(block_sets)
    mask3 = jnp.tile(mask1, (1, 3))
    half = HD // 2
    freqs = THETA ** (-(jnp.arange(half, dtype=F32) * 2.0 / HD))
    angles = block_offsets.astype(F32)[:, None] * freqs[None, :]
    cosine, sine = jnp.cos(angles), jnp.sin(angles)
    cosine = jnp.concatenate([cosine, cosine], axis=1)
    sine = jnp.concatenate([-sine, sine], axis=1)
    seg_c, seg_r = seq_block[:, None], seq_block[None, :]

    x_all = x_shards.reshape(block, MODEL_WIDTH)
    down3 = down_full[:, :span3]
    lowered = (mm(x_all, down3) * mask3).astype(BF)
    up_own = lax.dynamic_slice_in_dim(up_full[:span3], group * GROUP_WIDTH, GROUP_WIDTH, 1)
    none = jnp.zeros((SPAN, GROUP_WIDTH), BF)
    up_diagonal = jnp.concatenate(
        [
            jnp.concatenate(
                [up_own[j * SPAN : (j + 1) * SPAN] if i == j else none for i in range(3)], axis=1
            )
            for j in range(3)
        ],
        axis=0,
    )
    projected = mm(x_all, qkv_rows) + mm(lowered, up_diagonal)
    part_q, part_k = projected[:, :GROUP_WIDTH], projected[:, GROUP_WIDTH : 2 * GROUP_WIDTH]

    def over_group(first, second, identity):
        both = jnp.stack([first, second]).reshape(-1, 128)
        return group_sum(both, identity).reshape(2, block)

    squares = over_group(jnp.sum(part_q * part_q, axis=1), jnp.sum(part_k * part_k, axis=1), 4)
    inverse = lax.rsqrt(squares / MODEL_WIDTH + EPSILON)
    rq, rk = inverse[0][:, None], inverse[1][:, None]
    gains = [
        lax.dynamic_slice_in_dim(g, group * GROUP_WIDTH, GROUP_WIDTH)[None, :]
        for g in (gain_query, gain_key)
    ]
    q, k, v, attended_heads, lse = attend(
        projected, rq, rk, *gains, cosine, sine, seg_c, seg_r
    )
    attended = to_tokens(attended_heads.reshape(4, tok, GROUP_WIDTH))

    down_o, up_o = down_full[:, span3:], up_full[span3:]
    out_lower = (mm(attended, down_o) * mask).astype(BF)
    branch = mm(attended, out_full) + mm(out_lower, up_o)
    middle = inputs + branch
    normed2 = rms_scale(middle, gain_mlp).astype(BF)
    router_lower = (mm(normed2, rdown_full) * mask).astype(BF)
    logits = mm(normed2, router_full) + mm(router_lower, rup_full)
    probs = jax.nn.softmax(logits, axis=-1)
    hits = jnp.sum(
        (routes[0][:, :, None] == jnp.arange(experts, dtype=jnp.int32)[None, None, :]).astype(F32),
        axis=1,
    )
    place = jnp.arange(tok, dtype=jnp.int32)
    before = (place[None, :] < place[:, None]).astype(BF)
    ranks = jnp.where(hits > 0, mm(before, hits.astype(BF)), -1.0).astype(BF)
    gates = hits * probs
    gates_high = gates.astype(BF)
    gates_low = (gates - gates_high.astype(F32)).astype(BF)
    side = jnp.concatenate(
        [ranks, gates_high, gates_low, chosen.astype(BF)[:, None]], axis=1
    )
    payload = jnp.concatenate(
        [normed2, jnp.pad(side, ((0, 0), (0, extra - side.shape[1])))], axis=1
    )
    weights = (
        gate_up_weight,
        down_weight,
        expert_input_down,
        expert_input_up,
        expert_output_down,
        expert_output_up,
    )
    grads_all = grad_rows_all.reshape(n_fsdp, tok, MODEL_WIDTH)
    if n_c == 4:
        out_parts, returned, expert_terms = run_experts(
            payload, grads_all, weights, experts, slots, n_c, True
        )
    else:
        rows_all = lax.all_gather(payload, FSDP, axis=0, tiled=True)
        out_parts, row_parts, expert_terms = run_experts(
            rows_all.reshape(n_fsdp, tok, -1), grads_all, weights, experts, slots, n_c, False
        )
        returned = lax.psum_scatter(
            row_parts.reshape(n_fsdp * tok, -1), FSDP, scatter_dimension=0, tiled=True
        )
    mixed = lax.psum_scatter(
        out_parts.reshape(n_fsdp * tok, -1), FSDP, scatter_dimension=0, tiled=True
    )
    grad_out = cotangent[0].astype(F32)
    returned = returned.astype(F32)
    back = returned[:, MODEL_WIDTH:]
    grad_probs = back[:, :experts] + back[:, experts : 2 * experts]
    grad_logits = probs * (grad_probs - jnp.sum(probs * grad_probs, axis=-1, keepdims=True))
    grad_router_lower = exact("te,re->tr", grad_logits, rup_full.astype(F32)) * mask
    grad_normed2 = (
        returned[:, :MODEL_WIDTH]
        + mm_t(grad_logits.astype(BF), router_full)
        + mm_t(grad_router_lower.astype(BF), rdown_full)
    )
    grad_rup = t_mm(router_lower, grad_logits.astype(BF))
    grad_rdown = t_mm(normed2, grad_router_lower.astype(BF))
    grad_middle = grad_out + rms_back(middle, gain_mlp, grad_normed2)
    grad_branch = grad_middle.astype(BF)
    grad_out_lower = (mm_t(grad_branch, up_o) * mask).astype(BF)
    grad_attended = (mm_t(grad_branch, out_full) + mm_t(grad_out_lower, down_o)).astype(BF)
    head_grad = to_heads(grad_attended).reshape(block, GROUP_WIDTH)
    if n_c == 4:
        first_terms, second_terms = expert_terms
        second_terms, head_grad = lax.optimization_barrier((second_terms, head_grad))
        second_terms = lax.all_to_all(second_terms, SEQ, split_axis=0, concat_axis=0, tiled=True)
    else:
        expert_terms = lax.psum_scatter(expert_terms, SEQ, scatter_dimension=0, tiled=True)
    grad_up_o = t_mm(out_lower, grad_branch)
    grad_down_o = t_mm(attended, grad_out_lower)
    if n_c == 4:
        up_rows = SPAN // n_fsdp
        up_blocks = grad_up_o.astype(BF).reshape(n_fsdp, up_rows, 16, SPAN).transpose(0, 2, 1, 3)
        by_owner = lambda t: t.astype(BF).reshape(n_seq, n_fsdp, -1, SPAN).transpose(1, 0, 2, 3)
        rup_rows = jnp.pad(grad_rup.reshape(n_seq * n_fsdp, 1, -1), ((0, 0), (0, 15), (0, 0)))
        rup_rows = jnp.pad(rup_rows, ((0, 0), (0, 0), (0, SPAN - rup_rows.shape[2])))
        rest = jnp.concatenate(
            [by_owner(grad_down_o), by_owner(grad_rdown), by_owner(rup_rows)], axis=2
        )
        early = jnp.concatenate(
            [up_blocks.reshape(n_fsdp, -1, SPAN), rest.reshape(n_fsdp, -1, SPAN)], axis=1
        )
        early = lax.psum_scatter(early.reshape(-1, SPAN), FSDP, scatter_dimension=0, tiled=True)

    uq, uk, grad_v, mq, mk = attend_back(
        q, k, v, head_grad, lse, projected, *gains, cosine, sine, seg_c, seg_r
    )
    moments = over_group(jnp.sum(mq[..., 0], axis=0), jnp.sum(mk[..., 0], axis=0), 5) / MODEL_WIDTH

    def rms_inner(values, scale, gain, turned, moment):
        return (scale * gain * turned - values * (scale * scale * scale) * moment).astype(BF)

    grad_projected = jnp.concatenate(
        [
            rms_inner(part_q, rq, gains[0], uq, moments[0][:, None]),
            rms_inner(part_k, rk, gains[1], uk, moments[1][:, None]),
            grad_v,
        ],
        axis=1,
    )
    if n_c == 4:
        grad_lowered, late = late_gradients(
            grad_projected, up_own, mask1, lowered, x_all, n_fsdp
        )
    else:
        grad_lowered = (mm_t(grad_projected, up_diagonal) * mask3).astype(BF)
    grad_normed_part = (mm_t(grad_projected, qkv_rows) + mm_t(grad_lowered, down3)).astype(BF)
    grad_normed_part = grad_normed_part.reshape(4, tok, MODEL_WIDTH)
    if n_c == 4:
        grad_normed, flat = finish(grad_normed_part, late, early, n_c)
    else:
        grad_normed = sum_to_tokens(grad_normed_part)
    grad_inputs = grad_middle + rms_back(inputs, gain_attn, grad_normed)

    down_rows, up_rows = MODEL_WIDTH // (n_seq * n_fsdp), SPAN // n_fsdp
    rup_shape = (SPAN // (n_seq * n_fsdp), experts)
    if n_c == 4:
        blocks = [flat[j * down_rows : (j + 1) * down_rows] for j in range(3)]
        at = 3 * down_rows
        up_blocks = [flat[at + n * up_rows : at + (n + 1) * up_rows] for n in range(16)]
        at += 16 * up_rows
        blocks.append(flat[at : at + down_rows])
        at += down_rows
        summed = [
            jnp.concatenate(blocks, axis=1),
            jnp.concatenate(up_blocks, axis=1),
            flat[at : at + down_rows],
        ]
        at += down_rows
        summed.append(flat[at, : rup_shape[0] * rup_shape[1]].reshape(rup_shape))
    else:
        grad_up_own = [
            t_mm(
                lowered[:, j * SPAN : (j + 1) * SPAN],
                grad_projected[:, j * GROUP_WIDTH : (j + 1) * GROUP_WIDTH],
            )
            for j in range(3)
        ]
        grad_down_qkv = t_mm(x_all, grad_lowered)
        grad_down_all = jnp.concatenate([grad_down_qkv, grad_down_o], axis=1).astype(BF)
        wide_up = lax.dynamic_update_slice_in_dim(
            jnp.zeros((span3, MODEL_WIDTH), F32),
            jnp.concatenate(grad_up_own, axis=0),
            group * GROUP_WIDTH,
            1,
        )
        grad_up_all = jnp.concatenate([wide_up, grad_up_o], axis=0).astype(BF)
        terms = (grad_down_all, grad_up_all, grad_rdown.astype(BF), grad_rup.astype(BF))
        own_shapes = [(t.shape[0] // (n_seq * n_fsdp), t.shape[1]) for t in terms]
        flat = jnp.concatenate(
            [t.reshape(n_seq, n_fsdp, -1).transpose(1, 0, 2) for t in terms], axis=2
        )
        used = flat.shape[2]
        flat = jnp.pad(flat, ((0, 0), (0, 0), (0, -used % 1024))).reshape(n_fsdp * n_seq, -1, 128)
        flat = lax.psum_scatter(flat, FSDP, scatter_dimension=0, tiled=True)
        flat = lax.psum_scatter(flat, SEQ, scatter_dimension=0, tiled=True)
        flat = flat.astype(F32).reshape(-1)
        summed, at = [], 0
        for shape in own_shapes:
            size = shape[0] * shape[1]
            summed.append(flat[at : at + size].reshape(shape))
            at += size

    mixed, grad_inputs = lax.optimization_barrier((mixed, grad_inputs))
    output = (middle + mixed.astype(F32)).astype(BF)
    if n_c == 4:
        expert_terms = jnp.stack(
            [jnp.sum(t.astype(F32), axis=0) for t in (first_terms, second_terms)]
        )
    else:
        expert_terms = expert_terms[0].astype(F32)
    rows = MODEL_WIDTH // 4
    at = rows + 2 * SPAN
    halves = expert_terms[:, at : at + SPAN]
    low = at + SPAN
    expert_sums = [
        expert_terms[:, :rows],
        expert_terms[:, rows:at].reshape(EXP_DEV, 2, SPAN, EXPERT_HIDDEN // 4),
        jnp.concatenate([halves[..., :SPAN], halves[..., SPAN:]], axis=1),
        jnp.concatenate(
            [expert_terms[:, low : low + SPAN], expert_terms[:, low + SPAN : low + 2 * SPAN]],
            axis=2,
        ),
    ]
    return (output[None], grad_inputs[None], *summed, *expert_sums)


def solution(mesh):
    n_seq, n_fsdp = mesh.shape["seq"], mesh.shape["fsdp"]
    fine = Mesh(
        mesh.devices.reshape(2, n_seq // 2, n_fsdp // 2, 2), ("zh", "zl", "c", "core")
    )
    split = P(FSDP, SEQ, None)
    rows = P(FSDP, None)
    three = P(FSDP, None, None)
    in_specs = (
        split,
        split,
        rows,
        rows,
        split,
        P(),
        P(),
        P(),
        P(),
        rows,
        rows,
        rows,
        three,
        three,
        rows,
        rows,
        rows,
        rows,
        three,
        P(FSDP, None, None, None),
        three,
        three,
    )
    owners = P((*SEQ, *FSDP), None)
    out_specs = (
        split,
        split,
        owners,
        owners,
        owners,
        owners,
        split,
        P(FSDP, None, None, SEQ),
        split,
        P(FSDP, None, SEQ),
    )
    return jax.shard_map(
        on_device, mesh=fine, in_specs=in_specs, out_specs=out_specs, check_vma=False
    )
```

```python
import functools

import jax
import jax.numpy as jnp
from jax import lax
from jax.experimental import pallas as pl
from jax.experimental.pallas import tpu as pltpu
from jax.sharding import Mesh
from jax.sharding import PartitionSpec as P

MODEL_WIDTH = 2048
H = 16
HD = 128
EXPERT_HIDDEN = 1024
TOP = 8
EXP_DEV = 2
ADAPTER_RANK = 16
SPAN = 128
GROUPS = 4
GROUP_WIDTH = MODEL_WIDTH // GROUPS
HEADS = H // GROUPS

EPSILON = 1e-05
THETA = 10000.0
NEGATIVE = -1e30
BF = jnp.bfloat16
F32 = jnp.float32
ANY = pl.ANY
VMEM = pltpu.VMEM
SEQ = ("zh", "zl")
FSDP = ("c", "core")


def mm(left, right):
    return lax.dot_general(left, right, (((1,), (0,)), ((), ())), preferred_element_type=F32)


def mm_t(left, right):
    return lax.dot_general(left, right, (((1,), (1,)), ((), ())), preferred_element_type=F32)


def t_mm(left, right):
    return lax.dot_general(left, right, (((0,), (0,)), ((), ())), preferred_element_type=F32)


def exact(form, left, right):
    return jnp.einsum(form, left, right, precision=lax.Precision.HIGHEST, preferred_element_type=F32)


def rms_scale(values, gain):
    return values * lax.rsqrt(jnp.mean(values * values, axis=-1, keepdims=True) + EPSILON) * gain


def rms_back(values, gain, grad):
    inverse = lax.rsqrt(jnp.mean(values * values, axis=-1, keepdims=True) + EPSILON)
    scaled = grad * gain
    return inverse * scaled - values * inverse * inverse * inverse * jnp.mean(
        values * scaled, axis=-1, keepdims=True
    )


def token_meta(lengths_row, sets_row, places):
    count = lengths_row.shape[0]
    running = [lengths_row[0]]
    for n in range(1, count):
        running.append(running[-1] + lengths_row[n])
    ends = jnp.stack(running)
    starts = ends - lengths_row
    member = ((places[:, None] >= starts[None, :]) & (places[:, None] < ends[None, :])).astype(
        jnp.int32
    )
    seq_ids = jnp.sum(member * jnp.arange(count, dtype=jnp.int32)[None, :], axis=1)
    offsets = places - jnp.sum(member * starts[None, :], axis=1)
    chosen = jnp.sum(member * sets_row[None, :], axis=1)
    return (seq_ids, offsets, chosen)


def set_mask(chosen):
    column_range = jnp.arange(SPAN, dtype=jnp.int32) // ADAPTER_RANK
    return (chosen[..., None] == column_range).astype(F32)


def here():
    return tuple(lax.axis_index(n) for n in ("zh", "zl", "c", "core"))


def signal_all(peers):
    barrier = pltpu.get_barrier_semaphore()
    for peer in peers:
        pl.semaphore_signal(barrier, inc=1, device_id=peer, device_id_type=pl.DeviceIdType.MESH)
    pl.semaphore_wait(barrier, len(peers))


def remote(src, dst, send, recv, device):
    return pltpu.make_async_remote_copy(
        src_ref=src,
        dst_ref=dst,
        send_sem=send,
        recv_sem=recv,
        device_id=device,
        device_id_type=pl.DeviceIdType.MESH,
    )


def column_peers(zh, zl, c, core):
    return [
        (zh ^ a, zl ^ b, c, core ^ k)
        for a in range(2)
        for b in range(2)
        for k in range(2)
        if (a, b, k) != (0, 0, 0)
    ]


def gather_kernel(n_c, x_ref, w_ref, xg_ref, wg_ref, xs, xr, fs, fr, ws, wr, own):
    zh, zl, c, core = here()
    tok = x_ref.shape[0]
    half = tok // 2
    rows = w_ref.shape[0]
    plane = [(zh, zl, lax.rem(c + i, n_c), core ^ k) for i in range(n_c) for k in range(2)][2:]
    signal_all(column_peers(zh, zl, c, core) + plane)
    me = zh * 2 + zl
    for a in range(2):
        for k in range(2):
            piece = pl.ds(k * half, half)
            src, dst = x_ref.at[piece], xg_ref.at[me, piece]
            is_self = (core == zh) & (zl == a) & (core == k)

            @pl.when(is_self)
            def _():
                pltpu.make_async_copy(src, dst, xr.at[me]).start()

            @pl.when(jnp.logical_not(is_self))
            def _():
                remote(src, dst, xs.at[a, k], xr.at[me], (core, a, c, k)).start()

    f = c * 2 + core
    row_block = pl.ds(pl.multiple_of(f * rows, rows), rows)

    def pieces(group):
        for j in range(3):
            start = pl.multiple_of(j * MODEL_WIDTH + group * GROUP_WIDTH, GROUP_WIDTH)
            yield (
                w_ref.at[:, pl.ds(start, GROUP_WIDTH)],
                wg_ref.at[row_block, pl.ds(j * GROUP_WIDTH, GROUP_WIDTH)],
            )

    for src, dst in pieces(zl * 2 + core):
        pltpu.make_async_copy(src, dst, own).start()
    slots = [(i, k) for i in range(n_c) for k in range(2)][1:]
    for i, k in slots:
        target_c, target_core = lax.rem(c + i, n_c), core ^ k
        for src, dst in pieces(zl * 2 + target_core):
            remote(
                src, dst, ws.at[i * 2 + k], wr.at[i * 2 + k], (zh, zl, target_c, target_core)
            ).start()
    mine = pl.ds(pl.multiple_of(core * half, half), half)
    theirs = pl.ds(pl.multiple_of((1 - core) * half, half), half)
    sibling = (zh, zl, c, 1 - core)
    for s in range(4):
        pltpu.make_async_copy(xg_ref.at[s, mine], xg_ref.at[s, mine], xr.at[s]).wait()
        remote(xg_ref.at[s, mine], xg_ref.at[s, mine], fs.at[s], fr.at[s], sibling).start()
    for s in range(4):
        got = xg_ref.at[s, theirs]
        pltpu.make_async_copy(got, got, fr.at[s]).wait()
    for s in range(4):
        got = xg_ref.at[s, mine]
        pltpu.make_async_copy(got, got, fs.at[s]).wait()
    for a in range(2):
        for k in range(2):
            is_self = (core == zh) & (zl == a) & (core == k)
            src = x_ref.at[pl.ds(k * half, half)]

            @pl.when(jnp.logical_not(is_self))
            def _():
                pltpu.make_async_copy(src, src, xs.at[a, k]).wait()

    block = wg_ref.at[row_block]
    pltpu.make_async_copy(block, block, own).wait()
    for i, k in slots:
        pltpu.make_async_copy(block, block, ws.at[i * 2 + k]).wait()
        source = lax.rem(c + n_c - i, n_c) * 2 + (core ^ k)
        got = wg_ref.at[pl.ds(pl.multiple_of(source * rows, rows), rows)]
        pltpu.make_async_copy(got, got, wr.at[i * 2 + k]).wait()


def gather_to_heads(x, w, n_c):
    tok, rows = x.shape[0], w.shape[0]
    n_f = 2 * n_c
    dma = pltpu.SemaphoreType.DMA
    return pl.pallas_call(
        functools.partial(gather_kernel, n_c),
        out_shape=(
            jax.ShapeDtypeStruct((4, tok, MODEL_WIDTH), BF),
            jax.ShapeDtypeStruct((n_f * rows, 3 * GROUP_WIDTH), BF),
        ),
        in_specs=[pl.BlockSpec(memory_space=VMEM)] * 2,
        out_specs=[pl.BlockSpec(memory_space=ANY)] * 2,
        scratch_shapes=[
            dma((2, 2)),
            dma((4,)),
            dma((4,)),
            dma((4,)),
            dma((n_f,)),
            dma((n_f,)),
            dma,
        ],
        compiler_params=pltpu.CompilerParams(collective_id=0, has_side_effects=True),
        name="gather_to_heads",
    )(x, w)


PROJECT_WIDTH = 3 * GROUP_WIDTH + 3 * SPAN


def project_kernel(x_ref, w_ref, down_ref, up_ref, mask, xg_o, wg_o, upg, proj_o, low, acc, xg, wg, xs, xr, fs, fr, ws, wr, us, ur, own, out):
    zh, zl, c, core = here()
    tok = x_ref.shape[0]
    half = tok // 2
    rows = w_ref.shape[0]
    up_rows = up_ref.shape[0]
    near = lambda i: (
        lax.rem(c // 2 + i // 2, 2) * 2 + lax.rem(lax.rem(c, 2) + lax.rem(i, 2), 2)
    )
    chips = [near(i) for i in range(4)]
    plane = [(zh, zl, chips[i], core ^ k) for i in range(4) for k in range(2)]
    sibling, beside, above = plane[1], plane[2], plane[4]
    signal_all(column_peers(zh, zl, c, core) + plane[2:])
    me = zh * 2 + zl
    f = c * 2 + core
    block = lambda source: wg.at[pl.ds(pl.multiple_of(source * rows, rows), rows)]
    source = lambda i, k: chips[i] * 2 + k

    def pieces(group):
        to = pl.ds(pl.multiple_of(f * rows, rows), rows)
        for j in range(3):
            start = pl.multiple_of(j * MODEL_WIDTH + group * GROUP_WIDTH, GROUP_WIDTH)
            yield (
                w_ref.at[:, pl.ds(start, GROUP_WIDTH)],
                wg.at[to, pl.ds(j * GROUP_WIDTH, GROUP_WIDTH)],
            )
        yield down_ref, wg.at[to, pl.ds(3 * GROUP_WIDTH, 3 * SPAN)]

    for src, dst in pieces(zl * 2 + core):
        pltpu.make_async_copy(src, dst, own.at[0]).start()
    for src, dst in pieces(zl * 2 + 1 - core):
        remote(src, dst, ws.at[0], wr.at[0], sibling).start()
    for a in range(2):
        for k in range(2):
            piece = pl.ds(k * half, half)
            src, dst = x_ref.at[piece], xg.at[me, piece]
            is_self = (core == zh) & (zl == a) & (core == k)

            @pl.when(is_self)
            def _():
                pltpu.make_async_copy(src, dst, xr.at[me]).start()

            @pl.when(jnp.logical_not(is_self))
            def _():
                remote(src, dst, xs.at[a, k], xr.at[me], (core, a, c, k)).start()

    wait_for(block(f), own.at[0])
    remote(block(f), block(f), ws.at[1], wr.at[1], beside).start()
    remote(block(f), block(f), ws.at[2], wr.at[2], above).start()
    up_to = pl.ds(pl.multiple_of(f * up_rows, up_rows), up_rows)
    for n, peer in enumerate(plane):
        start = pl.multiple_of((zl * 2 + peer[3]) * GROUP_WIDTH, GROUP_WIDTH)
        src, dst = up_ref.at[:, pl.ds(start, GROUP_WIDTH)], upg.at[up_to]
        if n:
            remote(src, dst, us.at[n], ur.at[n], peer).start()
        else:
            pltpu.make_async_copy(src, dst, own.at[1]).start()
    other = c * 2 + 1 - core
    wait_for(block(other), wr.at[0])
    remote(block(other), block(other), ws.at[3], wr.at[3], beside).start()
    remote(block(other), block(other), ws.at[4], wr.at[4], above).start()
    mine = pl.ds(pl.multiple_of(core * half, half), half)
    theirs = pl.ds(pl.multiple_of((1 - core) * half, half), half)

    shards = [k + zh * (3 - 2 * k) for k in range(4)]

    def pass_tokens(k):
        s = shards[k]
        wait_for(xg.at[s, mine], xr.at[s])
        remote(xg.at[s, mine], xg.at[s, mine], fs.at[s], fr.at[s], sibling).start()

    def take_tokens(k):
        s = shards[k]
        wait_for(xg.at[s, theirs], fr.at[s])
        pltpu.make_async_copy(xg.at[s], xg_o.at[s], out.at[0]).start()

    def multiply(i, k):
        at = pl.ds(pl.multiple_of(chips[i] * (2 * rows), 2 * rows), 2 * rows)
        s = shards[k]
        value = mm(xg[s, :, at], wg[at, :])
        acc[s] = value if i == 0 else acc[s] + value

    own_x, other_x = source(1, core), source(1, 1 - core)
    own_y, other_y = source(2, core), source(2, 1 - core)
    pass_tokens(0)
    take_tokens(0)
    multiply(0, 0)
    wait_for(block(own_x), wr.at[1])
    remote(block(own_x), block(own_x), ws.at[5], wr.at[5], above).start()
    pass_tokens(1)
    take_tokens(1)
    multiply(0, 1)
    wait_for(block(own_y), wr.at[2])
    wait_for(block(other_y), wr.at[4])
    remote(block(other_y), block(other_y), ws.at[6], wr.at[6], beside).start()
    pass_tokens(2)
    wait_for(block(other_x), wr.at[3])
    for k in range(2):
        multiply(1, k)
        multiply(2, k)
    take_tokens(2)
    for i in range(3):
        multiply(i, 2)
    pass_tokens(3)
    take_tokens(3)
    for i in range(3):
        multiply(i, 3)
    wait_for(block(source(3, core)), wr.at[5])
    wait_for(block(source(3, 1 - core)), wr.at[6])
    save = pltpu.make_async_copy(wg, wg_o, out.at[1])
    save.start()
    for k in range(4):
        multiply(3, k)
    up_block = lambda n: upg.at[pl.ds(pl.multiple_of(n * up_rows, up_rows), up_rows)]
    wait_for(up_block(f), own.at[1])
    for n, peer in enumerate(plane):
        if n:
            wait_for(up_block(peer[2] * 2 + peer[3]), ur.at[n])

    for s in range(4):
        for j in range(3):
            span = slice(j * SPAN, (j + 1) * SPAN)
            wide = slice(j * GROUP_WIDTH, (j + 1) * GROUP_WIDTH)
            at = 3 * GROUP_WIDTH + j * SPAN
            lowered = (acc[s, :, at : at + SPAN] * mask[s]).astype(BF)
            low[s, :, span] = lowered
            acc[s, :, wide] = acc[s, :, wide] + mm(lowered, upg[span])
        pltpu.make_async_copy(acc.at[s, :, pl.ds(0, 3 * GROUP_WIDTH)], proj_o.at[s], out.at[2]).start()

    for s in range(4):
        wait_for(xg.at[s, mine], fs.at[s])
    for a in range(2):
        for k in range(2):
            is_self = (core == zh) & (zl == a) & (core == k)

            @pl.when(jnp.logical_not(is_self))
            def _():
                wait_for(x_ref.at[pl.ds(k * half, half)], xs.at[a, k])

    save.wait()
    wait_for(xg_o, out.at[0])
    wait_for(proj_o, out.at[2])
    for n in range(7):
        wait_for(block(f), ws.at[n])
    for n in range(1, 8):
        wait_for(up_block(f), us.at[n])


def gather_project(x, w, down3, up, mask):
    tok, rows = x.shape[0], w.shape[0]
    dma = pltpu.SemaphoreType.DMA
    vmem = pl.BlockSpec(memory_space=VMEM)
    hbm = pl.BlockSpec(memory_space=ANY)
    return pl.pallas_call(
        project_kernel,
        out_shape=(
            jax.ShapeDtypeStruct((4, tok, MODEL_WIDTH), BF),
            jax.ShapeDtypeStruct((8 * rows, PROJECT_WIDTH), BF),
            jax.ShapeDtypeStruct((8 * up.shape[0], GROUP_WIDTH), BF),
            jax.ShapeDtypeStruct((4, tok, 3 * GROUP_WIDTH), F32),
            jax.ShapeDtypeStruct((4, tok, 3 * SPAN), BF),
        ),
        in_specs=[vmem] * 5,
        out_specs=[hbm, hbm, vmem, hbm, vmem],
        scratch_shapes=[
            VMEM((4, tok, PROJECT_WIDTH), F32),
            VMEM((4, tok, MODEL_WIDTH), BF),
            VMEM((8 * rows, PROJECT_WIDTH), BF),
            dma((2, 2)),
            dma((4,)),
            dma((4,)),
            dma((4,)),
            dma((7,)),
            dma((7,)),
            dma((8,)),
            dma((8,)),
            dma((2,)),
            dma((3,)),
        ],
        compiler_params=pltpu.CompilerParams(
            collective_id=8, has_side_effects=True, vmem_limit_bytes=58 * 2**20
        ),
        name="gather_project",
    )(x, w, down3, up, mask)


def to_tokens_kernel(a_ref, o_ref, send, recv):
    zh, zl, c, core = here()
    signal_all(column_peers(zh, zl, c, core))
    group = zl * 2 + core
    columns = pl.ds(pl.multiple_of(group * GROUP_WIDTH, GROUP_WIDTH), GROUP_WIDTH)
    for s in range(4):
        a, b = s // 2, s % 2
        is_self = (a == zh) & (b == zl) & (core == zh)
        src, dst = a_ref.at[s], o_ref.at[:, columns]

        @pl.when(is_self)
        def _():
            pltpu.make_async_copy(src, dst, recv.at[group]).start()

        @pl.when(jnp.logical_not(is_self))
        def _():
            remote(src, dst, send.at[s], recv.at[group], (a, b, c, zh)).start()

    for s in range(4):
        a, b = s // 2, s % 2
        is_self = (a == zh) & (b == zl) & (core == zh)
        got = o_ref.at[:, pl.ds(s * GROUP_WIDTH, GROUP_WIDTH)]
        pltpu.make_async_copy(got, got, recv.at[s]).wait()

        @pl.when(jnp.logical_not(is_self))
        def _():
            pltpu.make_async_copy(a_ref.at[s], a_ref.at[s], send.at[s]).wait()


def to_tokens(rows):
    tok = rows.shape[1]
    dma = pltpu.SemaphoreType.DMA
    return pl.pallas_call(
        to_tokens_kernel,
        out_shape=jax.ShapeDtypeStruct((tok, MODEL_WIDTH), BF),
        in_specs=[pl.BlockSpec(memory_space=VMEM)],
        out_specs=pl.BlockSpec(memory_space=ANY),
        scratch_shapes=[dma((4,)), dma((4,))],
        compiler_params=pltpu.CompilerParams(collective_id=1, has_side_effects=True),
        name="to_tokens",
    )(rows)


def to_heads_kernel(a_ref, o_ref, send, recv):
    zh, zl, c, core = here()
    signal_all(column_peers(zh, zl, c, core))
    me = zh * 2 + zl
    for g in range(4):
        b, k = g // 2, g % 2
        is_self = (core == zh) & (b == zl) & (core == k)
        src, dst = a_ref.at[:, pl.ds(g * GROUP_WIDTH, GROUP_WIDTH)], o_ref.at[me]

        @pl.when(is_self)
        def _():
            pltpu.make_async_copy(src, dst, recv.at[me]).start()

        @pl.when(jnp.logical_not(is_self))
        def _():
            remote(src, dst, send.at[g], recv.at[me], (core, b, c, k)).start()

    for g in range(4):
        b, k = g // 2, g % 2
        is_self = (core == zh) & (b == zl) & (core == k)
        pltpu.make_async_copy(o_ref.at[g], o_ref.at[g], recv.at[g]).wait()

        @pl.when(jnp.logical_not(is_self))
        def _():
            pltpu.make_async_copy(o_ref.at[g], o_ref.at[g], send.at[g]).wait()


def to_heads(rows):
    tok = rows.shape[0]
    dma = pltpu.SemaphoreType.DMA
    return pl.pallas_call(
        to_heads_kernel,
        out_shape=jax.ShapeDtypeStruct((4, tok, GROUP_WIDTH), BF),
        in_specs=[pl.BlockSpec(memory_space=VMEM)],
        out_specs=pl.BlockSpec(memory_space=ANY),
        scratch_shapes=[dma((4,)), dma((4,))],
        compiler_params=pltpu.CompilerParams(collective_id=2, has_side_effects=True),
        name="to_heads",
    )(rows)


def sum_to_tokens_kernel(p_ref, o_ref, sib, chip, rx, ss, sr, send, recv):
    zh, zl, c, core = here()
    signal_all(column_peers(zh, zl, c, core))
    width = o_ref.shape[1]
    half = width // 2
    sibling = (zh, zl, c, 1 - core)
    mine = pl.ds(pl.multiple_of(core * half, half), half)
    theirs = pl.ds(pl.multiple_of((1 - core) * half, half), half)
    for s in range(4):
        remote(p_ref.at[s, :, theirs], sib.at[s], ss.at[s], sr.at[s], sibling).start()

    def is_self(s):
        return (s // 2 == zh) & (s % 2 == zl) & (core == zh)

    for s in range(4):
        pltpu.make_async_copy(sib.at[s], sib.at[s], sr.at[s]).wait()
        chip[s] = (p_ref[s, :, mine].astype(F32) + sib[s].astype(F32)).astype(BF)
        src, dst = chip.at[s], rx.at[zl, core]

        @pl.when(is_self(s))
        def _():
            pltpu.make_async_copy(src, dst, recv.at[zl, core]).start()

        @pl.when(jnp.logical_not(is_self(s)))
        def _():
            remote(src, dst, send.at[s], recv.at[zl, core], (s // 2, s % 2, c, zh)).start()

    for s in range(4):
        pltpu.make_async_copy(sib.at[s], sib.at[s], ss.at[s]).wait()

        @pl.when(jnp.logical_not(is_self(s)))
        def _():
            pltpu.make_async_copy(chip.at[s], chip.at[s], send.at[s]).wait()

    for k in range(2):
        for b in range(2):
            pltpu.make_async_copy(rx.at[b, k], rx.at[b, k], recv.at[b, k]).wait()
        o_ref[:, k * half : (k + 1) * half] = rx[0, k].astype(F32) + rx[1, k].astype(F32)


def sum_to_tokens(parts):
    _, tok, width = parts.shape
    half = width // 2
    dma = pltpu.SemaphoreType.DMA
    return pl.pallas_call(
        sum_to_tokens_kernel,
        out_shape=jax.ShapeDtypeStruct((tok, width), F32),
        in_specs=[pl.BlockSpec(memory_space=VMEM)],
        out_specs=pl.BlockSpec(memory_space=VMEM),
        scratch_shapes=[
            VMEM((4, tok, half), BF),
            VMEM((4, tok, half), BF),
            VMEM((2, 2, tok, half), BF),
            dma((4,)),
            dma((4,)),
            dma((4,)),
            dma((2, 2)),
        ],
        compiler_params=pltpu.CompilerParams(
            collective_id=3, has_side_effects=True, vmem_limit_bytes=40 * 2**20
        ),
        name="sum_to_tokens",
    )(parts)


def finish_kernel(n_c, p_ref, late, early, o_ref, flat, sib, chip, rx, got_l, stage, got_z, ss, sr, send, recv, ls, lr, zs, zr):
    zh, zl, c, core = here()
    plane = [(zh, zl, lax.rem(c + i, n_c), core ^ k) for i in range(n_c) for k in range(2)]
    signal_all(column_peers(zh, zl, c, core) + plane[2:])
    width = o_ref.shape[1]
    half = width // 2
    sibling = (zh, zl, c, 1 - core)
    mine = pl.ds(pl.multiple_of(core * half, half), half)
    theirs = pl.ds(pl.multiple_of((1 - core) * half, half), half)
    for s in range(4):
        remote(p_ref.at[s, :, theirs], sib.at[s], ss.at[s], sr.at[s], sibling).start()
    me = c * 2 + core
    def is_self(s):
        return (s // 2 == zh) & (s % 2 == zl) & (core == zh)

    for s in range(4):
        pltpu.make_async_copy(sib.at[s], sib.at[s], sr.at[s]).wait()
        chip[s] = (p_ref[s, :, mine].astype(F32) + sib[s].astype(F32)).astype(BF)
        src, dst = chip.at[s], rx.at[zl, core]

        @pl.when(is_self(s))
        def _():
            pltpu.make_async_copy(src, dst, recv.at[zl, core]).start()

        @pl.when(jnp.logical_not(is_self(s)))
        def _():
            remote(src, dst, send.at[s], recv.at[zl, core], (s // 2, s % 2, c, zh)).start()

    count = len(plane)
    for n in range(1, count):
        peer = plane[n]
        remote(late.at[peer[2] * 2 + peer[3]], got_l.at[n], ls.at[n], lr.at[n], peer).start()
    late_sum = late[me].astype(F32)
    for n in range(1, count):
        wait_for(got_l.at[n], lr.at[n])
        late_sum = late_sum + got_l[n].astype(F32)
    late_sum = late_sum.astype(BF)
    down, up, wide, rest = finish_rows(n_c)
    for q in range(4):
        stage[q, :down] = late_sum[q * down : (q + 1) * down]
        if q < 3:
            at = 4 * down + q * up
            stage[q, down : down + up] = late_sum[at : at + up]
            stage[q, down + up : down + wide] = jnp.zeros((wide - up, SPAN), BF)
        else:
            stage[q, down : down + wide] = early[:wide]
        at = wide + q * rest
        stage[q, down + wide :] = early[at : at + rest]
    seq = zh * 2 + zl
    for q in range(4):

        @pl.when(seq == q)
        def _():
            got_z[q] = stage[q]

        @pl.when(seq != q)
        def _():
            remote(stage.at[q], got_z.at[seq], zs.at[q], zr.at[seq], (q // 2, q % 2, c, core)).start()

    for k in range(2):
        for b in range(2):
            pltpu.make_async_copy(rx.at[b, k], rx.at[b, k], recv.at[b, k]).wait()
        o_ref[:, k * half : (k + 1) * half] = rx[0, k].astype(F32) + rx[1, k].astype(F32)

    for q in range(4):

        @pl.when(seq != q)
        def _():
            wait_for(got_z.at[q], zr.at[q])

    terms = [got_z[q].astype(F32) for q in range(4)]
    flat[...] = (terms[0] + terms[1]) + (terms[2] + terms[3])

    @pl.when(seq < 3)
    def _():
        for b in range(2):
            pair = got_z[b, down : down + up].astype(F32) + got_z[2 + b, down : down + up].astype(F32)
            flat[down + b * up : down + (b + 1) * up] = pair

    for s in range(4):
        pltpu.make_async_copy(sib.at[s], sib.at[s], ss.at[s]).wait()

        @pl.when(jnp.logical_not(is_self(s)))
        def _():
            pltpu.make_async_copy(chip.at[s], chip.at[s], send.at[s]).wait()

        @pl.when(seq != s)
        def _():
            wait_for(stage.at[s], zs.at[s])

    for n in range(1, count):
        wait_for(got_l.at[n], ls.at[n])


def finish_rows(n_c):
    n_f = 2 * n_c
    down, up = MODEL_WIDTH // (4 * n_f), SPAN // n_f
    return 3 * down, 8 * up, 16 * up, 2 * down + 16


def finish(parts, late, early, n_c):
    _, tok, width = parts.shape
    half = width // 2
    down, up, wide, rest = finish_rows(n_c)
    n_f = 2 * n_c
    dma = pltpu.SemaphoreType.DMA
    vmem = pl.BlockSpec(memory_space=VMEM)
    return pl.pallas_call(
        functools.partial(finish_kernel, n_c),
        out_shape=(
            jax.ShapeDtypeStruct((tok, width), F32),
            jax.ShapeDtypeStruct((down + wide + rest, SPAN), F32),
        ),
        in_specs=[vmem] * 3,
        out_specs=[vmem] * 2,
        scratch_shapes=[
            VMEM((4, tok, half), BF),
            VMEM((4, tok, half), BF),
            VMEM((2, 2, tok, half), BF),
            VMEM(late.shape, BF),
            VMEM((4, down + wide + rest, SPAN), BF),
            VMEM((4, down + wide + rest, SPAN), BF),
            dma((4,)),
            dma((4,)),
            dma((4,)),
            dma((2, 2)),
            dma((n_f,)),
            dma((n_f,)),
            dma((4,)),
            dma((4,)),
        ],
        compiler_params=pltpu.CompilerParams(
            collective_id=7, has_side_effects=True, vmem_limit_bytes=50 * 2**20
        ),
        name="finish",
    )(parts, late, early)


def group_sum_kernel(x_ref, o_ref, rx, send, recv):
    zh, zl, c, core = here()
    peers = [(zh, zl, c, 1 - core), (zh, 1 - zl, c, core), (zh, 1 - zl, c, 1 - core)]
    signal_all(peers)
    copies = [remote(x_ref, rx.at[i], send.at[i], recv.at[i], p) for i, p in enumerate(peers)]
    for copy in copies:
        copy.start()
    for copy in copies:
        copy.wait()
    o_ref[...] = (x_ref[...] + rx[0]) + (rx[1] + rx[2])


def group_sum(values, identity):
    dma = pltpu.SemaphoreType.DMA
    return pl.pallas_call(
        group_sum_kernel,
        out_shape=jax.ShapeDtypeStruct(values.shape, F32),
        in_specs=[pl.BlockSpec(memory_space=VMEM)],
        out_specs=pl.BlockSpec(memory_space=VMEM),
        scratch_shapes=[VMEM((3, *values.shape), F32), dma((3,)), dma((3,))],
        compiler_params=pltpu.CompilerParams(collective_id=identity, has_side_effects=True),
        name="group_sum",
    )(values)


def turn(values, cosine, sine):
    return values * cosine + pltpu.roll(values, HD // 2, 1) * sine


def attention_rows(block):
    return 256 if block % 256 == 0 else block


def attend_kernel(
    pq, pk, pv, rq, rk, gq, gk, cosine, sine, seg_c, seg_r, q_ref, k_ref, v_ref, o_ref, lse_ref
):
    block = pq.shape[0]
    rows = attention_rows(block)
    scale = HD**-0.5
    q_ref[...] = turn(pq[...] * rq[...] * gq[...], cosine[...], sine[...]).astype(BF)
    k_ref[...] = turn(pk[...] * rk[...] * gk[...], cosine[...], sine[...]).astype(BF)
    v_ref[...] = pv[...].astype(BF)
    for i in range(block // rows):
        length = (i + 1) * rows
        own = slice(i * rows, length)
        scores = mm_t(q_ref[own], k_ref[:length]) * scale
        row = lax.broadcasted_iota(jnp.int32, (rows, length), 0) + i * rows
        column = lax.broadcasted_iota(jnp.int32, (rows, length), 1)
        allowed = (seg_c[own] == seg_r[:, :length]) & (column <= row)
        scores = jnp.where(allowed, scores, NEGATIVE)
        top = jnp.max(scores, axis=1, keepdims=True)
        weights = jnp.exp(scores - top)
        total = jnp.sum(weights, axis=1, keepdims=True)
        out = mm(weights.astype(BF), v_ref[:length]) / total
        o_ref[own] = out.astype(BF)
        lse_ref[0, own] = top + jnp.log(total)


def attend(projected, rq, rk, gq, gk, cosine, sine, seg_c, seg_r):
    block = projected.shape[0]
    head = lambda off: pl.BlockSpec((block, HD), lambda h: (0, off + h))
    gain = pl.BlockSpec((1, HD), lambda h: (0, h))
    fixed = lambda shape: pl.BlockSpec(shape, lambda h: (0, 0))
    wide = jax.ShapeDtypeStruct((block, GROUP_WIDTH), BF)
    return pl.pallas_call(
        attend_kernel,
        grid=(HEADS,),
        out_shape=(wide, wide, wide, wide, jax.ShapeDtypeStruct((HEADS, block, 1), F32)),
        in_specs=[
            head(0),
            head(HEADS),
            head(2 * HEADS),
            fixed((block, 1)),
            fixed((block, 1)),
            gain,
            gain,
            fixed((block, HD)),
            fixed((block, HD)),
            fixed((block, 1)),
            fixed((1, block)),
        ],
        out_specs=[head(0)] * 4 + [pl.BlockSpec((1, block, 1), lambda h: (h, 0, 0))],
        compiler_params=pltpu.CompilerParams(vmem_limit_bytes=60 * 2**20),
        name="attend",
    )(projected, projected, projected, rq, rk, gq, gk, cosine, sine, seg_c, seg_r)


def attend_send_kernel(
    pq, pk, pv, rq, rk, gq, gk, cosine, sine, seg_c, seg_r, q_ref, k_ref, v_ref, lse_ref, o_ref, held, send, recv
):
    zh, zl, c, core = here()
    h = pl.program_id(0)
    tok = o_ref.shape[0]
    group = zl * 2 + core

    @pl.when(h == 0)
    def _():
        signal_all(column_peers(zh, zl, c, core))

    attend_kernel(
        pq, pk, pv, rq, rk, gq, gk, cosine, sine, seg_c, seg_r, q_ref, k_ref, v_ref, held.at[h], lse_ref
    )
    columns = pl.ds(pl.multiple_of(group * GROUP_WIDTH + h * HD, HD), HD)
    is_self = lambda s: (s // 2 == zh) & (s % 2 == zl) & (core == zh)
    for s in range(4):
        src, dst = held.at[h, pl.ds(s * tok, tok)], o_ref.at[:, columns]

        @pl.when(is_self(s))
        def _():
            pltpu.make_async_copy(src, dst, recv.at[group, h]).start()

        @pl.when(jnp.logical_not(is_self(s)))
        def _():
            remote(src, dst, send.at[s, h], recv.at[group, h], (s // 2, s % 2, c, zh)).start()

    @pl.when(h == HEADS - 1)
    def _():
        for n in range(HEADS):
            for s in range(4):
                got = o_ref.at[:, pl.ds(s * GROUP_WIDTH + n * HD, HD)]
                wait_for(got, recv.at[s, n])

                @pl.when(jnp.logical_not(is_self(s)))
                def _():
                    wait_for(held.at[n, pl.ds(0, tok)], send.at[s, n])


def attend_send(projected, rq, rk, gq, gk, cosine, sine, seg_c, seg_r):
    block = projected.shape[0]
    tok = block // 4
    dma = pltpu.SemaphoreType.DMA
    head = lambda off: pl.BlockSpec((block, HD), lambda h: (0, off + h))
    gain = pl.BlockSpec((1, HD), lambda h: (0, h))
    fixed = lambda shape: pl.BlockSpec(shape, lambda h: (0, 0))
    wide = jax.ShapeDtypeStruct((block, GROUP_WIDTH), BF)
    return pl.pallas_call(
        attend_send_kernel,
        grid=(HEADS,),
        out_shape=(
            wide,
            wide,
            wide,
            jax.ShapeDtypeStruct((HEADS, block, 1), F32),
            jax.ShapeDtypeStruct((tok, MODEL_WIDTH), BF),
        ),
        in_specs=[
            head(0),
            head(HEADS),
            head(2 * HEADS),
            fixed((block, 1)),
            fixed((block, 1)),
            gain,
            gain,
            fixed((block, HD)),
            fixed((block, HD)),
            fixed((block, 1)),
            fixed((1, block)),
        ],
        out_specs=[head(0)] * 3
        + [pl.BlockSpec((1, block, 1), lambda h: (h, 0, 0)), pl.BlockSpec(memory_space=ANY)],
        scratch_shapes=[VMEM((HEADS, block, HD), BF), dma((4, HEADS)), dma((4, HEADS))],
        compiler_params=pltpu.CompilerParams(
            collective_id=9, has_side_effects=True, vmem_limit_bytes=60 * 2**20
        ),
        name="attend_send",
    )(projected, projected, projected, rq, rk, gq, gk, cosine, sine, seg_c, seg_r)


def attend_back_kernel(
    q_ref,
    k_ref,
    v_ref,
    g_ref,
    lse_ref,
    pq,
    pk,
    gq,
    gk,
    cosine,
    sine,
    seg_c,
    seg_r,
    uq_ref,
    uk_ref,
    dv_ref,
    mq_ref,
    mk_ref,
    dk_acc,
    dv_acc,
):
    block = q_ref.shape[0]
    rows = attention_rows(block)
    scale = HD**-0.5
    dk_acc[...] = jnp.zeros_like(dk_acc)
    dv_acc[...] = jnp.zeros_like(dv_acc)

    def back(grad, raw, gain):
        turned = turn(grad.astype(BF).astype(F32), cosine_of, -sine_of)
        return turned, jnp.sum(raw * gain[...] * turned, axis=1, keepdims=True)

    for i in range(block // rows):
        length = (i + 1) * rows
        own = slice(i * rows, length)
        scores = mm_t(q_ref[own], k_ref[:length]) * scale
        row = lax.broadcasted_iota(jnp.int32, (rows, length), 0) + i * rows
        column = lax.broadcasted_iota(jnp.int32, (rows, length), 1)
        allowed = (seg_c[own] == seg_r[:, :length]) & (column <= row)
        probs = jnp.where(allowed, jnp.exp(scores - lse_ref[0, own]), 0.0)
        grad_probs = mm_t(g_ref[own], v_ref[:length])
        delta = jnp.sum(probs * grad_probs, axis=1, keepdims=True)
        grad_scores = (probs * (grad_probs - delta)).astype(BF)
        grad_q = mm(grad_scores, k_ref[:length]) * scale
        cosine_of, sine_of = cosine[own], sine[own]
        turned, moment = back(grad_q, pq[own], gq)
        uq_ref[own] = turned
        mq_ref[0, own] = moment
        dk_acc[:length] += t_mm(grad_scores, q_ref[own])
        dv_acc[:length] += t_mm(probs.astype(BF), g_ref[own])
    cosine_of, sine_of = cosine[...], sine[...]
    turned, moment = back(dk_acc[...] * scale, pk[...], gk)
    uk_ref[...] = turned
    mk_ref[0] = moment
    dv_ref[...] = dv_acc[...].astype(BF)


def attend_back(q, k, v, grad, lse, projected, gq, gk, cosine, sine, seg_c, seg_r):
    block = q.shape[0]
    head = lambda off: pl.BlockSpec((block, HD), lambda h: (0, off + h))
    gain = pl.BlockSpec((1, HD), lambda h: (0, h))
    fixed = lambda shape: pl.BlockSpec(shape, lambda h: (0, 0))
    column = pl.BlockSpec((1, block, 1), lambda h: (h, 0, 0))
    wide = lambda t: jax.ShapeDtypeStruct((block, GROUP_WIDTH), t)
    moment = jax.ShapeDtypeStruct((HEADS, block, 1), F32)
    return pl.pallas_call(
        attend_back_kernel,
        grid=(HEADS,),
        out_shape=(wide(F32), wide(F32), wide(BF), moment, moment),
        in_specs=[
            head(0),
            head(0),
            head(0),
            head(0),
            column,
            head(0),
            head(HEADS),
            gain,
            gain,
            fixed((block, HD)),
            fixed((block, HD)),
            fixed((block, 1)),
            fixed((1, block)),
        ],
        out_specs=[head(0)] * 3 + [column] * 2,
        scratch_shapes=[VMEM((block, HD), F32), VMEM((block, HD), F32)],
        compiler_params=pltpu.CompilerParams(vmem_limit_bytes=60 * 2**20),
        name="attend_back",
    )(q, k, v, grad, lse, projected, projected, gq, gk, cosine, sine, seg_c, seg_r)


WIDE_IN = MODEL_WIDTH + 2 * SPAN
WIDE_OUT = MODEL_WIDTH + SPAN
CHUNK = 16
TERM_PARTS = 4
TERM_ROWS = MODEL_WIDTH // 4 + 2 * SPAN + SPAN + 2 * SPAN


def over_rows(count, body):
    def step(n, carry):
        body(pl.ds(pl.multiple_of(n * CHUNK, CHUNK), CHUNK))
        return carry

    lax.fori_loop(0, count // CHUNK, step, 0)


def wait_for(ref, sem):
    pltpu.make_async_copy(ref, ref, sem).wait()


def experts_kernel(n_c, experts, slots, comm, *refs):
    n_g = 10 if comm else 1
    x_ref, g_refs = refs[0], refs[1 : 1 + n_g]
    refs = refs[1 + n_g :]
    h_gu, h_d, h_id, h_iu, h_od, h_ou = refs[:6]
    refs = refs[6:]
    out_ref, row_ref, terms_o = refs[:3]
    refs = refs[3:]
    if comm:
        xg_ref, final, first_o = refs[:3]
        refs = refs[3:]
    else:
        xg_ref = x_ref
    (wb, db, xw, gw, xl, dr, gu, hl, dh, dgl, res, pick, gate, mom, mask) = refs[:15]
    (to, tr, gid, giu, god, gou, packed, wsem, csem, osem) = refs[15:25]
    refs = refs[25:]
    zh, zl, c, core = here()
    tok = xw.shape[1]
    extra = xw.shape[2] - MODEL_WIDTH
    tiles = n_c
    f = c * 2 + core
    near = lambda i: (
        lax.rem(c // 2 + i // 2, 2) * 2 + lax.rem(lax.rem(c, 2) + lax.rem(i, 2), 2)
    )

    def pair(ref, p):
        return ref.at[pl.ds(p * 2, 2)]

    def load_in(expert):
        yield pltpu.make_async_copy(h_id.at[expert], wb.at[:MODEL_WIDTH, MODEL_WIDTH:], wsem.at[0])
        yield pltpu.make_async_copy(h_gu.at[expert], wb.at[:MODEL_WIDTH, :MODEL_WIDTH], wsem.at[1])
        for j in range(2):
            rows = slice(MODEL_WIDTH + j * SPAN, MODEL_WIDTH + (j + 1) * SPAN)
            columns = slice(j * EXPERT_HIDDEN, (j + 1) * EXPERT_HIDDEN)
            yield pltpu.make_async_copy(h_iu.at[expert, j], wb.at[rows, columns], wsem.at[2 + j])

    def load_out(expert):
        yield pltpu.make_async_copy(h_d.at[expert], db.at[:EXPERT_HIDDEN, :MODEL_WIDTH], wsem.at[4])
        yield pltpu.make_async_copy(h_od.at[expert], db.at[:EXPERT_HIDDEN, MODEL_WIDTH:], wsem.at[5])
        yield pltpu.make_async_copy(h_ou.at[expert], db.at[EXPERT_HIDDEN:, :MODEL_WIDTH], wsem.at[6])

    terms = (gid, giu, god, gou)

    def term_copy(e):
        return pltpu.make_async_copy(packed, terms_o if comm else terms_o.at[:, e], osem.at[0])

    def send_first_terms():
        pltpu.make_async_copy(packed.at[seq], first_o.at[seq], osem.at[0]).start()
        for q in range(TERM_PARTS):

            @pl.when(seq != q)
            def _():
                remote(packed.at[q], first_o.at[seq], tsend.at[q], trecv.at[seq], (q // 2, q % 2, c, core)).start()

    def wait_first_terms(sent):
        for q in range(TERM_PARTS):

            @pl.when(seq != q)
            def _():
                if sent:
                    wait_for(packed.at[q], tsend.at[q])
                else:
                    wait_for(first_o.at[q], trecv.at[q])

        if sent:
            wait_for(packed.at[0], osem.at[0])

    def pack_terms():
        for q in range(TERM_PARTS):
            rows, columns = MODEL_WIDTH // 4, EXPERT_HIDDEN // 4
            packed[q, :rows] = gid[q * rows : (q + 1) * rows].astype(BF)
            for j in range(2):
                at = rows + j * SPAN
                packed[q, at : at + SPAN] = giu[j, :, q * columns : (q + 1) * columns].astype(BF)
            at = rows + 2 * SPAN
            for j in range(2):
                half = slice(j * SPAN, (j + 1) * SPAN)
                row = q * columns + j * SPAN
                packed[q, at : at + SPAN, half] = god[row : row + SPAN].astype(BF)
                column = q * rows + j * 256
                low = at + (j + 1) * SPAN
                packed[q, low : low + SPAN] = gou[:, column : column + 256].astype(BF)

    if comm:
        sib, la, lb, fx, fy, sums, sendx, recvx, sends, recvs, tsend, trecv = refs
        seq = zh * 2 + zl
        same = lambda i: (zh, zl, near(i), core)
        sibling = (zh, zl, c, 1 - core)
        low_half, high_half = pl.ds(0, tok // 2), pl.ds(tok // 2, tok // 2)
        column = [(zh ^ 1, zl, c, core), (zh, zl ^ 1, c, core), (zh ^ 1, zl ^ 1, c, core)]
        signal_all([sibling, same(1), same(2), *column])
        first = [
            remote(x_ref, xg_ref.at[f], sendx.at[n], recvx.at[n], to_)
            for n, to_ in enumerate((sibling, same(1), same(2)))
        ]
        for copy in first:
            copy.start()
        fx1, fy1, fd1 = near(1) * 2 + core, near(2) * 2 + core, near(3) * 2 + core
        forward = [
            remote(xg_ref.at[fx1, low_half], xg_ref.at[fx1, low_half], sendx.at[3], recvx.at[3], same(2)),
            remote(xg_ref.at[fy1, high_half], xg_ref.at[fy1, high_half], sendx.at[4], recvx.at[4], same(1)),
            remote(xg_ref.at[fx1], xg_ref.at[fx1], sendx.at[5], recvx.at[5], sibling),
            remote(xg_ref.at[fy1], xg_ref.at[fy1], sendx.at[6], recvx.at[6], sibling),
        ]
        across = remote(xg_ref.at[fd1], xg_ref.at[fd1], sendx.at[7], recvx.at[7], sibling)

    for copy in (*load_in(0), *load_out(0)):
        copy.start()
    spare = EXPERT_HIDDEN
    wb[MODEL_WIDTH : MODEL_WIDTH + SPAN, spare:] = jnp.zeros((SPAN, WIDE_IN - spare), BF)
    wb[MODEL_WIDTH + SPAN :, :spare] = jnp.zeros((SPAN, spare), BF)
    for ref in terms:
        ref[...] = jnp.zeros_like(ref)

    def order(s):
        e = s // tiles
        i = s + e * (2 * tiles - 1 - 2 * s)
        return e, i, (near(i) if comm else i)

    def fetch_x(p):
        return pltpu.make_async_copy(pair(xg_ref, p), xw, csem.at[0])

    def fetch_own():
        other = xg_ref.at[c * 2 + 1 - core]
        pltpu.make_async_copy(x_ref, xw.at[core], csem.at[0]).start()
        pltpu.make_async_copy(other, xw.at[1 - core], csem.at[0]).start()

    def fetch_g(i):
        if not comm:
            pltpu.make_async_copy(pair(g_refs[0], i), gw, csem.at[1]).start()
            return
        for n in range(4):

            @pl.when(i == n)
            def _():
                for k, held in ((core, g_refs[:5]), (1 - core, g_refs[5:])):
                    if n < 3:
                        pltpu.make_async_copy(held[n], gw.at[k], csem.at[1]).start()
                    else:
                        pltpu.make_async_copy(held[3], gw.at[k, low_half], csem.at[1]).start()
                        pltpu.make_async_copy(held[4], gw.at[k, high_half], csem.at[1]).start()

    if comm:
        fetch_g(0)
        wait_for(xg_ref.at[c * 2 + 1 - core], recvx.at[0])
        fetch_own()
    else:
        fetch_g(0)
        fetch_x(0).start()

    def write_out(p):
        return pltpu.make_async_copy(to, pair(out_ref, p), csem.at[2])

    def write_row(p):
        return pltpu.make_async_copy(tr, pair(row_ref, p), csem.at[3])

    def read_out(p):
        return pltpu.make_async_copy(pair(out_ref, p), to, csem.at[4])

    def read_row(p):
        return pltpu.make_async_copy(pair(row_ref, p), tr, csem.at[5])

    both = 2 * slots
    steps = 2 * tiles
    part = lambda d: slice(d * slots, (d + 1) * slots)
    pieces = [
        (
            slice(r, r + CHUNK),
            slice(h * 512, (h + 1) * 512),
            slice(EXPERT_HIDDEN + h * 512, EXPERT_HIDDEN + (h + 1) * 512),
        )
        for r in range(0, both, CHUNK)
        for h in range(2)
    ]

    def step(s, carry):
        e, i, p = order(s)
        _, after_i, after = order(jnp.minimum(s + 1, steps - 1))
        number = c * (2 * EXP_DEV) + core * EXP_DEV + e
        fetch_x(p).wait()
        wait_for(gw, csem.at[1])
        lane = lax.broadcasted_iota(jnp.int32, (tok, extra), 1)
        lane_s = lax.broadcasted_iota(jnp.int32, (slots, extra), 1)
        for d in range(2):
            side = xw[d, :, MODEL_WIDTH:].astype(F32)
            place = jnp.sum(jnp.where(lane == number, side, 0.0), axis=1, keepdims=True)
            slot = lax.broadcasted_iota(jnp.int32, (tok, slots), 1).astype(F32)
            pick[d] = jnp.where(slot == place, 1.0, 0.0).astype(BF)
            sub = lax.broadcasted_iota(jnp.int32, (extra, tok), 0)
            place_t = jnp.sum(jnp.where(sub == number, side.T, 0.0), axis=0, keepdims=True)
            slot_t = lax.broadcasted_iota(jnp.int32, (slots, tok), 0).astype(F32)
            pickt = jnp.where(slot_t == place_t, 1.0, 0.0).astype(BF)
            xl[part(d), :MODEL_WIDTH] = mm(pickt, xw[d, :, :MODEL_WIDTH]).astype(BF)
            dr[part(d), :MODEL_WIDTH] = mm(pickt, gw[d]).astype(BF)
            side = mm(pickt, xw[d, :, MODEL_WIDTH:])
            read = lambda which: jnp.sum(jnp.where(which, side, 0.0), axis=1, keepdims=True)
            gate[part(d)] = read((lane_s == experts + number) | (lane_s == 2 * experts + number))
            columns = lax.broadcasted_iota(jnp.int32, (slots, SPAN), 1) // ADAPTER_RANK
            mask[part(d)] = jnp.where(columns.astype(F32) == read(lane_s == 3 * experts), 1.0, 0.0)

        @pl.when((s > 0) & (s <= tiles) if comm else s > 0)
        def _():
            write_row(p).wait()

        @pl.when(s > 0)
        def _():
            write_out(p).wait()

        @pl.when(e > 0)
        def _():
            read_out(p).start()
            read_row(p).start()

        @pl.when(s == 0)
        def _():
            for copy in (*load_in(0), *load_out(0)):
                copy.wait()

        @pl.when(s == tiles)
        def _():
            for copy in (*load_in(1), *load_out(1), *(() if comm else (term_copy(0),))):
                copy.wait()
            for ref in terms:
                ref[...] = jnp.zeros_like(ref)

        mask2 = lambda: jnp.concatenate([mask[...], mask[...]], axis=1)
        xl[:, MODEL_WIDTH:] = (mm(xl[:, :MODEL_WIDTH], wb[:MODEL_WIDTH, MODEL_WIDTH:]) * mask2()).astype(BF)
        gu[...] = mm(xl[...], wb[:, :MODEL_WIDTH])

        for rows, a, b in pieces:
            gate_part = gu[rows, a]
            hl[rows, a] = (gate_part / (1.0 + jnp.exp(-gate_part)) * gu[rows, b]).astype(BF)
        hl[:, EXPERT_HIDDEN:] = (
            mm(hl[:, :EXPERT_HIDDEN], db[:EXPERT_HIDDEN, MODEL_WIDTH:]) * mask[...]
        ).astype(BF)
        for n in range(4):
            a = slice(n * 512, (n + 1) * 512)
            res[:, a] = (mm(hl[...], db[:, a]) * gate[...]).astype(BF)

        @pl.when(e > 0)
        def _():
            read_out(p).wait()

        def add_picked(target, d):
            for n in range(4):
                a = slice(n * 512, (n + 1) * 512)
                before = jnp.where(e > 0, target[d, :, a].astype(F32), 0.0)
                target[d, :, a] = (before + mm(pick[d], res[part(d), a])).astype(BF)

        for d in range(2):
            add_picked(to, d)
        write_out(p).start()

        @pl.when(s < steps - 1)
        def _():
            fetch_g(after_i)

        dr[:, MODEL_WIDTH:] = (
            mm_t(dr[:, :MODEL_WIDTH], db[EXPERT_HIDDEN:, :MODEL_WIDTH]) * mask[...]
        ).astype(BF)
        dh[...] = mm_t(dr[...], db[:EXPERT_HIDDEN, :])

        @pl.when(s == tiles - 1)
        def _():
            for copy in load_out(1):
                copy.start()

        mom[...] = jnp.zeros_like(mom)
        for rows, a, b in pieces:
            gate_part, up_part, grad = gu[rows, a], gu[rows, b], dh[rows, a]
            sigmoid = 1.0 / (1.0 + jnp.exp(-gate_part))
            activated = gate_part * sigmoid
            plain = grad * activated
            mom[rows] += jnp.sum(plain * up_part, axis=1, keepdims=True)
            dgl[rows, b] = (plain * gate[rows]).astype(BF)
            slope = sigmoid + activated - activated * sigmoid
            dgl[rows, a] = (grad * gate[rows] * up_part * slope).astype(BF)
        dgl[:, MODEL_WIDTH:] = (
            mm_t(dgl[:, :MODEL_WIDTH], wb[MODEL_WIDTH:, :MODEL_WIDTH]) * mask2()
        ).astype(BF)
        for n in range(4):
            a = slice(n * 512, (n + 1) * 512)
            res[:, a] = mm_t(dgl[...], wb[a, :]).astype(BF)

        @pl.when(s == tiles - 1)
        def _():
            for copy in load_in(1):
                copy.start()

        if comm:
            @pl.when(s == 0)
            def _():
                wait_for(xg_ref.at[fx1], recvx.at[1])
                forward[0].start()
                forward[2].start()
                wait_for(xg_ref.at[fy1], recvx.at[2])
                forward[1].start()
                forward[3].start()
                wait_for(xg_ref.at[fx1], recvx.at[5])

            @pl.when(s == 1)
            def _():
                wait_for(xg_ref.at[fd1, low_half], recvx.at[3])
                wait_for(xg_ref.at[fd1, high_half], recvx.at[4])
                across.start()
                wait_for(xg_ref.at[fy1], recvx.at[6])

            @pl.when(s == 2)
            def _():
                wait_for(xg_ref.at[fd1], recvx.at[7])

        @pl.when(s < steps - (2 if comm else 1))
        def _():
            fetch_x(after).start()

        if comm:

            @pl.when(s == steps - 2)
            def _():
                fetch_own()

        @pl.when(e > 0)
        def _():
            read_row(p).wait()

        for d in range(2):
            add_picked(tr, d)
            moment = mom[part(d)]
            high = moment.astype(BF).astype(F32)
            side = jnp.where(lane_s == number, high, 0.0) + jnp.where(
                lane_s == experts + number, moment - high, 0.0
            )
            before = jnp.where(e > 0, tr[d, :, MODEL_WIDTH:].astype(F32), 0.0)
            tr[d, :, MODEL_WIDTH:] = (before + mm(pick[d], side.astype(BF))).astype(BF)

        if comm:
            to_sibling = remote(
                tr.at[1 - core], sib.at[lax.rem(i, 2)], sends.at[lax.rem(i, 2)],
                recvs.at[lax.rem(i, 2)], sibling,
            )

            @pl.when(e == 0)
            def _():
                write_row(p).start()

            @pl.when(e > 0)
            def _():
                to_sibling.start()
        else:
            write_row(p).start()

        gid[...] += t_mm(xl[:, :MODEL_WIDTH], dgl[:, MODEL_WIDTH:])
        for j in range(2):
            giu[j] += t_mm(
                xl[:, MODEL_WIDTH + j * SPAN : MODEL_WIDTH + (j + 1) * SPAN],
                dgl[:, j * EXPERT_HIDDEN : (j + 1) * EXPERT_HIDDEN],
            )
        god[...] += t_mm(hl[:, :EXPERT_HIDDEN], (dr[:, MODEL_WIDTH:].astype(F32) * gate[...]).astype(BF))
        gou[...] += t_mm((hl[:, EXPERT_HIDDEN:].astype(F32) * gate[...]).astype(BF), dr[:, :MODEL_WIDTH])

        @pl.when(s == tiles - 1)
        def _():
            pack_terms()
            if comm:
                send_first_terms()
            else:
                term_copy(0).start()

        if comm:
            half = tok // 2

            def chip_sum(at, rows):
                return tr[core, rows].astype(F32) + sib[at, rows].astype(F32)

            @pl.when(e > 0)
            def _():
                to_sibling.wait()

            @pl.when(s == steps - 4)
            def _():
                def body(rows):
                    sums[0, rows] = chip_sum(1, rows).astype(BF)

                over_rows(tok, body)
                remote(sums.at[0, low_half], la, sends.at[2], recvs.at[2], same(1)).start()
                remote(sums.at[0, high_half], lb, sends.at[3], recvs.at[3], same(2)).start()

            @pl.when(s == steps - 3)
            def _():
                wait_for(la, recvs.at[2])

                def body(rows):
                    sums[1, rows] = (chip_sum(0, rows) + la[rows].astype(F32)).astype(BF)

                def rest(rows):
                    rows = pl.ds(pl.multiple_of(rows.start + half, CHUNK), CHUNK)
                    sums[1, rows] = chip_sum(0, rows).astype(BF)

                over_rows(half, body)
                over_rows(half, rest)
                remote(sums.at[1], fy, sends.at[4], recvs.at[4], same(2)).start()

            @pl.when(s == steps - 2)
            def _():
                wait_for(lb, recvs.at[3])

                def body(rows):
                    sums[2, rows] = chip_sum(1, rows).astype(BF)

                def rest(rows):
                    upper = pl.ds(pl.multiple_of(rows.start + half, CHUNK), CHUNK)
                    sums[2, upper] = (chip_sum(1, upper) + lb[rows].astype(F32)).astype(BF)

                over_rows(half, body)
                over_rows(half, rest)
                remote(sums.at[2], fx, sends.at[5], recvs.at[5], same(1)).start()

        return carry

    lax.fori_loop(0, steps, step, 0)
    if comm:
        wait_first_terms(True)
    pack_terms()
    term_copy(1).start()
    _, _, last = order(steps - 1)
    write_out(last).wait()
    if comm:
        wait_for(fx, recvs.at[5])
        wait_for(fy, recvs.at[4])

        def body(rows):
            total = tr[core, rows].astype(F32) + sib[0, rows].astype(F32)
            final[rows] = (total + (fx[rows].astype(F32) + fy[rows].astype(F32))).astype(BF)

        over_rows(tok, body)
        wait_for(la, sends.at[2])
        wait_for(lb, sends.at[3])
        wait_for(fy, sends.at[4])
        wait_for(fx, sends.at[5])
        for copy in first:
            copy.wait_send()
        for copy in forward:
            copy.wait_send()
        across.wait_send()
        wait_first_terms(False)
    else:
        write_row(last).wait()
    term_copy(1).wait()


def run_experts(x, g, weights, experts, slots, n_c, comm):
    tok, wide = x.shape[-2:]
    sources = 2 * n_c
    both = 2 * slots
    dma = pltpu.SemaphoreType.DMA
    term_shapes = (
        (MODEL_WIDTH, 2 * SPAN),
        (2, SPAN, EXPERT_HIDDEN),
        (EXPERT_HIDDEN, SPAN),
        (SPAN, MODEL_WIDTH),
    )
    any_spec = pl.BlockSpec(memory_space=ANY)
    out_shape = [
        jax.ShapeDtypeStruct((sources, tok, MODEL_WIDTH), BF),
        jax.ShapeDtypeStruct((sources, tok, wide), BF),
        jax.ShapeDtypeStruct(
            (TERM_PARTS, TERM_ROWS, 256) if comm else (TERM_PARTS, EXP_DEV, TERM_ROWS, 256), BF
        ),
    ]
    out_specs = [any_spec] * 3
    scratch = [
        VMEM((WIDE_IN, WIDE_IN), BF),
        VMEM((EXPERT_HIDDEN + SPAN, WIDE_OUT), BF),
        VMEM((2, tok, wide), BF),
        VMEM((2, tok, MODEL_WIDTH), BF),
        VMEM((both, WIDE_IN), BF),
        VMEM((both, WIDE_OUT), BF),
        VMEM((both, MODEL_WIDTH), F32),
        VMEM((both, EXPERT_HIDDEN + SPAN), BF),
        VMEM((both, EXPERT_HIDDEN), F32),
        VMEM((both, WIDE_IN), BF),
        VMEM((both, MODEL_WIDTH), BF),
        VMEM((2, tok, slots), BF),
        VMEM((both, 1), F32),
        VMEM((both, 1), F32),
        VMEM((both, SPAN), F32),
        VMEM((2, tok, MODEL_WIDTH), BF),
        VMEM((2, tok, wide), BF),
        *(VMEM(s, F32) for s in term_shapes),
        VMEM((TERM_PARTS, TERM_ROWS, 256), BF),
        dma((7,)),
        dma((6,)),
        dma((1,)),
    ]
    params = {}
    if comm:
        out_shape += [
            jax.ShapeDtypeStruct((sources, tok, wide), BF),
            jax.ShapeDtypeStruct((tok, wide), BF),
            jax.ShapeDtypeStruct((TERM_PARTS, TERM_ROWS, 256), BF),
        ]
        out_specs += [any_spec, pl.BlockSpec(memory_space=VMEM), any_spec]
        scratch += [
            VMEM((2, tok, wide), BF),
            VMEM((tok // 2, wide), BF),
            VMEM((tok // 2, wide), BF),
            VMEM((tok, wide), BF),
            VMEM((tok, wide), BF),
            VMEM((3, tok, wide), BF),
            dma((8,)),
            dma((8,)),
            dma((6,)),
            dma((6,)),
            dma((TERM_PARTS,)),
            dma((TERM_PARTS,)),
        ]
        params = dict(collective_id=6, has_side_effects=True)
    flops = 2 * sources * EXP_DEV * slots * MODEL_WIDTH * EXPERT_HIDDEN * 8
    g = g if comm else [g]
    results = pl.pallas_call(
        functools.partial(experts_kernel, n_c, experts, slots, comm),
        out_shape=out_shape,
        in_specs=[any_spec] * (7 + len(g)),
        out_specs=out_specs,
        scratch_shapes=scratch,
        compiler_params=pltpu.CompilerParams(vmem_limit_bytes=63 * 2**20, **params),
        cost_estimate=pl.CostEstimate(flops=flops, bytes_accessed=10**8, transcendentals=10**7),
        name="experts",
    )(x, *g, *weights)
    if comm:
        return results[0], results[4], (results[5], results[2])
    return results[0], results[1], results[2]


def late_kernel(n_f, dp, up, mask, low, x, dlow, packed):
    core = lax.axis_index("core")
    down_rows = MODEL_WIDTH // (4 * n_f)
    up_rows = SPAN // n_f
    base = 12 * down_rows
    packed[:, base:] = jnp.zeros((n_f, 24 * up_rows, SPAN), BF)
    for j in range(3):
        own = slice(j * SPAN, (j + 1) * SPAN)
        wide = slice(j * GROUP_WIDTH, (j + 1) * GROUP_WIDTH)
        lowered = (mm_t(dp[:, wide], up[own]) * mask[...]).astype(BF)
        dlow[:, own] = lowered
        grad_up = t_mm(low[:, own], dp[:, wide]).astype(BF)
        grad_down = t_mm(x[...], lowered).astype(BF)
        for f in range(n_f):
            for b in range(4):
                at = base + (j * 8 + core * 4 + b) * up_rows
                packed[f, pl.ds(pl.multiple_of(at, up_rows), up_rows)] = grad_up[
                    f * up_rows : (f + 1) * up_rows, b * SPAN : (b + 1) * SPAN
                ]
            for q in range(4):
                row = (q * n_f + f) * down_rows
                at = (q * 3 + j) * down_rows
                packed[f, at : at + down_rows] = grad_down[row : row + down_rows]


def late_gradients(grad_projected, up_own, mask, lowered, x, n_f):
    block = x.shape[0]
    rows = 12 * MODEL_WIDTH // (4 * n_f) + 24 * SPAN // n_f
    return pl.pallas_call(
        functools.partial(late_kernel, n_f),
        out_shape=(
            jax.ShapeDtypeStruct((block, 3 * SPAN), BF),
            jax.ShapeDtypeStruct((n_f, rows, SPAN), BF),
        ),
        in_specs=[pl.BlockSpec(memory_space=VMEM)] * 5,
        out_specs=[pl.BlockSpec(memory_space=VMEM)] * 2,
        compiler_params=pltpu.CompilerParams(vmem_limit_bytes=50 * 2**20),
        cost_estimate=pl.CostEstimate(flops=4 * 10**9, bytes_accessed=2 * 10**7, transcendentals=0),
        name="late_gradients",
    )(grad_projected, up_own, mask, lowered, x)


def plane_rows(rows):
    half = rows.shape[0] // 2
    along_x = lambda t: lax.ppermute(t, "c", [(0, 1), (1, 0), (2, 3), (3, 2)])
    along_y = lambda t: lax.ppermute(t, "c", [(0, 2), (2, 0), (1, 3), (3, 1)])
    to_sibling = lambda t: lax.ppermute(t, "core", [(0, 1), (1, 0)])
    beside, above = along_x(rows), along_y(rows)
    parts = [rows, beside, above, along_y(beside[:half]), along_x(above[half:])]
    return parts + [to_sibling(t) for t in parts]


def on_device(
    tokens,
    cotangent,
    lengths,
    sets,
    routes,
    gain_attn,
    gain_query,
    gain_key,
    gain_mlp,
    query_key_value_weight,
    out_weight,
    router_weight,
    gate_up_weight,
    down_weight,
    attention_down_factors,
    attention_up_factors,
    router_down_factors,
    router_up_factors,
    expert_input_down,
    expert_input_up,
    expert_output_down,
    expert_output_up,
):
    zh, zl, c, core = here()
    n_c = lax.axis_size("c")
    n_fsdp = 2 * n_c
    n_seq = lax.axis_size("zh") * lax.axis_size("zl")
    tok = tokens.shape[1]
    block = tok * n_seq
    experts = EXP_DEV * n_fsdp
    capacity = 5 * tok * TOP // (4 * experts)
    slots = -(-capacity // 16) * 16
    extra = -(-(3 * experts + 1) // 128) * 128
    span3 = 3 * SPAN
    group = zl * 2 + core
    shard = zh * 2 + zl

    both_lengths = lax.all_gather(
        jnp.concatenate([lengths[0], sets[0]]), "core", axis=0, tiled=False
    )
    held_lengths = lax.dynamic_index_in_dim(both_lengths, zh, 0, keepdims=False)
    count = lengths.shape[1]

    inputs = tokens[0].astype(F32)
    normalized = rms_scale(inputs, gain_attn).astype(BF)
    seq_block, block_offsets, block_sets = token_meta(
        held_lengths[:count], held_lengths[count:], jnp.arange(block, dtype=jnp.int32)
    )
    mask1 = set_mask(block_sets)
    if n_c == 4:
        x_shards, head_rows, up_group, projected, lowered = gather_project(
            normalized,
            query_key_value_weight,
            attention_down_factors[:, :span3],
            attention_up_factors,
            mask1.reshape(4, tok, SPAN),
        )
        projected, lowered = projected.reshape(block, -1), lowered.reshape(block, span3)
        up_own = up_group[:span3]
    else:
        x_shards, qkv_rows = gather_to_heads(normalized, query_key_value_weight, n_c)

    first_column = span3 if n_c == 4 else 0
    rows_local = query_key_value_weight.shape[0]
    factors = jnp.concatenate(
        [
            attention_down_factors[:, first_column:],
            attention_up_factors.reshape(rows_local, -1),
            router_down_factors,
            router_weight,
            router_up_factors.reshape(rows_local, -1),
        ],
        axis=1,
    )
    factor_width = factors.shape[1]
    factors = jnp.pad(factors, ((0, 0), (0, -factor_width % 128)))
    factors = lax.all_gather(factors, FSDP, axis=0, tiled=True)
    up_columns = attention_up_factors.size // rows_local
    at = 4 * SPAN - first_column
    down_full = factors[:, :at]
    down_o = down_full[:, span3 - first_column :]
    up_full = factors[:, at : at + up_columns].reshape(4 * SPAN, MODEL_WIDTH)
    at += up_columns
    rdown_full = factors[:, at : at + SPAN]
    at += SPAN
    router_full = factors[:, at : at + experts]
    at += experts
    rup_full = factors[:, at:factor_width].reshape(SPAN, experts)
    if n_c == 4:
        projected, out_weight, rows = lax.optimization_barrier(
            (projected, out_weight, cotangent[0])
        )
        grads_all = plane_rows(rows)
    else:
        grads_all = lax.all_gather(cotangent[0], FSDP, axis=0, tiled=False)
    out_full = lax.all_gather(out_weight, FSDP, axis=0, tiled=True)

    seq_local, _, chosen = token_meta(
        lengths[0], sets[0], shard * tok + jnp.arange(tok, dtype=jnp.int32)
    )
    mask = set_mask(chosen)
    half = HD // 2
    freqs = THETA ** (-(jnp.arange(half, dtype=F32) * 2.0 / HD))
    angles = block_offsets.astype(F32)[:, None] * freqs[None, :]
    cosine, sine = jnp.cos(angles), jnp.sin(angles)
    cosine = jnp.concatenate([cosine, cosine], axis=1)
    sine = jnp.concatenate([-sine, sine], axis=1)
    seg_c, seg_r = seq_block[:, None], seq_block[None, :]

    x_all = x_shards.reshape(block, MODEL_WIDTH)
    if n_c != 4:
        mask3 = jnp.tile(mask1, (1, 3))
        down3 = down_full[:, :span3]
        lowered = (mm(x_all, down3) * mask3).astype(BF)
        up_own = lax.dynamic_slice_in_dim(up_full[:span3], group * GROUP_WIDTH, GROUP_WIDTH, 1)
        none = jnp.zeros((SPAN, GROUP_WIDTH), BF)
        up_diagonal = jnp.concatenate(
            [
                jnp.concatenate(
                    [up_own[j * SPAN : (j + 1) * SPAN] if i == j else none for i in range(3)], axis=1
                )
                for j in range(3)
            ],
            axis=0,
        )
        projected = mm(x_all, qkv_rows) + mm(lowered, up_diagonal)
    part_q, part_k = projected[:, :GROUP_WIDTH], projected[:, GROUP_WIDTH : 2 * GROUP_WIDTH]

    def over_group(first, second, identity):
        both = jnp.stack([first, second]).reshape(-1, 128)
        return group_sum(both, identity).reshape(2, block)

    squares = over_group(jnp.sum(part_q * part_q, axis=1), jnp.sum(part_k * part_k, axis=1), 4)
    inverse = lax.rsqrt(squares / MODEL_WIDTH + EPSILON)
    rq, rk = inverse[0][:, None], inverse[1][:, None]
    gains = [
        lax.dynamic_slice_in_dim(g, group * GROUP_WIDTH, GROUP_WIDTH)[None, :]
        for g in (gain_query, gain_key)
    ]
    if n_c == 4:
        q, k, v, lse, attended = attend_send(
            projected, rq, rk, *gains, cosine, sine, seg_c, seg_r
        )
    else:
        q, k, v, attended_heads, lse = attend(
            projected, rq, rk, *gains, cosine, sine, seg_c, seg_r
        )
        attended = to_tokens(attended_heads.reshape(4, tok, GROUP_WIDTH))

    up_o = up_full[span3:]
    out_lower = (mm(attended, down_o) * mask).astype(BF)
    branch = mm(attended, out_full) + mm(out_lower, up_o)
    middle = inputs + branch
    normed2 = rms_scale(middle, gain_mlp).astype(BF)
    router_lower = (mm(normed2, rdown_full) * mask).astype(BF)
    logits = mm(normed2, router_full) + mm(router_lower, rup_full)
    probs = jax.nn.softmax(logits, axis=-1)
    hits = jnp.sum(
        (routes[0][:, :, None] == jnp.arange(experts, dtype=jnp.int32)[None, None, :]).astype(F32),
        axis=1,
    )
    place = jnp.arange(tok, dtype=jnp.int32)
    before = (place[None, :] < place[:, None]).astype(BF)
    ranks = jnp.where(hits > 0, mm(before, hits.astype(BF)), -1.0).astype(BF)
    gates = hits * probs
    gates_high = gates.astype(BF)
    gates_low = (gates - gates_high.astype(F32)).astype(BF)
    side = jnp.concatenate(
        [ranks, gates_high, gates_low, chosen.astype(BF)[:, None]], axis=1
    )
    payload = jnp.concatenate(
        [normed2, jnp.pad(side, ((0, 0), (0, extra - side.shape[1])))], axis=1
    )
    weights = (
        gate_up_weight,
        down_weight,
        expert_input_down,
        expert_input_up,
        expert_output_down,
        expert_output_up,
    )
    if n_c == 4:
        out_parts, returned, expert_terms = run_experts(
            payload, grads_all, weights, experts, slots, n_c, True
        )
    else:
        rows_all = lax.all_gather(payload, FSDP, axis=0, tiled=True)
        out_parts, row_parts, expert_terms = run_experts(
            rows_all.reshape(n_fsdp, tok, -1), grads_all, weights, experts, slots, n_c, False
        )
        returned = lax.psum_scatter(
            row_parts.reshape(n_fsdp * tok, -1), FSDP, scatter_dimension=0, tiled=True
        )
    mixed = lax.psum_scatter(
        out_parts.reshape(n_fsdp * tok, -1), FSDP, scatter_dimension=0, tiled=True
    )
    grad_out = cotangent[0].astype(F32)
    returned = returned.astype(F32)
    back = returned[:, MODEL_WIDTH:]
    grad_probs = back[:, :experts] + back[:, experts : 2 * experts]
    grad_logits = probs * (grad_probs - jnp.sum(probs * grad_probs, axis=-1, keepdims=True))
    grad_router_lower = exact("te,re->tr", grad_logits, rup_full.astype(F32)) * mask
    grad_normed2 = (
        returned[:, :MODEL_WIDTH]
        + mm_t(grad_logits.astype(BF), router_full)
        + mm_t(grad_router_lower.astype(BF), rdown_full)
    )
    grad_rup = t_mm(router_lower, grad_logits.astype(BF))
    grad_rdown = t_mm(normed2, grad_router_lower.astype(BF))
    grad_middle = grad_out + rms_back(middle, gain_mlp, grad_normed2)
    grad_branch = grad_middle.astype(BF)
    grad_out_lower = (mm_t(grad_branch, up_o) * mask).astype(BF)
    grad_attended = (mm_t(grad_branch, out_full) + mm_t(grad_out_lower, down_o)).astype(BF)
    head_grad = to_heads(grad_attended).reshape(block, GROUP_WIDTH)
    if n_c == 4:
        first_terms, second_terms = expert_terms
        second_terms, head_grad = lax.optimization_barrier((second_terms, head_grad))
        second_terms = lax.all_to_all(second_terms, SEQ, split_axis=0, concat_axis=0, tiled=True)
    else:
        expert_terms = lax.psum_scatter(expert_terms, SEQ, scatter_dimension=0, tiled=True)
    grad_up_o = t_mm(out_lower, grad_branch)
    grad_down_o = t_mm(attended, grad_out_lower)
    if n_c == 4:
        up_rows = SPAN // n_fsdp
        up_blocks = grad_up_o.astype(BF).reshape(n_fsdp, up_rows, 16, SPAN).transpose(0, 2, 1, 3)
        by_owner = lambda t: t.astype(BF).reshape(n_seq, n_fsdp, -1, SPAN).transpose(1, 0, 2, 3)
        rup_rows = jnp.pad(grad_rup.reshape(n_seq * n_fsdp, 1, -1), ((0, 0), (0, 15), (0, 0)))
        rup_rows = jnp.pad(rup_rows, ((0, 0), (0, 0), (0, SPAN - rup_rows.shape[2])))
        rest = jnp.concatenate(
            [by_owner(grad_down_o), by_owner(grad_rdown), by_owner(rup_rows)], axis=2
        )
        early = jnp.concatenate(
            [up_blocks.reshape(n_fsdp, -1, SPAN), rest.reshape(n_fsdp, -1, SPAN)], axis=1
        )
        early = lax.psum_scatter(early.reshape(-1, SPAN), FSDP, scatter_dimension=0, tiled=True)

    uq, uk, grad_v, mq, mk = attend_back(
        q, k, v, head_grad, lse, projected, *gains, cosine, sine, seg_c, seg_r
    )
    moments = over_group(jnp.sum(mq[..., 0], axis=0), jnp.sum(mk[..., 0], axis=0), 5) / MODEL_WIDTH

    def rms_inner(values, scale, gain, turned, moment):
        return (scale * gain * turned - values * (scale * scale * scale) * moment).astype(BF)

    grad_projected = jnp.concatenate(
        [
            rms_inner(part_q, rq, gains[0], uq, moments[0][:, None]),
            rms_inner(part_k, rk, gains[1], uk, moments[1][:, None]),
            grad_v,
        ],
        axis=1,
    )
    if n_c == 4:
        grad_lowered, late = late_gradients(
            grad_projected, up_own, mask1, lowered, x_all, n_fsdp
        )
    else:
        grad_lowered = (mm_t(grad_projected, up_diagonal) * mask3).astype(BF)
    if n_c == 4:
        both = jnp.concatenate([grad_projected, grad_lowered], axis=1)
        grad_normed_part = mm_t(both, head_rows).astype(BF)
    else:
        grad_normed_part = (
            mm_t(grad_projected, qkv_rows) + mm_t(grad_lowered, down3)
        ).astype(BF)
    grad_normed_part = grad_normed_part.reshape(4, tok, MODEL_WIDTH)
    if n_c == 4:
        grad_normed, flat = finish(grad_normed_part, late, early, n_c)
    else:
        grad_normed = sum_to_tokens(grad_normed_part)
    grad_inputs = grad_middle + rms_back(inputs, gain_attn, grad_normed)

    down_rows, up_rows = MODEL_WIDTH // (n_seq * n_fsdp), SPAN // n_fsdp
    rup_shape = (SPAN // (n_seq * n_fsdp), experts)
    if n_c == 4:
        blocks = [flat[j * down_rows : (j + 1) * down_rows] for j in range(3)]
        at = 3 * down_rows
        up_blocks = [flat[at + n * up_rows : at + (n + 1) * up_rows] for n in range(16)]
        at += 16 * up_rows
        blocks.append(flat[at : at + down_rows])
        at += down_rows
        summed = [
            jnp.concatenate(blocks, axis=1),
            jnp.concatenate(up_blocks, axis=1),
            flat[at : at + down_rows],
        ]
        at += down_rows
        summed.append(flat[at, : rup_shape[0] * rup_shape[1]].reshape(rup_shape))
    else:
        grad_up_own = [
            t_mm(
                lowered[:, j * SPAN : (j + 1) * SPAN],
                grad_projected[:, j * GROUP_WIDTH : (j + 1) * GROUP_WIDTH],
            )
            for j in range(3)
        ]
        grad_down_qkv = t_mm(x_all, grad_lowered)
        grad_down_all = jnp.concatenate([grad_down_qkv, grad_down_o], axis=1).astype(BF)
        wide_up = lax.dynamic_update_slice_in_dim(
            jnp.zeros((span3, MODEL_WIDTH), F32),
            jnp.concatenate(grad_up_own, axis=0),
            group * GROUP_WIDTH,
            1,
        )
        grad_up_all = jnp.concatenate([wide_up, grad_up_o], axis=0).astype(BF)
        terms = (grad_down_all, grad_up_all, grad_rdown.astype(BF), grad_rup.astype(BF))
        own_shapes = [(t.shape[0] // (n_seq * n_fsdp), t.shape[1]) for t in terms]
        flat = jnp.concatenate(
            [t.reshape(n_seq, n_fsdp, -1).transpose(1, 0, 2) for t in terms], axis=2
        )
        used = flat.shape[2]
        flat = jnp.pad(flat, ((0, 0), (0, 0), (0, -used % 1024))).reshape(n_fsdp * n_seq, -1, 128)
        flat = lax.psum_scatter(flat, FSDP, scatter_dimension=0, tiled=True)
        flat = lax.psum_scatter(flat, SEQ, scatter_dimension=0, tiled=True)
        flat = flat.astype(F32).reshape(-1)
        summed, at = [], 0
        for shape in own_shapes:
            size = shape[0] * shape[1]
            summed.append(flat[at : at + size].reshape(shape))
            at += size

    mixed, grad_inputs = lax.optimization_barrier((mixed, grad_inputs))
    output = (middle + mixed.astype(F32)).astype(BF)
    if n_c == 4:
        expert_terms = jnp.stack(
            [jnp.sum(t.astype(F32), axis=0) for t in (first_terms, second_terms)]
        )
    else:
        expert_terms = expert_terms[0].astype(F32)
    rows = MODEL_WIDTH // 4
    at = rows + 2 * SPAN
    halves = expert_terms[:, at : at + SPAN]
    low = at + SPAN
    expert_sums = [
        expert_terms[:, :rows],
        expert_terms[:, rows:at].reshape(EXP_DEV, 2, SPAN, EXPERT_HIDDEN // 4),
        jnp.concatenate([halves[..., :SPAN], halves[..., SPAN:]], axis=1),
        jnp.concatenate(
            [expert_terms[:, low : low + SPAN], expert_terms[:, low + SPAN : low + 2 * SPAN]],
            axis=2,
        ),
    ]
    return (output[None], grad_inputs[None], *summed, *expert_sums)


def solution(mesh):
    n_seq, n_fsdp = mesh.shape["seq"], mesh.shape["fsdp"]
    fine = Mesh(
        mesh.devices.reshape(2, n_seq // 2, n_fsdp // 2, 2), ("zh", "zl", "c", "core")
    )
    split = P(FSDP, SEQ, None)
    rows = P(FSDP, None)
    three = P(FSDP, None, None)
    in_specs = (
        split,
        split,
        rows,
        rows,
        split,
        P(),
        P(),
        P(),
        P(),
        rows,
        rows,
        rows,
        three,
        three,
        rows,
        rows,
        rows,
        rows,
        three,
        P(FSDP, None, None, None),
        three,
        three,
    )
    owners = P((*SEQ, *FSDP), None)
    out_specs = (
        split,
        split,
        owners,
        owners,
        owners,
        owners,
        split,
        P(FSDP, None, None, SEQ),
        split,
        P(FSDP, None, SEQ),
    )
    return jax.shard_map(
        on_device, mesh=fine, in_specs=in_specs, out_specs=out_specs, check_vma=False
    )
```

```python
import functools

import jax
import jax.numpy as jnp
from jax import lax
from jax.experimental import pallas as pl
from jax.experimental.pallas import tpu as pltpu
from jax.sharding import Mesh
from jax.sharding import PartitionSpec as P

MODEL_WIDTH = 2048
H = 16
HD = 128
EXPERT_HIDDEN = 1024
TOP = 8
EXP_DEV = 2
ADAPTER_RANK = 16
SPAN = 128
GROUPS = 4
GROUP_WIDTH = MODEL_WIDTH // GROUPS
HEADS = H // GROUPS

EPSILON = 1e-05
THETA = 10000.0
NEGATIVE = -1e30
BF = jnp.bfloat16
F32 = jnp.float32
ANY = pl.ANY
VMEM = pltpu.VMEM
SEQ = ("zh", "zl")
FSDP = ("c", "core")


def mm(left, right):
    return lax.dot_general(left, right, (((1,), (0,)), ((), ())), preferred_element_type=F32)


def mm_t(left, right):
    return lax.dot_general(left, right, (((1,), (1,)), ((), ())), preferred_element_type=F32)


def t_mm(left, right):
    return lax.dot_general(left, right, (((0,), (0,)), ((), ())), preferred_element_type=F32)


def exact(form, left, right):
    return jnp.einsum(form, left, right, precision=lax.Precision.HIGHEST, preferred_element_type=F32)


def rms_scale(values, gain):
    return values * lax.rsqrt(jnp.mean(values * values, axis=-1, keepdims=True) + EPSILON) * gain


def rms_back(values, gain, grad):
    inverse = lax.rsqrt(jnp.mean(values * values, axis=-1, keepdims=True) + EPSILON)
    scaled = grad * gain
    return inverse * scaled - values * inverse * inverse * inverse * jnp.mean(
        values * scaled, axis=-1, keepdims=True
    )


def token_meta(lengths_row, sets_row, places):
    count = lengths_row.shape[0]
    running = [lengths_row[0]]
    for n in range(1, count):
        running.append(running[-1] + lengths_row[n])
    ends = jnp.stack(running)
    starts = ends - lengths_row
    member = ((places[:, None] >= starts[None, :]) & (places[:, None] < ends[None, :])).astype(
        jnp.int32
    )
    seq_ids = jnp.sum(member * jnp.arange(count, dtype=jnp.int32)[None, :], axis=1)
    offsets = places - jnp.sum(member * starts[None, :], axis=1)
    chosen = jnp.sum(member * sets_row[None, :], axis=1)
    return (seq_ids, offsets, chosen)


def set_mask(chosen):
    column_range = jnp.arange(SPAN, dtype=jnp.int32) // ADAPTER_RANK
    return (chosen[..., None] == column_range).astype(F32)


def here():
    return tuple(lax.axis_index(n) for n in ("zh", "zl", "c", "core"))


def signal_all(peers):
    barrier = pltpu.get_barrier_semaphore()
    for peer in peers:
        pl.semaphore_signal(barrier, inc=1, device_id=peer, device_id_type=pl.DeviceIdType.MESH)
    pl.semaphore_wait(barrier, len(peers))


def remote(src, dst, send, recv, device):
    return pltpu.make_async_remote_copy(
        src_ref=src,
        dst_ref=dst,
        send_sem=send,
        recv_sem=recv,
        device_id=device,
        device_id_type=pl.DeviceIdType.MESH,
    )


def column_peers(zh, zl, c, core):
    return [
        (zh ^ a, zl ^ b, c, core ^ k)
        for a in range(2)
        for b in range(2)
        for k in range(2)
        if (a, b, k) != (0, 0, 0)
    ]


def gather_kernel(n_c, x_ref, w_ref, xg_ref, wg_ref, xs, xr, fs, fr, ws, wr, own):
    zh, zl, c, core = here()
    tok = x_ref.shape[0]
    half = tok // 2
    rows = w_ref.shape[0]
    plane = [(zh, zl, lax.rem(c + i, n_c), core ^ k) for i in range(n_c) for k in range(2)][2:]
    signal_all(column_peers(zh, zl, c, core) + plane)
    me = zh * 2 + zl
    for a in range(2):
        for k in range(2):
            piece = pl.ds(k * half, half)
            src, dst = x_ref.at[piece], xg_ref.at[me, piece]
            is_self = (core == zh) & (zl == a) & (core == k)

            @pl.when(is_self)
            def _():
                pltpu.make_async_copy(src, dst, xr.at[me]).start()

            @pl.when(jnp.logical_not(is_self))
            def _():
                remote(src, dst, xs.at[a, k], xr.at[me], (core, a, c, k)).start()

    f = c * 2 + core
    row_block = pl.ds(pl.multiple_of(f * rows, rows), rows)

    def pieces(group):
        for j in range(3):
            start = pl.multiple_of(j * MODEL_WIDTH + group * GROUP_WIDTH, GROUP_WIDTH)
            yield (
                w_ref.at[:, pl.ds(start, GROUP_WIDTH)],
                wg_ref.at[row_block, pl.ds(j * GROUP_WIDTH, GROUP_WIDTH)],
            )

    for src, dst in pieces(zl * 2 + core):
        pltpu.make_async_copy(src, dst, own).start()
    slots = [(i, k) for i in range(n_c) for k in range(2)][1:]
    for i, k in slots:
        target_c, target_core = lax.rem(c + i, n_c), core ^ k
        for src, dst in pieces(zl * 2 + target_core):
            remote(
                src, dst, ws.at[i * 2 + k], wr.at[i * 2 + k], (zh, zl, target_c, target_core)
            ).start()
    mine = pl.ds(pl.multiple_of(core * half, half), half)
    theirs = pl.ds(pl.multiple_of((1 - core) * half, half), half)
    sibling = (zh, zl, c, 1 - core)
    for s in range(4):
        pltpu.make_async_copy(xg_ref.at[s, mine], xg_ref.at[s, mine], xr.at[s]).wait()
        remote(xg_ref.at[s, mine], xg_ref.at[s, mine], fs.at[s], fr.at[s], sibling).start()
    for s in range(4):
        got = xg_ref.at[s, theirs]
        pltpu.make_async_copy(got, got, fr.at[s]).wait()
    for s in range(4):
        got = xg_ref.at[s, mine]
        pltpu.make_async_copy(got, got, fs.at[s]).wait()
    for a in range(2):
        for k in range(2):
            is_self = (core == zh) & (zl == a) & (core == k)
            src = x_ref.at[pl.ds(k * half, half)]

            @pl.when(jnp.logical_not(is_self))
            def _():
                pltpu.make_async_copy(src, src, xs.at[a, k]).wait()

    block = wg_ref.at[row_block]
    pltpu.make_async_copy(block, block, own).wait()
    for i, k in slots:
        pltpu.make_async_copy(block, block, ws.at[i * 2 + k]).wait()
        source = lax.rem(c + n_c - i, n_c) * 2 + (core ^ k)
        got = wg_ref.at[pl.ds(pl.multiple_of(source * rows, rows), rows)]
        pltpu.make_async_copy(got, got, wr.at[i * 2 + k]).wait()


def gather_to_heads(x, w, n_c):
    tok, rows = x.shape[0], w.shape[0]
    n_f = 2 * n_c
    dma = pltpu.SemaphoreType.DMA
    return pl.pallas_call(
        functools.partial(gather_kernel, n_c),
        out_shape=(
            jax.ShapeDtypeStruct((4, tok, MODEL_WIDTH), BF),
            jax.ShapeDtypeStruct((n_f * rows, 3 * GROUP_WIDTH), BF),
        ),
        in_specs=[pl.BlockSpec(memory_space=VMEM)] * 2,
        out_specs=[pl.BlockSpec(memory_space=ANY)] * 2,
        scratch_shapes=[
            dma((2, 2)),
            dma((4,)),
            dma((4,)),
            dma((4,)),
            dma((n_f,)),
            dma((n_f,)),
            dma,
        ],
        compiler_params=pltpu.CompilerParams(collective_id=0, has_side_effects=True),
        name="gather_to_heads",
    )(x, w)


PROJECT_WIDTH = 3 * GROUP_WIDTH + 3 * SPAN


def project_kernel(x_ref, w_ref, down_ref, up_ref, mask, xg_o, wg_o, upg, proj_o, low, acc, xg, wg, xs, xr, fs, fr, ws, wr, us, ur, own, out):
    zh, zl, c, core = here()
    tok = x_ref.shape[0]
    half = tok // 2
    rows = w_ref.shape[0]
    up_rows = up_ref.shape[0]
    near = lambda i: (
        lax.rem(c // 2 + i // 2, 2) * 2 + lax.rem(lax.rem(c, 2) + lax.rem(i, 2), 2)
    )
    chips = [near(i) for i in range(4)]
    plane = [(zh, zl, chips[i], core ^ k) for i in range(4) for k in range(2)]
    sibling, beside, above = plane[1], plane[2], plane[4]
    signal_all(column_peers(zh, zl, c, core) + plane[2:])
    me = zh * 2 + zl
    f = c * 2 + core
    block = lambda source: wg.at[pl.ds(pl.multiple_of(source * rows, rows), rows)]
    source = lambda i, k: chips[i] * 2 + k

    def pieces(group):
        to = pl.ds(pl.multiple_of(f * rows, rows), rows)
        for j in range(3):
            start = pl.multiple_of(j * MODEL_WIDTH + group * GROUP_WIDTH, GROUP_WIDTH)
            yield (
                w_ref.at[:, pl.ds(start, GROUP_WIDTH)],
                wg.at[to, pl.ds(j * GROUP_WIDTH, GROUP_WIDTH)],
            )
        yield down_ref, wg.at[to, pl.ds(3 * GROUP_WIDTH, 3 * SPAN)]

    for src, dst in pieces(zl * 2 + core):
        pltpu.make_async_copy(src, dst, own.at[0]).start()
    for src, dst in pieces(zl * 2 + 1 - core):
        remote(src, dst, ws.at[0], wr.at[0], sibling).start()
    for a in range(2):
        for k in range(2):
            piece = pl.ds(k * half, half)
            src, dst = x_ref.at[piece], xg.at[me, piece]
            is_self = (core == zh) & (zl == a) & (core == k)

            @pl.when(is_self)
            def _():
                pltpu.make_async_copy(src, dst, xr.at[me]).start()

            @pl.when(jnp.logical_not(is_self))
            def _():
                remote(src, dst, xs.at[a, k], xr.at[me], (core, a, c, k)).start()

    wait_for(block(f), own.at[0])
    remote(block(f), block(f), ws.at[1], wr.at[1], beside).start()
    remote(block(f), block(f), ws.at[2], wr.at[2], above).start()
    up_to = pl.ds(pl.multiple_of(f * up_rows, up_rows), up_rows)
    for n, peer in enumerate(plane):
        start = pl.multiple_of((zl * 2 + peer[3]) * GROUP_WIDTH, GROUP_WIDTH)
        src, dst = up_ref.at[:, pl.ds(start, GROUP_WIDTH)], upg.at[up_to]
        if n:
            remote(src, dst, us.at[n], ur.at[n], peer).start()
        else:
            pltpu.make_async_copy(src, dst, own.at[1]).start()
    other = c * 2 + 1 - core
    wait_for(block(other), wr.at[0])
    remote(block(other), block(other), ws.at[3], wr.at[3], beside).start()
    remote(block(other), block(other), ws.at[4], wr.at[4], above).start()
    mine = pl.ds(pl.multiple_of(core * half, half), half)
    theirs = pl.ds(pl.multiple_of((1 - core) * half, half), half)

    shards = [k + zh * (3 - 2 * k) for k in range(4)]

    def pass_tokens(k):
        s = shards[k]
        wait_for(xg.at[s, mine], xr.at[s])
        remote(xg.at[s, mine], xg.at[s, mine], fs.at[s], fr.at[s], sibling).start()

    def take_tokens(k):
        s = shards[k]
        wait_for(xg.at[s, theirs], fr.at[s])
        pltpu.make_async_copy(xg.at[s], xg_o.at[s], out.at[0]).start()

    def multiply(i, k):
        at = pl.ds(pl.multiple_of(chips[i] * (2 * rows), 2 * rows), 2 * rows)
        s = shards[k]
        value = mm(xg[s, :, at], wg[at, :])
        acc[s] = value if i == 0 else acc[s] + value

    own_x, other_x = source(1, core), source(1, 1 - core)
    own_y, other_y = source(2, core), source(2, 1 - core)
    pass_tokens(0)
    take_tokens(0)
    multiply(0, 0)
    wait_for(block(own_x), wr.at[1])
    remote(block(own_x), block(own_x), ws.at[5], wr.at[5], above).start()
    pass_tokens(1)
    take_tokens(1)
    multiply(0, 1)
    wait_for(block(own_y), wr.at[2])
    wait_for(block(other_y), wr.at[4])
    remote(block(other_y), block(other_y), ws.at[6], wr.at[6], beside).start()
    pass_tokens(2)
    wait_for(block(other_x), wr.at[3])
    for k in range(2):
        multiply(1, k)
        multiply(2, k)
    take_tokens(2)
    for i in range(3):
        multiply(i, 2)
    pass_tokens(3)
    take_tokens(3)
    for i in range(3):
        multiply(i, 3)
    wait_for(block(source(3, core)), wr.at[5])
    wait_for(block(source(3, 1 - core)), wr.at[6])
    save = pltpu.make_async_copy(wg, wg_o, out.at[1])
    save.start()
    for k in range(4):
        multiply(3, k)
    up_block = lambda n: upg.at[pl.ds(pl.multiple_of(n * up_rows, up_rows), up_rows)]
    wait_for(up_block(f), own.at[1])
    for n, peer in enumerate(plane):
        if n:
            wait_for(up_block(peer[2] * 2 + peer[3]), ur.at[n])

    for s in range(4):
        for j in range(3):
            span = slice(j * SPAN, (j + 1) * SPAN)
            wide = slice(j * GROUP_WIDTH, (j + 1) * GROUP_WIDTH)
            at = 3 * GROUP_WIDTH + j * SPAN
            lowered = (acc[s, :, at : at + SPAN] * mask[s]).astype(BF)
            low[s, :, span] = lowered
            acc[s, :, wide] = acc[s, :, wide] + mm(lowered, upg[span])
        pltpu.make_async_copy(acc.at[s, :, pl.ds(0, 3 * GROUP_WIDTH)], proj_o.at[s], out.at[2]).start()

    for s in range(4):
        wait_for(xg.at[s, mine], fs.at[s])
    for a in range(2):
        for k in range(2):
            is_self = (core == zh) & (zl == a) & (core == k)

            @pl.when(jnp.logical_not(is_self))
            def _():
                wait_for(x_ref.at[pl.ds(k * half, half)], xs.at[a, k])

    save.wait()
    wait_for(xg_o, out.at[0])
    wait_for(proj_o, out.at[2])
    for n in range(7):
        wait_for(block(f), ws.at[n])
    for n in range(1, 8):
        wait_for(up_block(f), us.at[n])


def gather_project(x, w, down3, up, mask):
    tok, rows = x.shape[0], w.shape[0]
    dma = pltpu.SemaphoreType.DMA
    vmem = pl.BlockSpec(memory_space=VMEM)
    hbm = pl.BlockSpec(memory_space=ANY)
    return pl.pallas_call(
        project_kernel,
        out_shape=(
            jax.ShapeDtypeStruct((4, tok, MODEL_WIDTH), BF),
            jax.ShapeDtypeStruct((8 * rows, PROJECT_WIDTH), BF),
            jax.ShapeDtypeStruct((8 * up.shape[0], GROUP_WIDTH), BF),
            jax.ShapeDtypeStruct((4, tok, 3 * GROUP_WIDTH), F32),
            jax.ShapeDtypeStruct((4, tok, 3 * SPAN), BF),
        ),
        in_specs=[vmem] * 5,
        out_specs=[hbm, hbm, vmem, hbm, vmem],
        scratch_shapes=[
            VMEM((4, tok, PROJECT_WIDTH), F32),
            VMEM((4, tok, MODEL_WIDTH), BF),
            VMEM((8 * rows, PROJECT_WIDTH), BF),
            dma((2, 2)),
            dma((4,)),
            dma((4,)),
            dma((4,)),
            dma((7,)),
            dma((7,)),
            dma((8,)),
            dma((8,)),
            dma((2,)),
            dma((3,)),
        ],
        compiler_params=pltpu.CompilerParams(
            collective_id=8, has_side_effects=True, vmem_limit_bytes=58 * 2**20
        ),
        name="gather_project",
    )(x, w, down3, up, mask)


def to_tokens_kernel(a_ref, o_ref, send, recv):
    zh, zl, c, core = here()
    signal_all(column_peers(zh, zl, c, core))
    group = zl * 2 + core
    columns = pl.ds(pl.multiple_of(group * GROUP_WIDTH, GROUP_WIDTH), GROUP_WIDTH)
    for s in range(4):
        a, b = s // 2, s % 2
        is_self = (a == zh) & (b == zl) & (core == zh)
        src, dst = a_ref.at[s], o_ref.at[:, columns]

        @pl.when(is_self)
        def _():
            pltpu.make_async_copy(src, dst, recv.at[group]).start()

        @pl.when(jnp.logical_not(is_self))
        def _():
            remote(src, dst, send.at[s], recv.at[group], (a, b, c, zh)).start()

    for s in range(4):
        a, b = s // 2, s % 2
        is_self = (a == zh) & (b == zl) & (core == zh)
        got = o_ref.at[:, pl.ds(s * GROUP_WIDTH, GROUP_WIDTH)]
        pltpu.make_async_copy(got, got, recv.at[s]).wait()

        @pl.when(jnp.logical_not(is_self))
        def _():
            pltpu.make_async_copy(a_ref.at[s], a_ref.at[s], send.at[s]).wait()


def to_tokens(rows):
    tok = rows.shape[1]
    dma = pltpu.SemaphoreType.DMA
    return pl.pallas_call(
        to_tokens_kernel,
        out_shape=jax.ShapeDtypeStruct((tok, MODEL_WIDTH), BF),
        in_specs=[pl.BlockSpec(memory_space=VMEM)],
        out_specs=pl.BlockSpec(memory_space=ANY),
        scratch_shapes=[dma((4,)), dma((4,))],
        compiler_params=pltpu.CompilerParams(collective_id=1, has_side_effects=True),
        name="to_tokens",
    )(rows)


def to_heads_kernel(a_ref, o_ref, send, recv):
    zh, zl, c, core = here()
    signal_all(column_peers(zh, zl, c, core))
    me = zh * 2 + zl
    for g in range(4):
        b, k = g // 2, g % 2
        is_self = (core == zh) & (b == zl) & (core == k)
        src, dst = a_ref.at[:, pl.ds(g * GROUP_WIDTH, GROUP_WIDTH)], o_ref.at[me]

        @pl.when(is_self)
        def _():
            pltpu.make_async_copy(src, dst, recv.at[me]).start()

        @pl.when(jnp.logical_not(is_self))
        def _():
            remote(src, dst, send.at[g], recv.at[me], (core, b, c, k)).start()

    for g in range(4):
        b, k = g // 2, g % 2
        is_self = (core == zh) & (b == zl) & (core == k)
        pltpu.make_async_copy(o_ref.at[g], o_ref.at[g], recv.at[g]).wait()

        @pl.when(jnp.logical_not(is_self))
        def _():
            pltpu.make_async_copy(o_ref.at[g], o_ref.at[g], send.at[g]).wait()


def to_heads(rows):
    tok = rows.shape[0]
    dma = pltpu.SemaphoreType.DMA
    return pl.pallas_call(
        to_heads_kernel,
        out_shape=jax.ShapeDtypeStruct((4, tok, GROUP_WIDTH), BF),
        in_specs=[pl.BlockSpec(memory_space=VMEM)],
        out_specs=pl.BlockSpec(memory_space=ANY),
        scratch_shapes=[dma((4,)), dma((4,))],
        compiler_params=pltpu.CompilerParams(collective_id=2, has_side_effects=True),
        name="to_heads",
    )(rows)


def sum_to_tokens_kernel(p_ref, o_ref, sib, chip, rx, ss, sr, send, recv):
    zh, zl, c, core = here()
    signal_all(column_peers(zh, zl, c, core))
    width = o_ref.shape[1]
    half = width // 2
    sibling = (zh, zl, c, 1 - core)
    mine = pl.ds(pl.multiple_of(core * half, half), half)
    theirs = pl.ds(pl.multiple_of((1 - core) * half, half), half)
    for s in range(4):
        remote(p_ref.at[s, :, theirs], sib.at[s], ss.at[s], sr.at[s], sibling).start()

    def is_self(s):
        return (s // 2 == zh) & (s % 2 == zl) & (core == zh)

    for s in range(4):
        pltpu.make_async_copy(sib.at[s], sib.at[s], sr.at[s]).wait()
        chip[s] = (p_ref[s, :, mine].astype(F32) + sib[s].astype(F32)).astype(BF)
        src, dst = chip.at[s], rx.at[zl, core]

        @pl.when(is_self(s))
        def _():
            pltpu.make_async_copy(src, dst, recv.at[zl, core]).start()

        @pl.when(jnp.logical_not(is_self(s)))
        def _():
            remote(src, dst, send.at[s], recv.at[zl, core], (s // 2, s % 2, c, zh)).start()

    for s in range(4):
        pltpu.make_async_copy(sib.at[s], sib.at[s], ss.at[s]).wait()

        @pl.when(jnp.logical_not(is_self(s)))
        def _():
            pltpu.make_async_copy(chip.at[s], chip.at[s], send.at[s]).wait()

    for k in range(2):
        for b in range(2):
            pltpu.make_async_copy(rx.at[b, k], rx.at[b, k], recv.at[b, k]).wait()
        o_ref[:, k * half : (k + 1) * half] = rx[0, k].astype(F32) + rx[1, k].astype(F32)


def sum_to_tokens(parts):
    _, tok, width = parts.shape
    half = width // 2
    dma = pltpu.SemaphoreType.DMA
    return pl.pallas_call(
        sum_to_tokens_kernel,
        out_shape=jax.ShapeDtypeStruct((tok, width), F32),
        in_specs=[pl.BlockSpec(memory_space=VMEM)],
        out_specs=pl.BlockSpec(memory_space=VMEM),
        scratch_shapes=[
            VMEM((4, tok, half), BF),
            VMEM((4, tok, half), BF),
            VMEM((2, 2, tok, half), BF),
            dma((4,)),
            dma((4,)),
            dma((4,)),
            dma((2, 2)),
        ],
        compiler_params=pltpu.CompilerParams(
            collective_id=3, has_side_effects=True, vmem_limit_bytes=40 * 2**20
        ),
        name="sum_to_tokens",
    )(parts)


def finish_kernel(
    n_c,
    both,
    weight,
    late,
    early,
    middle,
    mixed,
    tokens,
    grad_middle,
    gain,
    output,
    grad_tokens,
    grad_down,
    grad_up,
    grad_rdown,
    grad_rup,
    give,
    keep,
    sib,
    fwd,
    rx,
    got_l,
    got_e,
    stage,
    got_z,
    ss,
    sr,
    gs,
    gr,
    send,
    recv,
    ls,
    lr,
    es,
    er,
    zs,
    zr,
):
    zh, zl, c, core = here()
    plane = [(zh, zl, lax.rem(c + i, n_c), core ^ k) for i in range(n_c) for k in range(2)]
    signal_all(column_peers(zh, zl, c, core) + plane[2:])
    tok, width = output.shape
    half = width // 2
    sibling = (zh, zl, c, 1 - core)
    mine = pl.ds(pl.multiple_of(core * half, half), half)
    theirs = pl.ds(pl.multiple_of((1 - core) * half, half), half)
    me = c * 2 + core
    count = len(plane)
    for n in range(1, count):
        peer = plane[n]
        f = peer[2] * 2 + peer[3]
        remote(early.at[f], got_e.at[n], es.at[n], er.at[n], peer).start()
        remote(late.at[f], got_l.at[n], ls.at[n], lr.at[n], peer).start()
    at_end = zl == zh
    inner = zl != zh
    shard = lambda p: p + zh * (3 - 2 * p)
    owner = lambda p: (shard(p) // 2, lax.rem(shard(p), 2), c, zh)
    local = core == zh

    def deliver(n, p, slot):
        remote(give.at[n], rx.at[slot, core], send.at[n], recv.at[slot, core], owner(p)).start()

    def stay(n, slot):
        pltpu.make_async_copy(give.at[n], rx.at[slot, core], recv.at[slot, core]).start()

    def settle(n, p):
        pltpu.make_async_copy(sib.at[n], sib.at[n], sr.at[n]).wait()
        wait_for(give.at[n], ss.at[n])
        give[n] = (keep[n] + sib[n].astype(F32)).astype(BF)
        if p >= 2:

            @pl.when(at_end)
            def _():
                remote(give.at[n], fwd.at[n], gs.at[n], gr.at[n], (zh, 1 - zl, c, core)).start()

        else:
            home = at_end if p == 0 else inner

            @pl.when(home & local)
            def _():
                stay(n, p)

            @pl.when(home & jnp.logical_not(local))
            def _():
                deliver(n, p, p)

            @pl.when(jnp.logical_not(home))
            def _():
                deliver(n, p, 1 - p)

    order = (3, 2, 1, 0)
    for n, p in enumerate(order):
        rows = pl.ds(pl.multiple_of(shard(p) * tok, tok), tok)
        give[n] = mm_t(both[rows], weight[theirs]).astype(BF)
        remote(give.at[n], sib.at[n], ss.at[n], sr.at[n], sibling).start()
        keep[n] = mm_t(both[rows], weight[mine])
        if n:
            settle(n - 1, order[n - 1])
    settle(3, 0)

    @pl.when(inner)
    def _():
        for n in range(2):
            wait_for(fwd.at[n], gr.at[n])
            give[n] = (give[n].astype(F32) + fwd[n].astype(F32)).astype(BF)
            deliver(n, order[n], 1)

    output[...] = (middle[...] + mixed[...].astype(F32)).astype(BF)

    def total(own, got, arrived):
        value = own[me].astype(F32)
        for n in range(1, count):
            wait_for(got.at[n], arrived.at[n])
            value = value + got[n].astype(F32)
        return value.astype(BF)

    early_sum = total(early, got_e, er)
    late_sum = total(late, got_l, lr)
    down, up, wide, rest = finish_rows(n_c)
    for q in range(4):
        stage[q, :down] = late_sum[q * down : (q + 1) * down]
        if q < 3:
            at = 4 * down + q * up
            stage[q, down : down + up] = late_sum[at : at + up]
            stage[q, down + up : down + wide] = jnp.zeros((wide - up, SPAN), BF)
        else:
            stage[q, down : down + wide] = early_sum[:wide]
        at = wide + q * rest
        stage[q, down + wide :] = early_sum[at : at + rest]
    seq = zh * 2 + zl
    for q in range(4):

        @pl.when(seq == q)
        def _():
            got_z[q] = stage[q]

        @pl.when(seq != q)
        def _():
            remote(stage.at[q], got_z.at[seq], zs.at[q], zr.at[seq], (q // 2, q % 2, c, core)).start()

    paired = zh == core

    @pl.when(paired)
    def _():
        for k in range(2):
            wait_for(rx.at[0, k], recv.at[0, k])

    @pl.when(jnp.logical_not(paired))
    def _():
        rx[0] = jnp.zeros_like(rx[0])

    for k in range(2):
        wait_for(rx.at[1, k], recv.at[1, k])
    for n in range(tok // 32):
        rows = slice(n * 32, (n + 1) * 32)
        grad = jnp.concatenate(
            [rx[0, k, rows].astype(F32) + rx[1, k, rows].astype(F32) for k in range(2)], axis=1
        )
        grad_tokens[rows] = grad_middle[rows] + rms_back(tokens[rows].astype(F32), gain[...], grad)

    for q in range(4):

        @pl.when(seq != q)
        def _():
            wait_for(got_z.at[q], zr.at[q])

    def along_z(rows):
        return (got_z[0, rows].astype(F32) + got_z[1, rows].astype(F32)) + (
            got_z[2, rows].astype(F32) + got_z[3, rows].astype(F32)
        )

    r, u = down // 3, up // 8
    for j in range(4):
        start = j * r if j < 3 else down + wide
        grad_down[:, j * SPAN : (j + 1) * SPAN] = along_z(slice(start, start + r))
    grad_rdown[...] = along_z(slice(down + wide + r, down + wide + 2 * r))
    grad_rup[...] = along_z(slice(down + wide + 2 * r, down + wide + rest))
    for n in range(16):
        b, m = n // 8, n % 8
        part = slice(down + m * u, down + (m + 1) * u)
        halves = got_z[b, part].astype(F32) + got_z[2 + b, part].astype(F32)
        whole = along_z(slice(down + n * u, down + (n + 1) * u))
        grad_up[:, n * SPAN : (n + 1) * SPAN] = jnp.where(seq < 3, halves, whole)

    for s in range(4):

        @pl.when(seq != s)
        def _():
            wait_for(stage.at[s], zs.at[s])

    for n, p in enumerate(order):
        if p >= 2:

            @pl.when(at_end)
            def _():
                wait_for(give.at[n], gs.at[n])

            @pl.when(inner)
            def _():
                wait_for(give.at[n], send.at[n])

        else:
            home = at_end if p == 0 else inner

            @pl.when(jnp.logical_not(home & local))
            def _():
                wait_for(give.at[n], send.at[n])

    for n in range(1, count):
        wait_for(got_l.at[n], ls.at[n])
        wait_for(got_e.at[n], es.at[n])


def finish_rows(n_c):
    n_f = 2 * n_c
    down, up = MODEL_WIDTH // (4 * n_f), SPAN // n_f
    return 3 * down, 8 * up, 16 * up, 2 * down + 16


def finish(both, weight, late, early, middle, mixed, tokens, grad_middle, gain, n_c):
    tok, width = middle.shape
    half = width // 2
    down, up, wide, rest = finish_rows(n_c)
    n_f = 2 * n_c
    dma = pltpu.SemaphoreType.DMA
    vmem = pl.BlockSpec(memory_space=VMEM)
    return pl.pallas_call(
        functools.partial(finish_kernel, n_c),
        out_shape=(
            jax.ShapeDtypeStruct((tok, width), BF),
            jax.ShapeDtypeStruct((tok, width), F32),
            jax.ShapeDtypeStruct((down // 3, 4 * SPAN), F32),
            jax.ShapeDtypeStruct((up // 8, 16 * SPAN), F32),
            jax.ShapeDtypeStruct((down // 3, SPAN), F32),
            jax.ShapeDtypeStruct((16, SPAN), F32),
        ),
        in_specs=[vmem] * 9,
        out_specs=[vmem] * 6,
        scratch_shapes=[
            VMEM((4, tok, half), BF),
            VMEM((4, tok, half), F32),
            VMEM((4, tok, half), BF),
            VMEM((2, tok, half), BF),
            VMEM((2, 2, tok, half), BF),
            VMEM(late.shape, BF),
            VMEM(early.shape, BF),
            VMEM((4, down + wide + rest, SPAN), BF),
            VMEM((4, down + wide + rest, SPAN), BF),
            dma((4,)),
            dma((4,)),
            dma((2,)),
            dma((2,)),
            dma((4,)),
            dma((2, 2)),
            dma((n_f,)),
            dma((n_f,)),
            dma((n_f,)),
            dma((n_f,)),
            dma((4,)),
            dma((4,)),
        ],
        compiler_params=pltpu.CompilerParams(
            collective_id=7, has_side_effects=True, vmem_limit_bytes=60 * 2**20
        ),
        name="finish",
    )(both, weight, late, early, middle, mixed, tokens, grad_middle, gain)


def group_sum_kernel(x_ref, o_ref, rx, send, recv):
    zh, zl, c, core = here()
    peers = [(zh, zl, c, 1 - core), (zh, 1 - zl, c, core), (zh, 1 - zl, c, 1 - core)]
    signal_all(peers)
    copies = [remote(x_ref, rx.at[i], send.at[i], recv.at[i], p) for i, p in enumerate(peers)]
    for copy in copies:
        copy.start()
    for copy in copies:
        copy.wait()
    o_ref[...] = (x_ref[...] + rx[0]) + (rx[1] + rx[2])


def group_sum(values, identity):
    dma = pltpu.SemaphoreType.DMA
    return pl.pallas_call(
        group_sum_kernel,
        out_shape=jax.ShapeDtypeStruct(values.shape, F32),
        in_specs=[pl.BlockSpec(memory_space=VMEM)],
        out_specs=pl.BlockSpec(memory_space=VMEM),
        scratch_shapes=[VMEM((3, *values.shape), F32), dma((3,)), dma((3,))],
        compiler_params=pltpu.CompilerParams(collective_id=identity, has_side_effects=True),
        name="group_sum",
    )(values)


def turn(values, cosine, sine):
    return values * cosine + pltpu.roll(values, HD // 2, 1) * sine


def attention_rows(block):
    return 256 if block % 256 == 0 else block


def attend_kernel(
    pq, pk, pv, rq, rk, gq, gk, cosine, sine, seg_c, seg_r, q_ref, k_ref, v_ref, o_ref, lse_ref
):
    block = pq.shape[0]
    rows = attention_rows(block)
    scale = HD**-0.5
    q_ref[...] = turn(pq[...] * rq[...] * gq[...], cosine[...], sine[...]).astype(BF)
    k_ref[...] = turn(pk[...] * rk[...] * gk[...], cosine[...], sine[...]).astype(BF)
    v_ref[...] = pv[...].astype(BF)
    for i in range(block // rows):
        length = (i + 1) * rows
        own = slice(i * rows, length)
        scores = mm_t(q_ref[own], k_ref[:length]) * scale
        row = lax.broadcasted_iota(jnp.int32, (rows, length), 0) + i * rows
        column = lax.broadcasted_iota(jnp.int32, (rows, length), 1)
        allowed = (seg_c[own] == seg_r[:, :length]) & (column <= row)
        scores = jnp.where(allowed, scores, NEGATIVE)
        top = jnp.max(scores, axis=1, keepdims=True)
        weights = jnp.exp(scores - top)
        total = jnp.sum(weights, axis=1, keepdims=True)
        out = mm(weights.astype(BF), v_ref[:length]) / total
        o_ref[own] = out.astype(BF)
        lse_ref[0, own] = top + jnp.log(total)


def attend(projected, rq, rk, gq, gk, cosine, sine, seg_c, seg_r):
    block = projected.shape[0]
    head = lambda off: pl.BlockSpec((block, HD), lambda h: (0, off + h))
    gain = pl.BlockSpec((1, HD), lambda h: (0, h))
    fixed = lambda shape: pl.BlockSpec(shape, lambda h: (0, 0))
    wide = jax.ShapeDtypeStruct((block, GROUP_WIDTH), BF)
    return pl.pallas_call(
        attend_kernel,
        grid=(HEADS,),
        out_shape=(wide, wide, wide, wide, jax.ShapeDtypeStruct((HEADS, block, 1), F32)),
        in_specs=[
            head(0),
            head(HEADS),
            head(2 * HEADS),
            fixed((block, 1)),
            fixed((block, 1)),
            gain,
            gain,
            fixed((block, HD)),
            fixed((block, HD)),
            fixed((block, 1)),
            fixed((1, block)),
        ],
        out_specs=[head(0)] * 4 + [pl.BlockSpec((1, block, 1), lambda h: (h, 0, 0))],
        compiler_params=pltpu.CompilerParams(vmem_limit_bytes=60 * 2**20),
        name="attend",
    )(projected, projected, projected, rq, rk, gq, gk, cosine, sine, seg_c, seg_r)


def attend_send_kernel(
    pq, pk, pv, rq, rk, gq, gk, cosine, sine, seg_c, seg_r, q_ref, k_ref, v_ref, lse_ref, o_ref, held, send, recv
):
    zh, zl, c, core = here()
    h = pl.program_id(0)
    tok = o_ref.shape[0]
    group = zl * 2 + core

    @pl.when(h == 0)
    def _():
        signal_all(column_peers(zh, zl, c, core))

    attend_kernel(
        pq, pk, pv, rq, rk, gq, gk, cosine, sine, seg_c, seg_r, q_ref, k_ref, v_ref, held.at[h], lse_ref
    )
    columns = pl.ds(pl.multiple_of(group * GROUP_WIDTH + h * HD, HD), HD)
    is_self = lambda s: (s // 2 == zh) & (s % 2 == zl) & (core == zh)
    for s in range(4):
        src, dst = held.at[h, pl.ds(s * tok, tok)], o_ref.at[:, columns]

        @pl.when(is_self(s))
        def _():
            pltpu.make_async_copy(src, dst, recv.at[group, h]).start()

        @pl.when(jnp.logical_not(is_self(s)))
        def _():
            remote(src, dst, send.at[s, h], recv.at[group, h], (s // 2, s % 2, c, zh)).start()

    @pl.when(h == HEADS - 1)
    def _():
        for n in range(HEADS):
            for s in range(4):
                got = o_ref.at[:, pl.ds(s * GROUP_WIDTH + n * HD, HD)]
                wait_for(got, recv.at[s, n])

                @pl.when(jnp.logical_not(is_self(s)))
                def _():
                    wait_for(held.at[n, pl.ds(0, tok)], send.at[s, n])


def attend_send(projected, rq, rk, gq, gk, cosine, sine, seg_c, seg_r):
    block = projected.shape[0]
    tok = block // 4
    dma = pltpu.SemaphoreType.DMA
    head = lambda off: pl.BlockSpec((block, HD), lambda h: (0, off + h))
    gain = pl.BlockSpec((1, HD), lambda h: (0, h))
    fixed = lambda shape: pl.BlockSpec(shape, lambda h: (0, 0))
    wide = jax.ShapeDtypeStruct((block, GROUP_WIDTH), BF)
    return pl.pallas_call(
        attend_send_kernel,
        grid=(HEADS,),
        out_shape=(
            wide,
            wide,
            wide,
            jax.ShapeDtypeStruct((HEADS, block, 1), F32),
            jax.ShapeDtypeStruct((tok, MODEL_WIDTH), BF),
        ),
        in_specs=[
            head(0),
            head(HEADS),
            head(2 * HEADS),
            fixed((block, 1)),
            fixed((block, 1)),
            gain,
            gain,
            fixed((block, HD)),
            fixed((block, HD)),
            fixed((block, 1)),
            fixed((1, block)),
        ],
        out_specs=[head(0)] * 3
        + [pl.BlockSpec((1, block, 1), lambda h: (h, 0, 0)), pl.BlockSpec(memory_space=ANY)],
        scratch_shapes=[VMEM((HEADS, block, HD), BF), dma((4, HEADS)), dma((4, HEADS))],
        compiler_params=pltpu.CompilerParams(
            collective_id=9, has_side_effects=True, vmem_limit_bytes=60 * 2**20
        ),
        name="attend_send",
    )(projected, projected, projected, rq, rk, gq, gk, cosine, sine, seg_c, seg_r)


def attend_back_kernel(
    q_ref,
    k_ref,
    v_ref,
    g_ref,
    lse_ref,
    pq,
    pk,
    gq,
    gk,
    cosine,
    sine,
    seg_c,
    seg_r,
    uq_ref,
    uk_ref,
    dv_ref,
    mq_ref,
    mk_ref,
    dk_acc,
    dv_acc,
):
    block = q_ref.shape[0]
    rows = attention_rows(block)
    scale = HD**-0.5
    dk_acc[...] = jnp.zeros_like(dk_acc)
    dv_acc[...] = jnp.zeros_like(dv_acc)

    @pl.when(pl.program_id(0) == 0)
    def _():
        mq_ref[...] = jnp.zeros_like(mq_ref)
        mk_ref[...] = jnp.zeros_like(mk_ref)


    def back(grad, raw, gain):
        turned = turn(grad.astype(BF).astype(F32), cosine_of, -sine_of)
        return turned, jnp.sum(raw * gain[...] * turned, axis=1, keepdims=True)

    for i in range(block // rows):
        length = (i + 1) * rows
        own = slice(i * rows, length)
        scores = mm_t(q_ref[own], k_ref[:length]) * scale
        row = lax.broadcasted_iota(jnp.int32, (rows, length), 0) + i * rows
        column = lax.broadcasted_iota(jnp.int32, (rows, length), 1)
        allowed = (seg_c[own] == seg_r[:, :length]) & (column <= row)
        probs = jnp.where(allowed, jnp.exp(scores - lse_ref[0, own]), 0.0)
        grad_probs = mm_t(g_ref[own], v_ref[:length])
        delta = jnp.sum(probs * grad_probs, axis=1, keepdims=True)
        grad_scores = (probs * (grad_probs - delta)).astype(BF)
        grad_q = mm(grad_scores, k_ref[:length]) * scale
        cosine_of, sine_of = cosine[own], sine[own]
        turned, moment = back(grad_q, pq[own], gq)
        uq_ref[own] = turned
        mq_ref[own] += moment
        dk_acc[:length] += t_mm(grad_scores, q_ref[own])
        dv_acc[:length] += t_mm(probs.astype(BF), g_ref[own])
    cosine_of, sine_of = cosine[...], sine[...]
    turned, moment = back(dk_acc[...] * scale, pk[...], gk)
    uk_ref[...] = turned
    mk_ref[...] += moment
    dv_ref[...] = dv_acc[...].astype(BF)


def attend_back(q, k, v, grad, lse, projected, gq, gk, cosine, sine, seg_c, seg_r):
    block = q.shape[0]
    head = lambda off: pl.BlockSpec((block, HD), lambda h: (0, off + h))
    gain = pl.BlockSpec((1, HD), lambda h: (0, h))
    fixed = lambda shape: pl.BlockSpec(shape, lambda h: (0, 0))
    column = pl.BlockSpec((1, block, 1), lambda h: (h, 0, 0))
    wide = lambda t: jax.ShapeDtypeStruct((block, GROUP_WIDTH), t)
    moment = jax.ShapeDtypeStruct((block, 1), F32)
    return pl.pallas_call(
        attend_back_kernel,
        grid=(HEADS,),
        out_shape=(wide(F32), wide(F32), wide(BF), moment, moment),
        in_specs=[
            head(0),
            head(0),
            head(0),
            head(0),
            column,
            head(0),
            head(HEADS),
            gain,
            gain,
            fixed((block, HD)),
            fixed((block, HD)),
            fixed((block, 1)),
            fixed((1, block)),
        ],
        out_specs=[head(0)] * 3 + [fixed((block, 1))] * 2,
        scratch_shapes=[VMEM((block, HD), F32), VMEM((block, HD), F32)],
        compiler_params=pltpu.CompilerParams(vmem_limit_bytes=60 * 2**20),
        name="attend_back",
    )(q, k, v, grad, lse, projected, projected, gq, gk, cosine, sine, seg_c, seg_r)


WIDE_IN = MODEL_WIDTH + 2 * SPAN
WIDE_OUT = MODEL_WIDTH + SPAN
CHUNK = 16
TERM_PARTS = 4
TERM_ROWS = MODEL_WIDTH // 4 + 2 * SPAN + SPAN + 2 * SPAN


def over_rows(count, body):
    def step(n, carry):
        body(pl.ds(pl.multiple_of(n * CHUNK, CHUNK), CHUNK))
        return carry

    lax.fori_loop(0, count // CHUNK, step, 0)


def wait_for(ref, sem):
    pltpu.make_async_copy(ref, ref, sem).wait()


def experts_kernel(n_c, experts, slots, comm, *refs):
    n_g = 10 if comm else 1
    x_ref, g_refs = refs[0], refs[1 : 1 + n_g]
    refs = refs[1 + n_g :]
    h_gu, h_d, h_id, h_iu, h_od, h_ou = refs[:6]
    refs = refs[6:]
    out_ref, row_ref, terms_o = refs[:3]
    refs = refs[3:]
    if comm:
        xg_ref, final, first_o = refs[:3]
        refs = refs[3:]
    else:
        xg_ref = x_ref
    (wb, db, xw, gw, xl, dr, gu, hl, dh, dgl, res, pick, gate, mom, mask) = refs[:15]
    (to, tr, gid, giu, god, gou, packed, wsem, csem, osem) = refs[15:25]
    refs = refs[25:]
    zh, zl, c, core = here()
    tok = xw.shape[1]
    extra = xw.shape[2] - MODEL_WIDTH
    tiles = n_c
    f = c * 2 + core
    near = lambda i: (
        lax.rem(c // 2 + i // 2, 2) * 2 + lax.rem(lax.rem(c, 2) + lax.rem(i, 2), 2)
    )

    def pair(ref, p):
        return ref.at[pl.ds(p * 2, 2)]

    def load_in(expert):
        yield pltpu.make_async_copy(h_id.at[expert], wb.at[:MODEL_WIDTH, MODEL_WIDTH:], wsem.at[0])
        yield pltpu.make_async_copy(h_gu.at[expert], wb.at[:MODEL_WIDTH, :MODEL_WIDTH], wsem.at[1])
        for j in range(2):
            rows = slice(MODEL_WIDTH + j * SPAN, MODEL_WIDTH + (j + 1) * SPAN)
            columns = slice(j * EXPERT_HIDDEN, (j + 1) * EXPERT_HIDDEN)
            yield pltpu.make_async_copy(h_iu.at[expert, j], wb.at[rows, columns], wsem.at[2 + j])

    def load_out(expert):
        yield pltpu.make_async_copy(h_d.at[expert], db.at[:EXPERT_HIDDEN, :MODEL_WIDTH], wsem.at[4])
        yield pltpu.make_async_copy(h_od.at[expert], db.at[:EXPERT_HIDDEN, MODEL_WIDTH:], wsem.at[5])
        yield pltpu.make_async_copy(h_ou.at[expert], db.at[EXPERT_HIDDEN:, :MODEL_WIDTH], wsem.at[6])

    terms = (gid, giu, god, gou)

    def term_copy(e):
        return pltpu.make_async_copy(packed, terms_o if comm else terms_o.at[:, e], osem.at[0])

    def send_first_terms():
        pltpu.make_async_copy(packed.at[seq], first_o.at[seq], osem.at[0]).start()
        for q in range(TERM_PARTS):

            @pl.when(seq != q)
            def _():
                remote(packed.at[q], first_o.at[seq], tsend.at[q], trecv.at[seq], (q // 2, q % 2, c, core)).start()

    def wait_first_terms(sent):
        for q in range(TERM_PARTS):

            @pl.when(seq != q)
            def _():
                if sent:
                    wait_for(packed.at[q], tsend.at[q])
                else:
                    wait_for(first_o.at[q], trecv.at[q])

        if sent:
            wait_for(packed.at[0], osem.at[0])

    def pack_terms():
        for q in range(TERM_PARTS):
            rows, columns = MODEL_WIDTH // 4, EXPERT_HIDDEN // 4
            packed[q, :rows] = gid[q * rows : (q + 1) * rows].astype(BF)
            for j in range(2):
                at = rows + j * SPAN
                packed[q, at : at + SPAN] = giu[j, :, q * columns : (q + 1) * columns].astype(BF)
            at = rows + 2 * SPAN
            for j in range(2):
                half = slice(j * SPAN, (j + 1) * SPAN)
                row = q * columns + j * SPAN
                packed[q, at : at + SPAN, half] = god[row : row + SPAN].astype(BF)
                column = q * rows + j * 256
                low = at + (j + 1) * SPAN
                packed[q, low : low + SPAN] = gou[:, column : column + 256].astype(BF)

    if comm:
        sib, la, lb, fx, fy, sums, sendx, recvx, sends, recvs, tsend, trecv = refs
        seq = zh * 2 + zl
        same = lambda i: (zh, zl, near(i), core)
        sibling = (zh, zl, c, 1 - core)
        low_half, high_half = pl.ds(0, tok // 2), pl.ds(tok // 2, tok // 2)
        column = [(zh ^ 1, zl, c, core), (zh, zl ^ 1, c, core), (zh ^ 1, zl ^ 1, c, core)]
        signal_all([sibling, same(1), same(2), *column])
        first = [
            remote(x_ref, xg_ref.at[f], sendx.at[n], recvx.at[n], to_)
            for n, to_ in enumerate((sibling, same(1), same(2)))
        ]
        for copy in first:
            copy.start()
        fx1, fy1, fd1 = near(1) * 2 + core, near(2) * 2 + core, near(3) * 2 + core
        forward = [
            remote(xg_ref.at[fx1, low_half], xg_ref.at[fx1, low_half], sendx.at[3], recvx.at[3], same(2)),
            remote(xg_ref.at[fy1, high_half], xg_ref.at[fy1, high_half], sendx.at[4], recvx.at[4], same(1)),
            remote(xg_ref.at[fx1], xg_ref.at[fx1], sendx.at[5], recvx.at[5], sibling),
            remote(xg_ref.at[fy1], xg_ref.at[fy1], sendx.at[6], recvx.at[6], sibling),
        ]
        across = remote(xg_ref.at[fd1], xg_ref.at[fd1], sendx.at[7], recvx.at[7], sibling)

    for copy in (*load_in(0), *load_out(0)):
        copy.start()
    spare = EXPERT_HIDDEN
    wb[MODEL_WIDTH : MODEL_WIDTH + SPAN, spare:] = jnp.zeros((SPAN, WIDE_IN - spare), BF)
    wb[MODEL_WIDTH + SPAN :, :spare] = jnp.zeros((SPAN, spare), BF)
    for ref in terms:
        ref[...] = jnp.zeros_like(ref)

    def order(s):
        e = s // tiles
        i = s + e * (2 * tiles - 1 - 2 * s)
        return e, i, (near(i) if comm else i)

    def fetch_x(p):
        return pltpu.make_async_copy(pair(xg_ref, p), xw, csem.at[0])

    def fetch_own():
        other = xg_ref.at[c * 2 + 1 - core]
        pltpu.make_async_copy(x_ref, xw.at[core], csem.at[0]).start()
        pltpu.make_async_copy(other, xw.at[1 - core], csem.at[0]).start()

    def fetch_g(i):
        if not comm:
            pltpu.make_async_copy(pair(g_refs[0], i), gw, csem.at[1]).start()
            return
        for n in range(4):

            @pl.when(i == n)
            def _():
                for k, held in ((core, g_refs[:5]), (1 - core, g_refs[5:])):
                    if n < 3:
                        pltpu.make_async_copy(held[n], gw.at[k], csem.at[1]).start()
                    else:
                        pltpu.make_async_copy(held[3], gw.at[k, low_half], csem.at[1]).start()
                        pltpu.make_async_copy(held[4], gw.at[k, high_half], csem.at[1]).start()

    if comm:
        fetch_g(0)
        wait_for(xg_ref.at[c * 2 + 1 - core], recvx.at[0])
        fetch_own()
    else:
        fetch_g(0)
        fetch_x(0).start()

    def write_out(p):
        return pltpu.make_async_copy(to, pair(out_ref, p), csem.at[2])

    def write_row(p):
        return pltpu.make_async_copy(tr, pair(row_ref, p), csem.at[3])

    def read_out(p):
        return pltpu.make_async_copy(pair(out_ref, p), to, csem.at[4])

    def read_row(p):
        return pltpu.make_async_copy(pair(row_ref, p), tr, csem.at[5])

    both = 2 * slots
    steps = 2 * tiles
    part = lambda d: slice(d * slots, (d + 1) * slots)
    pieces = [
        (
            slice(r, r + CHUNK),
            slice(h * 512, (h + 1) * 512),
            slice(EXPERT_HIDDEN + h * 512, EXPERT_HIDDEN + (h + 1) * 512),
        )
        for r in range(0, both, CHUNK)
        for h in range(2)
    ]

    def step(s, carry):
        e, i, p = order(s)
        _, after_i, after = order(jnp.minimum(s + 1, steps - 1))
        number = c * (2 * EXP_DEV) + core * EXP_DEV + e
        fetch_x(p).wait()
        wait_for(gw, csem.at[1])
        lane = lax.broadcasted_iota(jnp.int32, (tok, extra), 1)
        lane_s = lax.broadcasted_iota(jnp.int32, (slots, extra), 1)
        for d in range(2):
            side = xw[d, :, MODEL_WIDTH:].astype(F32)
            place = jnp.sum(jnp.where(lane == number, side, 0.0), axis=1, keepdims=True)
            slot = lax.broadcasted_iota(jnp.int32, (tok, slots), 1).astype(F32)
            pick[d] = jnp.where(slot == place, 1.0, 0.0).astype(BF)
            sub = lax.broadcasted_iota(jnp.int32, (extra, tok), 0)
            place_t = jnp.sum(jnp.where(sub == number, side.T, 0.0), axis=0, keepdims=True)
            slot_t = lax.broadcasted_iota(jnp.int32, (slots, tok), 0).astype(F32)
            pickt = jnp.where(slot_t == place_t, 1.0, 0.0).astype(BF)
            xl[part(d), :MODEL_WIDTH] = mm(pickt, xw[d, :, :MODEL_WIDTH]).astype(BF)
            dr[part(d), :MODEL_WIDTH] = mm(pickt, gw[d]).astype(BF)
            side = mm(pickt, xw[d, :, MODEL_WIDTH:])
            read = lambda which: jnp.sum(jnp.where(which, side, 0.0), axis=1, keepdims=True)
            gate[part(d)] = read((lane_s == experts + number) | (lane_s == 2 * experts + number))
            columns = lax.broadcasted_iota(jnp.int32, (slots, SPAN), 1) // ADAPTER_RANK
            mask[part(d)] = jnp.where(columns.astype(F32) == read(lane_s == 3 * experts), 1.0, 0.0)

        @pl.when((s > 0) & (s <= tiles) if comm else s > 0)
        def _():
            write_row(p).wait()

        @pl.when(s > 0)
        def _():
            write_out(p).wait()

        @pl.when(e > 0)
        def _():
            read_out(p).start()
            read_row(p).start()

        @pl.when(s == 0)
        def _():
            for copy in (*load_in(0), *load_out(0)):
                copy.wait()

        @pl.when(s == tiles)
        def _():
            for copy in (*load_in(1), *load_out(1), *(() if comm else (term_copy(0),))):
                copy.wait()
            for ref in terms:
                ref[...] = jnp.zeros_like(ref)

        mask2 = lambda: jnp.concatenate([mask[...], mask[...]], axis=1)
        xl[:, MODEL_WIDTH:] = (mm(xl[:, :MODEL_WIDTH], wb[:MODEL_WIDTH, MODEL_WIDTH:]) * mask2()).astype(BF)
        gu[...] = mm(xl[...], wb[:, :MODEL_WIDTH])

        for rows, a, b in pieces:
            gate_part = gu[rows, a]
            hl[rows, a] = (gate_part / (1.0 + jnp.exp(-gate_part)) * gu[rows, b]).astype(BF)
        hl[:, EXPERT_HIDDEN:] = (
            mm(hl[:, :EXPERT_HIDDEN], db[:EXPERT_HIDDEN, MODEL_WIDTH:]) * mask[...]
        ).astype(BF)
        for n in range(4):
            a = slice(n * 512, (n + 1) * 512)
            res[:, a] = (mm(hl[...], db[:, a]) * gate[...]).astype(BF)

        @pl.when(e > 0)
        def _():
            read_out(p).wait()

        def add_picked(target, d):
            for n in range(4):
                a = slice(n * 512, (n + 1) * 512)
                before = jnp.where(e > 0, target[d, :, a].astype(F32), 0.0)
                target[d, :, a] = (before + mm(pick[d], res[part(d), a])).astype(BF)

        for d in range(2):
            add_picked(to, d)
        write_out(p).start()

        @pl.when(s < steps - 1)
        def _():
            fetch_g(after_i)

        dr[:, MODEL_WIDTH:] = (
            mm_t(dr[:, :MODEL_WIDTH], db[EXPERT_HIDDEN:, :MODEL_WIDTH]) * mask[...]
        ).astype(BF)
        dh[...] = mm_t(dr[...], db[:EXPERT_HIDDEN, :])

        @pl.when(s == tiles - 1)
        def _():
            for copy in load_out(1):
                copy.start()

        mom[...] = jnp.zeros_like(mom)
        for rows, a, b in pieces:
            gate_part, up_part, grad = gu[rows, a], gu[rows, b], dh[rows, a]
            sigmoid = 1.0 / (1.0 + jnp.exp(-gate_part))
            activated = gate_part * sigmoid
            plain = grad * activated
            mom[rows] += jnp.sum(plain * up_part, axis=1, keepdims=True)
            dgl[rows, b] = (plain * gate[rows]).astype(BF)
            slope = sigmoid + activated - activated * sigmoid
            dgl[rows, a] = (grad * gate[rows] * up_part * slope).astype(BF)
        dgl[:, MODEL_WIDTH:] = (
            mm_t(dgl[:, :MODEL_WIDTH], wb[MODEL_WIDTH:, :MODEL_WIDTH]) * mask2()
        ).astype(BF)
        for n in range(4):
            a = slice(n * 512, (n + 1) * 512)
            res[:, a] = mm_t(dgl[...], wb[a, :]).astype(BF)

        @pl.when(s == tiles - 1)
        def _():
            for copy in load_in(1):
                copy.start()

        if comm:
            @pl.when(s == 0)
            def _():
                wait_for(xg_ref.at[fx1], recvx.at[1])
                forward[0].start()
                forward[2].start()
                wait_for(xg_ref.at[fy1], recvx.at[2])
                forward[1].start()
                forward[3].start()
                wait_for(xg_ref.at[fx1], recvx.at[5])

            @pl.when(s == 1)
            def _():
                wait_for(xg_ref.at[fd1, low_half], recvx.at[3])
                wait_for(xg_ref.at[fd1, high_half], recvx.at[4])
                across.start()
                wait_for(xg_ref.at[fy1], recvx.at[6])

            @pl.when(s == 2)
            def _():
                wait_for(xg_ref.at[fd1], recvx.at[7])

        @pl.when(s < steps - (2 if comm else 1))
        def _():
            fetch_x(after).start()

        if comm:

            @pl.when(s == steps - 2)
            def _():
                fetch_own()

        @pl.when(e > 0)
        def _():
            read_row(p).wait()

        for d in range(2):
            add_picked(tr, d)
            moment = mom[part(d)]
            high = moment.astype(BF).astype(F32)
            side = jnp.where(lane_s == number, high, 0.0) + jnp.where(
                lane_s == experts + number, moment - high, 0.0
            )
            before = jnp.where(e > 0, tr[d, :, MODEL_WIDTH:].astype(F32), 0.0)
            tr[d, :, MODEL_WIDTH:] = (before + mm(pick[d], side.astype(BF))).astype(BF)

        if comm:
            to_sibling = remote(
                tr.at[1 - core], sib.at[lax.rem(i, 2)], sends.at[lax.rem(i, 2)],
                recvs.at[lax.rem(i, 2)], sibling,
            )

            @pl.when(e == 0)
            def _():
                write_row(p).start()

            @pl.when(e > 0)
            def _():
                to_sibling.start()
        else:
            write_row(p).start()

        gid[...] += t_mm(xl[:, :MODEL_WIDTH], dgl[:, MODEL_WIDTH:])
        for j in range(2):
            giu[j] += t_mm(
                xl[:, MODEL_WIDTH + j * SPAN : MODEL_WIDTH + (j + 1) * SPAN],
                dgl[:, j * EXPERT_HIDDEN : (j + 1) * EXPERT_HIDDEN],
            )
        god[...] += t_mm(hl[:, :EXPERT_HIDDEN], (dr[:, MODEL_WIDTH:].astype(F32) * gate[...]).astype(BF))
        gou[...] += t_mm((hl[:, EXPERT_HIDDEN:].astype(F32) * gate[...]).astype(BF), dr[:, :MODEL_WIDTH])

        @pl.when(s == tiles - 1)
        def _():
            pack_terms()
            if comm:
                send_first_terms()
            else:
                term_copy(0).start()

        if comm:
            half = tok // 2

            def chip_sum(at, rows):
                return tr[core, rows].astype(F32) + sib[at, rows].astype(F32)

            @pl.when(e > 0)
            def _():
                to_sibling.wait()

            @pl.when(s == steps - 4)
            def _():
                def body(rows):
                    sums[0, rows] = chip_sum(1, rows).astype(BF)

                over_rows(tok, body)
                remote(sums.at[0, low_half], la, sends.at[2], recvs.at[2], same(1)).start()
                remote(sums.at[0, high_half], lb, sends.at[3], recvs.at[3], same(2)).start()

            @pl.when(s == steps - 3)
            def _():
                wait_for(la, recvs.at[2])

                def body(rows):
                    sums[1, rows] = (chip_sum(0, rows) + la[rows].astype(F32)).astype(BF)

                def rest(rows):
                    rows = pl.ds(pl.multiple_of(rows.start + half, CHUNK), CHUNK)
                    sums[1, rows] = chip_sum(0, rows).astype(BF)

                over_rows(half, body)
                over_rows(half, rest)
                remote(sums.at[1], fy, sends.at[4], recvs.at[4], same(2)).start()

            @pl.when(s == steps - 2)
            def _():
                wait_for(lb, recvs.at[3])

                def body(rows):
                    sums[2, rows] = chip_sum(1, rows).astype(BF)

                def rest(rows):
                    upper = pl.ds(pl.multiple_of(rows.start + half, CHUNK), CHUNK)
                    sums[2, upper] = (chip_sum(1, upper) + lb[rows].astype(F32)).astype(BF)

                over_rows(half, body)
                over_rows(half, rest)
                remote(sums.at[2], fx, sends.at[5], recvs.at[5], same(1)).start()

        return carry

    lax.fori_loop(0, steps, step, 0)
    if comm:
        wait_first_terms(True)
    pack_terms()
    term_copy(1).start()
    _, _, last = order(steps - 1)
    write_out(last).wait()
    if comm:
        wait_for(fx, recvs.at[5])
        wait_for(fy, recvs.at[4])

        def body(rows):
            total = tr[core, rows].astype(F32) + sib[0, rows].astype(F32)
            final[rows] = (total + (fx[rows].astype(F32) + fy[rows].astype(F32))).astype(BF)

        over_rows(tok, body)
        wait_for(la, sends.at[2])
        wait_for(lb, sends.at[3])
        wait_for(fy, sends.at[4])
        wait_for(fx, sends.at[5])
        for copy in first:
            copy.wait_send()
        for copy in forward:
            copy.wait_send()
        across.wait_send()
        wait_first_terms(False)
    else:
        write_row(last).wait()
    term_copy(1).wait()


def run_experts(x, g, weights, experts, slots, n_c, comm):
    tok, wide = x.shape[-2:]
    sources = 2 * n_c
    both = 2 * slots
    dma = pltpu.SemaphoreType.DMA
    term_shapes = (
        (MODEL_WIDTH, 2 * SPAN),
        (2, SPAN, EXPERT_HIDDEN),
        (EXPERT_HIDDEN, SPAN),
        (SPAN, MODEL_WIDTH),
    )
    any_spec = pl.BlockSpec(memory_space=ANY)
    out_shape = [
        jax.ShapeDtypeStruct((sources, tok, MODEL_WIDTH), BF),
        jax.ShapeDtypeStruct((sources, tok, wide), BF),
        jax.ShapeDtypeStruct(
            (TERM_PARTS, TERM_ROWS, 256) if comm else (TERM_PARTS, EXP_DEV, TERM_ROWS, 256), BF
        ),
    ]
    out_specs = [any_spec] * 3
    scratch = [
        VMEM((WIDE_IN, WIDE_IN), BF),
        VMEM((EXPERT_HIDDEN + SPAN, WIDE_OUT), BF),
        VMEM((2, tok, wide), BF),
        VMEM((2, tok, MODEL_WIDTH), BF),
        VMEM((both, WIDE_IN), BF),
        VMEM((both, WIDE_OUT), BF),
        VMEM((both, MODEL_WIDTH), F32),
        VMEM((both, EXPERT_HIDDEN + SPAN), BF),
        VMEM((both, EXPERT_HIDDEN), F32),
        VMEM((both, WIDE_IN), BF),
        VMEM((both, MODEL_WIDTH), BF),
        VMEM((2, tok, slots), BF),
        VMEM((both, 1), F32),
        VMEM((both, 1), F32),
        VMEM((both, SPAN), F32),
        VMEM((2, tok, MODEL_WIDTH), BF),
        VMEM((2, tok, wide), BF),
        *(VMEM(s, F32) for s in term_shapes),
        VMEM((TERM_PARTS, TERM_ROWS, 256), BF),
        dma((7,)),
        dma((6,)),
        dma((1,)),
    ]
    params = {}
    if comm:
        out_shape += [
            jax.ShapeDtypeStruct((sources, tok, wide), BF),
            jax.ShapeDtypeStruct((tok, wide), BF),
            jax.ShapeDtypeStruct((TERM_PARTS, TERM_ROWS, 256), BF),
        ]
        out_specs += [any_spec, pl.BlockSpec(memory_space=VMEM), any_spec]
        scratch += [
            VMEM((2, tok, wide), BF),
            VMEM((tok // 2, wide), BF),
            VMEM((tok // 2, wide), BF),
            VMEM((tok, wide), BF),
            VMEM((tok, wide), BF),
            VMEM((3, tok, wide), BF),
            dma((8,)),
            dma((8,)),
            dma((6,)),
            dma((6,)),
            dma((TERM_PARTS,)),
            dma((TERM_PARTS,)),
        ]
        params = dict(collective_id=6, has_side_effects=True)
    flops = 2 * sources * EXP_DEV * slots * MODEL_WIDTH * EXPERT_HIDDEN * 8
    g = g if comm else [g]
    results = pl.pallas_call(
        functools.partial(experts_kernel, n_c, experts, slots, comm),
        out_shape=out_shape,
        in_specs=[any_spec] * (7 + len(g)),
        out_specs=out_specs,
        scratch_shapes=scratch,
        compiler_params=pltpu.CompilerParams(vmem_limit_bytes=63 * 2**20, **params),
        cost_estimate=pl.CostEstimate(flops=flops, bytes_accessed=10**8, transcendentals=10**7),
        name="experts",
    )(x, *g, *weights)
    if comm:
        return results[0], results[4], (results[5], results[2])
    return results[0], results[1], results[2]


def late_kernel(n_f, dp, up, mask, low, x, both, packed):
    core = lax.axis_index("core")
    down_rows = MODEL_WIDTH // (4 * n_f)
    up_rows = SPAN // n_f
    base = 12 * down_rows
    packed[:, base:] = jnp.zeros((n_f, 24 * up_rows, SPAN), BF)
    for j in range(3):
        own = slice(j * SPAN, (j + 1) * SPAN)
        wide = slice(j * GROUP_WIDTH, (j + 1) * GROUP_WIDTH)
        lowered = (mm_t(dp[:, wide], up[own]) * mask[...]).astype(BF)
        both[:, wide] = dp[:, wide]
        both[:, 3 * GROUP_WIDTH + j * SPAN : 3 * GROUP_WIDTH + (j + 1) * SPAN] = lowered
        grad_up = t_mm(low[:, own], dp[:, wide]).astype(BF)
        grad_down = t_mm(x[...], lowered).astype(BF)
        for f in range(n_f):
            for b in range(4):
                at = base + (j * 8 + core * 4 + b) * up_rows
                packed[f, pl.ds(pl.multiple_of(at, up_rows), up_rows)] = grad_up[
                    f * up_rows : (f + 1) * up_rows, b * SPAN : (b + 1) * SPAN
                ]
            for q in range(4):
                row = (q * n_f + f) * down_rows
                at = (q * 3 + j) * down_rows
                packed[f, at : at + down_rows] = grad_down[row : row + down_rows]


def late_gradients(grad_projected, up_own, mask, lowered, x, n_f):
    block = x.shape[0]
    rows = 12 * MODEL_WIDTH // (4 * n_f) + 24 * SPAN // n_f
    return pl.pallas_call(
        functools.partial(late_kernel, n_f),
        out_shape=(
            jax.ShapeDtypeStruct((block, PROJECT_WIDTH), BF),
            jax.ShapeDtypeStruct((n_f, rows, SPAN), BF),
        ),
        in_specs=[pl.BlockSpec(memory_space=VMEM)] * 5,
        out_specs=[pl.BlockSpec(memory_space=VMEM)] * 2,
        compiler_params=pltpu.CompilerParams(vmem_limit_bytes=50 * 2**20),
        cost_estimate=pl.CostEstimate(flops=4 * 10**9, bytes_accessed=2 * 10**7, transcendentals=0),
        name="late_gradients",
    )(grad_projected, up_own, mask, lowered, x)


def plane_rows(rows):
    half = rows.shape[0] // 2
    along_x = lambda t: lax.ppermute(t, "c", [(0, 1), (1, 0), (2, 3), (3, 2)])
    along_y = lambda t: lax.ppermute(t, "c", [(0, 2), (2, 0), (1, 3), (3, 1)])
    to_sibling = lambda t: lax.ppermute(t, "core", [(0, 1), (1, 0)])
    beside, above = along_x(rows), along_y(rows)
    parts = [rows, beside, above, along_y(beside[:half]), along_x(above[half:])]
    return parts + [to_sibling(t) for t in parts]


def on_device(
    tokens,
    cotangent,
    lengths,
    sets,
    routes,
    gain_attn,
    gain_query,
    gain_key,
    gain_mlp,
    query_key_value_weight,
    out_weight,
    router_weight,
    gate_up_weight,
    down_weight,
    attention_down_factors,
    attention_up_factors,
    router_down_factors,
    router_up_factors,
    expert_input_down,
    expert_input_up,
    expert_output_down,
    expert_output_up,
):
    zh, zl, c, core = here()
    n_c = lax.axis_size("c")
    n_fsdp = 2 * n_c
    n_seq = lax.axis_size("zh") * lax.axis_size("zl")
    tok = tokens.shape[1]
    block = tok * n_seq
    experts = EXP_DEV * n_fsdp
    capacity = 5 * tok * TOP // (4 * experts)
    slots = -(-capacity // 16) * 16
    extra = -(-(3 * experts + 1) // 128) * 128
    span3 = 3 * SPAN
    group = zl * 2 + core
    shard = zh * 2 + zl

    both_lengths = lax.all_gather(
        jnp.concatenate([lengths[0], sets[0]]), "core", axis=0, tiled=False
    )
    held_lengths = lax.dynamic_index_in_dim(both_lengths, zh, 0, keepdims=False)
    count = lengths.shape[1]

    inputs = tokens[0].astype(F32)
    normalized = rms_scale(inputs, gain_attn).astype(BF)
    seq_block, block_offsets, block_sets = token_meta(
        held_lengths[:count], held_lengths[count:], jnp.arange(block, dtype=jnp.int32)
    )
    mask1 = set_mask(block_sets)
    if n_c == 4:
        x_shards, head_rows, up_group, projected, lowered = gather_project(
            normalized,
            query_key_value_weight,
            attention_down_factors[:, :span3],
            attention_up_factors,
            mask1.reshape(4, tok, SPAN),
        )
        projected, lowered = projected.reshape(block, -1), lowered.reshape(block, span3)
        up_own = up_group[:span3]
    else:
        x_shards, qkv_rows = gather_to_heads(normalized, query_key_value_weight, n_c)

    first_column = span3 if n_c == 4 else 0
    rows_local = query_key_value_weight.shape[0]
    factors = jnp.concatenate(
        [
            attention_down_factors[:, first_column:],
            attention_up_factors.reshape(rows_local, -1),
            router_down_factors,
            router_weight,
            router_up_factors.reshape(rows_local, -1),
        ],
        axis=1,
    )
    factor_width = factors.shape[1]
    factors = jnp.pad(factors, ((0, 0), (0, -factor_width % 128)))
    factors = lax.all_gather(factors, FSDP, axis=0, tiled=True)
    up_columns = attention_up_factors.size // rows_local
    at = 4 * SPAN - first_column
    down_full = factors[:, :at]
    down_o = down_full[:, span3 - first_column :]
    up_full = factors[:, at : at + up_columns].reshape(4 * SPAN, MODEL_WIDTH)
    at += up_columns
    rdown_full = factors[:, at : at + SPAN]
    at += SPAN
    router_full = factors[:, at : at + experts]
    at += experts
    rup_full = factors[:, at:factor_width].reshape(SPAN, experts)
    if n_c == 4:
        projected, out_weight, rows = lax.optimization_barrier(
            (projected, out_weight, cotangent[0])
        )
        grads_all = plane_rows(rows)
    else:
        grads_all = lax.all_gather(cotangent[0], FSDP, axis=0, tiled=False)
    out_full = lax.all_gather(out_weight, FSDP, axis=0, tiled=True)

    seq_local, _, chosen = token_meta(
        lengths[0], sets[0], shard * tok + jnp.arange(tok, dtype=jnp.int32)
    )
    mask = set_mask(chosen)
    half = HD // 2
    freqs = THETA ** (-(jnp.arange(half, dtype=F32) * 2.0 / HD))
    angles = block_offsets.astype(F32)[:, None] * freqs[None, :]
    cosine, sine = jnp.cos(angles), jnp.sin(angles)
    cosine = jnp.concatenate([cosine, cosine], axis=1)
    sine = jnp.concatenate([-sine, sine], axis=1)
    seg_c, seg_r = seq_block[:, None], seq_block[None, :]

    x_all = x_shards.reshape(block, MODEL_WIDTH)
    if n_c != 4:
        mask3 = jnp.tile(mask1, (1, 3))
        down3 = down_full[:, :span3]
        lowered = (mm(x_all, down3) * mask3).astype(BF)
        up_own = lax.dynamic_slice_in_dim(up_full[:span3], group * GROUP_WIDTH, GROUP_WIDTH, 1)
        none = jnp.zeros((SPAN, GROUP_WIDTH), BF)
        up_diagonal = jnp.concatenate(
            [
                jnp.concatenate(
                    [up_own[j * SPAN : (j + 1) * SPAN] if i == j else none for i in range(3)], axis=1
                )
                for j in range(3)
            ],
            axis=0,
        )
        projected = mm(x_all, qkv_rows) + mm(lowered, up_diagonal)
    part_q, part_k = projected[:, :GROUP_WIDTH], projected[:, GROUP_WIDTH : 2 * GROUP_WIDTH]

    def over_group(first, second, identity):
        both = jnp.stack([first, second]).reshape(-1, 128)
        return group_sum(both, identity).reshape(2, block)

    squares = over_group(jnp.sum(part_q * part_q, axis=1), jnp.sum(part_k * part_k, axis=1), 4)
    inverse = lax.rsqrt(squares / MODEL_WIDTH + EPSILON)
    rq, rk = inverse[0][:, None], inverse[1][:, None]
    gains = [
        lax.dynamic_slice_in_dim(g, group * GROUP_WIDTH, GROUP_WIDTH)[None, :]
        for g in (gain_query, gain_key)
    ]
    if n_c == 4:
        q, k, v, lse, attended = attend_send(
            projected, rq, rk, *gains, cosine, sine, seg_c, seg_r
        )
    else:
        q, k, v, attended_heads, lse = attend(
            projected, rq, rk, *gains, cosine, sine, seg_c, seg_r
        )
        attended = to_tokens(attended_heads.reshape(4, tok, GROUP_WIDTH))

    up_o = up_full[span3:]
    out_lower = (mm(attended, down_o) * mask).astype(BF)
    branch = mm(attended, out_full) + mm(out_lower, up_o)
    middle = inputs + branch
    normed2 = rms_scale(middle, gain_mlp).astype(BF)
    router_lower = (mm(normed2, rdown_full) * mask).astype(BF)
    logits = mm(normed2, router_full) + mm(router_lower, rup_full)
    probs = jax.nn.softmax(logits, axis=-1)
    hits = jnp.sum(
        (routes[0][:, :, None] == jnp.arange(experts, dtype=jnp.int32)[None, None, :]).astype(F32),
        axis=1,
    )
    place = jnp.arange(tok, dtype=jnp.int32)
    before = (place[None, :] < place[:, None]).astype(BF)
    ranks = jnp.where(hits > 0, mm(before, hits.astype(BF)), -1.0).astype(BF)
    gates = hits * probs
    gates_high = gates.astype(BF)
    gates_low = (gates - gates_high.astype(F32)).astype(BF)
    side = jnp.concatenate(
        [ranks, gates_high, gates_low, chosen.astype(BF)[:, None]], axis=1
    )
    payload = jnp.concatenate(
        [normed2, jnp.pad(side, ((0, 0), (0, extra - side.shape[1])))], axis=1
    )
    weights = (
        gate_up_weight,
        down_weight,
        expert_input_down,
        expert_input_up,
        expert_output_down,
        expert_output_up,
    )
    if n_c == 4:
        out_parts, returned, expert_terms = run_experts(
            payload, grads_all, weights, experts, slots, n_c, True
        )
    else:
        rows_all = lax.all_gather(payload, FSDP, axis=0, tiled=True)
        out_parts, row_parts, expert_terms = run_experts(
            rows_all.reshape(n_fsdp, tok, -1), grads_all, weights, experts, slots, n_c, False
        )
        returned = lax.psum_scatter(
            row_parts.reshape(n_fsdp * tok, -1), FSDP, scatter_dimension=0, tiled=True
        )
    mixed = lax.psum_scatter(
        out_parts.reshape(n_fsdp * tok, -1), FSDP, scatter_dimension=0, tiled=True
    )
    grad_out = cotangent[0].astype(F32)
    returned = returned.astype(F32)
    back = returned[:, MODEL_WIDTH:]
    grad_probs = back[:, :experts] + back[:, experts : 2 * experts]
    grad_logits = probs * (grad_probs - jnp.sum(probs * grad_probs, axis=-1, keepdims=True))
    grad_router_lower = exact("te,re->tr", grad_logits, rup_full.astype(F32)) * mask
    grad_normed2 = (
        returned[:, :MODEL_WIDTH]
        + mm_t(grad_logits.astype(BF), router_full)
        + mm_t(grad_router_lower.astype(BF), rdown_full)
    )
    grad_rup = t_mm(router_lower, grad_logits.astype(BF))
    grad_rdown = t_mm(normed2, grad_router_lower.astype(BF))
    grad_middle = grad_out + rms_back(middle, gain_mlp, grad_normed2)
    grad_branch = grad_middle.astype(BF)
    grad_out_lower = (mm_t(grad_branch, up_o) * mask).astype(BF)
    grad_attended = (mm_t(grad_branch, out_full) + mm_t(grad_out_lower, down_o)).astype(BF)
    head_grad = to_heads(grad_attended).reshape(block, GROUP_WIDTH)
    if n_c == 4:
        first_terms, second_terms = expert_terms
        second_terms, head_grad = lax.optimization_barrier((second_terms, head_grad))
        second_terms = lax.all_to_all(second_terms, SEQ, split_axis=0, concat_axis=0, tiled=True)
    else:
        expert_terms = lax.psum_scatter(expert_terms, SEQ, scatter_dimension=0, tiled=True)
    grad_up_o = t_mm(out_lower, grad_branch)
    grad_down_o = t_mm(attended, grad_out_lower)
    if n_c == 4:
        up_rows = SPAN // n_fsdp
        up_blocks = grad_up_o.astype(BF).reshape(n_fsdp, up_rows, 16, SPAN).transpose(0, 2, 1, 3)
        by_owner = lambda t: t.astype(BF).reshape(n_seq, n_fsdp, -1, SPAN).transpose(1, 0, 2, 3)
        rup_rows = jnp.pad(grad_rup.reshape(n_seq * n_fsdp, 1, -1), ((0, 0), (0, 15), (0, 0)))
        rup_rows = jnp.pad(rup_rows, ((0, 0), (0, 0), (0, SPAN - rup_rows.shape[2])))
        rest = jnp.concatenate(
            [by_owner(grad_down_o), by_owner(grad_rdown), by_owner(rup_rows)], axis=2
        )
        early = jnp.concatenate(
            [up_blocks.reshape(n_fsdp, -1, SPAN), rest.reshape(n_fsdp, -1, SPAN)], axis=1
        )

    uq, uk, grad_v, mq, mk = attend_back(
        q, k, v, head_grad, lse, projected, *gains, cosine, sine, seg_c, seg_r
    )
    moments = over_group(mq[:, 0], mk[:, 0], 5) / MODEL_WIDTH

    def rms_inner(values, scale, gain, turned, moment):
        return (scale * gain * turned - values * (scale * scale * scale) * moment).astype(BF)

    grad_projected = jnp.concatenate(
        [
            rms_inner(part_q, rq, gains[0], uq, moments[0][:, None]),
            rms_inner(part_k, rk, gains[1], uk, moments[1][:, None]),
            grad_v,
        ],
        axis=1,
    )
    if n_c == 4:
        both, late = late_gradients(
            grad_projected, up_own, mask1, lowered, x_all, n_fsdp
        )
    else:
        grad_lowered = (mm_t(grad_projected, up_diagonal) * mask3).astype(BF)
    if n_c == 4:
        output, grad_inputs, *summed = finish(
            both,
            head_rows,
            late,
            early,
            middle,
            mixed,
            tokens[0],
            grad_middle,
            gain_attn[None, :],
            n_c,
        )
    else:
        grad_normed_part = (
            mm_t(grad_projected, qkv_rows) + mm_t(grad_lowered, down3)
        ).astype(BF)
        grad_normed = sum_to_tokens(grad_normed_part.reshape(4, tok, MODEL_WIDTH))
        grad_inputs = grad_middle + rms_back(inputs, gain_attn, grad_normed)
        output = (middle + mixed.astype(F32)).astype(BF)

    rup_shape = (SPAN // (n_seq * n_fsdp), experts)
    if n_c == 4:
        summed[3] = summed[3][0, : rup_shape[0] * rup_shape[1]].reshape(rup_shape)
    else:
        grad_up_own = [
            t_mm(
                lowered[:, j * SPAN : (j + 1) * SPAN],
                grad_projected[:, j * GROUP_WIDTH : (j + 1) * GROUP_WIDTH],
            )
            for j in range(3)
        ]
        grad_down_qkv = t_mm(x_all, grad_lowered)
        grad_down_all = jnp.concatenate([grad_down_qkv, grad_down_o], axis=1).astype(BF)
        wide_up = lax.dynamic_update_slice_in_dim(
            jnp.zeros((span3, MODEL_WIDTH), F32),
            jnp.concatenate(grad_up_own, axis=0),
            group * GROUP_WIDTH,
            1,
        )
        grad_up_all = jnp.concatenate([wide_up, grad_up_o], axis=0).astype(BF)
        terms = (grad_down_all, grad_up_all, grad_rdown.astype(BF), grad_rup.astype(BF))
        own_shapes = [(t.shape[0] // (n_seq * n_fsdp), t.shape[1]) for t in terms]
        flat = jnp.concatenate(
            [t.reshape(n_seq, n_fsdp, -1).transpose(1, 0, 2) for t in terms], axis=2
        )
        used = flat.shape[2]
        flat = jnp.pad(flat, ((0, 0), (0, 0), (0, -used % 1024))).reshape(n_fsdp * n_seq, -1, 128)
        flat = lax.psum_scatter(flat, FSDP, scatter_dimension=0, tiled=True)
        flat = lax.psum_scatter(flat, SEQ, scatter_dimension=0, tiled=True)
        flat = flat.astype(F32).reshape(-1)
        summed, at = [], 0
        for shape in own_shapes:
            size = shape[0] * shape[1]
            summed.append(flat[at : at + size].reshape(shape))
            at += size

    if n_c == 4:
        expert_terms = jnp.stack(
            [jnp.sum(t.astype(F32), axis=0) for t in (first_terms, second_terms)]
        )
    else:
        expert_terms = expert_terms[0].astype(F32)
    rows = MODEL_WIDTH // 4
    at = rows + 2 * SPAN
    halves = expert_terms[:, at : at + SPAN]
    low = at + SPAN
    expert_sums = [
        expert_terms[:, :rows],
        expert_terms[:, rows:at].reshape(EXP_DEV, 2, SPAN, EXPERT_HIDDEN // 4),
        jnp.concatenate([halves[..., :SPAN], halves[..., SPAN:]], axis=1),
        jnp.concatenate(
            [expert_terms[:, low : low + SPAN], expert_terms[:, low + SPAN : low + 2 * SPAN]],
            axis=2,
        ),
    ]
    return (output[None], grad_inputs[None], *summed, *expert_sums)


def solution(mesh):
    n_seq, n_fsdp = mesh.shape["seq"], mesh.shape["fsdp"]
    fine = Mesh(
        mesh.devices.reshape(2, n_seq // 2, n_fsdp // 2, 2), ("zh", "zl", "c", "core")
    )
    split = P(FSDP, SEQ, None)
    rows = P(FSDP, None)
    three = P(FSDP, None, None)
    in_specs = (
        split,
        split,
        rows,
        rows,
        split,
        P(),
        P(),
        P(),
        P(),
        rows,
        rows,
        rows,
        three,
        three,
        rows,
        rows,
        rows,
        rows,
        three,
        P(FSDP, None, None, None),
        three,
        three,
    )
    owners = P((*SEQ, *FSDP), None)
    out_specs = (
        split,
        split,
        owners,
        owners,
        owners,
        owners,
        split,
        P(FSDP, None, None, SEQ),
        split,
        P(FSDP, None, SEQ),
    )
    return jax.shard_map(
        on_device, mesh=fine, in_specs=in_specs, out_specs=out_specs, check_vma=False
    )
```

```python
import functools

import jax
import jax.numpy as jnp
from jax import lax
from jax.experimental import pallas as pl
from jax.experimental.pallas import tpu as pltpu
from jax.sharding import Mesh
from jax.sharding import PartitionSpec as P

MODEL_WIDTH = 2048
H = 16
HD = 128
EXPERT_HIDDEN = 1024
TOP = 8
EXP_DEV = 2
ADAPTER_RANK = 16
SPAN = 128
GROUPS = 4
GROUP_WIDTH = MODEL_WIDTH // GROUPS
HEADS = H // GROUPS

EPSILON = 1e-05
THETA = 10000.0
NEGATIVE = -1e30
BF = jnp.bfloat16
F32 = jnp.float32
ANY = pl.ANY
VMEM = pltpu.VMEM
SEQ = ("zh", "zl")
FSDP = ("c", "core")


def mm(left, right):
    return lax.dot_general(left, right, (((1,), (0,)), ((), ())), preferred_element_type=F32)


def mm_t(left, right):
    return lax.dot_general(left, right, (((1,), (1,)), ((), ())), preferred_element_type=F32)


def t_mm(left, right):
    return lax.dot_general(left, right, (((0,), (0,)), ((), ())), preferred_element_type=F32)


def exact(form, left, right):
    return jnp.einsum(form, left, right, precision=lax.Precision.HIGHEST, preferred_element_type=F32)


def rms_scale(values, gain):
    return values * lax.rsqrt(jnp.mean(values * values, axis=-1, keepdims=True) + EPSILON) * gain


def rms_back(values, gain, grad):
    inverse = lax.rsqrt(jnp.mean(values * values, axis=-1, keepdims=True) + EPSILON)
    scaled = grad * gain
    return inverse * scaled - values * inverse * inverse * inverse * jnp.mean(
        values * scaled, axis=-1, keepdims=True
    )


def token_meta(lengths_row, sets_row, places):
    count = lengths_row.shape[0]
    running = [lengths_row[0]]
    for n in range(1, count):
        running.append(running[-1] + lengths_row[n])
    ends = jnp.stack(running)
    starts = ends - lengths_row
    member = ((places[:, None] >= starts[None, :]) & (places[:, None] < ends[None, :])).astype(
        jnp.int32
    )
    seq_ids = jnp.sum(member * jnp.arange(count, dtype=jnp.int32)[None, :], axis=1)
    offsets = places - jnp.sum(member * starts[None, :], axis=1)
    chosen = jnp.sum(member * sets_row[None, :], axis=1)
    return (seq_ids, offsets, chosen)


def set_mask(chosen):
    column_range = jnp.arange(SPAN, dtype=jnp.int32) // ADAPTER_RANK
    return (chosen[..., None] == column_range).astype(F32)


def here():
    return tuple(lax.axis_index(n) for n in ("zh", "zl", "c", "core"))


def signal_all(peers):
    barrier = pltpu.get_barrier_semaphore()
    for peer in peers:
        pl.semaphore_signal(barrier, inc=1, device_id=peer, device_id_type=pl.DeviceIdType.MESH)
    pl.semaphore_wait(barrier, len(peers))


def remote(src, dst, send, recv, device):
    return pltpu.make_async_remote_copy(
        src_ref=src,
        dst_ref=dst,
        send_sem=send,
        recv_sem=recv,
        device_id=device,
        device_id_type=pl.DeviceIdType.MESH,
    )


def column_peers(zh, zl, c, core):
    return [
        (zh ^ a, zl ^ b, c, core ^ k)
        for a in range(2)
        for b in range(2)
        for k in range(2)
        if (a, b, k) != (0, 0, 0)
    ]


def gather_kernel(n_c, x_ref, w_ref, xg_ref, wg_ref, xs, xr, fs, fr, ws, wr, own):
    zh, zl, c, core = here()
    tok = x_ref.shape[0]
    half = tok // 2
    rows = w_ref.shape[0]
    plane = [(zh, zl, lax.rem(c + i, n_c), core ^ k) for i in range(n_c) for k in range(2)][2:]
    signal_all(column_peers(zh, zl, c, core) + plane)
    me = zh * 2 + zl
    for a in range(2):
        for k in range(2):
            piece = pl.ds(k * half, half)
            src, dst = x_ref.at[piece], xg_ref.at[me, piece]
            is_self = (core == zh) & (zl == a) & (core == k)

            @pl.when(is_self)
            def _():
                pltpu.make_async_copy(src, dst, xr.at[me]).start()

            @pl.when(jnp.logical_not(is_self))
            def _():
                remote(src, dst, xs.at[a, k], xr.at[me], (core, a, c, k)).start()

    f = c * 2 + core
    row_block = pl.ds(pl.multiple_of(f * rows, rows), rows)

    def pieces(group):
        for j in range(3):
            start = pl.multiple_of(j * MODEL_WIDTH + group * GROUP_WIDTH, GROUP_WIDTH)
            yield (
                w_ref.at[:, pl.ds(start, GROUP_WIDTH)],
                wg_ref.at[row_block, pl.ds(j * GROUP_WIDTH, GROUP_WIDTH)],
            )

    for src, dst in pieces(zl * 2 + core):
        pltpu.make_async_copy(src, dst, own).start()
    slots = [(i, k) for i in range(n_c) for k in range(2)][1:]
    for i, k in slots:
        target_c, target_core = lax.rem(c + i, n_c), core ^ k
        for src, dst in pieces(zl * 2 + target_core):
            remote(
                src, dst, ws.at[i * 2 + k], wr.at[i * 2 + k], (zh, zl, target_c, target_core)
            ).start()
    mine = pl.ds(pl.multiple_of(core * half, half), half)
    theirs = pl.ds(pl.multiple_of((1 - core) * half, half), half)
    sibling = (zh, zl, c, 1 - core)
    for s in range(4):
        pltpu.make_async_copy(xg_ref.at[s, mine], xg_ref.at[s, mine], xr.at[s]).wait()
        remote(xg_ref.at[s, mine], xg_ref.at[s, mine], fs.at[s], fr.at[s], sibling).start()
    for s in range(4):
        got = xg_ref.at[s, theirs]
        pltpu.make_async_copy(got, got, fr.at[s]).wait()
    for s in range(4):
        got = xg_ref.at[s, mine]
        pltpu.make_async_copy(got, got, fs.at[s]).wait()
    for a in range(2):
        for k in range(2):
            is_self = (core == zh) & (zl == a) & (core == k)
            src = x_ref.at[pl.ds(k * half, half)]

            @pl.when(jnp.logical_not(is_self))
            def _():
                pltpu.make_async_copy(src, src, xs.at[a, k]).wait()

    block = wg_ref.at[row_block]
    pltpu.make_async_copy(block, block, own).wait()
    for i, k in slots:
        pltpu.make_async_copy(block, block, ws.at[i * 2 + k]).wait()
        source = lax.rem(c + n_c - i, n_c) * 2 + (core ^ k)
        got = wg_ref.at[pl.ds(pl.multiple_of(source * rows, rows), rows)]
        pltpu.make_async_copy(got, got, wr.at[i * 2 + k]).wait()


def gather_to_heads(x, w, n_c):
    tok, rows = x.shape[0], w.shape[0]
    n_f = 2 * n_c
    dma = pltpu.SemaphoreType.DMA
    return pl.pallas_call(
        functools.partial(gather_kernel, n_c),
        out_shape=(
            jax.ShapeDtypeStruct((4, tok, MODEL_WIDTH), BF),
            jax.ShapeDtypeStruct((n_f * rows, 3 * GROUP_WIDTH), BF),
        ),
        in_specs=[pl.BlockSpec(memory_space=VMEM)] * 2,
        out_specs=[pl.BlockSpec(memory_space=ANY)] * 2,
        scratch_shapes=[
            dma((2, 2)),
            dma((4,)),
            dma((4,)),
            dma((4,)),
            dma((n_f,)),
            dma((n_f,)),
            dma,
        ],
        compiler_params=pltpu.CompilerParams(collective_id=0, has_side_effects=True),
        name="gather_to_heads",
    )(x, w)


PROJECT_WIDTH = 3 * GROUP_WIDTH + 3 * SPAN


def project_kernel(x_ref, w_ref, down_ref, up_ref, mask, xg_o, wg_o, upg, proj_o, low, acc, xg, wg, xs, xr, fs, fr, ws, wr, us, ur, own, out):
    zh, zl, c, core = here()
    tok = x_ref.shape[0]
    half = tok // 2
    rows = w_ref.shape[0]
    up_rows = up_ref.shape[0]
    near = lambda i: (
        lax.rem(c // 2 + i // 2, 2) * 2 + lax.rem(lax.rem(c, 2) + lax.rem(i, 2), 2)
    )
    chips = [near(i) for i in range(4)]
    plane = [(zh, zl, chips[i], core ^ k) for i in range(4) for k in range(2)]
    sibling, beside, above = plane[1], plane[2], plane[4]
    signal_all(column_peers(zh, zl, c, core) + plane[2:])
    me = zh * 2 + zl
    f = c * 2 + core
    block = lambda source: wg.at[pl.ds(pl.multiple_of(source * rows, rows), rows)]
    source = lambda i, k: chips[i] * 2 + k

    def pieces(group):
        to = pl.ds(pl.multiple_of(f * rows, rows), rows)
        for j in range(3):
            start = pl.multiple_of(j * MODEL_WIDTH + group * GROUP_WIDTH, GROUP_WIDTH)
            yield (
                w_ref.at[:, pl.ds(start, GROUP_WIDTH)],
                wg.at[to, pl.ds(j * GROUP_WIDTH, GROUP_WIDTH)],
            )
        yield down_ref, wg.at[to, pl.ds(3 * GROUP_WIDTH, 3 * SPAN)]

    for src, dst in pieces(zl * 2 + core):
        pltpu.make_async_copy(src, dst, own.at[0]).start()
    for src, dst in pieces(zl * 2 + 1 - core):
        remote(src, dst, ws.at[0], wr.at[0], sibling).start()
    for a in range(2):
        for k in range(2):
            piece = pl.ds(k * half, half)
            src, dst = x_ref.at[piece], xg.at[me, piece]
            is_self = (core == zh) & (zl == a) & (core == k)

            @pl.when(is_self)
            def _():
                pltpu.make_async_copy(src, dst, xr.at[me]).start()

            @pl.when(jnp.logical_not(is_self))
            def _():
                remote(src, dst, xs.at[a, k], xr.at[me], (core, a, c, k)).start()

    wait_for(block(f), own.at[0])
    remote(block(f), block(f), ws.at[1], wr.at[1], beside).start()
    remote(block(f), block(f), ws.at[2], wr.at[2], above).start()
    up_to = pl.ds(pl.multiple_of(f * up_rows, up_rows), up_rows)
    for n, peer in enumerate(plane):
        start = pl.multiple_of((zl * 2 + peer[3]) * GROUP_WIDTH, GROUP_WIDTH)
        src, dst = up_ref.at[:, pl.ds(start, GROUP_WIDTH)], upg.at[up_to]
        if n:
            remote(src, dst, us.at[n], ur.at[n], peer).start()
        else:
            pltpu.make_async_copy(src, dst, own.at[1]).start()
    other = c * 2 + 1 - core
    wait_for(block(other), wr.at[0])
    remote(block(other), block(other), ws.at[3], wr.at[3], beside).start()
    remote(block(other), block(other), ws.at[4], wr.at[4], above).start()
    mine = pl.ds(pl.multiple_of(core * half, half), half)
    theirs = pl.ds(pl.multiple_of((1 - core) * half, half), half)

    shards = [k + zh * (3 - 2 * k) for k in range(4)]

    def pass_tokens(k):
        s = shards[k]
        wait_for(xg.at[s, mine], xr.at[s])
        remote(xg.at[s, mine], xg.at[s, mine], fs.at[s], fr.at[s], sibling).start()

    def take_tokens(k):
        s = shards[k]
        wait_for(xg.at[s, theirs], fr.at[s])
        pltpu.make_async_copy(xg.at[s], xg_o.at[s], out.at[0]).start()

    def multiply(i, k):
        at = pl.ds(pl.multiple_of(chips[i] * (2 * rows), 2 * rows), 2 * rows)
        s = shards[k]
        value = mm(xg[s, :, at], wg[at, :])
        acc[s] = value if i == 0 else acc[s] + value

    own_x, other_x = source(1, core), source(1, 1 - core)
    own_y, other_y = source(2, core), source(2, 1 - core)
    pass_tokens(0)
    take_tokens(0)
    multiply(0, 0)
    wait_for(block(own_x), wr.at[1])
    remote(block(own_x), block(own_x), ws.at[5], wr.at[5], above).start()
    pass_tokens(1)
    take_tokens(1)
    multiply(0, 1)
    wait_for(block(own_y), wr.at[2])
    wait_for(block(other_y), wr.at[4])
    remote(block(other_y), block(other_y), ws.at[6], wr.at[6], beside).start()
    pass_tokens(2)
    wait_for(block(other_x), wr.at[3])
    for k in range(2):
        multiply(1, k)
        multiply(2, k)
    take_tokens(2)
    for i in range(3):
        multiply(i, 2)
    pass_tokens(3)
    take_tokens(3)
    for i in range(3):
        multiply(i, 3)
    wait_for(block(source(3, core)), wr.at[5])
    wait_for(block(source(3, 1 - core)), wr.at[6])
    save = pltpu.make_async_copy(wg, wg_o, out.at[1])
    save.start()
    for k in range(4):
        multiply(3, k)
    up_block = lambda n: upg.at[pl.ds(pl.multiple_of(n * up_rows, up_rows), up_rows)]
    wait_for(up_block(f), own.at[1])
    for n, peer in enumerate(plane):
        if n:
            wait_for(up_block(peer[2] * 2 + peer[3]), ur.at[n])

    for s in range(4):
        for j in range(3):
            span = slice(j * SPAN, (j + 1) * SPAN)
            wide = slice(j * GROUP_WIDTH, (j + 1) * GROUP_WIDTH)
            at = 3 * GROUP_WIDTH + j * SPAN
            lowered = (acc[s, :, at : at + SPAN] * mask[s]).astype(BF)
            low[s, :, span] = lowered
            acc[s, :, wide] = acc[s, :, wide] + mm(lowered, upg[span])
        pltpu.make_async_copy(acc.at[s, :, pl.ds(0, 3 * GROUP_WIDTH)], proj_o.at[s], out.at[2]).start()

    for s in range(4):
        wait_for(xg.at[s, mine], fs.at[s])
    for a in range(2):
        for k in range(2):
            is_self = (core == zh) & (zl == a) & (core == k)

            @pl.when(jnp.logical_not(is_self))
            def _():
                wait_for(x_ref.at[pl.ds(k * half, half)], xs.at[a, k])

    save.wait()
    wait_for(xg_o, out.at[0])
    wait_for(proj_o, out.at[2])
    for n in range(7):
        wait_for(block(f), ws.at[n])
    for n in range(1, 8):
        wait_for(up_block(f), us.at[n])


def gather_project(x, w, down3, up, mask):
    tok, rows = x.shape[0], w.shape[0]
    dma = pltpu.SemaphoreType.DMA
    vmem = pl.BlockSpec(memory_space=VMEM)
    hbm = pl.BlockSpec(memory_space=ANY)
    return pl.pallas_call(
        project_kernel,
        out_shape=(
            jax.ShapeDtypeStruct((4, tok, MODEL_WIDTH), BF),
            jax.ShapeDtypeStruct((8 * rows, PROJECT_WIDTH), BF),
            jax.ShapeDtypeStruct((8 * up.shape[0], GROUP_WIDTH), BF),
            jax.ShapeDtypeStruct((4, tok, 3 * GROUP_WIDTH), F32),
            jax.ShapeDtypeStruct((4, tok, 3 * SPAN), BF),
        ),
        in_specs=[vmem] * 5,
        out_specs=[hbm, hbm, vmem, hbm, vmem],
        scratch_shapes=[
            VMEM((4, tok, PROJECT_WIDTH), F32),
            VMEM((4, tok, MODEL_WIDTH), BF),
            VMEM((8 * rows, PROJECT_WIDTH), BF),
            dma((2, 2)),
            dma((4,)),
            dma((4,)),
            dma((4,)),
            dma((7,)),
            dma((7,)),
            dma((8,)),
            dma((8,)),
            dma((2,)),
            dma((3,)),
        ],
        compiler_params=pltpu.CompilerParams(
            collective_id=8, has_side_effects=True, vmem_limit_bytes=58 * 2**20
        ),
        name="gather_project",
    )(x, w, down3, up, mask)


def to_tokens_kernel(a_ref, o_ref, send, recv):
    zh, zl, c, core = here()
    signal_all(column_peers(zh, zl, c, core))
    group = zl * 2 + core
    columns = pl.ds(pl.multiple_of(group * GROUP_WIDTH, GROUP_WIDTH), GROUP_WIDTH)
    for s in range(4):
        a, b = s // 2, s % 2
        is_self = (a == zh) & (b == zl) & (core == zh)
        src, dst = a_ref.at[s], o_ref.at[:, columns]

        @pl.when(is_self)
        def _():
            pltpu.make_async_copy(src, dst, recv.at[group]).start()

        @pl.when(jnp.logical_not(is_self))
        def _():
            remote(src, dst, send.at[s], recv.at[group], (a, b, c, zh)).start()

    for s in range(4):
        a, b = s // 2, s % 2
        is_self = (a == zh) & (b == zl) & (core == zh)
        got = o_ref.at[:, pl.ds(s * GROUP_WIDTH, GROUP_WIDTH)]
        pltpu.make_async_copy(got, got, recv.at[s]).wait()

        @pl.when(jnp.logical_not(is_self))
        def _():
            pltpu.make_async_copy(a_ref.at[s], a_ref.at[s], send.at[s]).wait()


def to_tokens(rows):
    tok = rows.shape[1]
    dma = pltpu.SemaphoreType.DMA
    return pl.pallas_call(
        to_tokens_kernel,
        out_shape=jax.ShapeDtypeStruct((tok, MODEL_WIDTH), BF),
        in_specs=[pl.BlockSpec(memory_space=VMEM)],
        out_specs=pl.BlockSpec(memory_space=ANY),
        scratch_shapes=[dma((4,)), dma((4,))],
        compiler_params=pltpu.CompilerParams(collective_id=1, has_side_effects=True),
        name="to_tokens",
    )(rows)


def to_heads_kernel(a_ref, o_ref, send, recv):
    zh, zl, c, core = here()
    signal_all(column_peers(zh, zl, c, core))
    me = zh * 2 + zl
    for g in range(4):
        b, k = g // 2, g % 2
        is_self = (core == zh) & (b == zl) & (core == k)
        src, dst = a_ref.at[:, pl.ds(g * GROUP_WIDTH, GROUP_WIDTH)], o_ref.at[me]

        @pl.when(is_self)
        def _():
            pltpu.make_async_copy(src, dst, recv.at[me]).start()

        @pl.when(jnp.logical_not(is_self))
        def _():
            remote(src, dst, send.at[g], recv.at[me], (core, b, c, k)).start()

    for g in range(4):
        b, k = g // 2, g % 2
        is_self = (core == zh) & (b == zl) & (core == k)
        pltpu.make_async_copy(o_ref.at[g], o_ref.at[g], recv.at[g]).wait()

        @pl.when(jnp.logical_not(is_self))
        def _():
            pltpu.make_async_copy(o_ref.at[g], o_ref.at[g], send.at[g]).wait()


def to_heads(rows):
    tok = rows.shape[0]
    dma = pltpu.SemaphoreType.DMA
    return pl.pallas_call(
        to_heads_kernel,
        out_shape=jax.ShapeDtypeStruct((4, tok, GROUP_WIDTH), BF),
        in_specs=[pl.BlockSpec(memory_space=VMEM)],
        out_specs=pl.BlockSpec(memory_space=ANY),
        scratch_shapes=[dma((4,)), dma((4,))],
        compiler_params=pltpu.CompilerParams(collective_id=2, has_side_effects=True),
        name="to_heads",
    )(rows)


def sum_to_tokens_kernel(p_ref, o_ref, sib, chip, rx, ss, sr, send, recv):
    zh, zl, c, core = here()
    signal_all(column_peers(zh, zl, c, core))
    width = o_ref.shape[1]
    half = width // 2
    sibling = (zh, zl, c, 1 - core)
    mine = pl.ds(pl.multiple_of(core * half, half), half)
    theirs = pl.ds(pl.multiple_of((1 - core) * half, half), half)
    for s in range(4):
        remote(p_ref.at[s, :, theirs], sib.at[s], ss.at[s], sr.at[s], sibling).start()

    def is_self(s):
        return (s // 2 == zh) & (s % 2 == zl) & (core == zh)

    for s in range(4):
        pltpu.make_async_copy(sib.at[s], sib.at[s], sr.at[s]).wait()
        chip[s] = (p_ref[s, :, mine].astype(F32) + sib[s].astype(F32)).astype(BF)
        src, dst = chip.at[s], rx.at[zl, core]

        @pl.when(is_self(s))
        def _():
            pltpu.make_async_copy(src, dst, recv.at[zl, core]).start()

        @pl.when(jnp.logical_not(is_self(s)))
        def _():
            remote(src, dst, send.at[s], recv.at[zl, core], (s // 2, s % 2, c, zh)).start()

    for s in range(4):
        pltpu.make_async_copy(sib.at[s], sib.at[s], ss.at[s]).wait()

        @pl.when(jnp.logical_not(is_self(s)))
        def _():
            pltpu.make_async_copy(chip.at[s], chip.at[s], send.at[s]).wait()

    for k in range(2):
        for b in range(2):
            pltpu.make_async_copy(rx.at[b, k], rx.at[b, k], recv.at[b, k]).wait()
        o_ref[:, k * half : (k + 1) * half] = rx[0, k].astype(F32) + rx[1, k].astype(F32)


def sum_to_tokens(parts):
    _, tok, width = parts.shape
    half = width // 2
    dma = pltpu.SemaphoreType.DMA
    return pl.pallas_call(
        sum_to_tokens_kernel,
        out_shape=jax.ShapeDtypeStruct((tok, width), F32),
        in_specs=[pl.BlockSpec(memory_space=VMEM)],
        out_specs=pl.BlockSpec(memory_space=VMEM),
        scratch_shapes=[
            VMEM((4, tok, half), BF),
            VMEM((4, tok, half), BF),
            VMEM((2, 2, tok, half), BF),
            dma((4,)),
            dma((4,)),
            dma((4,)),
            dma((2, 2)),
        ],
        compiler_params=pltpu.CompilerParams(
            collective_id=3, has_side_effects=True, vmem_limit_bytes=40 * 2**20
        ),
        name="sum_to_tokens",
    )(parts)


def finish_kernel(
    n_c,
    both,
    h_weight,
    late,
    early,
    h_middle,
    h_mixed,
    h_tokens,
    h_grad_middle,
    gain,
    output,
    grad_tokens,
    grad_down,
    grad_up,
    grad_rdown,
    grad_rup,
    give,
    keep,
    sib,
    fwd,
    rx,
    got_l,
    got_e,
    stage,
    got_z,
    ss,
    sr,
    gs,
    gr,
    send,
    recv,
    ls,
    lr,
    es,
    er,
    zs,
    zr,
    weight,
    middle,
    mixed,
    tokens,
    grad_middle,
    loaded,
):
    zh, zl, c, core = here()
    held = (weight, middle, mixed, tokens, grad_middle)
    loads = [
        pltpu.make_async_copy(src, dst, loaded.at[n])
        for n, (src, dst) in enumerate(
            zip((h_weight, h_middle, h_mixed, h_tokens, h_grad_middle), held, strict=True)
        )
    ]
    for load in loads:
        load.start()
    plane = [(zh, zl, lax.rem(c + i, n_c), core ^ k) for i in range(n_c) for k in range(2)]
    signal_all(column_peers(zh, zl, c, core) + plane[2:])
    tok, width = output.shape
    half = width // 2
    sibling = (zh, zl, c, 1 - core)
    mine = pl.ds(pl.multiple_of(core * half, half), half)
    theirs = pl.ds(pl.multiple_of((1 - core) * half, half), half)
    me = c * 2 + core
    count = len(plane)
    for n in range(1, count):
        peer = plane[n]
        f = peer[2] * 2 + peer[3]
        remote(early.at[f], got_e.at[n], es.at[n], er.at[n], peer).start()
        remote(late.at[f], got_l.at[n], ls.at[n], lr.at[n], peer).start()
    at_end = zl == zh
    inner = zl != zh
    shard = lambda p: p + zh * (3 - 2 * p)
    owner = lambda p: (shard(p) // 2, lax.rem(shard(p), 2), c, zh)
    local = core == zh

    def deliver(n, p, slot):
        remote(give.at[n], rx.at[slot, core], send.at[n], recv.at[slot, core], owner(p)).start()

    def stay(n, slot):
        pltpu.make_async_copy(give.at[n], rx.at[slot, core], recv.at[slot, core]).start()

    def settle(n, p):
        pltpu.make_async_copy(sib.at[n], sib.at[n], sr.at[n]).wait()
        wait_for(give.at[n], ss.at[n])
        give[n] = (keep[n] + sib[n].astype(F32)).astype(BF)
        if p >= 2:

            @pl.when(at_end)
            def _():
                remote(give.at[n], fwd.at[n], gs.at[n], gr.at[n], (zh, 1 - zl, c, core)).start()

        else:
            home = at_end if p == 0 else inner

            @pl.when(home & local)
            def _():
                stay(n, p)

            @pl.when(home & jnp.logical_not(local))
            def _():
                deliver(n, p, p)

            @pl.when(jnp.logical_not(home))
            def _():
                deliver(n, p, 1 - p)

    order = (3, 2, 1, 0)
    loads[0].wait()
    for n, p in enumerate(order):
        rows = pl.ds(pl.multiple_of(shard(p) * tok, tok), tok)
        give[n] = mm_t(both[rows], weight[theirs]).astype(BF)
        remote(give.at[n], sib.at[n], ss.at[n], sr.at[n], sibling).start()
        keep[n] = mm_t(both[rows], weight[mine])
        if n:
            settle(n - 1, order[n - 1])
    settle(3, 0)

    @pl.when(inner)
    def _():
        for n in range(2):
            wait_for(fwd.at[n], gr.at[n])
            give[n] = (give[n].astype(F32) + fwd[n].astype(F32)).astype(BF)
            deliver(n, order[n], 1)

    for load in loads[1:]:
        load.wait()
    output[...] = (middle[...] + mixed[...].astype(F32)).astype(BF)

    def total(own, got, arrived):
        value = own[me].astype(F32)
        for n in range(1, count):
            wait_for(got.at[n], arrived.at[n])
            value = value + got[n].astype(F32)
        return value.astype(BF)

    early_sum = total(early, got_e, er)
    late_sum = total(late, got_l, lr)
    down, up, wide, rest = finish_rows(n_c)
    for q in range(4):
        stage[q, :down] = late_sum[q * down : (q + 1) * down]
        if q < 3:
            at = 4 * down + q * up
            stage[q, down : down + up] = late_sum[at : at + up]
            stage[q, down + up : down + wide] = jnp.zeros((wide - up, SPAN), BF)
        else:
            stage[q, down : down + wide] = early_sum[:wide]
        at = wide + q * rest
        stage[q, down + wide :] = early_sum[at : at + rest]
    seq = zh * 2 + zl
    for q in range(4):

        @pl.when(seq == q)
        def _():
            got_z[q] = stage[q]

        @pl.when(seq != q)
        def _():
            remote(stage.at[q], got_z.at[seq], zs.at[q], zr.at[seq], (q // 2, q % 2, c, core)).start()

    paired = zh == core

    @pl.when(paired)
    def _():
        for k in range(2):
            wait_for(rx.at[0, k], recv.at[0, k])

    @pl.when(jnp.logical_not(paired))
    def _():
        rx[0] = jnp.zeros_like(rx[0])

    for k in range(2):
        wait_for(rx.at[1, k], recv.at[1, k])
    for n in range(tok // 32):
        rows = slice(n * 32, (n + 1) * 32)
        grad = jnp.concatenate(
            [rx[0, k, rows].astype(F32) + rx[1, k, rows].astype(F32) for k in range(2)], axis=1
        )
        grad_tokens[rows] = grad_middle[rows] + rms_back(tokens[rows].astype(F32), gain[...], grad)

    for q in range(4):

        @pl.when(seq != q)
        def _():
            wait_for(got_z.at[q], zr.at[q])

    def along_z(rows):
        return (got_z[0, rows].astype(F32) + got_z[1, rows].astype(F32)) + (
            got_z[2, rows].astype(F32) + got_z[3, rows].astype(F32)
        )

    r, u = down // 3, up // 8
    for j in range(4):
        start = j * r if j < 3 else down + wide
        grad_down[:, j * SPAN : (j + 1) * SPAN] = along_z(slice(start, start + r))
    grad_rdown[...] = along_z(slice(down + wide + r, down + wide + 2 * r))
    grad_rup[...] = along_z(slice(down + wide + 2 * r, down + wide + rest))
    for n in range(16):
        b, m = n // 8, n % 8
        part = slice(down + m * u, down + (m + 1) * u)
        halves = got_z[b, part].astype(F32) + got_z[2 + b, part].astype(F32)
        whole = along_z(slice(down + n * u, down + (n + 1) * u))
        grad_up[:, n * SPAN : (n + 1) * SPAN] = jnp.where(seq < 3, halves, whole)

    for s in range(4):

        @pl.when(seq != s)
        def _():
            wait_for(stage.at[s], zs.at[s])

    for n, p in enumerate(order):
        if p >= 2:

            @pl.when(at_end)
            def _():
                wait_for(give.at[n], gs.at[n])

            @pl.when(inner)
            def _():
                wait_for(give.at[n], send.at[n])

        else:
            home = at_end if p == 0 else inner

            @pl.when(jnp.logical_not(home & local))
            def _():
                wait_for(give.at[n], send.at[n])

    for n in range(1, count):
        wait_for(got_l.at[n], ls.at[n])
        wait_for(got_e.at[n], es.at[n])


def finish_rows(n_c):
    n_f = 2 * n_c
    down, up = MODEL_WIDTH // (4 * n_f), SPAN // n_f
    return 3 * down, 8 * up, 16 * up, 2 * down + 16


def finish(both, weight, late, early, middle, mixed, tokens, grad_middle, gain, n_c):
    tok, width = middle.shape
    half = width // 2
    down, up, wide, rest = finish_rows(n_c)
    n_f = 2 * n_c
    dma = pltpu.SemaphoreType.DMA
    vmem = pl.BlockSpec(memory_space=VMEM)
    hbm = pl.BlockSpec(memory_space=ANY)
    return pl.pallas_call(
        functools.partial(finish_kernel, n_c),
        out_shape=(
            jax.ShapeDtypeStruct((tok, width), BF),
            jax.ShapeDtypeStruct((tok, width), F32),
            jax.ShapeDtypeStruct((down // 3, 4 * SPAN), F32),
            jax.ShapeDtypeStruct((up // 8, 16 * SPAN), F32),
            jax.ShapeDtypeStruct((down // 3, SPAN), F32),
            jax.ShapeDtypeStruct((16, SPAN), F32),
        ),
        in_specs=[vmem, hbm, vmem, vmem, hbm, hbm, hbm, hbm, vmem],
        out_specs=[vmem] * 6,
        scratch_shapes=[
            VMEM((4, tok, half), BF),
            VMEM((4, tok, half), F32),
            VMEM((4, tok, half), BF),
            VMEM((2, tok, half), BF),
            VMEM((2, 2, tok, half), BF),
            VMEM(late.shape, BF),
            VMEM(early.shape, BF),
            VMEM((4, down + wide + rest, SPAN), BF),
            VMEM((4, down + wide + rest, SPAN), BF),
            dma((4,)),
            dma((4,)),
            dma((2,)),
            dma((2,)),
            dma((4,)),
            dma((2, 2)),
            dma((n_f,)),
            dma((n_f,)),
            dma((n_f,)),
            dma((n_f,)),
            dma((4,)),
            dma((4,)),
            *(VMEM(t.shape, t.dtype) for t in (weight, middle, mixed, tokens, grad_middle)),
            dma((5,)),
        ],
        compiler_params=pltpu.CompilerParams(
            collective_id=7, has_side_effects=True, vmem_limit_bytes=60 * 2**20
        ),
        name="finish",
    )(both, weight, late, early, middle, mixed, tokens, grad_middle, gain)


def group_sum_kernel(x_ref, o_ref, rx, send, recv):
    zh, zl, c, core = here()
    peers = [(zh, zl, c, 1 - core), (zh, 1 - zl, c, core), (zh, 1 - zl, c, 1 - core)]
    signal_all(peers)
    copies = [remote(x_ref, rx.at[i], send.at[i], recv.at[i], p) for i, p in enumerate(peers)]
    for copy in copies:
        copy.start()
    for copy in copies:
        copy.wait()
    o_ref[...] = (x_ref[...] + rx[0]) + (rx[1] + rx[2])


def group_sum(values, identity):
    dma = pltpu.SemaphoreType.DMA
    return pl.pallas_call(
        group_sum_kernel,
        out_shape=jax.ShapeDtypeStruct(values.shape, F32),
        in_specs=[pl.BlockSpec(memory_space=VMEM)],
        out_specs=pl.BlockSpec(memory_space=VMEM),
        scratch_shapes=[VMEM((3, *values.shape), F32), dma((3,)), dma((3,))],
        compiler_params=pltpu.CompilerParams(collective_id=identity, has_side_effects=True),
        name="group_sum",
    )(values)


def turn(values, cosine, sine):
    return values * cosine + pltpu.roll(values, HD // 2, 1) * sine


def attention_rows(block):
    return 256 if block % 256 == 0 else block


def attend_kernel(
    pq, pk, pv, rq, rk, gq, gk, cosine, sine, seg_c, seg_r, q_ref, k_ref, v_ref, o_ref, lse_ref
):
    block = pq.shape[0]
    rows = attention_rows(block)
    scale = HD**-0.5
    q_ref[...] = turn(pq[...] * rq[...] * gq[...], cosine[...], sine[...]).astype(BF)
    k_ref[...] = turn(pk[...] * rk[...] * gk[...], cosine[...], sine[...]).astype(BF)
    v_ref[...] = pv[...].astype(BF)
    for i in range(block // rows):
        length = (i + 1) * rows
        own = slice(i * rows, length)
        scores = mm_t(q_ref[own], k_ref[:length]) * scale
        row = lax.broadcasted_iota(jnp.int32, (rows, length), 0) + i * rows
        column = lax.broadcasted_iota(jnp.int32, (rows, length), 1)
        allowed = (seg_c[own] == seg_r[:, :length]) & (column <= row)
        scores = jnp.where(allowed, scores, NEGATIVE)
        top = jnp.max(scores, axis=1, keepdims=True)
        weights = jnp.exp(scores - top)
        total = jnp.sum(weights, axis=1, keepdims=True)
        out = mm(weights.astype(BF), v_ref[:length]) / total
        o_ref[own] = out.astype(BF)
        lse_ref[0, own] = top + jnp.log(total)


def attend(projected, rq, rk, gq, gk, cosine, sine, seg_c, seg_r):
    block = projected.shape[0]
    head = lambda off: pl.BlockSpec((block, HD), lambda h: (0, off + h))
    gain = pl.BlockSpec((1, HD), lambda h: (0, h))
    fixed = lambda shape: pl.BlockSpec(shape, lambda h: (0, 0))
    wide = jax.ShapeDtypeStruct((block, GROUP_WIDTH), BF)
    return pl.pallas_call(
        attend_kernel,
        grid=(HEADS,),
        out_shape=(wide, wide, wide, wide, jax.ShapeDtypeStruct((HEADS, block, 1), F32)),
        in_specs=[
            head(0),
            head(HEADS),
            head(2 * HEADS),
            fixed((block, 1)),
            fixed((block, 1)),
            gain,
            gain,
            fixed((block, HD)),
            fixed((block, HD)),
            fixed((block, 1)),
            fixed((1, block)),
        ],
        out_specs=[head(0)] * 4 + [pl.BlockSpec((1, block, 1), lambda h: (h, 0, 0))],
        compiler_params=pltpu.CompilerParams(vmem_limit_bytes=60 * 2**20),
        name="attend",
    )(projected, projected, projected, rq, rk, gq, gk, cosine, sine, seg_c, seg_r)


def attend_send_kernel(
    pq, pk, pv, rq, rk, gq, gk, cosine, sine, seg_c, seg_r, q_ref, k_ref, v_ref, lse_ref, o_ref, held, send, recv
):
    zh, zl, c, core = here()
    h = pl.program_id(0)
    tok = o_ref.shape[0]
    group = zl * 2 + core

    @pl.when(h == 0)
    def _():
        signal_all(column_peers(zh, zl, c, core))

    attend_kernel(
        pq, pk, pv, rq, rk, gq, gk, cosine, sine, seg_c, seg_r, q_ref, k_ref, v_ref, held.at[h], lse_ref
    )
    columns = pl.ds(pl.multiple_of(group * GROUP_WIDTH + h * HD, HD), HD)
    is_self = lambda s: (s // 2 == zh) & (s % 2 == zl) & (core == zh)
    for s in range(4):
        src, dst = held.at[h, pl.ds(s * tok, tok)], o_ref.at[:, columns]

        @pl.when(is_self(s))
        def _():
            pltpu.make_async_copy(src, dst, recv.at[group, h]).start()

        @pl.when(jnp.logical_not(is_self(s)))
        def _():
            remote(src, dst, send.at[s, h], recv.at[group, h], (s // 2, s % 2, c, zh)).start()

    @pl.when(h == HEADS - 1)
    def _():
        for n in range(HEADS):
            for s in range(4):
                got = o_ref.at[:, pl.ds(s * GROUP_WIDTH + n * HD, HD)]
                wait_for(got, recv.at[s, n])

                @pl.when(jnp.logical_not(is_self(s)))
                def _():
                    wait_for(held.at[n, pl.ds(0, tok)], send.at[s, n])


def attend_send(projected, rq, rk, gq, gk, cosine, sine, seg_c, seg_r):
    block = projected.shape[0]
    tok = block // 4
    dma = pltpu.SemaphoreType.DMA
    head = lambda off: pl.BlockSpec((block, HD), lambda h: (0, off + h))
    gain = pl.BlockSpec((1, HD), lambda h: (0, h))
    fixed = lambda shape: pl.BlockSpec(shape, lambda h: (0, 0))
    wide = jax.ShapeDtypeStruct((block, GROUP_WIDTH), BF)
    return pl.pallas_call(
        attend_send_kernel,
        grid=(HEADS,),
        out_shape=(
            wide,
            wide,
            wide,
            jax.ShapeDtypeStruct((HEADS, block, 1), F32),
            jax.ShapeDtypeStruct((tok, MODEL_WIDTH), BF),
        ),
        in_specs=[
            head(0),
            head(HEADS),
            head(2 * HEADS),
            fixed((block, 1)),
            fixed((block, 1)),
            gain,
            gain,
            fixed((block, HD)),
            fixed((block, HD)),
            fixed((block, 1)),
            fixed((1, block)),
        ],
        out_specs=[head(0)] * 3
        + [pl.BlockSpec((1, block, 1), lambda h: (h, 0, 0)), pl.BlockSpec(memory_space=ANY)],
        scratch_shapes=[VMEM((HEADS, block, HD), BF), dma((4, HEADS)), dma((4, HEADS))],
        compiler_params=pltpu.CompilerParams(
            collective_id=9, has_side_effects=True, vmem_limit_bytes=60 * 2**20
        ),
        name="attend_send",
    )(projected, projected, projected, rq, rk, gq, gk, cosine, sine, seg_c, seg_r)


def attend_back_kernel(
    q_ref,
    k_ref,
    v_ref,
    g_ref,
    lse_ref,
    pq,
    pk,
    gq,
    gk,
    cosine,
    sine,
    seg_c,
    seg_r,
    uq_ref,
    uk_ref,
    dv_ref,
    mq_ref,
    mk_ref,
    dk_acc,
    dv_acc,
):
    block = q_ref.shape[0]
    rows = attention_rows(block)
    scale = HD**-0.5
    dk_acc[...] = jnp.zeros_like(dk_acc)
    dv_acc[...] = jnp.zeros_like(dv_acc)

    @pl.when(pl.program_id(0) == 0)
    def _():
        mq_ref[...] = jnp.zeros_like(mq_ref)
        mk_ref[...] = jnp.zeros_like(mk_ref)


    def back(grad, raw, gain):
        turned = turn(grad.astype(BF).astype(F32), cosine_of, -sine_of)
        return turned, jnp.sum(raw * gain[...] * turned, axis=1, keepdims=True)

    for i in range(block // rows):
        length = (i + 1) * rows
        own = slice(i * rows, length)
        scores = mm_t(q_ref[own], k_ref[:length]) * scale
        row = lax.broadcasted_iota(jnp.int32, (rows, length), 0) + i * rows
        column = lax.broadcasted_iota(jnp.int32, (rows, length), 1)
        allowed = (seg_c[own] == seg_r[:, :length]) & (column <= row)
        probs = jnp.where(allowed, jnp.exp(scores - lse_ref[0, own]), 0.0)
        grad_probs = mm_t(g_ref[own], v_ref[:length])
        delta = jnp.sum(probs * grad_probs, axis=1, keepdims=True)
        grad_scores = (probs * (grad_probs - delta)).astype(BF)
        grad_q = mm(grad_scores, k_ref[:length]) * scale
        cosine_of, sine_of = cosine[own], sine[own]
        turned, moment = back(grad_q, pq[own], gq)
        uq_ref[own] = turned
        mq_ref[own] += moment
        dk_acc[:length] += t_mm(grad_scores, q_ref[own])
        dv_acc[:length] += t_mm(probs.astype(BF), g_ref[own])
    cosine_of, sine_of = cosine[...], sine[...]
    turned, moment = back(dk_acc[...] * scale, pk[...], gk)
    uk_ref[...] = turned
    mk_ref[...] += moment
    dv_ref[...] = dv_acc[...].astype(BF)


def attend_back(q, k, v, grad, lse, projected, gq, gk, cosine, sine, seg_c, seg_r):
    block = q.shape[0]
    head = lambda off: pl.BlockSpec((block, HD), lambda h: (0, off + h))
    gain = pl.BlockSpec((1, HD), lambda h: (0, h))
    fixed = lambda shape: pl.BlockSpec(shape, lambda h: (0, 0))
    column = pl.BlockSpec((1, block, 1), lambda h: (h, 0, 0))
    wide = lambda t: jax.ShapeDtypeStruct((block, GROUP_WIDTH), t)
    moment = jax.ShapeDtypeStruct((block, 1), F32)
    return pl.pallas_call(
        attend_back_kernel,
        grid=(HEADS,),
        out_shape=(wide(F32), wide(F32), wide(BF), moment, moment),
        in_specs=[
            head(0),
            head(0),
            head(0),
            head(0),
            column,
            head(0),
            head(HEADS),
            gain,
            gain,
            fixed((block, HD)),
            fixed((block, HD)),
            fixed((block, 1)),
            fixed((1, block)),
        ],
        out_specs=[head(0)] * 3 + [fixed((block, 1))] * 2,
        scratch_shapes=[VMEM((block, HD), F32), VMEM((block, HD), F32)],
        compiler_params=pltpu.CompilerParams(vmem_limit_bytes=60 * 2**20),
        name="attend_back",
    )(q, k, v, grad, lse, projected, projected, gq, gk, cosine, sine, seg_c, seg_r)


WIDE_IN = MODEL_WIDTH + 2 * SPAN
WIDE_OUT = MODEL_WIDTH + SPAN
CHUNK = 16
TERM_PARTS = 4
TERM_ROWS = MODEL_WIDTH // 4 + 2 * SPAN + SPAN + 2 * SPAN


def over_rows(count, body):
    def step(n, carry):
        body(pl.ds(pl.multiple_of(n * CHUNK, CHUNK), CHUNK))
        return carry

    lax.fori_loop(0, count // CHUNK, step, 0)


def wait_for(ref, sem):
    pltpu.make_async_copy(ref, ref, sem).wait()


def experts_kernel(n_c, experts, slots, comm, *refs):
    n_g = 10 if comm else 1
    x_ref, g_refs = refs[0], refs[1 : 1 + n_g]
    refs = refs[1 + n_g :]
    h_gu, h_d, h_id, h_iu, h_od, h_ou = refs[:6]
    refs = refs[6:]
    out_ref, row_ref, terms_o = refs[:3]
    refs = refs[3:]
    if comm:
        xg_ref, final, first_o = refs[:3]
        refs = refs[3:]
    else:
        xg_ref = x_ref
    (wb, db, xw, gw, xl, dr, gu, hl, dh, dgl, res, pick, gate, mom, mask) = refs[:15]
    (to, tr, gid, giu, god, gou, packed, wsem, csem, osem) = refs[15:25]
    refs = refs[25:]
    zh, zl, c, core = here()
    tok = xw.shape[1]
    extra = xw.shape[2] - MODEL_WIDTH
    tiles = n_c
    f = c * 2 + core
    near = lambda i: (
        lax.rem(c // 2 + i // 2, 2) * 2 + lax.rem(lax.rem(c, 2) + lax.rem(i, 2), 2)
    )

    def pair(ref, p):
        return ref.at[pl.ds(p * 2, 2)]

    def load_in(expert):
        yield pltpu.make_async_copy(h_id.at[expert], wb.at[:MODEL_WIDTH, MODEL_WIDTH:], wsem.at[0])
        yield pltpu.make_async_copy(h_gu.at[expert], wb.at[:MODEL_WIDTH, :MODEL_WIDTH], wsem.at[1])
        for j in range(2):
            rows = slice(MODEL_WIDTH + j * SPAN, MODEL_WIDTH + (j + 1) * SPAN)
            columns = slice(j * EXPERT_HIDDEN, (j + 1) * EXPERT_HIDDEN)
            yield pltpu.make_async_copy(h_iu.at[expert, j], wb.at[rows, columns], wsem.at[2 + j])

    def load_out(expert):
        yield pltpu.make_async_copy(h_d.at[expert], db.at[:EXPERT_HIDDEN, :MODEL_WIDTH], wsem.at[4])
        yield pltpu.make_async_copy(h_od.at[expert], db.at[:EXPERT_HIDDEN, MODEL_WIDTH:], wsem.at[5])
        yield pltpu.make_async_copy(h_ou.at[expert], db.at[EXPERT_HIDDEN:, :MODEL_WIDTH], wsem.at[6])

    terms = (gid, giu, god, gou)

    def term_copy(e):
        return pltpu.make_async_copy(packed, terms_o if comm else terms_o.at[:, e], osem.at[0])

    def send_first_terms():
        pltpu.make_async_copy(packed.at[seq], first_o.at[seq], osem.at[0]).start()
        for q in range(TERM_PARTS):

            @pl.when(seq != q)
            def _():
                remote(packed.at[q], first_o.at[seq], tsend.at[q], trecv.at[seq], (q // 2, q % 2, c, core)).start()

    def wait_first_terms(sent):
        for q in range(TERM_PARTS):

            @pl.when(seq != q)
            def _():
                if sent:
                    wait_for(packed.at[q], tsend.at[q])
                else:
                    wait_for(first_o.at[q], trecv.at[q])

        if sent:
            wait_for(packed.at[0], osem.at[0])

    def pack_terms():
        for q in range(TERM_PARTS):
            rows, columns = MODEL_WIDTH // 4, EXPERT_HIDDEN // 4
            packed[q, :rows] = gid[q * rows : (q + 1) * rows].astype(BF)
            for j in range(2):
                at = rows + j * SPAN
                packed[q, at : at + SPAN] = giu[j, :, q * columns : (q + 1) * columns].astype(BF)
            at = rows + 2 * SPAN
            for j in range(2):
                half = slice(j * SPAN, (j + 1) * SPAN)
                row = q * columns + j * SPAN
                packed[q, at : at + SPAN, half] = god[row : row + SPAN].astype(BF)
                column = q * rows + j * 256
                low = at + (j + 1) * SPAN
                packed[q, low : low + SPAN] = gou[:, column : column + 256].astype(BF)

    if comm:
        sib, la, lb, fx, fy, sums, sendx, recvx, sends, recvs, tsend, trecv = refs
        seq = zh * 2 + zl
        same = lambda i: (zh, zl, near(i), core)
        sibling = (zh, zl, c, 1 - core)
        low_half, high_half = pl.ds(0, tok // 2), pl.ds(tok // 2, tok // 2)
        column = [(zh ^ 1, zl, c, core), (zh, zl ^ 1, c, core), (zh ^ 1, zl ^ 1, c, core)]
        signal_all([sibling, same(1), same(2), *column])
        first = [
            remote(x_ref, xg_ref.at[f], sendx.at[n], recvx.at[n], to_)
            for n, to_ in enumerate((sibling, same(1), same(2)))
        ]
        for copy in first:
            copy.start()
        fx1, fy1, fd1 = near(1) * 2 + core, near(2) * 2 + core, near(3) * 2 + core
        forward = [
            remote(xg_ref.at[fx1, low_half], xg_ref.at[fx1, low_half], sendx.at[3], recvx.at[3], same(2)),
            remote(xg_ref.at[fy1, high_half], xg_ref.at[fy1, high_half], sendx.at[4], recvx.at[4], same(1)),
            remote(xg_ref.at[fx1], xg_ref.at[fx1], sendx.at[5], recvx.at[5], sibling),
            remote(xg_ref.at[fy1], xg_ref.at[fy1], sendx.at[6], recvx.at[6], sibling),
        ]
        across = remote(xg_ref.at[fd1], xg_ref.at[fd1], sendx.at[7], recvx.at[7], sibling)

    for copy in (*load_in(0), *load_out(0)):
        copy.start()
    spare = EXPERT_HIDDEN
    wb[MODEL_WIDTH : MODEL_WIDTH + SPAN, spare:] = jnp.zeros((SPAN, WIDE_IN - spare), BF)
    wb[MODEL_WIDTH + SPAN :, :spare] = jnp.zeros((SPAN, spare), BF)
    for ref in terms:
        ref[...] = jnp.zeros_like(ref)

    def order(s):
        e = s // tiles
        i = s + e * (2 * tiles - 1 - 2 * s)
        return e, i, (near(i) if comm else i)

    def fetch_x(p):
        return pltpu.make_async_copy(pair(xg_ref, p), xw, csem.at[0])

    def fetch_own():
        other = xg_ref.at[c * 2 + 1 - core]
        pltpu.make_async_copy(x_ref, xw.at[core], csem.at[0]).start()
        pltpu.make_async_copy(other, xw.at[1 - core], csem.at[0]).start()

    def fetch_g(i):
        if not comm:
            pltpu.make_async_copy(pair(g_refs[0], i), gw, csem.at[1]).start()
            return
        for n in range(4):

            @pl.when(i == n)
            def _():
                for k, held in ((core, g_refs[:5]), (1 - core, g_refs[5:])):
                    if n < 3:
                        pltpu.make_async_copy(held[n], gw.at[k], csem.at[1]).start()
                    else:
                        pltpu.make_async_copy(held[3], gw.at[k, low_half], csem.at[1]).start()
                        pltpu.make_async_copy(held[4], gw.at[k, high_half], csem.at[1]).start()

    if comm:
        fetch_g(0)
        wait_for(xg_ref.at[c * 2 + 1 - core], recvx.at[0])
        fetch_own()
    else:
        fetch_g(0)
        fetch_x(0).start()

    def write_out(p):
        return pltpu.make_async_copy(to, pair(out_ref, p), csem.at[2])

    def write_row(p):
        return pltpu.make_async_copy(tr, pair(row_ref, p), csem.at[3])

    def read_out(p):
        return pltpu.make_async_copy(pair(out_ref, p), to, csem.at[4])

    def read_row(p):
        return pltpu.make_async_copy(pair(row_ref, p), tr, csem.at[5])

    both = 2 * slots
    steps = 2 * tiles
    part = lambda d: slice(d * slots, (d + 1) * slots)
    pieces = [
        (
            slice(r, r + CHUNK),
            slice(h * 512, (h + 1) * 512),
            slice(EXPERT_HIDDEN + h * 512, EXPERT_HIDDEN + (h + 1) * 512),
        )
        for r in range(0, both, CHUNK)
        for h in range(2)
    ]

    def step(s, carry):
        e, i, p = order(s)
        _, after_i, after = order(jnp.minimum(s + 1, steps - 1))
        number = c * (2 * EXP_DEV) + core * EXP_DEV + e
        fetch_x(p).wait()
        wait_for(gw, csem.at[1])
        lane = lax.broadcasted_iota(jnp.int32, (tok, extra), 1)
        lane_s = lax.broadcasted_iota(jnp.int32, (slots, extra), 1)
        for d in range(2):
            side = xw[d, :, MODEL_WIDTH:].astype(F32)
            place = jnp.sum(jnp.where(lane == number, side, 0.0), axis=1, keepdims=True)
            slot = lax.broadcasted_iota(jnp.int32, (tok, slots), 1).astype(F32)
            pick[d] = jnp.where(slot == place, 1.0, 0.0).astype(BF)
            sub = lax.broadcasted_iota(jnp.int32, (extra, tok), 0)
            place_t = jnp.sum(jnp.where(sub == number, side.T, 0.0), axis=0, keepdims=True)
            slot_t = lax.broadcasted_iota(jnp.int32, (slots, tok), 0).astype(F32)
            pickt = jnp.where(slot_t == place_t, 1.0, 0.0).astype(BF)
            xl[part(d), :MODEL_WIDTH] = mm(pickt, xw[d, :, :MODEL_WIDTH]).astype(BF)
            dr[part(d), :MODEL_WIDTH] = mm(pickt, gw[d]).astype(BF)
            side = mm(pickt, xw[d, :, MODEL_WIDTH:])
            read = lambda which: jnp.sum(jnp.where(which, side, 0.0), axis=1, keepdims=True)
            gate[part(d)] = read((lane_s == experts + number) | (lane_s == 2 * experts + number))
            columns = lax.broadcasted_iota(jnp.int32, (slots, SPAN), 1) // ADAPTER_RANK
            mask[part(d)] = jnp.where(columns.astype(F32) == read(lane_s == 3 * experts), 1.0, 0.0)

        @pl.when((s > 0) & (s <= tiles) if comm else s > 0)
        def _():
            write_row(p).wait()

        @pl.when(s > 0)
        def _():
            write_out(p).wait()

        @pl.when(e > 0)
        def _():
            read_out(p).start()
            read_row(p).start()

        @pl.when(s == 0)
        def _():
            for copy in (*load_in(0), *load_out(0)):
                copy.wait()

        @pl.when(s == tiles)
        def _():
            for copy in (*load_in(1), *load_out(1), *(() if comm else (term_copy(0),))):
                copy.wait()
            for ref in terms:
                ref[...] = jnp.zeros_like(ref)

        mask2 = lambda: jnp.concatenate([mask[...], mask[...]], axis=1)
        xl[:, MODEL_WIDTH:] = (mm(xl[:, :MODEL_WIDTH], wb[:MODEL_WIDTH, MODEL_WIDTH:]) * mask2()).astype(BF)
        gu[...] = mm(xl[...], wb[:, :MODEL_WIDTH])

        for rows, a, b in pieces:
            gate_part = gu[rows, a]
            hl[rows, a] = (gate_part / (1.0 + jnp.exp(-gate_part)) * gu[rows, b]).astype(BF)
        hl[:, EXPERT_HIDDEN:] = (
            mm(hl[:, :EXPERT_HIDDEN], db[:EXPERT_HIDDEN, MODEL_WIDTH:]) * mask[...]
        ).astype(BF)
        for n in range(4):
            a = slice(n * 512, (n + 1) * 512)
            res[:, a] = (mm(hl[...], db[:, a]) * gate[...]).astype(BF)

        @pl.when(e > 0)
        def _():
            read_out(p).wait()

        def add_picked(target, d):
            for n in range(4):
                a = slice(n * 512, (n + 1) * 512)
                before = jnp.where(e > 0, target[d, :, a].astype(F32), 0.0)
                target[d, :, a] = (before + mm(pick[d], res[part(d), a])).astype(BF)

        for d in range(2):
            add_picked(to, d)
        write_out(p).start()

        @pl.when(s < steps - 1)
        def _():
            fetch_g(after_i)

        dr[:, MODEL_WIDTH:] = (
            mm_t(dr[:, :MODEL_WIDTH], db[EXPERT_HIDDEN:, :MODEL_WIDTH]) * mask[...]
        ).astype(BF)
        dh[...] = mm_t(dr[...], db[:EXPERT_HIDDEN, :])

        @pl.when(s == tiles - 1)
        def _():
            for copy in load_out(1):
                copy.start()

        mom[...] = jnp.zeros_like(mom)
        for rows, a, b in pieces:
            gate_part, up_part, grad = gu[rows, a], gu[rows, b], dh[rows, a]
            sigmoid = 1.0 / (1.0 + jnp.exp(-gate_part))
            activated = gate_part * sigmoid
            plain = grad * activated
            mom[rows] += jnp.sum(plain * up_part, axis=1, keepdims=True)
            dgl[rows, b] = (plain * gate[rows]).astype(BF)
            slope = sigmoid + activated - activated * sigmoid
            dgl[rows, a] = (grad * gate[rows] * up_part * slope).astype(BF)
        dgl[:, MODEL_WIDTH:] = (
            mm_t(dgl[:, :MODEL_WIDTH], wb[MODEL_WIDTH:, :MODEL_WIDTH]) * mask2()
        ).astype(BF)
        for n in range(4):
            a = slice(n * 512, (n + 1) * 512)
            res[:, a] = mm_t(dgl[...], wb[a, :]).astype(BF)

        @pl.when(s == tiles - 1)
        def _():
            for copy in load_in(1):
                copy.start()

        if comm:
            @pl.when(s == 0)
            def _():
                wait_for(xg_ref.at[fx1], recvx.at[1])
                forward[0].start()
                forward[2].start()
                wait_for(xg_ref.at[fy1], recvx.at[2])
                forward[1].start()
                forward[3].start()
                wait_for(xg_ref.at[fx1], recvx.at[5])

            @pl.when(s == 1)
            def _():
                wait_for(xg_ref.at[fd1, low_half], recvx.at[3])
                wait_for(xg_ref.at[fd1, high_half], recvx.at[4])
                across.start()
                wait_for(xg_ref.at[fy1], recvx.at[6])

            @pl.when(s == 2)
            def _():
                wait_for(xg_ref.at[fd1], recvx.at[7])

        @pl.when(s < steps - (2 if comm else 1))
        def _():
            fetch_x(after).start()

        if comm:

            @pl.when(s == steps - 2)
            def _():
                fetch_own()

        @pl.when(e > 0)
        def _():
            read_row(p).wait()

        for d in range(2):
            add_picked(tr, d)
            moment = mom[part(d)]
            high = moment.astype(BF).astype(F32)
            side = jnp.where(lane_s == number, high, 0.0) + jnp.where(
                lane_s == experts + number, moment - high, 0.0
            )
            before = jnp.where(e > 0, tr[d, :, MODEL_WIDTH:].astype(F32), 0.0)
            tr[d, :, MODEL_WIDTH:] = (before + mm(pick[d], side.astype(BF))).astype(BF)

        if comm:
            to_sibling = remote(
                tr.at[1 - core], sib.at[lax.rem(i, 2)], sends.at[lax.rem(i, 2)],
                recvs.at[lax.rem(i, 2)], sibling,
            )

            @pl.when(e == 0)
            def _():
                write_row(p).start()

            @pl.when(e > 0)
            def _():
                to_sibling.start()
        else:
            write_row(p).start()

        gid[...] += t_mm(xl[:, :MODEL_WIDTH], dgl[:, MODEL_WIDTH:])
        for j in range(2):
            giu[j] += t_mm(
                xl[:, MODEL_WIDTH + j * SPAN : MODEL_WIDTH + (j + 1) * SPAN],
                dgl[:, j * EXPERT_HIDDEN : (j + 1) * EXPERT_HIDDEN],
            )
        god[...] += t_mm(hl[:, :EXPERT_HIDDEN], (dr[:, MODEL_WIDTH:].astype(F32) * gate[...]).astype(BF))
        gou[...] += t_mm((hl[:, EXPERT_HIDDEN:].astype(F32) * gate[...]).astype(BF), dr[:, :MODEL_WIDTH])

        @pl.when(s == tiles - 1)
        def _():
            pack_terms()
            if comm:
                send_first_terms()
            else:
                term_copy(0).start()

        if comm:
            half = tok // 2

            def chip_sum(at, rows):
                return tr[core, rows].astype(F32) + sib[at, rows].astype(F32)

            @pl.when(e > 0)
            def _():
                to_sibling.wait()

            @pl.when(s == steps - 4)
            def _():
                def body(rows):
                    sums[0, rows] = chip_sum(1, rows).astype(BF)

                over_rows(tok, body)
                remote(sums.at[0, low_half], la, sends.at[2], recvs.at[2], same(1)).start()
                remote(sums.at[0, high_half], lb, sends.at[3], recvs.at[3], same(2)).start()

            @pl.when(s == steps - 3)
            def _():
                wait_for(la, recvs.at[2])

                def body(rows):
                    sums[1, rows] = (chip_sum(0, rows) + la[rows].astype(F32)).astype(BF)

                def rest(rows):
                    rows = pl.ds(pl.multiple_of(rows.start + half, CHUNK), CHUNK)
                    sums[1, rows] = chip_sum(0, rows).astype(BF)

                over_rows(half, body)
                over_rows(half, rest)
                remote(sums.at[1], fy, sends.at[4], recvs.at[4], same(2)).start()

            @pl.when(s == steps - 2)
            def _():
                wait_for(lb, recvs.at[3])

                def body(rows):
                    sums[2, rows] = chip_sum(1, rows).astype(BF)

                def rest(rows):
                    upper = pl.ds(pl.multiple_of(rows.start + half, CHUNK), CHUNK)
                    sums[2, upper] = (chip_sum(1, upper) + lb[rows].astype(F32)).astype(BF)

                over_rows(half, body)
                over_rows(half, rest)
                remote(sums.at[2], fx, sends.at[5], recvs.at[5], same(1)).start()

        return carry

    lax.fori_loop(0, steps, step, 0)
    if comm:
        wait_first_terms(True)
    pack_terms()
    term_copy(1).start()
    _, _, last = order(steps - 1)
    write_out(last).wait()
    if comm:
        wait_for(fx, recvs.at[5])
        wait_for(fy, recvs.at[4])

        def body(rows):
            total = tr[core, rows].astype(F32) + sib[0, rows].astype(F32)
            final[rows] = (total + (fx[rows].astype(F32) + fy[rows].astype(F32))).astype(BF)

        over_rows(tok, body)
        wait_for(la, sends.at[2])
        wait_for(lb, sends.at[3])
        wait_for(fy, sends.at[4])
        wait_for(fx, sends.at[5])
        for copy in first:
            copy.wait_send()
        for copy in forward:
            copy.wait_send()
        across.wait_send()
        wait_first_terms(False)
    else:
        write_row(last).wait()
    term_copy(1).wait()


def run_experts(x, g, weights, experts, slots, n_c, comm):
    tok, wide = x.shape[-2:]
    sources = 2 * n_c
    both = 2 * slots
    dma = pltpu.SemaphoreType.DMA
    term_shapes = (
        (MODEL_WIDTH, 2 * SPAN),
        (2, SPAN, EXPERT_HIDDEN),
        (EXPERT_HIDDEN, SPAN),
        (SPAN, MODEL_WIDTH),
    )
    any_spec = pl.BlockSpec(memory_space=ANY)
    out_shape = [
        jax.ShapeDtypeStruct((sources, tok, MODEL_WIDTH), BF),
        jax.ShapeDtypeStruct((sources, tok, wide), BF),
        jax.ShapeDtypeStruct(
            (TERM_PARTS, TERM_ROWS, 256) if comm else (TERM_PARTS, EXP_DEV, TERM_ROWS, 256), BF
        ),
    ]
    out_specs = [any_spec] * 3
    scratch = [
        VMEM((WIDE_IN, WIDE_IN), BF),
        VMEM((EXPERT_HIDDEN + SPAN, WIDE_OUT), BF),
        VMEM((2, tok, wide), BF),
        VMEM((2, tok, MODEL_WIDTH), BF),
        VMEM((both, WIDE_IN), BF),
        VMEM((both, WIDE_OUT), BF),
        VMEM((both, MODEL_WIDTH), F32),
        VMEM((both, EXPERT_HIDDEN + SPAN), BF),
        VMEM((both, EXPERT_HIDDEN), F32),
        VMEM((both, WIDE_IN), BF),
        VMEM((both, MODEL_WIDTH), BF),
        VMEM((2, tok, slots), BF),
        VMEM((both, 1), F32),
        VMEM((both, 1), F32),
        VMEM((both, SPAN), F32),
        VMEM((2, tok, MODEL_WIDTH), BF),
        VMEM((2, tok, wide), BF),
        *(VMEM(s, F32) for s in term_shapes),
        VMEM((TERM_PARTS, TERM_ROWS, 256), BF),
        dma((7,)),
        dma((6,)),
        dma((1,)),
    ]
    params = {}
    if comm:
        out_shape += [
            jax.ShapeDtypeStruct((sources, tok, wide), BF),
            jax.ShapeDtypeStruct((tok, wide), BF),
            jax.ShapeDtypeStruct((TERM_PARTS, TERM_ROWS, 256), BF),
        ]
        out_specs += [any_spec, pl.BlockSpec(memory_space=VMEM), any_spec]
        scratch += [
            VMEM((2, tok, wide), BF),
            VMEM((tok // 2, wide), BF),
            VMEM((tok // 2, wide), BF),
            VMEM((tok, wide), BF),
            VMEM((tok, wide), BF),
            VMEM((3, tok, wide), BF),
            dma((8,)),
            dma((8,)),
            dma((6,)),
            dma((6,)),
            dma((TERM_PARTS,)),
            dma((TERM_PARTS,)),
        ]
        params = dict(collective_id=6, has_side_effects=True)
    flops = 2 * sources * EXP_DEV * slots * MODEL_WIDTH * EXPERT_HIDDEN * 8
    g = g if comm else [g]
    results = pl.pallas_call(
        functools.partial(experts_kernel, n_c, experts, slots, comm),
        out_shape=out_shape,
        in_specs=[any_spec] * (7 + len(g)),
        out_specs=out_specs,
        scratch_shapes=scratch,
        compiler_params=pltpu.CompilerParams(vmem_limit_bytes=63 * 2**20, **params),
        cost_estimate=pl.CostEstimate(flops=flops, bytes_accessed=10**8, transcendentals=10**7),
        name="experts",
    )(x, *g, *weights)
    if comm:
        return results[0], results[4], (results[5], results[2])
    return results[0], results[1], results[2]


def late_kernel(n_f, dp, up, mask, low, x, both, packed):
    core = lax.axis_index("core")
    down_rows = MODEL_WIDTH // (4 * n_f)
    up_rows = SPAN // n_f
    base = 12 * down_rows
    packed[:, base:] = jnp.zeros((n_f, 24 * up_rows, SPAN), BF)
    for j in range(3):
        own = slice(j * SPAN, (j + 1) * SPAN)
        wide = slice(j * GROUP_WIDTH, (j + 1) * GROUP_WIDTH)
        lowered = (mm_t(dp[:, wide], up[own]) * mask[...]).astype(BF)
        both[:, wide] = dp[:, wide]
        both[:, 3 * GROUP_WIDTH + j * SPAN : 3 * GROUP_WIDTH + (j + 1) * SPAN] = lowered
        grad_up = t_mm(low[:, own], dp[:, wide]).astype(BF)
        grad_down = t_mm(x[...], lowered).astype(BF)
        for f in range(n_f):
            for b in range(4):
                at = base + (j * 8 + core * 4 + b) * up_rows
                packed[f, pl.ds(pl.multiple_of(at, up_rows), up_rows)] = grad_up[
                    f * up_rows : (f + 1) * up_rows, b * SPAN : (b + 1) * SPAN
                ]
            for q in range(4):
                row = (q * n_f + f) * down_rows
                at = (q * 3 + j) * down_rows
                packed[f, at : at + down_rows] = grad_down[row : row + down_rows]


def late_gradients(grad_projected, up_own, mask, lowered, x, n_f):
    block = x.shape[0]
    rows = 12 * MODEL_WIDTH // (4 * n_f) + 24 * SPAN // n_f
    return pl.pallas_call(
        functools.partial(late_kernel, n_f),
        out_shape=(
            jax.ShapeDtypeStruct((block, PROJECT_WIDTH), BF),
            jax.ShapeDtypeStruct((n_f, rows, SPAN), BF),
        ),
        in_specs=[pl.BlockSpec(memory_space=VMEM)] * 5,
        out_specs=[pl.BlockSpec(memory_space=VMEM)] * 2,
        compiler_params=pltpu.CompilerParams(vmem_limit_bytes=50 * 2**20),
        cost_estimate=pl.CostEstimate(flops=4 * 10**9, bytes_accessed=2 * 10**7, transcendentals=0),
        name="late_gradients",
    )(grad_projected, up_own, mask, lowered, x)


def plane_rows(rows):
    half = rows.shape[0] // 2
    along_x = lambda t: lax.ppermute(t, "c", [(0, 1), (1, 0), (2, 3), (3, 2)])
    along_y = lambda t: lax.ppermute(t, "c", [(0, 2), (2, 0), (1, 3), (3, 1)])
    to_sibling = lambda t: lax.ppermute(t, "core", [(0, 1), (1, 0)])
    beside, above = along_x(rows), along_y(rows)
    parts = [rows, beside, above, along_y(beside[:half]), along_x(above[half:])]
    return parts + [to_sibling(t) for t in parts]


def on_device(
    tokens,
    cotangent,
    lengths,
    sets,
    routes,
    gain_attn,
    gain_query,
    gain_key,
    gain_mlp,
    query_key_value_weight,
    out_weight,
    router_weight,
    gate_up_weight,
    down_weight,
    attention_down_factors,
    attention_up_factors,
    router_down_factors,
    router_up_factors,
    expert_input_down,
    expert_input_up,
    expert_output_down,
    expert_output_up,
):
    zh, zl, c, core = here()
    n_c = lax.axis_size("c")
    n_fsdp = 2 * n_c
    n_seq = lax.axis_size("zh") * lax.axis_size("zl")
    tok = tokens.shape[1]
    block = tok * n_seq
    experts = EXP_DEV * n_fsdp
    capacity = 5 * tok * TOP // (4 * experts)
    slots = -(-capacity // 16) * 16
    extra = -(-(3 * experts + 1) // 128) * 128
    span3 = 3 * SPAN
    group = zl * 2 + core
    shard = zh * 2 + zl

    both_lengths = lax.all_gather(
        jnp.concatenate([lengths[0], sets[0]]), "core", axis=0, tiled=False
    )
    held_lengths = lax.dynamic_index_in_dim(both_lengths, zh, 0, keepdims=False)
    count = lengths.shape[1]

    inputs = tokens[0].astype(F32)
    normalized = rms_scale(inputs, gain_attn).astype(BF)
    seq_block, block_offsets, block_sets = token_meta(
        held_lengths[:count], held_lengths[count:], jnp.arange(block, dtype=jnp.int32)
    )
    mask1 = set_mask(block_sets)
    if n_c == 4:
        x_shards, head_rows, up_group, projected, lowered = gather_project(
            normalized,
            query_key_value_weight,
            attention_down_factors[:, :span3],
            attention_up_factors,
            mask1.reshape(4, tok, SPAN),
        )
        projected, lowered = projected.reshape(block, -1), lowered.reshape(block, span3)
        up_own = up_group[:span3]
    else:
        x_shards, qkv_rows = gather_to_heads(normalized, query_key_value_weight, n_c)

    first_column = span3 if n_c == 4 else 0
    rows_local = query_key_value_weight.shape[0]
    factors = jnp.concatenate(
        [
            attention_down_factors[:, first_column:],
            attention_up_factors.reshape(rows_local, -1),
            router_down_factors,
            router_weight,
            router_up_factors.reshape(rows_local, -1),
        ],
        axis=1,
    )
    factor_width = factors.shape[1]
    factors = jnp.pad(factors, ((0, 0), (0, -factor_width % 128)))
    factors = lax.all_gather(factors, FSDP, axis=0, tiled=True)
    up_columns = attention_up_factors.size // rows_local
    at = 4 * SPAN - first_column
    down_full = factors[:, :at]
    down_o = down_full[:, span3 - first_column :]
    up_full = factors[:, at : at + up_columns].reshape(4 * SPAN, MODEL_WIDTH)
    at += up_columns
    rdown_full = factors[:, at : at + SPAN]
    at += SPAN
    router_full = factors[:, at : at + experts]
    at += experts
    rup_full = factors[:, at:factor_width].reshape(SPAN, experts)
    if n_c == 4:
        projected, out_weight, rows = lax.optimization_barrier(
            (projected, out_weight, cotangent[0])
        )
        grads_all = plane_rows(rows)
    else:
        grads_all = lax.all_gather(cotangent[0], FSDP, axis=0, tiled=False)
    out_full = lax.all_gather(out_weight, FSDP, axis=0, tiled=True)

    seq_local, _, chosen = token_meta(
        lengths[0], sets[0], shard * tok + jnp.arange(tok, dtype=jnp.int32)
    )
    mask = set_mask(chosen)
    half = HD // 2
    freqs = THETA ** (-(jnp.arange(half, dtype=F32) * 2.0 / HD))
    angles = block_offsets.astype(F32)[:, None] * freqs[None, :]
    cosine, sine = jnp.cos(angles), jnp.sin(angles)
    cosine = jnp.concatenate([cosine, cosine], axis=1)
    sine = jnp.concatenate([-sine, sine], axis=1)
    seg_c, seg_r = seq_block[:, None], seq_block[None, :]

    x_all = x_shards.reshape(block, MODEL_WIDTH)
    if n_c != 4:
        mask3 = jnp.tile(mask1, (1, 3))
        down3 = down_full[:, :span3]
        lowered = (mm(x_all, down3) * mask3).astype(BF)
        up_own = lax.dynamic_slice_in_dim(up_full[:span3], group * GROUP_WIDTH, GROUP_WIDTH, 1)
        none = jnp.zeros((SPAN, GROUP_WIDTH), BF)
        up_diagonal = jnp.concatenate(
            [
                jnp.concatenate(
                    [up_own[j * SPAN : (j + 1) * SPAN] if i == j else none for i in range(3)], axis=1
                )
                for j in range(3)
            ],
            axis=0,
        )
        projected = mm(x_all, qkv_rows) + mm(lowered, up_diagonal)
    part_q, part_k = projected[:, :GROUP_WIDTH], projected[:, GROUP_WIDTH : 2 * GROUP_WIDTH]

    def over_group(first, second, identity):
        both = jnp.stack([first, second]).reshape(-1, 128)
        return group_sum(both, identity).reshape(2, block)

    squares = over_group(jnp.sum(part_q * part_q, axis=1), jnp.sum(part_k * part_k, axis=1), 4)
    inverse = lax.rsqrt(squares / MODEL_WIDTH + EPSILON)
    rq, rk = inverse[0][:, None], inverse[1][:, None]
    gains = [
        lax.dynamic_slice_in_dim(g, group * GROUP_WIDTH, GROUP_WIDTH)[None, :]
        for g in (gain_query, gain_key)
    ]
    if n_c == 4:
        q, k, v, lse, attended = attend_send(
            projected, rq, rk, *gains, cosine, sine, seg_c, seg_r
        )
    else:
        q, k, v, attended_heads, lse = attend(
            projected, rq, rk, *gains, cosine, sine, seg_c, seg_r
        )
        attended = to_tokens(attended_heads.reshape(4, tok, GROUP_WIDTH))

    up_o = up_full[span3:]
    out_lower = (mm(attended, down_o) * mask).astype(BF)
    branch = mm(attended, out_full) + mm(out_lower, up_o)
    middle = inputs + branch
    normed2 = rms_scale(middle, gain_mlp).astype(BF)
    router_lower = (mm(normed2, rdown_full) * mask).astype(BF)
    logits = mm(normed2, router_full) + mm(router_lower, rup_full)
    probs = jax.nn.softmax(logits, axis=-1)
    hits = jnp.sum(
        (routes[0][:, :, None] == jnp.arange(experts, dtype=jnp.int32)[None, None, :]).astype(F32),
        axis=1,
    )
    place = jnp.arange(tok, dtype=jnp.int32)
    before = (place[None, :] < place[:, None]).astype(BF)
    ranks = jnp.where(hits > 0, mm(before, hits.astype(BF)), -1.0).astype(BF)
    gates = hits * probs
    gates_high = gates.astype(BF)
    gates_low = (gates - gates_high.astype(F32)).astype(BF)
    side = jnp.concatenate(
        [ranks, gates_high, gates_low, chosen.astype(BF)[:, None]], axis=1
    )
    payload = jnp.concatenate(
        [normed2, jnp.pad(side, ((0, 0), (0, extra - side.shape[1])))], axis=1
    )
    weights = (
        gate_up_weight,
        down_weight,
        expert_input_down,
        expert_input_up,
        expert_output_down,
        expert_output_up,
    )
    if n_c == 4:
        out_parts, returned, expert_terms = run_experts(
            payload, grads_all, weights, experts, slots, n_c, True
        )
    else:
        rows_all = lax.all_gather(payload, FSDP, axis=0, tiled=True)
        out_parts, row_parts, expert_terms = run_experts(
            rows_all.reshape(n_fsdp, tok, -1), grads_all, weights, experts, slots, n_c, False
        )
        returned = lax.psum_scatter(
            row_parts.reshape(n_fsdp * tok, -1), FSDP, scatter_dimension=0, tiled=True
        )
    mixed = lax.psum_scatter(
        out_parts.reshape(n_fsdp * tok, -1), FSDP, scatter_dimension=0, tiled=True
    )
    grad_out = cotangent[0].astype(F32)
    returned = returned.astype(F32)
    back = returned[:, MODEL_WIDTH:]
    grad_probs = back[:, :experts] + back[:, experts : 2 * experts]
    grad_logits = probs * (grad_probs - jnp.sum(probs * grad_probs, axis=-1, keepdims=True))
    grad_router_lower = exact("te,re->tr", grad_logits, rup_full.astype(F32)) * mask
    grad_normed2 = (
        returned[:, :MODEL_WIDTH]
        + mm_t(grad_logits.astype(BF), router_full)
        + mm_t(grad_router_lower.astype(BF), rdown_full)
    )
    grad_rup = t_mm(router_lower, grad_logits.astype(BF))
    grad_rdown = t_mm(normed2, grad_router_lower.astype(BF))
    grad_middle = grad_out + rms_back(middle, gain_mlp, grad_normed2)
    grad_branch = grad_middle.astype(BF)
    grad_out_lower = (mm_t(grad_branch, up_o) * mask).astype(BF)
    grad_attended = (mm_t(grad_branch, out_full) + mm_t(grad_out_lower, down_o)).astype(BF)
    head_grad = to_heads(grad_attended).reshape(block, GROUP_WIDTH)
    if n_c == 4:
        first_terms, second_terms = expert_terms
        second_terms, head_grad = lax.optimization_barrier((second_terms, head_grad))
        second_terms = lax.all_to_all(second_terms, SEQ, split_axis=0, concat_axis=0, tiled=True)
    else:
        expert_terms = lax.psum_scatter(expert_terms, SEQ, scatter_dimension=0, tiled=True)
    grad_up_o = t_mm(out_lower, grad_branch)
    grad_down_o = t_mm(attended, grad_out_lower)
    if n_c == 4:
        up_rows = SPAN // n_fsdp
        up_blocks = grad_up_o.astype(BF).reshape(n_fsdp, up_rows, 16, SPAN).transpose(0, 2, 1, 3)
        by_owner = lambda t: t.astype(BF).reshape(n_seq, n_fsdp, -1, SPAN).transpose(1, 0, 2, 3)
        rup_rows = jnp.pad(grad_rup.reshape(n_seq * n_fsdp, 1, -1), ((0, 0), (0, 15), (0, 0)))
        rup_rows = jnp.pad(rup_rows, ((0, 0), (0, 0), (0, SPAN - rup_rows.shape[2])))
        rest = jnp.concatenate(
            [by_owner(grad_down_o), by_owner(grad_rdown), by_owner(rup_rows)], axis=2
        )
        early = jnp.concatenate(
            [up_blocks.reshape(n_fsdp, -1, SPAN), rest.reshape(n_fsdp, -1, SPAN)], axis=1
        )

    uq, uk, grad_v, mq, mk = attend_back(
        q, k, v, head_grad, lse, projected, *gains, cosine, sine, seg_c, seg_r
    )
    moments = over_group(mq[:, 0], mk[:, 0], 5) / MODEL_WIDTH

    def rms_inner(values, scale, gain, turned, moment):
        return (scale * gain * turned - values * (scale * scale * scale) * moment).astype(BF)

    grad_projected = jnp.concatenate(
        [
            rms_inner(part_q, rq, gains[0], uq, moments[0][:, None]),
            rms_inner(part_k, rk, gains[1], uk, moments[1][:, None]),
            grad_v,
        ],
        axis=1,
    )
    if n_c == 4:
        both, late = late_gradients(
            grad_projected, up_own, mask1, lowered, x_all, n_fsdp
        )
    else:
        grad_lowered = (mm_t(grad_projected, up_diagonal) * mask3).astype(BF)
    if n_c == 4:
        output, grad_inputs, *summed = finish(
            both,
            head_rows,
            late,
            early,
            middle,
            mixed,
            tokens[0],
            grad_middle,
            gain_attn[None, :],
            n_c,
        )
    else:
        grad_normed_part = (
            mm_t(grad_projected, qkv_rows) + mm_t(grad_lowered, down3)
        ).astype(BF)
        grad_normed = sum_to_tokens(grad_normed_part.reshape(4, tok, MODEL_WIDTH))
        grad_inputs = grad_middle + rms_back(inputs, gain_attn, grad_normed)
        output = (middle + mixed.astype(F32)).astype(BF)

    rup_shape = (SPAN // (n_seq * n_fsdp), experts)
    if n_c == 4:
        summed[3] = summed[3][0, : rup_shape[0] * rup_shape[1]].reshape(rup_shape)
    else:
        grad_up_own = [
            t_mm(
                lowered[:, j * SPAN : (j + 1) * SPAN],
                grad_projected[:, j * GROUP_WIDTH : (j + 1) * GROUP_WIDTH],
            )
            for j in range(3)
        ]
        grad_down_qkv = t_mm(x_all, grad_lowered)
        grad_down_all = jnp.concatenate([grad_down_qkv, grad_down_o], axis=1).astype(BF)
        wide_up = lax.dynamic_update_slice_in_dim(
            jnp.zeros((span3, MODEL_WIDTH), F32),
            jnp.concatenate(grad_up_own, axis=0),
            group * GROUP_WIDTH,
            1,
        )
        grad_up_all = jnp.concatenate([wide_up, grad_up_o], axis=0).astype(BF)
        terms = (grad_down_all, grad_up_all, grad_rdown.astype(BF), grad_rup.astype(BF))
        own_shapes = [(t.shape[0] // (n_seq * n_fsdp), t.shape[1]) for t in terms]
        flat = jnp.concatenate(
            [t.reshape(n_seq, n_fsdp, -1).transpose(1, 0, 2) for t in terms], axis=2
        )
        used = flat.shape[2]
        flat = jnp.pad(flat, ((0, 0), (0, 0), (0, -used % 1024))).reshape(n_fsdp * n_seq, -1, 128)
        flat = lax.psum_scatter(flat, FSDP, scatter_dimension=0, tiled=True)
        flat = lax.psum_scatter(flat, SEQ, scatter_dimension=0, tiled=True)
        flat = flat.astype(F32).reshape(-1)
        summed, at = [], 0
        for shape in own_shapes:
            size = shape[0] * shape[1]
            summed.append(flat[at : at + size].reshape(shape))
            at += size

    if n_c == 4:
        expert_terms = jnp.stack(
            [jnp.sum(t.astype(F32), axis=0) for t in (first_terms, second_terms)]
        )
    else:
        expert_terms = expert_terms[0].astype(F32)
    rows = MODEL_WIDTH // 4
    at = rows + 2 * SPAN
    halves = expert_terms[:, at : at + SPAN]
    low = at + SPAN
    expert_sums = [
        expert_terms[:, :rows],
        expert_terms[:, rows:at].reshape(EXP_DEV, 2, SPAN, EXPERT_HIDDEN // 4),
        jnp.concatenate([halves[..., :SPAN], halves[..., SPAN:]], axis=1),
        jnp.concatenate(
            [expert_terms[:, low : low + SPAN], expert_terms[:, low + SPAN : low + 2 * SPAN]],
            axis=2,
        ),
    ]
    return (output[None], grad_inputs[None], *summed, *expert_sums)


def solution(mesh):
    n_seq, n_fsdp = mesh.shape["seq"], mesh.shape["fsdp"]
    fine = Mesh(
        mesh.devices.reshape(2, n_seq // 2, n_fsdp // 2, 2), ("zh", "zl", "c", "core")
    )
    split = P(FSDP, SEQ, None)
    rows = P(FSDP, None)
    three = P(FSDP, None, None)
    in_specs = (
        split,
        split,
        rows,
        rows,
        split,
        P(),
        P(),
        P(),
        P(),
        rows,
        rows,
        rows,
        three,
        three,
        rows,
        rows,
        rows,
        rows,
        three,
        P(FSDP, None, None, None),
        three,
        three,
    )
    owners = P((*SEQ, *FSDP), None)
    out_specs = (
        split,
        split,
        owners,
        owners,
        owners,
        owners,
        split,
        P(FSDP, None, None, SEQ),
        split,
        P(FSDP, None, SEQ),
    )
    return jax.shard_map(
        on_device, mesh=fine, in_specs=in_specs, out_specs=out_specs, check_vma=False
    )
```
